32 devices in a mesh: dp: 4 (over z), expert: 8 (over y, x, core).
Axes of the slice: x: 2, y: 2, z: 4, core: 2. Of those that a mesh axis runs over, the one named last changes fastest.
Arguments:
- tokens: bfloat16 [1024, 2048], P('dp'), may hold values from -6 to 6
- expert_ids: int32 [1024, 8], P('dp', 'expert'), may hold values from 0 to 15, as said below
- gates: float32 [1024, 8], P('dp', 'expert'), may hold values from 0.05 to 0.25
- positives: int32 [16], P('dp'), may hold values from 0 to 15, as said below
- gate_up: bfloat16 [32, 2048, 768], P(('dp', 'expert')), may hold values from -0.125 to 0.125
- down: bfloat16 [32, 384, 2048], P(('dp', 'expert')), may hold values from -0.21875 to 0.21875
Outputs:
- layer_out: bfloat16 [1024, 2048], P('dp')
- grad_gate_up: bfloat16 [32, 2048, 768], P(('dp', 'expert'))
- grad_down: bfloat16 [32, 384, 2048], P(('dp', 'expert'))
The draws below stay inside these ranges and needn't reach their ends.
Inputs may be any that keep to these rules, and one draw needn't show every extreme that they name: `expert_ids`: each row names 8 different experts. In the 256 rows of one index of dp no expert is named more than 32 times in one column, and in each column one expert is named exactly 32 times in the rows of every index of dp. positives[i] != i and positives[positives[i]] = i.
All inputs are finite; a program needn't handle non-finite values.
Results may differ from the reference program's by a relative error of at most 0.015.
Values may be sent and summed in bfloat16 or wider, within the bound.
No kernel may reach another device: no remote copies, remote signals or barrier semaphores. Data moves between devices by JAX's collectives and lax.ppermute only.
A program may use at most 128 MiB of HBM per device.

```python
import jax
import jax.numpy as jnp
from jax import lax

D = 2048
FF = 768
TOPK = 8
TOK_DEV = 256
LENGTH = 64
EXPERTS = 16
SLICES = 32
HALF = 384
CAP = 32
TOKENS = 1024
SEQS = 16


def draw_expert_ids(key, part):
    base_key = jax.random.fold_in(key, 101)
    key_hot, key_offsets, key_blocks = jax.random.split(base_key, 3)
    hot_expert = jax.random.randint(key_hot, (), 0, EXPERTS).astype(jnp.int32)
    offsets = jax.random.permutation(key_offsets, EXPERTS)[:TOPK].astype(jnp.int32)
    hot_columns = (hot_expert + offsets) % EXPERTS
    labels = jnp.arange(EXPERTS, dtype=jnp.int32)
    is_hot = jnp.any(labels[:, None] == hot_columns[None, :], axis=1)
    pool_values = (hot_expert + 1 + jnp.arange((EXPERTS - 1) * CAP, dtype=jnp.int32) // CAP) % EXPERTS

    def one_block(block_key):
        key_pool, key_order, key_labels = jax.random.split(block_key, 3)
        chosen = jax.random.permutation(key_pool, pool_values)[:TOK_DEV - CAP].astype(jnp.int32)
        base_values = jnp.concatenate([jnp.full((CAP,), hot_expert, jnp.int32), chosen])
        base_values = jax.random.permutation(key_order, base_values)
        shifted = (base_values[:, None] + offsets[None, :]) % EXPERTS
        ranks = jax.random.permutation(key_labels, EXPERTS).astype(jnp.int32)
        first_order = jnp.argsort(jnp.where(is_hot, EXPERTS + labels, labels), stable=True)
        second_order = jnp.argsort(jnp.where(is_hot, EXPERTS + labels, ranks), stable=True)
        relabel = jnp.zeros((EXPERTS,), jnp.int32).at[first_order].set(second_order.astype(jnp.int32))
        return relabel[shifted]
    block_keys = jax.random.split(key_blocks, TOKENS // TOK_DEV)
    return jax.vmap(one_block)(block_keys).reshape(TOKENS, TOPK).astype(jnp.int32)


def draw_positives(key, part):
    pair_key = jax.random.fold_in(key, 202)
    order = jax.random.permutation(pair_key, SEQS).astype(jnp.int32)
    first_members = order[0::2]
    second_members = order[1::2]
    partner = jnp.zeros((SEQS,), jnp.int32)
    partner = partner.at[first_members].set(second_members)
    partner = partner.at[second_members].set(first_members)
    return partner


def block_scale(rng, dims, cuts, smallest, largest):
    factor_of, own = 1.0, jax.random.fold_in(rng, 6)
    for dim, blocks in cuts:
        steps = jnp.exp(jax.random.uniform(jax.random.fold_in(own, dim), (blocks,), jnp.float32, smallest / len(cuts), largest / len(cuts)))
        factor_of = factor_of * jnp.repeat(steps, dims[dim] // blocks).reshape([-1 if axis == dim else 1 for axis in range(len(dims))])
    return factor_of


def centred(key, extent, deviation, reach, cuts=(), kind=jnp.bfloat16):
    level = block_scale(key, extent, cuts, -0.22, 0.18) if cuts else 1.0
    values = jax.random.normal(key, extent, jnp.float32) * deviation * level
    return jnp.minimum(jnp.maximum(values, -reach), reach).astype(kind)


def setup_inputs(seed: int = 0) -> dict:
    splits = jax.random.split(jax.random.key(seed), 7)
    return {
        "tokens": centred(splits[0], (TOKENS, D), 1.0, 6.0, ((0, 4),)),
        "expert_ids": draw_expert_ids(jax.random.fold_in(splits[6], 71), 0),
        "gates": jnp.clip(0.05 + 0.2 * jax.random.uniform(splits[2], (TOKENS, TOPK), jnp.float32) ** block_scale(splits[2], (TOKENS, TOPK), ((0, 4), (1, 8)), -0.2, 0.2), 0.05, 0.25),
        "positives": draw_positives(jax.random.fold_in(splits[6], 71), 0),
        "gate_up": centred(splits[4], (SLICES, D, 2 * HALF), D ** -0.5, 0.125, ((0, 32),)),
        "down": centred(splits[5], (SLICES, HALF, D), FF ** -0.5, 0.21875, ((0, 32),)),
    }


logit_divisor = 0.05
grad_scale = 256.0
epsilon = 1e-06

def row_tables(expert_ids):
    blocks = TOKENS // TOK_DEV
    rows_each = blocks * TOPK * CAP
    grouped = expert_ids.reshape(blocks, TOK_DEV, TOPK)
    onehot = (grouped[..., None] == jnp.arange(EXPERTS, dtype=jnp.int32)).astype(jnp.int32)
    before = jnp.cumsum(onehot, axis=1) - onehot
    position = lax.optimization_barrier(jnp.sum(before * onehot, axis=3))
    block_index = jnp.arange(blocks, dtype=jnp.int32)[:, None, None]
    column = jnp.arange(TOPK, dtype=jnp.int32)[None, None, :]
    target = grouped * rows_each + (block_index * TOPK + column) * CAP + position
    token_index = block_index * TOK_DEV + jnp.arange(TOK_DEV, dtype=jnp.int32)[None, :, None]
    token_index = jnp.broadcast_to(token_index, (blocks, TOK_DEV, TOPK))
    table = jnp.full((EXPERTS * rows_each,), TOKENS, jnp.int32)
    table = table.at[target.reshape(-1)].set(token_index.reshape(-1))
    return table.reshape(EXPERTS, rows_each)

def expert_half(expert_rows, weight_in):
    projected = jnp.dot(expert_rows, weight_in, preferred_element_type=jnp.float32)
    gate_part = projected[:, :HALF]
    up_part = projected[:, HALF:]
    sigmoid_gate = jax.nn.sigmoid(gate_part)
    activated = gate_part * sigmoid_gate
    hidden = (activated * up_part).astype(jnp.bfloat16)
    return (gate_part, up_part, sigmoid_gate, activated, hidden)

def reference(tokens, expert_ids, gates, positives, gate_up, down):
    table = row_tables(expert_ids)
    rows_each = table.shape[1]
    column_of_row = jnp.arange(rows_each, dtype=jnp.int32) // CAP % TOPK
    tokens_padded = jnp.concatenate([tokens, jnp.zeros((1, D), tokens.dtype)], axis=0)
    gates_padded = jnp.concatenate([gates, jnp.zeros((1, TOPK), gates.dtype)], axis=0)
    weights_in = gate_up.reshape(EXPERTS, 2, D, 2 * HALF)
    weights_out = down.reshape(EXPERTS, 2, HALF, D)

    def forward_step(accumulated, item_parts):
        entries, pair_in, pair_out = item_parts
        expert_rows = tokens_padded[entries]
        route_total = jnp.zeros((rows_each, D), jnp.float32)
        for half_index in range(2):
            hidden = expert_half(expert_rows, pair_in[half_index])[4]
            half_out = jnp.dot(hidden, pair_out[half_index], preferred_element_type=jnp.float32).astype(jnp.bfloat16)
            route_total = route_total + lax.optimization_barrier(half_out).astype(jnp.float32)
        weight = gates_padded[entries, column_of_row]
        return (accumulated.at[entries].add(weight[:, None] * route_total), None)
    accumulated, _ = lax.scan(forward_step, jnp.zeros((TOKENS + 1, D), jnp.float32), (table, weights_in, weights_out))
    layer_out = (tokens.astype(jnp.float32) + accumulated[:TOKENS]).astype(jnp.bfloat16)
    last_rows = layer_out[LENGTH - 1::LENGTH]
    last_values = last_rows.astype(jnp.float32)
    embedding_lengths = jnp.sqrt(lax.optimization_barrier(jnp.sum(last_values * last_values, axis=1)) + epsilon)
    unit_length_embeddings = last_values / embedding_lengths[:, None]
    pairwise_dots = jnp.dot(last_rows, last_rows.T, preferred_element_type=jnp.float32)
    cosine_logits = pairwise_dots / (embedding_lengths[:, None] * embedding_lengths[None, :]) / logit_divisor
    seq_index = jnp.arange(SEQS, dtype=jnp.int32)
    keep_mask = seq_index[:, None] != seq_index[None, :]
    exp_scores = jnp.where(keep_mask, jnp.exp(cosine_logits), 0.0)
    probabilities = exp_scores / lax.optimization_barrier(jnp.sum(exp_scores, axis=1, keepdims=True))
    target = (seq_index[None, :] == positives[:, None]).astype(jnp.float32)
    objective_multiplier = grad_scale * (probabilities - target)
    slope_wrt_unit_embedding = (jnp.dot(objective_multiplier, unit_length_embeddings, precision=lax.Precision.HIGHEST, preferred_element_type=jnp.float32) + jnp.dot(objective_multiplier.T, unit_length_embeddings, precision=lax.Precision.HIGHEST, preferred_element_type=jnp.float32)) / logit_divisor
    projection = lax.optimization_barrier(jnp.sum(unit_length_embeddings * slope_wrt_unit_embedding, axis=1, keepdims=True))
    grad_last = (slope_wrt_unit_embedding - unit_length_embeddings * projection) / embedding_lengths[:, None]
    grad_padded = jnp.concatenate([grad_last, jnp.zeros((1, D), jnp.float32)], axis=0)

    def backward_step(item_parts):
        entries, pair_in, pair_out = item_parts
        expert_rows = tokens_padded[entries]
        live_rows = (entries < TOKENS) & (entries % LENGTH == LENGTH - 1)
        seq_of_row = jnp.where(live_rows, entries // LENGTH, SEQS).astype(jnp.int32)
        weight = gates_padded[entries, column_of_row]
        route_grad = (weight[:, None] * grad_padded[seq_of_row]).astype(jnp.bfloat16)
        grads_in = []
        grads_out = []
        for half_index in range(2):
            gate_part, up_part, sigmoid_gate, activated, hidden = expert_half(expert_rows, pair_in[half_index])
            grad_hidden = jnp.dot(route_grad, pair_out[half_index].T, preferred_element_type=jnp.float32)
            grads_out.append(jnp.dot(hidden.T, route_grad, preferred_element_type=jnp.float32).astype(jnp.bfloat16))
            gate_slope = sigmoid_gate * (1.0 + gate_part * (1.0 - sigmoid_gate))
            grad_projected = jnp.concatenate([grad_hidden * up_part * gate_slope, grad_hidden * activated], axis=1).astype(jnp.bfloat16)
            grads_in.append(jnp.dot(expert_rows.T, grad_projected, preferred_element_type=jnp.float32).astype(jnp.bfloat16))
        return (jnp.stack(grads_in), jnp.stack(grads_out))
    grads_in, grads_out = lax.map(backward_step, (table, weights_in, weights_out))
    return (layer_out, grads_in.reshape(SLICES, D, 2 * HALF), grads_out.reshape(SLICES, HALF, D))
```

```python
import jax
import jax.numpy as jnp
from jax import lax
from jax.sharding import PartitionSpec as P

logit_divisor = 0.05
grad_scale = 256.0
epsilon = 1e-06


def contract_rows(left_side, right_side):
    return lax.dot_general(
        left_side, right_side, (((0,), (0,)), ((), ())), preferred_element_type=jnp.float32
    )


def matmul(left_side, right_side):
    return jnp.dot(left_side, right_side, preferred_element_type=jnp.float32)


def gated(rows, weight_in):
    projected = matmul(rows, weight_in)
    half_width = weight_in.shape[1] // 2
    gate_part = projected[:, :half_width]
    up_part = projected[:, half_width:]
    sigmoid_gate = jax.nn.sigmoid(gate_part)
    activated = gate_part * sigmoid_gate
    hidden = (activated * up_part).astype(jnp.bfloat16)
    return gate_part, up_part, sigmoid_gate, activated, hidden


def weighted_rows(rows, weight, pairs):
    total = sum(matmul(gated(rows, w_in)[4], w_out) for w_in, w_out in pairs)
    return (weight[:, None] * total).astype(jnp.bfloat16)


def loss_gradient(last_rows, positives):
    values = last_rows.astype(jnp.float32)
    norms = jnp.sqrt(jnp.sum(values * values, axis=1) + epsilon)
    unit = values / norms[:, None]
    dots = lax.dot_general(
        last_rows, last_rows, (((1,), (1,)), ((), ())), preferred_element_type=jnp.float32
    )
    scores = dots / (norms[:, None] * norms[None, :]) / logit_divisor
    index = jnp.arange(last_rows.shape[0], dtype=jnp.int32)
    exp_scores = jnp.where(index[:, None] != index[None, :], jnp.exp(scores), 0.0)
    probabilities = exp_scores / jnp.sum(exp_scores, axis=1, keepdims=True)
    target = (index[None, :] == positives[:, None]).astype(jnp.float32)
    coefficient = grad_scale * (probabilities - target)
    grad_unit = (
        jnp.dot(
            coefficient + coefficient.T,
            unit,
            precision=lax.Precision.HIGHEST,
            preferred_element_type=jnp.float32,
        )
        / logit_divisor
    )
    projection = jnp.sum(unit * grad_unit, axis=1, keepdims=True)
    return (grad_unit - unit * projection) / norms[:, None]


def body(tokens, expert_ids, gates, positives, gate_up, down):
    dp_count = lax.axis_size("dp")
    expert_count = lax.axis_size("expert")
    chips = expert_count // 2
    tok_dev, width = tokens.shape
    seq_dev = positives.shape[0]
    seq_length = tok_dev // seq_dev
    part_rows = tok_dev // expert_count
    plane = lax.axis_index("dp")
    lane = lax.axis_index("expert")
    chip = lane // 2
    core = lane % 2
    own_expert = plane * chips + chip
    hops = range(1, dp_count)

    def partner(place, step):
        return place ^ step if chips & (chips - 1) == 0 else (place + step) % chips

    def giver(place, step):
        return place ^ step if chips & (chips - 1) == 0 else (place - step) % chips

    def to_chip(value, step):
        pairs = [
            (2 * place + side, 2 * partner(place, step) + side)
            for place in range(chips)
            for side in range(2)
        ]
        return lax.ppermute(value, "expert", pairs)

    def from_chip(value, step):
        pairs = [
            (2 * place + side, 2 * giver(place, step) + side)
            for place in range(chips)
            for side in range(2)
        ]
        return lax.ppermute(value, "expert", pairs)

    def swap_cores(value):
        return lax.ppermute(value, "expert", [(j, j ^ 1) for j in range(expert_count)])

    def up_planes(value, hop):
        return lax.ppermute(value, "dp", [(p, (p + hop) % dp_count) for p in range(dp_count)])

    own_part = lax.dynamic_slice_in_dim(tokens, lane * part_rows, part_rows, 0)
    far_parts = [up_planes(own_part, hop) for hop in hops]

    last_tokens = tokens[seq_length - 1 :: seq_length]
    last_width = width // expert_count
    last_share = lax.dynamic_slice_in_dim(last_tokens, lane * last_width, last_width, 1)
    notes = [
        expert_ids[:, 0].astype(jnp.float32),
        gates[:, 0],
        positives.astype(jnp.float32),
        last_share.astype(jnp.float32).reshape(-1),
    ]
    note_size = sum(note.shape[0] for note in notes)
    notes.append(jnp.zeros((-note_size % 1024,), jnp.float32))
    noted = lax.all_gather(jnp.concatenate(notes), ("dp", "expert"), axis=0, tiled=False)
    noted = noted.reshape(dp_count, expert_count, -1)

    other_in = swap_cores(gate_up[0])
    other_out = swap_cores(down[0])
    pairs = [(gate_up[0], down[0]), (other_in, other_out)]

    far_own = jnp.concatenate(far_parts, axis=0)
    far_rows = jnp.concatenate(
        [far_own] + [from_chip(far_own, step) for step in range(1, chips)], axis=0
    )

    all_ids = noted[:, :, :tok_dev].astype(jnp.int32)
    all_gates = noted[:, :, tok_dev : 2 * tok_dev]
    weight = jnp.sum(jnp.where(all_ids == own_expert, all_gates, 0.0), axis=1)
    all_positives = noted[:, 0, 2 * tok_dev : 2 * tok_dev + seq_dev].astype(jnp.int32).reshape(-1)
    last_all = noted[:, :, 2 * tok_dev + seq_dev : note_size]
    last_all = last_all.reshape(dp_count, expert_count, seq_dev, last_width)
    last_all = last_all.transpose(0, 2, 1, 3).reshape(dp_count * seq_dev, width)

    def part_weight(hop, step):
        source = (plane - hop) % dp_count
        place = partner(chip, step) * 2 + core
        return lax.dynamic_slice(weight, (source, place * part_rows), (1, part_rows))[0]

    last_rows_in = last_all.astype(jnp.bfloat16)
    gate_part, up_part, sigmoid_gate, activated, hidden = gated(last_rows_in, gate_up[0])
    last_weight = weight[:, seq_length - 1 :: seq_length].reshape(-1)
    last_half = matmul(hidden, down[0]).astype(jnp.bfloat16).astype(jnp.float32)
    last_sum = lax.psum(last_weight[:, None] * last_half, ("dp", "expert"))

    def own_rows(step):
        place = partner(chip, step) * 2 + core
        return lax.dynamic_slice_in_dim(tokens, place * part_rows, part_rows, 0)

    near_rows = jnp.concatenate([own_rows(step) for step in range(chips)], axis=0)
    near_weight = jnp.concatenate([part_weight(0, step) for step in range(chips)])
    near_out = weighted_rows(near_rows, near_weight, pairs).reshape(chips, 1, part_rows, width)
    far_weight = jnp.concatenate(
        [part_weight(hop, step) for step in range(chips) for hop in hops]
    )
    far_out = weighted_rows(far_rows, far_weight, pairs)
    far_out = far_out.reshape(chips, dp_count - 1, part_rows, width)

    def over_chips(parts):
        total = parts[0].astype(jnp.float32)
        for step in range(1, chips):
            total = total + to_chip(parts[step], step).astype(jnp.float32)
        return total

    far_sum = over_chips(far_out).astype(jnp.bfloat16)
    near_sum = over_chips(near_out)[0]
    total = near_sum + own_part.astype(jnp.float32)
    for hop in hops:
        total = total + up_planes(far_sum[hop - 1], dp_count - hop).astype(jnp.float32)
    layer_out = lax.all_gather(total.astype(jnp.bfloat16), "expert", axis=0, tiled=True)

    last_out = (last_all + last_sum).astype(jnp.bfloat16)
    grad_last = loss_gradient(last_out, all_positives)
    route_grad = (last_weight[:, None] * grad_last).astype(jnp.bfloat16)
    grad_hidden = lax.dot_general(
        route_grad, down[0], (((1,), (1,)), ((), ())), preferred_element_type=jnp.float32
    )
    grad_down = contract_rows(hidden, route_grad).astype(jnp.bfloat16)
    gate_slope = sigmoid_gate * (1.0 + gate_part * (1.0 - sigmoid_gate))
    grad_projected = jnp.concatenate(
        [grad_hidden * up_part * gate_slope, grad_hidden * activated], axis=1
    ).astype(jnp.bfloat16)
    grad_gate_up = contract_rows(last_rows_in, grad_projected).astype(jnp.bfloat16)
    return (layer_out, grad_gate_up[None], grad_down[None])


def solution(mesh):
    return jax.shard_map(
        body,
        mesh=mesh,
        in_specs=(
            P("dp", None),
            P("dp", "expert"),
            P("dp", "expert"),
            P("dp"),
            P(("dp", "expert"), None, None),
            P(("dp", "expert"), None, None),
        ),
        out_specs=(P("dp", None), P(("dp", "expert"), None, None), P(("dp", "expert"), None, None)),
        check_vma=False,
    )
```

```python
import jax
import jax.numpy as jnp
from jax import lax
from jax.sharding import PartitionSpec as P

logit_divisor = 0.05
grad_scale = 256.0
epsilon = 1e-06


def contract_rows(left_side, right_side):
    return lax.dot_general(
        left_side, right_side, (((0,), (0,)), ((), ())), preferred_element_type=jnp.float32
    )


def matmul(left_side, right_side):
    return jnp.dot(left_side, right_side, preferred_element_type=jnp.float32)


def gated(rows, weight_in):
    projected = matmul(rows, weight_in)
    half_width = weight_in.shape[1] // 2
    gate_part = projected[:, :half_width]
    up_part = projected[:, half_width:]
    sigmoid_gate = jax.nn.sigmoid(gate_part)
    activated = gate_part * sigmoid_gate
    hidden = (activated * up_part).astype(jnp.bfloat16)
    return gate_part, up_part, sigmoid_gate, activated, hidden


def weighted_rows(rows, weight, pairs):
    total = sum(matmul(gated(rows, w_in)[4], w_out) for w_in, w_out in pairs)
    return (weight[:, None] * total).astype(jnp.bfloat16)


def loss_gradient(last_rows, positives):
    values = last_rows.astype(jnp.float32)
    norms = jnp.sqrt(jnp.sum(values * values, axis=1) + epsilon)
    unit = values / norms[:, None]
    dots = lax.dot_general(
        last_rows, last_rows, (((1,), (1,)), ((), ())), preferred_element_type=jnp.float32
    )
    scores = dots / (norms[:, None] * norms[None, :]) / logit_divisor
    index = jnp.arange(last_rows.shape[0], dtype=jnp.int32)
    exp_scores = jnp.where(index[:, None] != index[None, :], jnp.exp(scores), 0.0)
    probabilities = exp_scores / jnp.sum(exp_scores, axis=1, keepdims=True)
    target = (index[None, :] == positives[:, None]).astype(jnp.float32)
    coefficient = grad_scale * (probabilities - target)
    grad_unit = (
        jnp.dot(
            coefficient + coefficient.T,
            unit,
            precision=lax.Precision.HIGHEST,
            preferred_element_type=jnp.float32,
        )
        / logit_divisor
    )
    projection = jnp.sum(unit * grad_unit, axis=1, keepdims=True)
    return (grad_unit - unit * projection) / norms[:, None]


def doublings(count):
    steps = [1 << bit for bit in range((count - 1).bit_length())]
    assert 1 << len(steps) == count
    return steps


def body(tokens, expert_ids, gates, positives, gate_up, down):
    dp_count = lax.axis_size("dp")
    expert_count = lax.axis_size("expert")
    chips = expert_count // 2
    tok_dev, width = tokens.shape
    seq_dev = positives.shape[0]
    seq_length = tok_dev // seq_dev
    part_rows = tok_dev // expert_count
    plane = lax.axis_index("dp")
    lane = lax.axis_index("expert")
    own_expert = plane * chips + lane // 2

    def to_lane(value, step):
        return lax.ppermute(value, "expert", [(j, j ^ step) for j in range(expert_count)])

    def to_plane(value, step):
        return lax.ppermute(value, "dp", [(p, p ^ step) for p in range(dp_count)])

    chip_steps = [2 * step for step in range(1, chips)]
    hop_groups = [range(first, 2 * first) for first in doublings(dp_count)]

    own_part = lax.dynamic_slice_in_dim(tokens, lane * part_rows, part_rows, 0)
    far_parts = [[to_plane(own_part, hop) for hop in group] for group in hop_groups]

    last_tokens = tokens[seq_length - 1 :: seq_length]
    last_width = width // expert_count
    last_share = lax.dynamic_slice_in_dim(last_tokens, lane * last_width, last_width, 1)
    gates_high = gates[:, 0].astype(jnp.bfloat16)
    gates_low = (gates[:, 0] - gates_high.astype(jnp.float32)).astype(jnp.bfloat16)
    notes = [
        expert_ids[:, 0].astype(jnp.bfloat16),
        gates_high,
        gates_low,
        last_share.reshape(-1),
        positives.astype(jnp.bfloat16),
    ]
    note_size = sum(note.shape[0] for note in notes)
    notes.append(jnp.zeros((-note_size % width,), jnp.bfloat16))
    noted = jnp.concatenate(notes).reshape(1, 1, -1)

    def joined(value, other, upper, axis):
        return jnp.where(
            upper,
            jnp.concatenate([other, value], axis=axis),
            jnp.concatenate([value, other], axis=axis),
        )

    for step in doublings(dp_count):
        noted = joined(noted, to_plane(noted, step), plane & step != 0, 0)
    for step in doublings(expert_count):
        noted = joined(noted, to_lane(noted, step), lane & step != 0, 1)

    other_in = to_lane(gate_up[0], 1)
    other_out = to_lane(down[0], 1)
    pairs = [(gate_up[0], down[0]), (other_in, other_out)]

    far_rows = []
    for parts in far_parts:
        own = jnp.concatenate(parts, axis=0)
        far_rows.append(
            jnp.concatenate([own] + [to_lane(own, step) for step in chip_steps], axis=0)
        )

    all_ids = noted[:, :, :tok_dev].astype(jnp.int32)
    all_gates = noted[:, :, tok_dev : 2 * tok_dev].astype(jnp.float32)
    all_gates = all_gates + noted[:, :, 2 * tok_dev : 3 * tok_dev].astype(jnp.float32)
    weight = jnp.sum(jnp.where(all_ids == own_expert, all_gates, 0.0), axis=1)
    last_start = 3 * tok_dev
    last_end = last_start + seq_dev * last_width
    all_positives = noted[:, 0, last_end : last_end + seq_dev].astype(jnp.int32).reshape(-1)
    last_all = noted[:, :, last_start:last_end]
    last_all = last_all.reshape(dp_count, expert_count, seq_dev, last_width)
    last_all = last_all.transpose(0, 2, 1, 3).reshape(dp_count * seq_dev, width)

    def part_weight(hop, step):
        source = plane ^ hop
        start = (lane ^ step) * part_rows
        return lax.dynamic_slice(weight, (source, start), (1, part_rows))[0]

    def group_weight(group):
        return jnp.concatenate(
            [part_weight(hop, step) for step in [0] + chip_steps for hop in group]
        )

    gate_part, up_part, sigmoid_gate, activated, hidden = gated(last_all, gate_up[0])
    last_weight = weight[:, seq_length - 1 :: seq_length].reshape(-1)
    last_half = matmul(hidden, down[0]).astype(jnp.bfloat16).astype(jnp.float32)
    last_sum = last_weight[:, None] * last_half
    for step in doublings(expert_count):
        last_sum = last_sum + to_lane(last_sum, step)
    for step in doublings(dp_count):
        last_sum = last_sum + to_plane(last_sum, step)

    def over_chips(parts):
        total = parts[0].astype(jnp.float32)
        for index, step in enumerate(chip_steps):
            total = total + to_lane(parts[index + 1], step).astype(jnp.float32)
        return total

    near_rows = jnp.concatenate(
        [
            lax.dynamic_slice_in_dim(tokens, (lane ^ step) * part_rows, part_rows, 0)
            for step in [0] + chip_steps
        ],
        axis=0,
    )
    near_out = weighted_rows(near_rows, group_weight([0]), pairs)
    total = over_chips(near_out.reshape(chips, part_rows, width)) + own_part.astype(jnp.float32)
    for group, rows in zip(hop_groups, far_rows):
        out = weighted_rows(rows, group_weight(group), pairs)
        out = over_chips(out.reshape(chips, len(group), part_rows, width)).astype(jnp.bfloat16)
        for index, hop in enumerate(group):
            total = total + to_plane(out[index], hop).astype(jnp.float32)

    own_out = total.astype(jnp.bfloat16)
    layer_out = jnp.zeros((tok_dev, width), jnp.bfloat16)
    pieces = [own_out] + [to_lane(own_out, step) for step in chip_steps]
    stacked = jnp.concatenate(pieces, axis=0)
    mirrored = to_lane(stacked, 1)
    for index, step in enumerate([0] + chip_steps):
        rows = slice(index * part_rows, (index + 1) * part_rows)
        for source, value in ((lane ^ step, stacked[rows]), (lane ^ step ^ 1, mirrored[rows])):
            layer_out = lax.dynamic_update_slice(layer_out, value, (source * part_rows, 0))

    last_out = (last_all.astype(jnp.float32) + last_sum).astype(jnp.bfloat16)
    grad_last = loss_gradient(last_out, all_positives)
    route_grad = (last_weight[:, None] * grad_last).astype(jnp.bfloat16)
    grad_hidden = lax.dot_general(
        route_grad, down[0], (((1,), (1,)), ((), ())), preferred_element_type=jnp.float32
    )
    grad_down = contract_rows(hidden, route_grad).astype(jnp.bfloat16)
    gate_slope = sigmoid_gate * (1.0 + gate_part * (1.0 - sigmoid_gate))
    grad_projected = jnp.concatenate(
        [grad_hidden * up_part * gate_slope, grad_hidden * activated], axis=1
    ).astype(jnp.bfloat16)
    grad_gate_up = contract_rows(last_all, grad_projected).astype(jnp.bfloat16)
    return (layer_out, grad_gate_up[None], grad_down[None])


def solution(mesh):
    return jax.shard_map(
        body,
        mesh=mesh,
        in_specs=(
            P("dp", None),
            P("dp", "expert"),
            P("dp", "expert"),
            P("dp"),
            P(("dp", "expert"), None, None),
            P(("dp", "expert"), None, None),
        ),
        out_specs=(P("dp", None), P(("dp", "expert"), None, None), P(("dp", "expert"), None, None)),
        check_vma=False,
    )
```

```python
import functools

import jax
import jax.numpy as jnp
from jax import lax
from jax.experimental import pallas as pl
from jax.experimental.pallas import tpu as pltpu
from jax.sharding import PartitionSpec as P

logit_divisor = 0.05
grad_scale = 256.0
epsilon = 1e-06
lanes = 128
tail = 16
bf16 = jnp.bfloat16
f32 = jnp.float32

anywhere = pl.BlockSpec(memory_space=pl.ANY)
in_vmem = pl.BlockSpec(memory_space=pltpu.VMEM)
in_smem = pl.BlockSpec(memory_space=pltpu.SMEM)


def params(mebibytes):
    return pltpu.CompilerParams(vmem_limit_bytes=mebibytes << 20)


def cost(flops, moved):
    return pl.CostEstimate(flops=flops, transcendentals=0, bytes_accessed=moved)


def dot(left, right, dims=((1,), (0,)), precision=None):
    return lax.dot_general(
        left, right, (dims, ((), ())), precision=precision, preferred_element_type=f32
    )


def doublings(count):
    steps = [1 << bit for bit in range((count - 1).bit_length())]
    assert 1 << len(steps) == count
    return steps


def column(table, wanted):
    index = lax.broadcasted_iota(jnp.int32, table.shape, 1)
    return jnp.sum(jnp.where(index == wanted, table, 0.0), axis=1, keepdims=True)


def note_kernel(seq_dev, part_rows, place, positives, dense, tokens, out, wide, table, rows, sems):
    seq_length = tokens.shape[0] // seq_dev
    copies = [
        pltpu.make_async_copy(
            tokens.at[pl.ds((seq + 1) * seq_length - tail, tail)], rows.at[seq], sems.at[seq]
        )
        for seq in range(seq_dev)
    ]
    for copy in copies:
        copy.start()
    table[...] = dense[...].astype(f32)
    start = pl.multiple_of(place[1] * part_rows, part_rows)
    wide[:part_rows, :] = table[pl.ds(start, part_rows), :]
    base = part_rows + 2 * seq_dev
    for seq in range(seq_dev):
        last = (seq + 1) * seq_length - 1
        wide[part_rows + seq : part_rows + seq + 1, :] = table[last : last + 1, :]
        own = jnp.full((1, wide.shape[1]), positives[seq], jnp.int32).astype(f32)
        wide[part_rows + seq_dev + seq : part_rows + seq_dev + seq + 1, :] = own
    for seq in range(seq_dev):
        copies[seq].wait()
        values = rows[seq].astype(f32)
        for chunk in range(tokens.shape[1] // lanes):
            row = base + chunk * seq_dev + seq
            wide[row : row + 1, :] = values[tail - 1 : tail, chunk * lanes : (chunk + 1) * lanes]
    out[...] = wide[...].astype(bf16)


def expert_kernel(layout, *refs):
    chips, part_rows, seq_dev, near, with_last, n_parts = layout
    refs = list(refs)
    place = refs.pop(0)
    tokens = refs.pop(0) if near else None
    noted = refs.pop(0) if with_last else None
    parts, refs = refs[:n_parts], refs[n_parts:]
    weights, refs = refs[:4], refs[4:]
    outs, refs = refs[:chips], refs[chips:]
    if with_last:
        last_rows, last_projected, last_out, last_marks, *refs = refs
        floats, joined, marks, *refs = refs
    rows, w_in, w_out, sems, weight_sems = refs
    targets = [w_in.at[0], w_out.at[0], w_in.at[1], w_out.at[1]]
    weight_copies = [
        pltpu.make_async_copy(source.at[0], target, weight_sems.at[index])
        for index, (source, target) in enumerate(zip(weights, targets))
    ]
    count = outs[0].shape[0] // part_rows
    copies = []

    def place_rows(source, start):
        target = rows.at[pl.ds(start, source.shape[0])]
        copies.append(pltpu.make_async_copy(source, target, sems.at[len(copies)]))

    block = count * part_rows
    if near:
        for chip in range(chips):
            start = pl.multiple_of((place[1] ^ (2 * chip)) * part_rows, part_rows)
            place_rows(tokens.at[pl.ds(start, part_rows)], chip * block)
    own_parts = count - 1 if near else count
    for index in range(own_parts):
        place_rows(parts[index], (index + count - own_parts) * part_rows)
    for chip in range(1, chips):
        place_rows(parts[own_parts + chip - 1], chip * block + (count - own_parts) * part_rows)
    for copy in copies:
        copy.start()
    for copy in weight_copies:
        copy.start()
    total = chips * block
    if with_last:
        base = part_rows + 2 * seq_dev
        floats[...] = noted[...].astype(f32)
        for plane in range(noted.shape[0]):
            own = slice(plane * seq_dev, (plane + 1) * seq_dev)
            marks[0, own, :] = floats[plane, part_rows : part_rows + seq_dev, :]
            marks[1, own, :] = floats[plane, part_rows + seq_dev : base, :]
            for chunk in range(rows.shape[1] // lanes):
                start = base + chunk * seq_dev
                joined[own, chunk * lanes : (chunk + 1) * lanes] = floats[
                    plane, start : start + seq_dev, :
                ]
        last_rows[...] = joined[...].astype(bf16)
        rows[total:, :] = joined[...].astype(bf16)
    for copy in copies:
        copy.wait()
    half_width = w_out.shape[1]
    result = None
    for half in range(2):
        weight_copies[2 * half].wait()
        used = rows[...] if half == 0 else rows[:total, :]
        projected = dot(used, w_in[half])
        gate, up = projected[:, :half_width], projected[:, half_width:]
        hidden = (gate * jax.nn.sigmoid(gate) * up).astype(bf16)
        weight_copies[2 * half + 1].wait()
        if half == 0 and with_last:
            last_projected[...] = projected[total:]
            weight = column(marks[0], place[2])
            own_last = dot(hidden[total:], w_out[0]).astype(bf16).astype(f32)
            last_out[...] = (weight * own_last).astype(bf16)
            last_marks[0, :, :] = jnp.broadcast_to(weight, marks.shape[1:])
            last_marks[1, :, :] = marks[1]
        part = dot(hidden[:total], w_out[half])
        result = part if half == 0 else result + part
    for chip in range(chips):
        outs[chip][...] = result[chip * block : (chip + 1) * block].astype(bf16)


def combine_kernel(layout, place, noted, own, *refs):
    chips, part_rows, group, n_outs = layout
    parts, outs = refs[:chips], refs[chips : chips + n_outs]
    first_expert = place[2] - place[1] // 2
    for index, hop in enumerate(group):
        table = noted[place[0] ^ hop, :part_rows, :].astype(f32)
        rows = slice(index * part_rows, (index + 1) * part_rows)
        total = own[...].astype(f32) if hop == 0 else None
        for chip in range(chips):
            weight = column(table, first_expert + ((place[1] // 2) ^ chip))
            term = weight * parts[chip][rows, :].astype(f32)
            total = term if total is None else total + term
        outs[index][...] = total.astype(outs[index].dtype)


def gather_kernel(chips, place, *refs):
    pieces, mirrored, out, sems = refs[:chips], refs[chips], refs[chips + 1], refs[chips + 2]
    part_rows = pieces[0].shape[0]
    copies = []
    for chip in range(chips):
        lane = place[1] ^ (2 * chip)
        for source, at in (
            (pieces[chip], lane),
            (mirrored.at[pl.ds(chip * part_rows, part_rows)], lane ^ 1),
        ):
            start = pl.multiple_of(at * part_rows, part_rows)
            target = out.at[pl.ds(start, part_rows)]
            copies.append(pltpu.make_async_copy(source, target, sems.at[len(copies)]))
    for copy in copies:
        copy.start()
    for copy in copies:
        copy.wait()


def gradient_kernel(
    last_all, last_block, last_sum, projected, marks, down, grad_in, grad_out, route, hidden, slope
):
    step = pl.program_id(0)
    half_width = down.shape[1]
    block = grad_out.shape[2]

    @pl.when(step == 0)
    def _():
        layer_last = (last_all[...].astype(f32) + last_sum[...].astype(f32)).astype(bf16)
        values = layer_last.astype(f32)
        count = values.shape[0]
        norms = jnp.sqrt(jnp.sum(values * values, axis=1, keepdims=True) + epsilon)
        unit = values / norms
        scores = dot(unit, unit, ((1,), (1,)), lax.Precision.HIGHEST) / logit_divisor
        row = lax.broadcasted_iota(jnp.int32, (count, count), 0)
        col = lax.broadcasted_iota(jnp.int32, (count, count), 1)
        exp_scores = jnp.where(row != col, jnp.exp(scores), 0.0)
        probabilities = exp_scores / jnp.sum(exp_scores, axis=1, keepdims=True)
        partner = marks[1][:, :1].astype(jnp.int32)
        coefficient = grad_scale * (probabilities - jnp.where(col == partner, 1.0, 0.0))
        high = lax.Precision.HIGHEST
        grad_unit = (
            dot(coefficient, unit, ((1,), (0,)), high) + dot(coefficient, unit, ((0,), (0,)), high)
        ) / logit_divisor
        projection = jnp.sum(unit * grad_unit, axis=1, keepdims=True)
        grad_last = (grad_unit - unit * projection) / norms
        route_grad = (marks[0][:, :1] * grad_last).astype(bf16)
        for index in range(route.shape[0]):
            route[index] = route_grad[:, index * block : (index + 1) * block]
        grad_hidden = dot(route_grad, down[0], ((1,), (1,)))
        gate, up = projected[:, :half_width], projected[:, half_width:]
        sigmoid_gate = jax.nn.sigmoid(gate)
        activated = gate * sigmoid_gate
        hidden[...] = (activated * up).astype(bf16)
        gate_slope = sigmoid_gate * (1.0 + gate * (1.0 - sigmoid_gate))
        slope[:, :half_width] = (grad_hidden * up * gate_slope).astype(bf16)
        slope[:, half_width:] = (grad_hidden * activated).astype(bf16)

    grad_in[0] = dot(last_block[...], slope[...], ((0,), (0,))).astype(bf16)
    grad_out[0] = dot(hidden[...], route[step], ((0,), (0,))).astype(bf16)


def body(tokens, expert_ids, gates, positives, gate_up, down):
    dp_count = lax.axis_size("dp")
    expert_count = lax.axis_size("expert")
    chips = expert_count // 2
    experts = dp_count * chips
    tok_dev, width = tokens.shape
    half_width = down.shape[1]
    seq_dev = positives.shape[0]
    seqs = dp_count * seq_dev
    seq_length = tok_dev // seq_dev
    part_rows = tok_dev // expert_count
    plane = lax.axis_index("dp")
    lane = lax.axis_index("expert")
    place = jnp.stack([plane, lane, plane * chips + lane // 2]).astype(jnp.int32)
    assert experts <= lanes and seq_length % tail == 0

    def to_lane(value, step):
        return lax.ppermute(value, "expert", [(j, j ^ step) for j in range(expert_count)])

    def to_plane(value, step):
        return lax.ppermute(value, "dp", [(p, p ^ step) for p in range(dp_count)])

    chip_steps = [2 * step for step in range(1, chips)]
    groups = [range(first, min(first + 2, dp_count)) for first in range(0, dp_count, 2)]

    own_part = lax.dynamic_slice_in_dim(tokens, lane * part_rows, part_rows, 0)
    arrivals = {hop: to_plane(own_part, hop) for hop in range(1, dp_count)}
    mate_in = to_lane(gate_up, 1)
    mate_out = to_lane(down, 1)
    weights = (gate_up, down, mate_in, mate_out)

    dense = jnp.where(
        expert_ids == jnp.arange(lanes, dtype=jnp.int32)[None, :], gates, 0.0
    ).astype(bf16)
    dense, _ = lax.optimization_barrier((dense, arrivals[1]))
    for step in doublings(expert_count):
        dense = dense + to_lane(dense, step)
    note_rows = part_rows + 2 * seq_dev + seq_dev * (width // lanes)
    noted = pl.pallas_call(
        functools.partial(note_kernel, seq_dev, part_rows),
        out_shape=jax.ShapeDtypeStruct((note_rows, lanes), bf16),
        in_specs=[in_smem, in_smem, in_vmem, anywhere],
        out_specs=in_vmem,
        scratch_shapes=[
            pltpu.VMEM((note_rows, lanes), f32),
            pltpu.VMEM((tok_dev, lanes), f32),
            pltpu.VMEM((seq_dev, tail, width), bf16),
            pltpu.SemaphoreType.DMA((seq_dev,)),
        ],
        cost_estimate=cost(0, 1 << 20),
        name="notes",
    )(place, positives, dense, tokens)[None]

    for step in doublings(dp_count):
        other = to_plane(noted, step)
        noted = jnp.where(
            plane & step != 0,
            jnp.concatenate([other, noted], axis=0),
            jnp.concatenate([noted, other], axis=0),
        )

    def expert(group, with_last):
        near = group[0] == 0
        own = [arrivals[hop] for hop in group if hop]
        joined = own[0] if len(own) == 1 else jnp.concatenate(own, axis=0)
        parts = own + [to_lane(joined, step) for step in chip_steps]
        block = len(group) * part_rows
        total = chips * block
        extra = seqs if with_last else 0
        out_shape = [jax.ShapeDtypeStruct((block, width), bf16)] * chips
        scratch = []
        if with_last:
            out_shape += [
                jax.ShapeDtypeStruct((seqs, width), bf16),
                jax.ShapeDtypeStruct((seqs, 2 * half_width), f32),
                jax.ShapeDtypeStruct((seqs, width), bf16),
                jax.ShapeDtypeStruct((2, seqs, lanes), f32),
            ]
            scratch += [
                pltpu.VMEM(noted.shape, f32),
                pltpu.VMEM((seqs, width), f32),
                pltpu.VMEM((2, seqs, lanes), f32),
            ]
        scratch += [
            pltpu.VMEM((total + extra, width), bf16),
            pltpu.VMEM((2, width, 2 * half_width), bf16),
            pltpu.VMEM((2, half_width, width), bf16),
            pltpu.SemaphoreType.DMA((2 * chips + len(group),)),
            pltpu.SemaphoreType.DMA((4,)),
        ]
        operands = [place] + [tokens] * near + [noted] * with_last + parts + list(weights)
        specs = [in_smem] + [anywhere] * near + [in_vmem] * with_last
        specs += [anywhere] * (len(parts) + 4)
        layout = (chips, part_rows, seq_dev, near, with_last, len(parts))
        return pl.pallas_call(
            functools.partial(expert_kernel, layout),
            out_shape=out_shape,
            in_specs=specs,
            out_specs=[in_vmem] * len(out_shape),
            scratch_shapes=scratch,
            compiler_params=params(32),
            cost_estimate=cost(2 * total * width * 6 * half_width, 12 << 20),
            name="experts",
        )(*operands)

    def combine(group, out):
        parts = [out[0]] + [to_lane(out[index + 1], step) for index, step in enumerate(chip_steps)]
        out_shape = [
            jax.ShapeDtypeStruct((part_rows, width), bf16 if hop else f32) for hop in group
        ]
        layout = (chips, part_rows, tuple(group), len(group))
        return pl.pallas_call(
            functools.partial(combine_kernel, layout),
            out_shape=out_shape,
            in_specs=[in_smem] + [in_vmem] * (2 + chips),
            out_specs=[in_vmem] * len(group),
            cost_estimate=cost(0, 3 << 20),
            name="combine",
        )(place, noted, own_part, *parts)

    last_group = min(1, len(groups) - 1)
    sums = {}
    for index, group in enumerate(groups):
        out = expert(group, index == last_group)
        if index == last_group:
            last_all, last_projected, last_sum, last_marks = out[chips:]
        for hop, value in zip(group, combine(group, out[:chips])):
            sums[hop] = value

    for step in doublings(expert_count):
        last_sum = (last_sum.astype(f32) + to_lane(last_sum, step).astype(f32)).astype(bf16)
    for step in doublings(dp_count):
        last_sum = (last_sum.astype(f32) + to_plane(last_sum, step).astype(f32)).astype(bf16)

    total = sums[0]
    for hop in range(1, dp_count):
        total = total + to_plane(sums[hop], hop).astype(f32)
    own_out = total.astype(bf16)
    pieces = [own_out] + [to_lane(own_out, step) for step in chip_steps]
    mirrored = to_lane(jnp.concatenate(pieces, axis=0), 1)
    layer_out = pl.pallas_call(
        functools.partial(gather_kernel, chips),
        out_shape=jax.ShapeDtypeStruct((tok_dev, width), bf16),
        in_specs=[in_smem] + [anywhere] * (chips + 1),
        out_specs=anywhere,
        scratch_shapes=[pltpu.SemaphoreType.DMA((expert_count,))],
        cost_estimate=cost(0, 2 << 20),
        name="gather",
    )(place, *pieces, mirrored)

    block = min(512, width)
    steps = width // block
    grad_gate_up, grad_down = pl.pallas_call(
        gradient_kernel,
        grid=(steps,),
        out_shape=[
            jax.ShapeDtypeStruct(gate_up.shape, bf16),
            jax.ShapeDtypeStruct(down.shape, bf16),
        ],
        in_specs=[
            pl.BlockSpec((seqs, width), lambda step: (0, 0)),
            pl.BlockSpec((seqs, block), lambda step: (0, step)),
            pl.BlockSpec((seqs, width), lambda step: (0, 0)),
            pl.BlockSpec((seqs, 2 * half_width), lambda step: (0, 0)),
            pl.BlockSpec((2, seqs, lanes), lambda step: (0, 0, 0)),
            pl.BlockSpec((1, half_width, width), lambda step: (0, 0, 0)),
        ],
        out_specs=[
            pl.BlockSpec((1, block, 2 * half_width), lambda step: (0, step, 0)),
            pl.BlockSpec((1, half_width, block), lambda step: (0, 0, step)),
        ],
        scratch_shapes=[
            pltpu.VMEM((steps, seqs, block), bf16),
            pltpu.VMEM((seqs, half_width), bf16),
            pltpu.VMEM((seqs, 2 * half_width), bf16),
        ],
        compiler_params=params(24),
        cost_estimate=cost(2 * seqs * width * 4 * half_width, 7 << 20),
        name="gradients",
    )(last_all, last_all, last_sum, last_projected, last_marks, down)
    return (layer_out, grad_gate_up, grad_down)


def solution(mesh):
    return jax.shard_map(
        body,
        mesh=mesh,
        in_specs=(
            P("dp", None),
            P("dp", "expert"),
            P("dp", "expert"),
            P("dp"),
            P(("dp", "expert"), None, None),
            P(("dp", "expert"), None, None),
        ),
        out_specs=(P("dp", None), P(("dp", "expert"), None, None), P(("dp", "expert"), None, None)),
        check_vma=False,
    )
```

```python
import functools

import jax
import jax.numpy as jnp
from jax import lax
from jax.experimental import pallas as pl
from jax.experimental.pallas import tpu as pltpu
from jax.sharding import PartitionSpec as P

logit_divisor = 0.05
grad_scale = 256.0
epsilon = 1e-06
lanes = 128
tail = 16
bf16 = jnp.bfloat16
f32 = jnp.float32

anywhere = pl.BlockSpec(memory_space=pl.ANY)
in_vmem = pl.BlockSpec(memory_space=pltpu.VMEM)
in_smem = pl.BlockSpec(memory_space=pltpu.SMEM)


def params(mebibytes):
    return pltpu.CompilerParams(vmem_limit_bytes=mebibytes << 20)


def cost(flops, moved):
    return pl.CostEstimate(flops=flops, transcendentals=0, bytes_accessed=moved)


def dot(left, right, dims=((1,), (0,)), precision=None):
    return lax.dot_general(
        left, right, (dims, ((), ())), precision=precision, preferred_element_type=f32
    )


def doublings(count):
    steps = [1 << bit for bit in range((count - 1).bit_length())]
    assert 1 << len(steps) == count
    return steps


def column(table, wanted):
    index = lax.broadcasted_iota(jnp.int32, table.shape, 1)
    return jnp.sum(jnp.where(index == wanted, table, 0.0), axis=1, keepdims=True)


def pack_kernel(seq_dev, place, positives, ids, gates, tokens, out, tile, rows, sems):
    part_rows, width = out.shape[0], tokens.shape[1]
    tok_dev = tokens.shape[0]
    seq_length = tok_dev // seq_dev
    share = rows.shape[2]
    column_at = pl.multiple_of(place[1] // 2 * share, lanes)
    start = pl.multiple_of(place[1] * part_rows, part_rows)
    copies = [
        pltpu.make_async_copy(
            tokens.at[pl.ds((seq + 1) * seq_length - tail, tail), pl.ds(column_at, share)],
            rows.at[seq],
            sems.at[seq],
        )
        for seq in range(seq_dev)
    ]
    own = pltpu.make_async_copy(
        tokens.at[pl.ds(start, part_rows)], out.at[:, pl.ds(0, width)], sems.at[seq_dev]
    )
    own.start()
    for copy in copies:
        copy.start()
    row_index = lax.broadcasted_iota(jnp.int32, (lanes, lanes), 0)
    diagonal = row_index == lax.broadcasted_iota(jnp.int32, (lanes, lanes), 1)
    note_rows = tok_dev // lanes
    tile[...] = jnp.zeros_like(tile)
    for index in range(note_rows):
        block = slice(index * lanes, (index + 1) * lanes)
        for offset, values in ((0, ids[block, :].astype(f32)), (note_rows, gates[block, :])):
            line = jnp.sum(jnp.where(diagonal, values, 0.0), axis=0, keepdims=True)
            tile[offset + index : offset + index + 1, :] = line
    for seq in range(seq_dev):
        row = 2 * note_rows + seq
        tile[row : row + 1, :] = jnp.full((1, lanes), positives[seq], jnp.int32).astype(f32)
    base = part_rows - seq_dev * (share // lanes)
    for seq in range(seq_dev):
        copies[seq].wait()
        values = rows[seq].astype(f32)
        for chunk in range(share // lanes):
            row = base + chunk * seq_dev + seq
            tile[row : row + 1, :] = values[tail - 1 : tail, chunk * lanes : (chunk + 1) * lanes]
    out[:, width:] = tile[...].astype(bf16)
    own.wait()


def table_kernel(layout, place, *refs):
    seq_dev, tok_dev, where_tiles, n_parts = layout
    parts = refs[:n_parts]
    kept, sent, last_rows, partners, tokens, routes, marks = refs[n_parts:]
    part_rows = parts[0].shape[0]
    dp_count, chunks = tokens.shape[:2]
    note_rows = tok_dev // lanes
    seq_length = tok_dev // seq_dev
    chips = len(where_tiles[0])
    share_chunks = chunks // chips
    base = part_rows - seq_dev * share_chunks
    lane_index = lax.broadcasted_iota(jnp.int32, (part_rows, lanes), 1)
    row_index = lax.broadcasted_iota(jnp.int32, (part_rows, lanes), 0)

    def dense_rows(tile, lane):
        start = lane * part_rows
        picked = lane_index == row_index + start % lanes
        found = []
        for offset in (0, note_rows):
            line = tile[offset : offset + 1, :]
            for index in range(1, note_rows):
                other = tile[offset + index : offset + index + 1, :]
                line = jnp.where(start // lanes == index, other, line)
            found.append(jnp.sum(jnp.where(picked, line, 0.0), axis=1, keepdims=True))
        return jnp.where(lane_index.astype(f32) == found[0], found[1], 0.0)

    for hop in range(dp_count):
        plane = place[0] ^ hop
        sums = [None, None]
        for chip in range(chips):
            source, row, at = where_tiles[hop][chip]
            tile = parts[source][row : row + part_rows, at : at + lanes].astype(f32)
            for index, lane in enumerate((place[1], place[1] ^ 1)):
                value = dense_rows(tile, lane)
                sums[index] = value if chip == 0 else sums[index] + value
            for seq in range(seq_dev):
                at_token = (seq + 1) * seq_length - 1
                row = at_token // lanes
                here = lane_index[:1] == at_token % lanes
                expert, gate = [
                    jnp.sum(
                        jnp.where(here, tile[offset + row : offset + row + 1, :], 0.0),
                        axis=1,
                        keepdims=True,
                    )
                    for offset in (0, note_rows)
                ]
                value = jnp.where(lane_index[:1].astype(f32) == expert, gate, 0.0)
                if chip:
                    value = value + routes[plane, seq : seq + 1, :]
                routes[plane, seq : seq + 1, :] = value
            if chip == 0:
                marks[plane, 0:seq_dev, :] = tile[2 * note_rows : 2 * note_rows + seq_dev, :]
            first = ((place[1] // 2) ^ chip) * share_chunks
            for chunk in range(share_chunks):
                row = base + chunk * seq_dev
                tokens[plane, first + chunk, 0:seq_dev, :] = tile[row : row + seq_dev, :]
        at = slice(hop * part_rows, (hop + 1) * part_rows)
        kept[at, :] = sums[0].astype(bf16)
        sent[at, :] = sums[1].astype(bf16)
    last = dp_count * part_rows
    joined, shared = [], []
    for plane in range(dp_count):
        shared.append(routes[plane, 0:seq_dev, :])
        partners[plane * seq_dev : (plane + 1) * seq_dev, :] = marks[plane, 0:seq_dev, :]
        lines = [tokens[plane, chunk, 0:seq_dev, :] for chunk in range(chunks)]
        joined.append(jnp.concatenate(lines, axis=1))
    last_rows[...] = jnp.concatenate(joined, axis=0).astype(bf16)
    seqs = dp_count * seq_dev
    value = jnp.concatenate(shared, axis=0).astype(bf16)
    kept[last : last + seqs, :] = value
    sent[last : last + seqs, :] = value


def hidden_parts(projected):
    half_width = projected.shape[1] // 2
    gate, up = projected[:, :half_width], projected[:, half_width:]
    sigmoid_gate = jax.nn.sigmoid(gate)
    return gate, up, sigmoid_gate, gate * sigmoid_gate


def expert_kernel(layout, *refs):
    chips, part_rows, near, n_parts = layout
    refs = list(refs)
    place = refs.pop(0)
    tokens = refs.pop(0) if near else None
    parts, refs = refs[:n_parts], refs[n_parts:]
    weights, refs = refs[:4], refs[4:]
    outs, (rows,) = refs[:chips], refs[chips:]
    count, width = outs[0].shape[0] // part_rows, outs[0].shape[1]
    block = count * part_rows
    if near:
        for chip in range(chips):
            start = pl.multiple_of((place[1] ^ (2 * chip)) * part_rows, part_rows)
            at = chip * block
            rows[at : at + part_rows, :] = tokens[pl.ds(start, part_rows), :]
    own_parts = count - 1 if near else count
    for index in range(own_parts):
        at = (index + count - own_parts) * part_rows
        rows[at : at + part_rows, :] = parts[index][:, :width]
    for chip in range(1, chips):
        at = chip * block + (count - own_parts) * part_rows
        rows[at : at + own_parts * part_rows, :] = parts[own_parts + chip - 1][:, :width]
    result = None
    for half in range(2):
        w_in, w_out = weights[2 * half], weights[2 * half + 1]
        _, up, _, activated = hidden_parts(dot(rows[...], w_in[0]))
        part = dot((activated * up).astype(bf16), w_out[0])
        result = part if half == 0 else result + part
    for chip in range(chips):
        outs[chip][...] = result[chip * block : (chip + 1) * block].astype(bf16)


def last_kernel(place, rows, kept, found, w_in, w_out, projected, out, weights):
    seqs = rows.shape[0]
    last = kept.shape[0] - seqs
    values = dot(rows[...], w_in[0])
    projected[...] = values
    _, up, _, activated = hidden_parts(values)
    half_out = dot((activated * up).astype(bf16), w_out[0]).astype(bf16).astype(f32)
    weight = column(kept[last:, :].astype(f32) + found[last:, :].astype(f32), place[2])
    out[...] = (weight * half_out).astype(bf16)
    weights[...] = jnp.broadcast_to(weight, weights.shape)


def combine_kernel(layout, place, kept, found, own, *refs):
    chips, part_rows, group, n_outs = layout
    parts, outs = refs[:chips], refs[chips : chips + n_outs]
    first_expert = place[2] - place[1] // 2
    width = parts[0].shape[1]
    for index, hop in enumerate(group):
        at = slice(hop * part_rows, (hop + 1) * part_rows)
        table = kept[at, :].astype(f32) + found[at, :].astype(f32)
        rows = slice(index * part_rows, (index + 1) * part_rows)
        total = own[:, :width].astype(f32) if hop == 0 else None
        for chip in range(chips):
            weight = column(table, first_expert + ((place[1] // 2) ^ chip))
            term = weight * parts[chip][rows, :].astype(f32)
            total = term if total is None else total + term
        outs[index][...] = total.astype(outs[index].dtype)


def gather_kernel(chips, place, *refs):
    out = refs[-1]
    part_rows = refs[0].shape[0]
    for chip in range(chips):
        lane = place[1] ^ (2 * chip)
        own = pl.multiple_of(lane * part_rows, part_rows)
        out[pl.ds(own, part_rows), :] = refs[chip][...]
        other = pl.multiple_of((lane ^ 1) * part_rows, part_rows)
        out[pl.ds(other, part_rows), :] = refs[chips + chip][...]


def gradient_kernel(
    last_all,
    last_block,
    last_sum,
    projected,
    weights,
    partners,
    down,
    grad_in,
    grad_out,
    route,
    hidden,
    slope,
):
    step = pl.program_id(0)
    half_width = down.shape[1]
    block = grad_out.shape[2]

    @pl.when(step == 0)
    def _():
        layer_last = (last_all[...].astype(f32) + last_sum[...].astype(f32)).astype(bf16)
        values = layer_last.astype(f32)
        count = values.shape[0]
        norms = jnp.sqrt(jnp.sum(values * values, axis=1, keepdims=True) + epsilon)
        unit = values / norms
        scores = dot(unit, unit, ((1,), (1,)), lax.Precision.HIGHEST) / logit_divisor
        row = lax.broadcasted_iota(jnp.int32, (count, count), 0)
        col = lax.broadcasted_iota(jnp.int32, (count, count), 1)
        exp_scores = jnp.where(row != col, jnp.exp(scores), 0.0)
        probabilities = exp_scores / jnp.sum(exp_scores, axis=1, keepdims=True)
        partner = partners[:, :1].astype(jnp.int32)
        coefficient = grad_scale * (probabilities - jnp.where(col == partner, 1.0, 0.0))
        high = lax.Precision.HIGHEST
        grad_unit = (
            dot(coefficient, unit, ((1,), (0,)), high) + dot(coefficient, unit, ((0,), (0,)), high)
        ) / logit_divisor
        projection = jnp.sum(unit * grad_unit, axis=1, keepdims=True)
        grad_last = (grad_unit - unit * projection) / norms
        route_grad = (weights[:, :1] * grad_last).astype(bf16)
        for index in range(route.shape[0]):
            route[index] = route_grad[:, index * block : (index + 1) * block]
        grad_hidden = dot(route_grad, down[0], ((1,), (1,)))
        gate, up, sigmoid_gate, activated = hidden_parts(projected[...])
        hidden[...] = (activated * up).astype(bf16)
        gate_slope = sigmoid_gate * (1.0 + gate * (1.0 - sigmoid_gate))
        slope[:, :half_width] = (grad_hidden * up * gate_slope).astype(bf16)
        slope[:, half_width:] = (grad_hidden * activated).astype(bf16)

    grad_in[0] = dot(last_block[...], slope[...], ((0,), (0,))).astype(bf16)
    grad_out[0] = dot(hidden[...], route[step], ((0,), (0,))).astype(bf16)


def body(tokens, expert_ids, gates, positives, gate_up, down):
    dp_count = lax.axis_size("dp")
    expert_count = lax.axis_size("expert")
    chips = expert_count // 2
    experts = dp_count * chips
    tok_dev, width = tokens.shape
    half_width = down.shape[1]
    seq_dev = positives.shape[0]
    seqs = dp_count * seq_dev
    seq_length = tok_dev // seq_dev
    part_rows = tok_dev // expert_count
    plane = lax.axis_index("dp")
    lane = lax.axis_index("expert")
    place = jnp.stack([plane, lane, plane * chips + lane // 2]).astype(jnp.int32)
    assert experts <= lanes and seq_length % tail == 0

    def to_lane(value, step):
        return lax.ppermute(value, "expert", [(j, j ^ step) for j in range(expert_count)])

    def to_plane(value, step):
        return lax.ppermute(value, "dp", [(p, p ^ step) for p in range(dp_count)])

    chip_steps = [2 * step for step in range(1, chips)]
    groups = [range(first, min(first + 2, dp_count)) for first in range(0, dp_count, 2)]

    share = width // chips
    packed = pl.pallas_call(
        functools.partial(pack_kernel, seq_dev),
        out_shape=jax.ShapeDtypeStruct((part_rows, width + lanes), bf16),
        in_specs=[in_smem, in_smem, in_vmem, in_vmem, anywhere],
        out_specs=in_vmem,
        scratch_shapes=[
            pltpu.VMEM((part_rows, lanes), f32),
            pltpu.VMEM((seq_dev, tail, share), bf16),
            pltpu.SemaphoreType.DMA((seq_dev + 1,)),
        ],
        compiler_params=params(4),
        cost_estimate=cost(0, 1 << 19),
        name="pack",
    )(place, positives, expert_ids, gates, tokens)
    arrivals = {hop: to_plane(packed, hop) for hop in range(1, dp_count)}
    mate_in = to_lane(gate_up, 1)
    mate_out = to_lane(down, 1)
    weights = (gate_up, down, mate_in, mate_out)

    groups.reverse()
    far_parts = []
    tiles = []
    where_tiles = [[None] * chips for _ in range(dp_count)]
    for group in groups:
        own = [arrivals[hop] for hop in group if hop]
        if group[0] == 0:
            joined = jnp.concatenate(own + [packed[:, width:]], axis=1)
        else:
            joined = jnp.concatenate(own, axis=0)
        received = [to_lane(joined, step) for step in chip_steps]
        far_parts.append(own + received)
        for index, hop in enumerate(group):
            tiles.append(packed if hop == 0 else arrivals[hop])
            where_tiles[hop][0] = (len(tiles) - 1, 0, width)
            for chip in range(1, chips):
                if group[0] == 0:
                    spot = (0, width if hop else width + lanes)
                else:
                    spot = (index * part_rows, width)
                where_tiles[hop][chip] = (chip,) + spot
        first = len(tiles)
        tiles += received
        for hop in group:
            for chip in range(1, chips):
                where_tiles[hop][chip] = (first + chip - 1,) + where_tiles[hop][chip][1:]

    def expert(group, parts, place):
        near = group[0] == 0
        block = len(group) * part_rows
        total = chips * block
        operands = [place] + [tokens] * near + parts + list(weights)
        return pl.pallas_call(
            functools.partial(expert_kernel, (chips, part_rows, near, len(parts))),
            out_shape=[jax.ShapeDtypeStruct((block, width), bf16)] * chips,
            in_specs=[in_smem] + [in_vmem] * (len(operands) - 1),
            out_specs=[in_vmem] * chips,
            scratch_shapes=[pltpu.VMEM((total, width), bf16)],
            compiler_params=params(32),
            cost_estimate=cost(2 * total * width * 6 * half_width, 12 << 20),
            name="experts",
        )(*operands)

    outs = []
    after = place
    for group, parts in zip(groups, far_parts):
        outs.append(expert(group, parts, after))
        after, _ = lax.optimization_barrier((place, outs[-1][0]))
    table_place, _ = lax.optimization_barrier((place, outs[0][0]))

    table_rows = dp_count * part_rows + seqs
    chunks = width // lanes
    sublanes = -(-seq_dev // 8) * 8
    kept, sent, last_all, partners = pl.pallas_call(
        functools.partial(table_kernel, (seq_dev, tok_dev, where_tiles, len(tiles))),
        out_shape=[
            jax.ShapeDtypeStruct((table_rows, lanes), bf16),
            jax.ShapeDtypeStruct((table_rows, lanes), bf16),
            jax.ShapeDtypeStruct((seqs, width), bf16),
            jax.ShapeDtypeStruct((seqs, lanes), f32),
        ],
        in_specs=[in_smem] + [in_vmem] * len(tiles),
        out_specs=[in_vmem] * 4,
        scratch_shapes=[
            pltpu.VMEM((dp_count, chunks, sublanes, lanes), f32),
            pltpu.VMEM((dp_count, sublanes, lanes), f32),
            pltpu.VMEM((dp_count, sublanes, lanes), f32),
        ],
        compiler_params=params(48 if dp_count > 8 else 12),
        cost_estimate=cost(0, 1 << 20),
        name="tables",
    )(table_place, *tiles)
    found = to_lane(sent, 1)

    last_projected, last_sum, last_weights = pl.pallas_call(
        last_kernel,
        out_shape=[
            jax.ShapeDtypeStruct((seqs, 2 * half_width), f32),
            jax.ShapeDtypeStruct((seqs, width), bf16),
            jax.ShapeDtypeStruct((seqs, lanes), f32),
        ],
        in_specs=[in_smem] + [in_vmem] * 5,
        out_specs=[in_vmem] * 3,
        compiler_params=params(16),
        cost_estimate=cost(2 * seqs * width * 3 * half_width, 5 << 20),
        name="last_rows",
    )(place, last_all, kept, found, gate_up, down)

    def combine(group, parts):
        out_shape = [
            jax.ShapeDtypeStruct((part_rows, width), bf16 if hop else f32) for hop in group
        ]
        layout = (chips, part_rows, tuple(group), len(group))
        return pl.pallas_call(
            functools.partial(combine_kernel, layout),
            out_shape=out_shape,
            in_specs=[in_smem] + [in_vmem] * (3 + chips),
            out_specs=[in_vmem] * len(group),
            compiler_params=params(8),
            cost_estimate=cost(0, 3 << 20),
            name="combine",
        )(place, kept, found, packed, *parts)

    sums = {}
    for group, out in zip(groups, outs):
        returned = [to_lane(out[index + 1], step) for index, step in enumerate(chip_steps)]
        for hop, value in zip(group, combine(group, [out[0]] + returned)):
            sums[hop] = value

    for step in doublings(expert_count):
        last_sum = (last_sum.astype(f32) + to_lane(last_sum, step).astype(f32)).astype(bf16)
    for step in doublings(dp_count):
        last_sum = (last_sum.astype(f32) + to_plane(last_sum, step).astype(f32)).astype(bf16)

    total = sums[0]
    for hop in range(1, dp_count):
        total = total + to_plane(sums[hop], hop).astype(f32)
    own_out = total.astype(bf16)
    pieces = [own_out] + [to_lane(own_out, step) for step in chip_steps]
    pieces += [to_lane(piece, 1) for piece in pieces]
    layer_out = pl.pallas_call(
        functools.partial(gather_kernel, chips),
        out_shape=jax.ShapeDtypeStruct((tok_dev, width), bf16),
        in_specs=[in_smem] + [in_vmem] * len(pieces),
        out_specs=in_vmem,
        compiler_params=params(4),
        cost_estimate=cost(0, 2 << 20),
        name="gather",
    )(place, *pieces)

    block = min(512, width)
    steps = width // block
    grad_gate_up, grad_down = pl.pallas_call(
        gradient_kernel,
        grid=(steps,),
        out_shape=[
            jax.ShapeDtypeStruct(gate_up.shape, bf16),
            jax.ShapeDtypeStruct(down.shape, bf16),
        ],
        in_specs=[
            pl.BlockSpec((seqs, width), lambda step: (0, 0)),
            pl.BlockSpec((seqs, block), lambda step: (0, step)),
            pl.BlockSpec((seqs, width), lambda step: (0, 0)),
            pl.BlockSpec((seqs, 2 * half_width), lambda step: (0, 0)),
            pl.BlockSpec((seqs, lanes), lambda step: (0, 0)),
            pl.BlockSpec((seqs, lanes), lambda step: (0, 0)),
            pl.BlockSpec((1, half_width, width), lambda step: (0, 0, 0)),
        ],
        out_specs=[
            pl.BlockSpec((1, block, 2 * half_width), lambda step: (0, step, 0)),
            pl.BlockSpec((1, half_width, block), lambda step: (0, 0, step)),
        ],
        scratch_shapes=[
            pltpu.VMEM((steps, seqs, block), bf16),
            pltpu.VMEM((seqs, half_width), bf16),
            pltpu.VMEM((seqs, 2 * half_width), bf16),
        ],
        compiler_params=params(24),
        cost_estimate=cost(2 * seqs * width * 4 * half_width, 7 << 20),
        name="gradients",
    )(last_all, last_all, last_sum, last_projected, last_weights, partners, down)
    return (layer_out, grad_gate_up, grad_down)


def solution(mesh):
    return jax.shard_map(
        body,
        mesh=mesh,
        in_specs=(
            P("dp", None),
            P("dp", "expert"),
            P("dp", "expert"),
            P("dp"),
            P(("dp", "expert"), None, None),
            P(("dp", "expert"), None, None),
        ),
        out_specs=(P("dp", None), P(("dp", "expert"), None, None), P(("dp", "expert"), None, None)),
        check_vma=False,
    )
```

```python
import functools

import jax
import jax.numpy as jnp
from jax import lax
from jax.experimental import pallas as pl
from jax.experimental.pallas import tpu as pltpu
from jax.sharding import PartitionSpec as P

logit_divisor = 0.05
grad_scale = 256.0
epsilon = 1e-06
lanes = 128
tail = 16
bf16 = jnp.bfloat16
f32 = jnp.float32

anywhere = pl.BlockSpec(memory_space=pl.ANY)
in_vmem = pl.BlockSpec(memory_space=pltpu.VMEM)
in_smem = pl.BlockSpec(memory_space=pltpu.SMEM)


def params(mebibytes):
    return pltpu.CompilerParams(vmem_limit_bytes=mebibytes << 20)


def cost(flops, moved):
    return pl.CostEstimate(flops=flops, transcendentals=0, bytes_accessed=moved)


def dot(left, right, dims=((1,), (0,)), precision=None):
    return lax.dot_general(
        left, right, (dims, ((), ())), precision=precision, preferred_element_type=f32
    )


def doublings(count):
    steps = [1 << bit for bit in range((count - 1).bit_length())]
    assert 1 << len(steps) == count
    return steps


def column(table, wanted):
    index = lax.broadcasted_iota(jnp.int32, table.shape, 1)
    return jnp.sum(jnp.where(index == wanted, table, 0.0), axis=1, keepdims=True)


def pack_kernel(seq_dev, place, ids, gates, tokens, out, tile, rows, sems):
    part_rows, width = out.shape[0], tokens.shape[1]
    tok_dev = tokens.shape[0]
    seq_length = tok_dev // seq_dev
    share = rows.shape[2]
    column_at = pl.multiple_of(place[1] // 2 * share, lanes)
    start = pl.multiple_of(place[1] * part_rows, part_rows)
    copies = [
        pltpu.make_async_copy(
            tokens.at[pl.ds((seq + 1) * seq_length - tail, tail), pl.ds(column_at, share)],
            rows.at[seq],
            sems.at[seq],
        )
        for seq in range(seq_dev)
    ]
    own = pltpu.make_async_copy(
        tokens.at[pl.ds(start, part_rows)], out.at[:, pl.ds(0, width)], sems.at[seq_dev]
    )
    own.start()
    for copy in copies:
        copy.start()
    note_rows = tok_dev // lanes
    tile[...] = jnp.zeros_like(tile)
    for index in range(note_rows):
        block = slice(index * lanes, (index + 1) * lanes)
        tile[index : index + 1, :] = ids[:, block].astype(f32)
        tile[note_rows + index : note_rows + index + 1, :] = gates[:, block]
    for seq in range(seq_dev):
        row = 2 * note_rows + seq
        tile[row : row + 1, :] = jnp.full((1, lanes), place[3 + seq], jnp.int32).astype(f32)
    base = part_rows - seq_dev * (share // lanes)
    for seq in range(seq_dev):
        copies[seq].wait()
        values = rows[seq].astype(f32)
        for chunk in range(share // lanes):
            row = base + chunk * seq_dev + seq
            tile[row : row + 1, :] = values[tail - 1 : tail, chunk * lanes : (chunk + 1) * lanes]
    out[:, width:] = tile[...].astype(bf16)
    own.wait()


def table_kernel(layout, place, *refs):
    seq_dev, tok_dev, where_tiles, n_parts = layout
    parts = refs[:n_parts]
    kept, sent, last_rows, partners, tokens, routes, marks = refs[n_parts:]
    part_rows = parts[0].shape[0]
    dp_count, chunks = tokens.shape[:2]
    note_rows = tok_dev // lanes
    seq_length = tok_dev // seq_dev
    chips = len(where_tiles[0])
    share_chunks = chunks // chips
    base = part_rows - seq_dev * share_chunks
    lane_index = lax.broadcasted_iota(jnp.int32, (part_rows, lanes), 1)
    row_index = lax.broadcasted_iota(jnp.int32, (part_rows, lanes), 0)

    def dense_rows(tile, lane):
        start = lane * part_rows
        picked = lane_index == row_index + start % lanes
        found = []
        for offset in (0, note_rows):
            line = tile[offset : offset + 1, :]
            for index in range(1, note_rows):
                other = tile[offset + index : offset + index + 1, :]
                line = jnp.where(start // lanes == index, other, line)
            found.append(jnp.sum(jnp.where(picked, line, 0.0), axis=1, keepdims=True))
        return jnp.where(lane_index.astype(f32) == found[0], found[1], 0.0)

    for hop in range(dp_count):
        plane = place[0] ^ hop
        sums = [None, None]
        for chip in range(chips):
            source, row, at = where_tiles[hop][chip]
            tile = parts[source][row : row + part_rows, at : at + lanes].astype(f32)
            for index, lane in enumerate((place[1], place[1] ^ 1)):
                value = dense_rows(tile, lane)
                sums[index] = value if chip == 0 else sums[index] + value
            for seq in range(seq_dev):
                at_token = (seq + 1) * seq_length - 1
                row = at_token // lanes
                here = lane_index[:1] == at_token % lanes
                expert, gate = [
                    jnp.sum(
                        jnp.where(here, tile[offset + row : offset + row + 1, :], 0.0),
                        axis=1,
                        keepdims=True,
                    )
                    for offset in (0, note_rows)
                ]
                value = jnp.where(lane_index[:1].astype(f32) == expert, gate, 0.0)
                if chip:
                    value = value + routes[plane, seq : seq + 1, :]
                routes[plane, seq : seq + 1, :] = value
            if chip == 0:
                marks[plane, 0:seq_dev, :] = tile[2 * note_rows : 2 * note_rows + seq_dev, :]
            first = ((place[1] // 2) ^ chip) * share_chunks
            for chunk in range(share_chunks):
                row = base + chunk * seq_dev
                tokens[plane, first + chunk, 0:seq_dev, :] = tile[row : row + seq_dev, :]
        at = slice(hop * part_rows, (hop + 1) * part_rows)
        kept[at, :] = sums[0].astype(bf16)
        sent[at, :] = sums[1].astype(bf16)
    last = dp_count * part_rows
    joined, shared = [], []
    for plane in range(dp_count):
        shared.append(routes[plane, 0:seq_dev, :])
        partners[plane * seq_dev : (plane + 1) * seq_dev, :] = marks[plane, 0:seq_dev, :]
        lines = [tokens[plane, chunk, 0:seq_dev, :] for chunk in range(chunks)]
        joined.append(jnp.concatenate(lines, axis=1))
    last_rows[...] = jnp.concatenate(joined, axis=0).astype(bf16)
    seqs = dp_count * seq_dev
    value = jnp.concatenate(shared, axis=0).astype(bf16)
    kept[last : last + seqs, :] = value
    sent[last : last + seqs, :] = value


def hidden_parts(projected):
    half_width = projected.shape[1] // 2
    gate, up = projected[:, :half_width], projected[:, half_width:]
    sigmoid_gate = jax.nn.sigmoid(gate)
    return gate, up, sigmoid_gate, gate * sigmoid_gate


def spread_rows(values, rows, blocks):
    chunks = values.shape[1] // lanes
    for index in range(values.shape[0] * chunks):
        row, chunk = index // chunks, index % chunks
        spot = slice(index % rows, index % rows + 1)
        block = slice(index // rows * lanes, (index // rows + 1) * lanes)
        blocks[spot, block] = values[row : row + 1, chunk * lanes : (chunk + 1) * lanes]


def expert_kernel(layout, *refs):
    chips, part_rows, near, with_last, n_parts = layout
    refs = list(refs)
    place = refs.pop(0)
    tokens = refs.pop(0) if near else None
    last_rows = refs.pop(0) if with_last else None
    parts, refs = refs[:n_parts], refs[n_parts:]
    weights, refs = refs[:4], refs[4:]
    outs, refs = refs[:chips], refs[chips:]
    if with_last:
        last_projected, own_last, by_lane, tile, *refs = refs
    (rows,) = refs
    count = outs[0].shape[0] // part_rows
    width = weights[0].shape[1]
    block = count * part_rows
    total = chips * block
    if near:
        for chip in range(chips):
            start = pl.multiple_of((place[1] ^ (2 * chip)) * part_rows, part_rows)
            at = chip * block
            rows[at : at + part_rows, :] = tokens[pl.ds(start, part_rows), :]
    own_parts = count - 1 if near else count
    for index in range(own_parts):
        at = (index + count - own_parts) * part_rows
        rows[at : at + part_rows, :] = parts[index][:, :width]
    for chip in range(1, chips):
        at = chip * block + (count - own_parts) * part_rows
        rows[at : at + own_parts * part_rows, :] = parts[own_parts + chip - 1][:, :width]
    if with_last:
        rows[total:, :] = last_rows[...]
    result = None
    for half in range(2):
        w_in, w_out = weights[2 * half], weights[2 * half + 1]
        projected = dot(rows[...], w_in[0])
        if half == 0 and with_last:
            last_projected[...] = projected[total:]
        _, up, _, activated = hidden_parts(projected)
        part = dot((activated * up).astype(bf16), w_out[0])
        result = part if half == 0 else result + part
    for chip in range(chips):
        outs[chip][:, :width] = result[chip * block : (chip + 1) * block].astype(bf16)
    if with_last:
        each = last_rows.shape[0] // by_lane.shape[0]
        floats = last_rows[...].astype(f32)
        for lane in range(by_lane.shape[0]):
            by_lane[lane, 0:each, :] = floats[lane * each : (lane + 1) * each]
        spread_rows(by_lane[place[1], 0:each, :], part_rows, tile)
        own_last[...] = tile[...]
        for lane in range(by_lane.shape[0]):
            first = total + lane * each
            by_lane[lane, 0:each, :] = result[first : first + each]
        for chip in range(chips):
            spread_rows(by_lane[place[1] ^ (2 * chip), 0:each, :], part_rows, tile)
            outs[chip][:part_rows, width:] = tile[...].astype(bf16)
            outs[chip][part_rows:, width:] = jnp.zeros((block - part_rows, tile.shape[1]), bf16)


def combine_kernel(layout, place, kept, found, *refs):
    chips, part_rows, group, with_last, width, each = layout
    own, refs = (refs[0], refs[1:]) if group[0] == 0 else (None, refs)
    last_in, refs = (None, refs) if with_last else (refs[0], refs[1:])
    parts, outs = refs[:chips], refs[chips : chips + len(group)]
    first_expert = place[2] - place[1] // 2
    experts = [first_expert + ((place[1] // 2) ^ chip) for chip in range(chips)]
    if with_last:
        last_out = refs[-1]
        last = kept.shape[0] - 2 * chips * each
        table = kept[last:, :].astype(f32) + found[last:, :].astype(f32)
        row_index = lax.broadcasted_iota(jnp.int32, table.shape, 0)
        chunks = width // lanes
        for row in range(each):
            mine = jnp.where(row_index == place[1] * each + row, table, 0.0)
            mine = jnp.sum(mine, axis=0, keepdims=True)
            first = row * chunks % part_rows
            spot = slice(first, first + chunks)
            at = row * chunks // part_rows * lanes
            total = None
            for chip in range(chips):
                values = parts[chip][spot, width + at : width + at + lanes].astype(f32)
                term = column(mine, experts[chip]) * values
                total = term if total is None else total + term
            last_out[spot, at : at + lanes] = total.astype(bf16)
        last_in = last_out
    for index, hop in enumerate(group):
        at = slice(hop * part_rows, (hop + 1) * part_rows)
        table = kept[at, :].astype(f32) + found[at, :].astype(f32)
        rows = slice(index * part_rows, (index + 1) * part_rows)
        total = own[:, :width].astype(f32) if hop == 0 else None
        for chip in range(chips):
            weight = column(table, experts[chip])
            term = weight * parts[chip][rows, :width].astype(f32)
            total = term if total is None else total + term
        outs[index][:, :width] = total.astype(outs[index].dtype)
        if hop:
            outs[index][:, width:] = last_in[...]


def finish_kernel(near, own_last, last_sum, *refs):
    parts, out = refs[:-1], refs[-1]
    width = near.shape[1]
    total = near[...]
    last = last_sum[...].astype(f32)
    for part in parts:
        total = total + part[:, :width].astype(f32)
        last = last + part[:, width:].astype(f32)
    out[:, :width] = total.astype(bf16)
    out[:, width:] = (own_last[...] + last).astype(bf16)


def gather_kernel(chips, each, place, *refs):
    pieces, (out, last_rows, by_lane) = refs[: 2 * chips], refs[2 * chips :]
    part_rows, width = pieces[0].shape[0], out.shape[1]
    chunks = width // lanes
    for index in range(2 * chips):
        lane = place[1] ^ (2 * (index % chips)) ^ (index // chips)
        piece = pieces[index]
        start = pl.multiple_of(lane * part_rows, part_rows)
        out[pl.ds(start, part_rows), :] = piece[:, :width]
        values = piece[:, width:].astype(f32)
        for spot in range(each * chunks):
            row, chunk = spot // chunks, spot % chunks
            at = spot // part_rows * lanes
            from_row = spot % part_rows
            by_lane[lane, row : row + 1, chunk * lanes : (chunk + 1) * lanes] = values[
                from_row : from_row + 1, at : at + lanes
            ]
    ordered = [by_lane[lane, 0:each, :] for lane in range(2 * chips)]
    last_rows[...] = jnp.concatenate(ordered, axis=0).astype(bf16)


def gradient_kernel(
    last_block,
    layer_last,
    projected,
    place,
    kept,
    found,
    partners,
    down,
    grad_in,
    grad_out,
    route,
    hidden,
    slope,
):
    step = pl.program_id(0)
    half_width = down.shape[1]
    block = grad_out.shape[2]

    @pl.when(step == 0)
    def _():
        values = layer_last[...].astype(f32)
        count = values.shape[0]
        last = kept.shape[0] - count
        table = kept[last:, :].astype(f32) + found[last:, :].astype(f32)
        norms = jnp.sqrt(jnp.sum(values * values, axis=1, keepdims=True) + epsilon)
        unit = values / norms
        scores = dot(unit, unit, ((1,), (1,)), lax.Precision.HIGHEST) / logit_divisor
        row = lax.broadcasted_iota(jnp.int32, (count, count), 0)
        col = lax.broadcasted_iota(jnp.int32, (count, count), 1)
        exp_scores = jnp.where(row != col, jnp.exp(scores), 0.0)
        probabilities = exp_scores / jnp.sum(exp_scores, axis=1, keepdims=True)
        partner = partners[:, :1].astype(jnp.int32)
        coefficient = grad_scale * (probabilities - jnp.where(col == partner, 1.0, 0.0))
        high = lax.Precision.HIGHEST
        grad_unit = (
            dot(coefficient, unit, ((1,), (0,)), high) + dot(coefficient, unit, ((0,), (0,)), high)
        ) / logit_divisor
        projection = jnp.sum(unit * grad_unit, axis=1, keepdims=True)
        grad_last = (grad_unit - unit * projection) / norms
        route_grad = (column(table, place[2]) * grad_last).astype(bf16)
        for index in range(route.shape[0]):
            route[index] = route_grad[:, index * block : (index + 1) * block]
        grad_hidden = dot(route_grad, down[0], ((1,), (1,)))
        gate, up, sigmoid_gate, activated = hidden_parts(projected[...])
        hidden[...] = (activated * up).astype(bf16)
        gate_slope = sigmoid_gate * (1.0 + gate * (1.0 - sigmoid_gate))
        slope[:, :half_width] = (grad_hidden * up * gate_slope).astype(bf16)
        slope[:, half_width:] = (grad_hidden * activated).astype(bf16)

    grad_in[0] = dot(last_block[...], slope[...], ((0,), (0,))).astype(bf16)
    grad_out[0] = dot(hidden[...], route[step], ((0,), (0,))).astype(bf16)


def body(tokens, expert_ids, gates, positives, gate_up, down):
    dp_count = lax.axis_size("dp")
    expert_count = lax.axis_size("expert")
    chips = expert_count // 2
    experts = dp_count * chips
    tok_dev, width = tokens.shape
    half_width = down.shape[1]
    seq_dev = positives.shape[0]
    seqs = dp_count * seq_dev
    seq_length = tok_dev // seq_dev
    part_rows = tok_dev // expert_count
    plane = lax.axis_index("dp")
    lane = lax.axis_index("expert")
    place = jnp.stack([plane, lane, plane * chips + lane // 2]).astype(jnp.int32)
    place = jnp.concatenate([place, positives])
    assert experts <= lanes and seq_length % tail == 0

    def to_lane(value, step):
        return lax.ppermute(value, "expert", [(j, j ^ step) for j in range(expert_count)])

    def to_plane(value, step):
        return lax.ppermute(value, "dp", [(p, p ^ step) for p in range(dp_count)])

    chip_steps = [2 * step for step in range(1, chips)]
    groups = [range(first, min(first + 2, dp_count)) for first in range(0, dp_count, 2)]

    share = width // chips
    packed = pl.pallas_call(
        functools.partial(pack_kernel, seq_dev),
        out_shape=jax.ShapeDtypeStruct((part_rows, width + lanes), bf16),
        in_specs=[in_smem, in_vmem, in_vmem, pl.BlockSpec(memory_space=pltpu.HBM)],
        out_specs=in_vmem,
        scratch_shapes=[
            pltpu.VMEM((part_rows, lanes), f32),
            pltpu.VMEM((seq_dev, tail, share), bf16),
            pltpu.SemaphoreType.DMA((seq_dev + 1,)),
        ],
        compiler_params=params(4),
        cost_estimate=cost(0, 1 << 19),
        name="pack",
    )(place, expert_ids.T, gates.T, tokens)
    arrivals = {hop: to_plane(packed, hop) for hop in range(1, dp_count)}
    mate_in = to_lane(gate_up, 1)
    mate_out = to_lane(down, 1)
    weights = (gate_up, down, mate_in, mate_out)

    far_parts = []
    tiles = []
    where_tiles = [[None] * chips for _ in range(dp_count)]
    for group in groups:
        own = [arrivals[hop] for hop in group if hop]
        if group[0] == 0:
            joined = jnp.concatenate(own + [packed[:, width:]], axis=1)
            joined, weights = lax.optimization_barrier((joined, weights))
        else:
            joined = jnp.concatenate(own, axis=0)
            joined, received = lax.optimization_barrier((joined, received))
            tiles[-len(received) :] = received
            far_parts[-1][-len(received) :] = received
        received = [to_lane(joined, step) for step in chip_steps]
        far_parts.append(own + received)
        for index, hop in enumerate(group):
            tiles.append(packed if hop == 0 else arrivals[hop])
            where_tiles[hop][0] = (len(tiles) - 1, 0, width)
            for chip in range(1, chips):
                if group[0] == 0:
                    spot = (0, width if hop else width + lanes)
                else:
                    spot = (index * part_rows, width)
                where_tiles[hop][chip] = (chip,) + spot
        first = len(tiles)
        tiles += received
        for hop in group:
            for chip in range(1, chips):
                where_tiles[hop][chip] = (first + chip - 1,) + where_tiles[hop][chip][1:]

    table_rows = dp_count * part_rows + seqs
    chunks = width // lanes
    sublanes = -(-seq_dev // 8) * 8
    kept, sent, last_all, partners = pl.pallas_call(
        functools.partial(table_kernel, (seq_dev, tok_dev, where_tiles, len(tiles))),
        out_shape=[
            jax.ShapeDtypeStruct((table_rows, lanes), bf16),
            jax.ShapeDtypeStruct((table_rows, lanes), bf16),
            jax.ShapeDtypeStruct((seqs, width), bf16),
            jax.ShapeDtypeStruct((seqs, lanes), f32),
        ],
        in_specs=[in_smem] + [in_vmem] * len(tiles),
        out_specs=[in_vmem] * 4,
        scratch_shapes=[
            pltpu.VMEM((dp_count, chunks, sublanes, lanes), f32),
            pltpu.VMEM((dp_count, sublanes, lanes), f32),
            pltpu.VMEM((dp_count, sublanes, lanes), f32),
        ],
        compiler_params=params(48 if dp_count > 8 else 12),
        cost_estimate=cost(0, 1 << 20),
        name="tables",
    )(place, *tiles)
    found = to_lane(sent, 1)

    each = seqs // expert_count
    extra = each * width // part_rows
    assert extra % lanes == 0 and part_rows % (width // lanes) == 0

    def expert(group, parts, place, with_last):
        near = group[0] == 0
        block = len(group) * part_rows
        total = chips * block + (seqs if with_last else 0)
        out_width = width + (extra if with_last else 0)
        out_shape = [jax.ShapeDtypeStruct((block, out_width), bf16)] * chips
        scratch = [pltpu.VMEM((total, width), bf16)]
        if with_last:
            out_shape += [
                jax.ShapeDtypeStruct((seqs, 2 * half_width), f32),
                jax.ShapeDtypeStruct((part_rows, extra), f32),
            ]
            scratch = [
                pltpu.VMEM((expert_count, -(-each // 8) * 8, width), f32),
                pltpu.VMEM((part_rows, extra), f32),
            ] + scratch
        operands = [place] + [tokens] * near + [last_all] * with_last + parts + list(weights)
        return pl.pallas_call(
            functools.partial(expert_kernel, (chips, part_rows, near, with_last, len(parts))),
            out_shape=out_shape,
            in_specs=[in_smem] + [in_vmem] * (len(operands) - 1),
            out_specs=[in_vmem] * len(out_shape),
            scratch_shapes=scratch,
            compiler_params=params(32),
            cost_estimate=cost(2 * total * width * 6 * half_width, 12 << 20),
            name="experts",
        )(*operands)

    def combine(group, parts, last_sum):
        with_last = last_sum is None
        out_shape = [
            jax.ShapeDtypeStruct((part_rows, width + extra), bf16)
            if hop
            else jax.ShapeDtypeStruct((part_rows, width), f32)
            for hop in group
        ]
        if with_last:
            out_shape.append(jax.ShapeDtypeStruct((part_rows, extra), bf16))
        layout = (chips, part_rows, tuple(group), with_last, width, each)
        operands = [place, kept, found]
        operands += [packed] * (group[0] == 0) + [last_sum] * (not with_last) + parts
        return pl.pallas_call(
            functools.partial(combine_kernel, layout),
            out_shape=out_shape,
            in_specs=[in_smem] + [in_vmem] * (len(operands) - 1),
            out_specs=[in_vmem] * len(out_shape),
            compiler_params=params(8),
            cost_estimate=cost(0, 3 << 20),
            name="combine",
        )(*operands)

    outs = []
    after = place
    for group, parts in zip(groups, far_parts):
        outs.append(expert(group, parts, after, group is groups[-1]))
        after, _ = lax.optimization_barrier((place, outs[-1][0]))
    last_projected, own_last = outs[-1][chips:]

    sums = {}
    last_sum = None
    returned = None
    for index in [len(groups) - 1] + list(range(len(groups) - 2, -1, -1)):
        group, sent_back = groups[index], list(outs[index][1:chips])
        if returned is None:
            sent_back, found = lax.optimization_barrier((sent_back, found))
        else:
            result = combine(before, [first] + returned, last_sum)
            sums.update(zip(before, result))
            last_sum = result[-1] if last_sum is None else last_sum
            sent_back, _ = lax.optimization_barrier((sent_back, result[0]))
        returned = [to_lane(value, step) for value, step in zip(sent_back, chip_steps)]
        before, first = group, outs[index][0]
    homeward = {hop: to_plane(value, hop) for hop, value in sums.items()}
    returned, homeward = lax.optimization_barrier((returned, homeward))
    result = combine(before, [first] + returned, last_sum)
    last_sum = result[-1] if last_sum is None else last_sum
    sums.update(zip(before, result))
    homeward.update({hop: to_plane(sums[hop], hop) for hop in before if hop})

    own_out = pl.pallas_call(
        finish_kernel,
        out_shape=jax.ShapeDtypeStruct((part_rows, width + extra), bf16),
        in_specs=[in_vmem] * (2 + dp_count),
        out_specs=in_vmem,
        compiler_params=params(16 if dp_count > 8 else 4),
        cost_estimate=cost(0, 1 << 20),
        name="finish",
    )(sums[0], own_last, last_sum, *homeward.values())
    pieces = [own_out] + [to_lane(own_out, step) for step in chip_steps]
    pieces += [to_lane(piece, 1) for piece in pieces]
    layer_out, layer_last = pl.pallas_call(
        functools.partial(gather_kernel, chips, each),
        out_shape=[
            jax.ShapeDtypeStruct((tok_dev, width), bf16),
            jax.ShapeDtypeStruct((seqs, width), bf16),
        ],
        in_specs=[in_smem] + [in_vmem] * len(pieces),
        out_specs=[in_vmem] * 2,
        scratch_shapes=[pltpu.VMEM((expert_count, -(-each // 8) * 8, width), f32)],
        compiler_params=params(8),
        cost_estimate=cost(0, 2 << 20),
        name="gather",
    )(place, *pieces)

    block = min(512, width)
    steps = width // block
    grad_gate_up, grad_down = pl.pallas_call(
        gradient_kernel,
        grid=(steps,),
        out_shape=[
            jax.ShapeDtypeStruct(gate_up.shape, bf16),
            jax.ShapeDtypeStruct(down.shape, bf16),
        ],
        in_specs=[
            pl.BlockSpec((seqs, block), lambda step: (0, step)),
            pl.BlockSpec((seqs, width), lambda step: (0, 0)),
            pl.BlockSpec((seqs, 2 * half_width), lambda step: (0, 0)),
            in_smem,
            pl.BlockSpec((table_rows, lanes), lambda step: (0, 0)),
            pl.BlockSpec((table_rows, lanes), lambda step: (0, 0)),
            pl.BlockSpec((seqs, lanes), lambda step: (0, 0)),
            pl.BlockSpec((1, half_width, width), lambda step: (0, 0, 0)),
        ],
        out_specs=[
            pl.BlockSpec((1, block, 2 * half_width), lambda step: (0, step, 0)),
            pl.BlockSpec((1, half_width, block), lambda step: (0, 0, step)),
        ],
        scratch_shapes=[
            pltpu.VMEM((steps, seqs, block), bf16),
            pltpu.VMEM((seqs, half_width), bf16),
            pltpu.VMEM((seqs, 2 * half_width), bf16),
        ],
        compiler_params=params(24),
        cost_estimate=cost(2 * seqs * width * 4 * half_width, 7 << 20),
        name="gradients",
    )(last_all, layer_last, last_projected, place, kept, found, partners, down)
    return (layer_out, grad_gate_up, grad_down)


def solution(mesh):
    return jax.shard_map(
        body,
        mesh=mesh,
        in_specs=(
            P("dp", None),
            P("dp", "expert"),
            P("dp", "expert"),
            P("dp"),
            P(("dp", "expert"), None, None),
            P(("dp", "expert"), None, None),
        ),
        out_specs=(P("dp", None), P(("dp", "expert"), None, None), P(("dp", "expert"), None, None)),
        check_vma=False,
    )
```

```python
import functools

import jax
import jax.numpy as jnp
from jax import lax
from jax.experimental import pallas as pl
from jax.experimental.pallas import tpu as pltpu
from jax.sharding import PartitionSpec as P

logit_divisor = 0.05
grad_scale = 256.0
epsilon = 1e-06
lanes = 128
tail = 16
bf16 = jnp.bfloat16
f32 = jnp.float32

anywhere = pl.BlockSpec(memory_space=pl.ANY)
in_vmem = pl.BlockSpec(memory_space=pltpu.VMEM)
in_smem = pl.BlockSpec(memory_space=pltpu.SMEM)


def params(mebibytes):
    return pltpu.CompilerParams(vmem_limit_bytes=mebibytes << 20)


def cost(flops, moved):
    return pl.CostEstimate(flops=flops, transcendentals=0, bytes_accessed=moved)


def dot(left, right, dims=((1,), (0,)), precision=None):
    return lax.dot_general(
        left, right, (dims, ((), ())), precision=precision, preferred_element_type=f32
    )


def doublings(count):
    steps = [1 << bit for bit in range((count - 1).bit_length())]
    assert 1 << len(steps) == count
    return steps


def column(table, wanted):
    index = lax.broadcasted_iota(jnp.int32, table.shape, 1)
    return jnp.sum(jnp.where(index == wanted, table, 0.0), axis=1, keepdims=True)


def pack_kernel(seq_dev, positives, ids, gates, tokens, out, tile, rows, sems):
    part_rows, width = out.shape[0], tokens.shape[1]
    tok_dev = tokens.shape[0]
    seq_length = tok_dev // seq_dev
    share = rows.shape[2]
    lane = lax.axis_index("expert")
    column_at = pl.multiple_of(lane // 2 * share, lanes)
    start = pl.multiple_of(lane * part_rows, part_rows)
    copies = [
        pltpu.make_async_copy(
            tokens.at[pl.ds((seq + 1) * seq_length - tail, tail), pl.ds(column_at, share)],
            rows.at[seq],
            sems.at[seq],
        )
        for seq in range(seq_dev)
    ]
    own = pltpu.make_async_copy(
        tokens.at[pl.ds(start, part_rows)], out.at[:, pl.ds(0, width)], sems.at[seq_dev]
    )
    own.start()
    for copy in copies:
        copy.start()
    note_rows = tok_dev // lanes
    tile[...] = jnp.zeros_like(tile)
    for index in range(note_rows):
        block = slice(index * lanes, (index + 1) * lanes)
        tile[index : index + 1, :] = ids[:, block].astype(f32)
        tile[note_rows + index : note_rows + index + 1, :] = gates[:, block]
    for seq in range(seq_dev):
        row = 2 * note_rows + seq
        tile[row : row + 1, :] = jnp.full((1, lanes), positives[seq], jnp.int32).astype(f32)
    base = part_rows - seq_dev * (share // lanes)
    for seq in range(seq_dev):
        copies[seq].wait()
        values = rows[seq].astype(f32)
        for chunk in range(share // lanes):
            row = base + chunk * seq_dev + seq
            tile[row : row + 1, :] = values[tail - 1 : tail, chunk * lanes : (chunk + 1) * lanes]
    out[:, width:] = tile[...].astype(bf16)
    own.wait()


def table_kernel(layout, place, *refs):
    seq_dev, tok_dev, where_tiles, n_parts = layout
    parts = refs[:n_parts]
    kept, sent, last_rows, partners, tokens, routes, marks = refs[n_parts:]
    part_rows = parts[0].shape[0]
    dp_count, chunks = tokens.shape[:2]
    note_rows = tok_dev // lanes
    seq_length = tok_dev // seq_dev
    chips = len(where_tiles[0])
    share_chunks = chunks // chips
    base = part_rows - seq_dev * share_chunks
    lane_index = lax.broadcasted_iota(jnp.int32, (part_rows, lanes), 1)
    row_index = lax.broadcasted_iota(jnp.int32, (part_rows, lanes), 0)

    def dense_rows(tile, lane):
        start = lane * part_rows
        picked = lane_index == row_index + start % lanes
        found = []
        for offset in (0, note_rows):
            line = tile[offset : offset + 1, :]
            for index in range(1, note_rows):
                other = tile[offset + index : offset + index + 1, :]
                line = jnp.where(start // lanes == index, other, line)
            found.append(jnp.sum(jnp.where(picked, line, 0.0), axis=1, keepdims=True))
        return jnp.where(lane_index.astype(f32) == found[0], found[1], 0.0)

    for hop in range(dp_count):
        plane = place[0] ^ hop
        sums = [None, None]
        for chip in range(chips):
            source, row, at = where_tiles[hop][chip]
            tile = parts[source][row : row + part_rows, at : at + lanes].astype(f32)
            for index, lane in enumerate((place[1], place[1] ^ 1)):
                value = dense_rows(tile, lane)
                sums[index] = value if chip == 0 else sums[index] + value
            for seq in range(seq_dev):
                at_token = (seq + 1) * seq_length - 1
                row = at_token // lanes
                here = lane_index[:1] == at_token % lanes
                expert, gate = [
                    jnp.sum(
                        jnp.where(here, tile[offset + row : offset + row + 1, :], 0.0),
                        axis=1,
                        keepdims=True,
                    )
                    for offset in (0, note_rows)
                ]
                value = jnp.where(lane_index[:1].astype(f32) == expert, gate, 0.0)
                if chip:
                    value = value + routes[plane, seq : seq + 1, :]
                routes[plane, seq : seq + 1, :] = value
            if chip == 0:
                marks[plane, 0:seq_dev, :] = tile[2 * note_rows : 2 * note_rows + seq_dev, :]
            first = ((place[1] // 2) ^ chip) * share_chunks
            for chunk in range(share_chunks):
                row = base + chunk * seq_dev
                tokens[plane, first + chunk, 0:seq_dev, :] = tile[row : row + seq_dev, :]
        at = slice(hop * part_rows, (hop + 1) * part_rows)
        kept[at, :] = sums[0].astype(bf16)
        sent[at, :] = sums[1].astype(bf16)
    last = dp_count * part_rows
    joined, shared = [], []
    for plane in range(dp_count):
        shared.append(routes[plane, 0:seq_dev, :])
        partners[plane * seq_dev : (plane + 1) * seq_dev, :] = marks[plane, 0:seq_dev, :]
        lines = [tokens[plane, chunk, 0:seq_dev, :] for chunk in range(chunks)]
        joined.append(jnp.concatenate(lines, axis=1))
    last_rows[...] = jnp.concatenate(joined, axis=0).astype(bf16)
    seqs = dp_count * seq_dev
    value = jnp.concatenate(shared, axis=0).astype(bf16)
    kept[last : last + seqs, :] = value
    sent[last : last + seqs, :] = value


def hidden_parts(projected):
    half_width = projected.shape[1] // 2
    gate, up = projected[:, :half_width], projected[:, half_width:]
    sigmoid_gate = jax.nn.sigmoid(gate)
    return gate, up, sigmoid_gate, gate * sigmoid_gate


def spread_rows(values, rows, blocks):
    chunks = values.shape[1] // lanes
    for index in range(values.shape[0] * chunks):
        row, chunk = index // chunks, index % chunks
        spot = slice(index % rows, index % rows + 1)
        block = slice(index // rows * lanes, (index // rows + 1) * lanes)
        blocks[spot, block] = values[row : row + 1, chunk * lanes : (chunk + 1) * lanes]


def expert_kernel(layout, *refs):
    group, chips, part_rows, with_last, sources, n_parts = layout
    refs = list(refs)
    place = refs.pop(0)
    near = 0 in group
    tokens = refs.pop(0) if near else None
    last_rows = refs.pop(0) if with_last else None
    parts, refs = refs[:n_parts], refs[n_parts:]
    weights, refs = refs[:4], refs[4:]
    n_outs = chips * len(group)
    outs, refs = refs[:n_outs], refs[n_outs:]
    if with_last:
        last_projected, own_last, by_lane, tile, *refs = refs
    (rows,) = refs
    width = weights[0].shape[1]
    total = n_outs * part_rows
    spots = [slice(index * part_rows, (index + 1) * part_rows) for index in range(n_outs)]
    if near:
        for chip in range(chips):
            start = pl.multiple_of((place[1] ^ (2 * chip)) * part_rows, part_rows)
            rows[spots[chip], :] = tokens[pl.ds(start, part_rows), :]
    for (index, row), spot in zip(sources, spots[n_outs - len(sources) :]):
        rows[spot, :] = parts[index][row : row + part_rows, :width]
    if with_last:
        rows[total:, :] = last_rows[...]
    result = None
    for half in range(2):
        w_in, w_out = weights[2 * half], weights[2 * half + 1]
        projected = dot(rows[...], w_in[0])
        if half == 0 and with_last:
            last_projected[...] = projected[total:]
        _, up, _, activated = hidden_parts(projected)
        part = dot((activated * up).astype(bf16), w_out[0])
        result = part if half == 0 else result + part
    for out, spot in zip(outs, spots):
        out[:, :width] = result[spot].astype(bf16)
    if with_last:
        each = last_rows.shape[0] // by_lane.shape[0]
        floats = last_rows[...].astype(f32)
        for lane in range(by_lane.shape[0]):
            by_lane[lane, 0:each, :] = floats[lane * each : (lane + 1) * each]
        spread_rows(by_lane[place[1], 0:each, :], part_rows, tile)
        own_last[...] = tile[...]
        for lane in range(by_lane.shape[0]):
            first = total + lane * each
            by_lane[lane, 0:each, :] = result[first : first + each]
        for chip in range(chips):
            spread_rows(by_lane[place[1] ^ (2 * chip), 0:each, :], part_rows, tile)
            outs[n_outs - chips + chip][:, width:] = tile[...].astype(bf16)


def combine_kernel(layout, place, kept, found, *refs):
    hop, chips, with_last, width, each = layout
    own, refs = (refs[0], refs[1:]) if hop == 0 else (None, refs)
    last_in, refs = (refs[0], refs[1:]) if hop and not with_last else (None, refs)
    parts, out = refs[:chips], refs[chips]
    part_rows = out.shape[0]
    first_expert = place[2] - place[1] // 2
    experts = [first_expert + ((place[1] // 2) ^ chip) for chip in range(chips)]
    if with_last:
        last_in = refs[-1]
        table = kept[-2 * chips * each :, :].astype(f32) + found[-2 * chips * each :, :].astype(f32)
        row_index = lax.broadcasted_iota(jnp.int32, table.shape, 0)
        chunks = width // lanes
        for row in range(each):
            mine = jnp.where(row_index == place[1] * each + row, table, 0.0)
            mine = jnp.sum(mine, axis=0, keepdims=True)
            first = row * chunks % part_rows
            spot = slice(first, first + chunks)
            at = row * chunks // part_rows * lanes
            total = None
            for chip in range(chips):
                values = parts[chip][spot, width + at : width + at + lanes].astype(f32)
                term = column(mine, experts[chip]) * values
                total = term if total is None else total + term
            last_in[spot, at : at + lanes] = total.astype(bf16)
    at = slice(hop * part_rows, (hop + 1) * part_rows)
    table = kept[at, :].astype(f32) + found[at, :].astype(f32)
    total = None if hop else own[:, :width].astype(f32)
    for chip in range(chips):
        term = column(table, experts[chip]) * parts[chip][:, :width].astype(f32)
        total = term if total is None else total + term
    out[:, :width] = total.astype(out.dtype)
    if hop:
        out[:, width:] = last_in[...]


def finish_kernel(near, own_last, last_sum, *refs):
    parts, out = refs[:-1], refs[-1]
    width = near.shape[1]
    total = near[...]
    last = last_sum[...].astype(f32)
    for part in parts:
        total = total + part[:, :width].astype(f32)
        last = last + part[:, width:].astype(f32)
    out[:, :width] = total.astype(bf16)
    out[:, width:] = (own_last[...] + last).astype(bf16)


def gather_kernel(chips, each, place, *refs):
    pieces, (out, last_rows, by_lane) = refs[: 2 * chips], refs[2 * chips :]
    part_rows, width = pieces[0].shape[0], out.shape[1]
    chunks = width // lanes
    for index in range(2 * chips):
        lane = place[1] ^ (2 * (index % chips)) ^ (index // chips)
        piece = pieces[index]
        start = pl.multiple_of(lane * part_rows, part_rows)
        out[pl.ds(start, part_rows), :] = piece[:, :width]
        values = piece[:, width:].astype(f32)
        for spot in range(each * chunks):
            row, chunk = spot // chunks, spot % chunks
            at = spot // part_rows * lanes
            from_row = spot % part_rows
            by_lane[lane, row : row + 1, chunk * lanes : (chunk + 1) * lanes] = values[
                from_row : from_row + 1, at : at + lanes
            ]
    ordered = [by_lane[lane, 0:each, :] for lane in range(2 * chips)]
    last_rows[...] = jnp.concatenate(ordered, axis=0).astype(bf16)


def gradient_kernel(
    last_block,
    layer_last,
    projected,
    place,
    kept,
    found,
    partners,
    down,
    grad_in,
    grad_out,
    route,
    hidden,
    slope,
):
    step = pl.program_id(0)
    half_width = down.shape[1]
    block = grad_out.shape[2]

    @pl.when(step == 0)
    def _():
        values = layer_last[...].astype(f32)
        count = values.shape[0]
        last = kept.shape[0] - count
        table = kept[last:, :].astype(f32) + found[last:, :].astype(f32)
        norms = jnp.sqrt(jnp.sum(values * values, axis=1, keepdims=True) + epsilon)
        unit = values / norms
        scores = dot(unit, unit, ((1,), (1,)), lax.Precision.HIGHEST) / logit_divisor
        row = lax.broadcasted_iota(jnp.int32, (count, count), 0)
        col = lax.broadcasted_iota(jnp.int32, (count, count), 1)
        exp_scores = jnp.where(row != col, jnp.exp(scores), 0.0)
        probabilities = exp_scores / jnp.sum(exp_scores, axis=1, keepdims=True)
        partner = partners[:, :1].astype(jnp.int32)
        coefficient = grad_scale * (probabilities - jnp.where(col == partner, 1.0, 0.0))
        high = lax.Precision.HIGHEST
        grad_unit = (
            dot(coefficient, unit, ((1,), (0,)), high) + dot(coefficient, unit, ((0,), (0,)), high)
        ) / logit_divisor
        projection = jnp.sum(unit * grad_unit, axis=1, keepdims=True)
        grad_last = (grad_unit - unit * projection) / norms
        route_grad = (column(table, place[2]) * grad_last).astype(bf16)
        for index in range(route.shape[0]):
            route[index] = route_grad[:, index * block : (index + 1) * block]
        grad_hidden = dot(route_grad, down[0], ((1,), (1,)))
        gate, up, sigmoid_gate, activated = hidden_parts(projected[...])
        hidden[...] = (activated * up).astype(bf16)
        gate_slope = sigmoid_gate * (1.0 + gate * (1.0 - sigmoid_gate))
        slope[:, :half_width] = (grad_hidden * up * gate_slope).astype(bf16)
        slope[:, half_width:] = (grad_hidden * activated).astype(bf16)

    grad_in[0] = dot(last_block[...], slope[...], ((0,), (0,))).astype(bf16)
    grad_out[0] = dot(hidden[...], route[step], ((0,), (0,))).astype(bf16)


def body(tokens, expert_ids, gates, positives, gate_up, down):
    dp_count = lax.axis_size("dp")
    expert_count = lax.axis_size("expert")
    chips = expert_count // 2
    experts = dp_count * chips
    tok_dev, width = tokens.shape
    half_width = down.shape[1]
    seq_dev = positives.shape[0]
    seqs = dp_count * seq_dev
    seq_length = tok_dev // seq_dev
    part_rows = tok_dev // expert_count
    plane = lax.axis_index("dp")
    lane = lax.axis_index("expert")
    place = jnp.stack([plane, lane, plane * chips + lane // 2]).astype(jnp.int32)
    assert experts <= lanes and seq_length % tail == 0

    def to_lane(value, step):
        return lax.ppermute(value, "expert", [(j, j ^ step) for j in range(expert_count)])

    def to_plane(value, step):
        return lax.ppermute(value, "dp", [(p, p ^ step) for p in range(dp_count)])

    chip_steps = [2 * step for step in range(1, chips)]
    groups = [range(first, min(first + 2, dp_count)) for first in range(0, dp_count, 2)]

    share = width // chips
    packed = pl.pallas_call(
        functools.partial(pack_kernel, seq_dev),
        out_shape=jax.ShapeDtypeStruct((part_rows, width + lanes), bf16),
        in_specs=[in_smem, in_vmem, in_vmem, pl.BlockSpec(memory_space=pltpu.HBM)],
        out_specs=in_vmem,
        scratch_shapes=[
            pltpu.VMEM((part_rows, lanes), f32),
            pltpu.VMEM((seq_dev, tail, share), bf16),
            pltpu.SemaphoreType.DMA((seq_dev + 1,)),
        ],
        cost_estimate=cost(0, 1 << 19),
        name="pack",
    )(positives, expert_ids.T, gates.T, tokens)
    arrivals = {hop: to_plane(packed, hop) for hop in range(1, dp_count)}
    mate_in = to_lane(gate_up, 1)
    mate_out = to_lane(down, 1)
    weights = (gate_up, down, mate_in, mate_out)

    tiles = [packed]
    spots = {}
    received = None
    for group in groups:
        own = [arrivals[hop] for hop in group if hop]
        if group[0] == 0:
            joined = jnp.concatenate(own + [packed[:, width:]], axis=1)
            joined, weights = lax.optimization_barrier((joined, weights))
        else:
            joined = jnp.concatenate(own, axis=0)
            joined, received = lax.optimization_barrier((joined, received))
            tiles[-len(received) :] = received
        first = len(tiles)
        received = [to_lane(joined, step) for step in chip_steps]
        tiles += own + received
        for index, hop in enumerate(group):
            if group[0] == 0:
                place_of = (first, 0, width) if hop else (0, 0, width)
                row, at = 0, width if hop else width + lanes
            else:
                place_of = (first + index, 0, width)
                row, at = index * part_rows, width
            spots[hop] = [place_of] + [
                (first + len(own) + chip, row, at) for chip in range(chips - 1)
            ]
    where_tiles = [spots[hop] for hop in range(dp_count)]

    table_rows = dp_count * part_rows + seqs
    chunks = width // lanes
    sublanes = -(-seq_dev // 8) * 8
    kept, sent, last_all, partners = pl.pallas_call(
        functools.partial(table_kernel, (seq_dev, tok_dev, where_tiles, len(tiles))),
        out_shape=[
            jax.ShapeDtypeStruct((table_rows, lanes), bf16),
            jax.ShapeDtypeStruct((table_rows, lanes), bf16),
            jax.ShapeDtypeStruct((seqs, width), bf16),
            jax.ShapeDtypeStruct((seqs, lanes), f32),
        ],
        in_specs=[in_smem] + [in_vmem] * len(tiles),
        out_specs=[in_vmem] * 4,
        scratch_shapes=[
            pltpu.VMEM((dp_count, chunks, sublanes, lanes), f32),
            pltpu.VMEM((dp_count, sublanes, lanes), f32),
            pltpu.VMEM((dp_count, sublanes, lanes), f32),
        ],
        compiler_params=params(48 if dp_count > 8 else 12),
        cost_estimate=cost(0, 1 << 20),
        name="tables",
    )(place, *tiles)
    found = to_lane(sent, 1)

    each = seqs // expert_count
    extra = each * width // part_rows
    assert extra % lanes == 0 and part_rows % (width // lanes) == 0

    def expert(group, place, with_last):
        near = 0 in group
        wanted = [spot for hop in group if hop for spot in where_tiles[hop]]
        used = sorted({spot[0] for spot in wanted})
        sources = tuple((used.index(spot[0]), spot[1]) for spot in wanted)
        parts = [tiles[index] for index in used]
        n_outs = chips * len(group)
        total = n_outs * part_rows + (seqs if with_last else 0)
        out_shape = [jax.ShapeDtypeStruct((part_rows, width), bf16)] * n_outs
        scratch = [pltpu.VMEM((total, width), bf16)]
        if with_last:
            wider = jax.ShapeDtypeStruct((part_rows, width + extra), bf16)
            out_shape[n_outs - chips :] = [wider] * chips
            out_shape += [
                jax.ShapeDtypeStruct((seqs, 2 * half_width), f32),
                jax.ShapeDtypeStruct((part_rows, extra), f32),
            ]
            scratch = [
                pltpu.VMEM((expert_count, -(-each // 8) * 8, width), f32),
                pltpu.VMEM((part_rows, extra), f32),
            ] + scratch
        operands = [place] + [tokens] * near + [last_all] * with_last + parts + list(weights)
        return pl.pallas_call(
            functools.partial(
                expert_kernel,
                (tuple(group), chips, part_rows, with_last, sources, len(parts)),
            ),
            out_shape=out_shape,
            in_specs=[in_smem] + [in_vmem] * (len(operands) - 1),
            out_specs=[in_vmem] * len(out_shape),
            scratch_shapes=scratch,
            compiler_params=params(32),
            cost_estimate=cost(2 * total * width * 6 * half_width, 12 << 20),
            name="experts",
        )(*operands)

    def combine(hop, parts, last_sum):
        with_last = last_sum is None
        out_shape = [jax.ShapeDtypeStruct((part_rows, width), f32)]
        if hop:
            out_shape = [jax.ShapeDtypeStruct((part_rows, width + extra), bf16)]
        if with_last:
            out_shape.append(jax.ShapeDtypeStruct((part_rows, extra), bf16))
        operands = [place, kept, found] + [packed] * (hop == 0)
        operands += [last_sum] * (hop > 0 and not with_last) + parts
        return pl.pallas_call(
            functools.partial(combine_kernel, (hop, chips, with_last, width, each)),
            out_shape=out_shape,
            in_specs=[in_smem] + [in_vmem] * (len(operands) - 1),
            out_specs=[in_vmem] * len(out_shape),
            compiler_params=params(8),
            cost_estimate=cost(0, 2 << 20),
            name="combine",
        )(*operands)

    outs = {}
    after = place
    for group in groups:
        out = expert(group, after, group is groups[-1])
        after, _ = lax.optimization_barrier((place, out[0]))
        for index, hop in enumerate(group):
            outs[hop] = out[index * chips : (index + 1) * chips]
    last_projected, own_last = out[-2:]

    returned = {}
    for hop in range(dp_count - 1, -1, -1):
        first, *sent_back = outs[hop]
        if hop == dp_count - 1:
            sent_back, found = lax.optimization_barrier((sent_back, found))
        returned[hop] = [first] + [to_lane(value, step) for value, step in zip(sent_back, chip_steps)]
    homeward = []
    last_sum = None
    for hop in range(dp_count - 1, 0, -1):
        result = combine(hop, returned[hop], last_sum)
        last_sum = result[1] if last_sum is None else last_sum
        homeward.append(to_plane(result[0], hop))
    near_sum = combine(0, returned[0], last_sum)[0]

    own_out = pl.pallas_call(
        finish_kernel,
        out_shape=jax.ShapeDtypeStruct((part_rows, width + extra), bf16),
        in_specs=[in_vmem] * (2 + dp_count),
        out_specs=in_vmem,
        compiler_params=params(16 if dp_count > 8 else 4),
        cost_estimate=cost(0, 1 << 20),
        name="finish",
    )(near_sum, own_last, last_sum, *homeward)
    pieces = [own_out] + [to_lane(own_out, step) for step in chip_steps]
    pieces += [to_lane(piece, 1) for piece in pieces]
    layer_out, layer_last = pl.pallas_call(
        functools.partial(gather_kernel, chips, each),
        out_shape=[
            jax.ShapeDtypeStruct((tok_dev, width), bf16),
            jax.ShapeDtypeStruct((seqs, width), bf16),
        ],
        in_specs=[in_smem] + [in_vmem] * len(pieces),
        out_specs=[in_vmem] * 2,
        scratch_shapes=[pltpu.VMEM((expert_count, -(-each // 8) * 8, width), f32)],
        compiler_params=params(8),
        cost_estimate=cost(0, 2 << 20),
        name="gather",
    )(place, *pieces)

    block = min(512, width)
    steps = width // block
    grad_gate_up, grad_down = pl.pallas_call(
        gradient_kernel,
        grid=(steps,),
        out_shape=[
            jax.ShapeDtypeStruct(gate_up.shape, bf16),
            jax.ShapeDtypeStruct(down.shape, bf16),
        ],
        in_specs=[
            pl.BlockSpec((seqs, block), lambda step: (0, step)),
            pl.BlockSpec((seqs, width), lambda step: (0, 0)),
            pl.BlockSpec((seqs, 2 * half_width), lambda step: (0, 0)),
            in_smem,
            pl.BlockSpec((table_rows, lanes), lambda step: (0, 0)),
            pl.BlockSpec((table_rows, lanes), lambda step: (0, 0)),
            pl.BlockSpec((seqs, lanes), lambda step: (0, 0)),
            pl.BlockSpec((1, half_width, width), lambda step: (0, 0, 0)),
        ],
        out_specs=[
            pl.BlockSpec((1, block, 2 * half_width), lambda step: (0, step, 0)),
            pl.BlockSpec((1, half_width, block), lambda step: (0, 0, step)),
        ],
        scratch_shapes=[
            pltpu.VMEM((steps, seqs, block), bf16),
            pltpu.VMEM((seqs, half_width), bf16),
            pltpu.VMEM((seqs, 2 * half_width), bf16),
        ],
        compiler_params=params(24),
        cost_estimate=cost(2 * seqs * width * 4 * half_width, 7 << 20),
        name="gradients",
    )(last_all, layer_last, last_projected, place, kept, found, partners, down)
    return (layer_out, grad_gate_up, grad_down)


def solution(mesh):
    return jax.shard_map(
        body,
        mesh=mesh,
        in_specs=(
            P("dp", None),
            P("dp", "expert"),
            P("dp", "expert"),
            P("dp"),
            P(("dp", "expert"), None, None),
            P(("dp", "expert"), None, None),
        ),
        out_specs=(P("dp", None), P(("dp", "expert"), None, None), P(("dp", "expert"), None, None)),
        check_vma=False,
    )
```

```python
import functools

import jax
import jax.numpy as jnp
from jax import lax
from jax.experimental import pallas as pl
from jax.experimental.pallas import tpu as pltpu
from jax.sharding import PartitionSpec as P

logit_divisor = 0.05
grad_scale = 256.0
epsilon = 1e-06
lanes = 128
tail = 16
bf16 = jnp.bfloat16
f32 = jnp.float32

anywhere = pl.BlockSpec(memory_space=pl.ANY)
in_vmem = pl.BlockSpec(memory_space=pltpu.VMEM)
in_smem = pl.BlockSpec(memory_space=pltpu.SMEM)


def params(mebibytes):
    return pltpu.CompilerParams(vmem_limit_bytes=mebibytes << 20)


def cost(flops, moved):
    return pl.CostEstimate(flops=flops, transcendentals=0, bytes_accessed=moved)


def dot(left, right, dims=((1,), (0,)), precision=None):
    return lax.dot_general(
        left, right, (dims, ((), ())), precision=precision, preferred_element_type=f32
    )


def doublings(count):
    steps = [1 << bit for bit in range((count - 1).bit_length())]
    assert 1 << len(steps) == count
    return steps


def column(table, wanted):
    index = lax.broadcasted_iota(jnp.int32, table.shape, 1)
    return jnp.sum(jnp.where(index == wanted, table, 0.0), axis=1, keepdims=True)


def pack_kernel(seq_dev, positives, ids, gates, tokens, out, tile, rows, sems):
    part_rows, width = out.shape[0], tokens.shape[1]
    tok_dev = tokens.shape[0]
    seq_length = tok_dev // seq_dev
    share = rows.shape[2]
    lane = lax.axis_index("expert")
    column_at = pl.multiple_of(lane // 2 * share, lanes)
    start = pl.multiple_of(lane * part_rows, part_rows)
    copies = [
        pltpu.make_async_copy(
            tokens.at[pl.ds((seq + 1) * seq_length - tail, tail), pl.ds(column_at, share)],
            rows.at[seq],
            sems.at[seq],
        )
        for seq in range(seq_dev)
    ]
    own = pltpu.make_async_copy(
        tokens.at[pl.ds(start, part_rows)], out.at[:, pl.ds(0, width)], sems.at[seq_dev]
    )
    own.start()
    for copy in copies:
        copy.start()
    note_rows = tok_dev // lanes
    tile[...] = jnp.zeros_like(tile)
    for index in range(note_rows):
        block = slice(index * lanes, (index + 1) * lanes)
        tile[index : index + 1, :] = ids[:, block].astype(f32)
        tile[note_rows + index : note_rows + index + 1, :] = gates[:, block]
    for seq in range(seq_dev):
        row = 2 * note_rows + seq
        tile[row : row + 1, :] = jnp.full((1, lanes), positives[seq], jnp.int32).astype(f32)
    base = part_rows - seq_dev * (share // lanes)
    for seq in range(seq_dev):
        copies[seq].wait()
        values = rows[seq].astype(f32)
        for chunk in range(share // lanes):
            row = base + chunk * seq_dev + seq
            tile[row : row + 1, :] = values[tail - 1 : tail, chunk * lanes : (chunk + 1) * lanes]
    out[:, width:] = tile[...].astype(bf16)
    own.wait()


def table_kernel(layout, place, *refs):
    seq_dev, tok_dev, where_tiles, n_parts = layout
    parts = refs[:n_parts]
    kept, sent, last_rows, partners, tokens, routes, marks = refs[n_parts:]
    part_rows = parts[0].shape[0]
    dp_count, chunks = tokens.shape[:2]
    note_rows = tok_dev // lanes
    seq_length = tok_dev // seq_dev
    chips = len(where_tiles[0])
    share_chunks = chunks // chips
    base = part_rows - seq_dev * share_chunks
    lane_index = lax.broadcasted_iota(jnp.int32, (part_rows, lanes), 1)
    row_index = lax.broadcasted_iota(jnp.int32, (part_rows, lanes), 0)

    def dense_rows(tile, lane):
        start = lane * part_rows
        picked = lane_index == row_index + start % lanes
        found = []
        for offset in (0, note_rows):
            line = tile[offset : offset + 1, :]
            for index in range(1, note_rows):
                other = tile[offset + index : offset + index + 1, :]
                line = jnp.where(start // lanes == index, other, line)
            found.append(jnp.sum(jnp.where(picked, line, 0.0), axis=1, keepdims=True))
        return jnp.where(lane_index.astype(f32) == found[0], found[1], 0.0)

    for hop in range(dp_count):
        plane = place[0] ^ hop
        sums = [None, None]
        for chip in range(chips):
            source, row, at = where_tiles[hop][chip]
            tile = parts[source][row : row + part_rows, at : at + lanes].astype(f32)
            for index, lane in enumerate((place[1], place[1] ^ 1)):
                value = dense_rows(tile, lane)
                sums[index] = value if chip == 0 else sums[index] + value
            for seq in range(seq_dev):
                at_token = (seq + 1) * seq_length - 1
                row = at_token // lanes
                here = lane_index[:1] == at_token % lanes
                expert, gate = [
                    jnp.sum(
                        jnp.where(here, tile[offset + row : offset + row + 1, :], 0.0),
                        axis=1,
                        keepdims=True,
                    )
                    for offset in (0, note_rows)
                ]
                value = jnp.where(lane_index[:1].astype(f32) == expert, gate, 0.0)
                if chip:
                    value = value + routes[plane, seq : seq + 1, :]
                routes[plane, seq : seq + 1, :] = value
            if chip == 0:
                marks[plane, 0:seq_dev, :] = tile[2 * note_rows : 2 * note_rows + seq_dev, :]
            first = ((place[1] // 2) ^ chip) * share_chunks
            for chunk in range(share_chunks):
                row = base + chunk * seq_dev
                tokens[plane, first + chunk, 0:seq_dev, :] = tile[row : row + seq_dev, :]
        at = slice(hop * part_rows, (hop + 1) * part_rows)
        kept[at, :] = sums[0].astype(bf16)
        sent[at, :] = sums[1].astype(bf16)
    last = dp_count * part_rows
    joined, shared = [], []
    for plane in range(dp_count):
        shared.append(routes[plane, 0:seq_dev, :])
        partners[plane * seq_dev : (plane + 1) * seq_dev, :] = marks[plane, 0:seq_dev, :]
        lines = [tokens[plane, chunk, 0:seq_dev, :] for chunk in range(chunks)]
        joined.append(jnp.concatenate(lines, axis=1))
    last_rows[...] = jnp.concatenate(joined, axis=0).astype(bf16)
    seqs = dp_count * seq_dev
    value = jnp.concatenate(shared, axis=0).astype(bf16)
    kept[last : last + seqs, :] = value
    sent[last : last + seqs, :] = value


def hidden_parts(projected):
    half_width = projected.shape[1] // 2
    gate, up = projected[:, :half_width], projected[:, half_width:]
    sigmoid_gate = jax.nn.sigmoid(gate)
    return gate, up, sigmoid_gate, gate * sigmoid_gate


def spread_rows(values, rows, blocks):
    chunks = values.shape[1] // lanes
    for index in range(values.shape[0] * chunks):
        row, chunk = index // chunks, index % chunks
        spot = slice(index % rows, index % rows + 1)
        block = slice(index // rows * lanes, (index // rows + 1) * lanes)
        blocks[spot, block] = values[row : row + 1, chunk * lanes : (chunk + 1) * lanes]


def expert_kernel(layout, *refs):
    group, chips, part_rows, with_last, sources, n_parts = layout
    refs = list(refs)
    place = refs.pop(0)
    near = 0 in group
    tokens = refs.pop(0) if near else None
    last_rows = refs.pop(0) if with_last else None
    parts, refs = refs[:n_parts], refs[n_parts:]
    weights, refs = refs[:4], refs[4:]
    n_outs = chips * len(group)
    outs, refs = refs[:n_outs], refs[n_outs:]
    if with_last:
        last_projected, own_last, by_lane, tile, *refs = refs
    (rows,) = refs
    width = weights[0].shape[1]
    total = n_outs * part_rows
    spots = [slice(index * part_rows, (index + 1) * part_rows) for index in range(n_outs)]
    if near:
        for chip in range(chips):
            start = pl.multiple_of((place[1] ^ (2 * chip)) * part_rows, part_rows)
            rows[spots[chip], :] = tokens[pl.ds(start, part_rows), :]
    for (index, row), spot in zip(sources, spots[n_outs - len(sources) :]):
        rows[spot, :] = parts[index][row : row + part_rows, :width]
    if with_last:
        rows[total:, :] = last_rows[...]
    result = None
    for half in range(2):
        w_in, w_out = weights[2 * half], weights[2 * half + 1]
        projected = dot(rows[...], w_in[0])
        if half == 0 and with_last:
            last_projected[...] = projected[total:]
        _, up, _, activated = hidden_parts(projected)
        part = dot((activated * up).astype(bf16), w_out[0])
        result = part if half == 0 else result + part
    for out, spot in zip(outs, spots):
        out[:, :width] = result[spot].astype(bf16)
    if with_last:
        each = last_rows.shape[0] // by_lane.shape[0]
        floats = last_rows[...].astype(f32)
        for lane in range(by_lane.shape[0]):
            by_lane[lane, 0:each, :] = floats[lane * each : (lane + 1) * each]
        spread_rows(by_lane[place[1], 0:each, :], part_rows, tile)
        own_last[...] = tile[...]
        for lane in range(by_lane.shape[0]):
            first = total + lane * each
            by_lane[lane, 0:each, :] = result[first : first + each]
        for chip in range(chips):
            spread_rows(by_lane[place[1] ^ (2 * chip), 0:each, :], part_rows, tile)
            outs[n_outs - chips + chip][:, width:] = tile[...].astype(bf16)


def combine_kernel(layout, place, kept, found, *refs):
    hop, chips, with_last, width, each = layout
    own, refs = (refs[0], refs[1:]) if hop == 0 else (None, refs)
    last_in, refs = (refs[0], refs[1:]) if hop and not with_last else (None, refs)
    parts, out = refs[:chips], refs[chips]
    part_rows = out.shape[0]
    first_expert = place[2] - place[1] // 2
    experts = [first_expert + ((place[1] // 2) ^ chip) for chip in range(chips)]
    if with_last:
        last_in = refs[-1]
        table = kept[-2 * chips * each :, :].astype(f32) + found[-2 * chips * each :, :].astype(f32)
        row_index = lax.broadcasted_iota(jnp.int32, table.shape, 0)
        chunks = width // lanes
        for row in range(each):
            mine = jnp.where(row_index == place[1] * each + row, table, 0.0)
            mine = jnp.sum(mine, axis=0, keepdims=True)
            first = row * chunks % part_rows
            spot = slice(first, first + chunks)
            at = row * chunks // part_rows * lanes
            total = None
            for chip in range(chips):
                values = parts[chip][spot, width + at : width + at + lanes].astype(f32)
                term = column(mine, experts[chip]) * values
                total = term if total is None else total + term
            last_in[spot, at : at + lanes] = total.astype(bf16)
    at = slice(hop * part_rows, (hop + 1) * part_rows)
    table = kept[at, :].astype(f32) + found[at, :].astype(f32)
    total = None if hop else own[:, :width].astype(f32)
    for chip in range(chips):
        term = column(table, experts[chip]) * parts[chip][:, :width].astype(f32)
        total = term if total is None else total + term
    out[:, :width] = total.astype(out.dtype)
    if hop:
        out[:, width:] = last_in[...]


def finish_kernel(near, own_last, last_sum, *refs):
    parts, (out, last_out) = refs[:-2], refs[-2:]
    width = near.shape[1]
    total = near[...]
    last = last_sum[...].astype(f32)
    for part in parts:
        total = total + part[:, :width].astype(f32)
        last = last + part[:, width:].astype(f32)
    out[...] = total.astype(bf16)
    last_out[...] = (own_last[...] + last).astype(bf16)


def gather_kernel(chips, place, *refs):
    pieces, out = refs[: 2 * chips], refs[-1]
    part_rows = pieces[0].shape[0]
    for index in range(2 * chips):
        lane = place[1] ^ (2 * (index % chips)) ^ (index // chips)
        start = pl.multiple_of(lane * part_rows, part_rows)
        out[pl.ds(start, part_rows), :] = pieces[index][...]


def collect_rows(lane, shares, by_lane, each):
    chunks = by_lane.shape[2] // lanes
    part_rows = shares[0].shape[0] // 2
    for index in range(2 * len(shares)):
        source = lane ^ index
        first = index % 2 * part_rows
        values = shares[index // 2][first : first + part_rows, :].astype(f32)
        for spot in range(each * chunks):
            row, chunk = spot // chunks, spot % chunks
            at = spot // part_rows * lanes
            from_row = spot % part_rows
            by_lane[source, row : row + 1, chunk * lanes : (chunk + 1) * lanes] = values[
                from_row : from_row + 1, at : at + lanes
            ]
    ordered = [by_lane[index, 0:each, :] for index in range(2 * len(shares))]
    return jnp.concatenate(ordered, axis=0)


def gradient_kernel(chips, *refs):
    shares, refs = refs[:chips], refs[chips:]
    last_block, projected, place, kept, found, partners, down, *refs = refs
    grad_in, grad_out, route, hidden, slope, by_lane = refs
    step = pl.program_id(0)
    half_width = down.shape[1]
    block = grad_out.shape[2]

    @pl.when(step == 0)
    def _():
        each = projected.shape[0] // by_lane.shape[0]
        values = collect_rows(place[1], shares, by_lane, each)
        count = values.shape[0]
        last = kept.shape[0] - count
        table = kept[last:, :].astype(f32) + found[last:, :].astype(f32)
        norms = jnp.sqrt(jnp.sum(values * values, axis=1, keepdims=True) + epsilon)
        unit = values / norms
        scores = dot(unit, unit, ((1,), (1,)), lax.Precision.HIGHEST) / logit_divisor
        row = lax.broadcasted_iota(jnp.int32, (count, count), 0)
        col = lax.broadcasted_iota(jnp.int32, (count, count), 1)
        exp_scores = jnp.where(row != col, jnp.exp(scores), 0.0)
        probabilities = exp_scores / jnp.sum(exp_scores, axis=1, keepdims=True)
        partner = partners[:, :1].astype(jnp.int32)
        coefficient = grad_scale * (probabilities - jnp.where(col == partner, 1.0, 0.0))
        high = lax.Precision.HIGHEST
        grad_unit = (
            dot(coefficient, unit, ((1,), (0,)), high) + dot(coefficient, unit, ((0,), (0,)), high)
        ) / logit_divisor
        projection = jnp.sum(unit * grad_unit, axis=1, keepdims=True)
        grad_last = (grad_unit - unit * projection) / norms
        route_grad = (column(table, place[2]) * grad_last).astype(bf16)
        for index in range(route.shape[0]):
            route[index] = route_grad[:, index * block : (index + 1) * block]
        grad_hidden = dot(route_grad, down[0], ((1,), (1,)))
        gate, up, sigmoid_gate, activated = hidden_parts(projected[...])
        hidden[...] = (activated * up).astype(bf16)
        gate_slope = sigmoid_gate * (1.0 + gate * (1.0 - sigmoid_gate))
        slope[:, :half_width] = (grad_hidden * up * gate_slope).astype(bf16)
        slope[:, half_width:] = (grad_hidden * activated).astype(bf16)

    grad_in[0] = dot(last_block[...], slope[...], ((0,), (0,))).astype(bf16)
    grad_out[0] = dot(hidden[...], route[step], ((0,), (0,))).astype(bf16)


def body(tokens, expert_ids, gates, positives, gate_up, down):
    dp_count = lax.axis_size("dp")
    expert_count = lax.axis_size("expert")
    chips = expert_count // 2
    experts = dp_count * chips
    tok_dev, width = tokens.shape
    half_width = down.shape[1]
    seq_dev = positives.shape[0]
    seqs = dp_count * seq_dev
    seq_length = tok_dev // seq_dev
    part_rows = tok_dev // expert_count
    plane = lax.axis_index("dp")
    lane = lax.axis_index("expert")
    place = jnp.stack([plane, lane, plane * chips + lane // 2]).astype(jnp.int32)
    assert experts <= lanes and seq_length % tail == 0

    def to_lane(value, step):
        return lax.ppermute(value, "expert", [(j, j ^ step) for j in range(expert_count)])

    def to_plane(value, step):
        return lax.ppermute(value, "dp", [(p, p ^ step) for p in range(dp_count)])

    chip_steps = [2 * step for step in range(1, chips)]
    groups = [range(first, min(first + 2, dp_count)) for first in range(0, dp_count, 2)]

    share = width // chips
    packed = pl.pallas_call(
        functools.partial(pack_kernel, seq_dev),
        out_shape=jax.ShapeDtypeStruct((part_rows, width + lanes), bf16),
        in_specs=[in_smem, in_vmem, in_vmem, pl.BlockSpec(memory_space=pltpu.HBM)],
        out_specs=in_vmem,
        scratch_shapes=[
            pltpu.VMEM((part_rows, lanes), f32),
            pltpu.VMEM((seq_dev, tail, share), bf16),
            pltpu.SemaphoreType.DMA((seq_dev + 1,)),
        ],
        cost_estimate=cost(0, 1 << 19),
        name="pack",
    )(positives, expert_ids.T, gates.T, tokens)
    arrivals = {hop: to_plane(packed, hop) for hop in range(1, dp_count)}
    mate_in = to_lane(gate_up, 1)
    mate_out = to_lane(down, 1)
    weights = (gate_up, down, mate_in, mate_out)

    tiles = [packed]
    spots = {}
    received = None
    for group in groups:
        own = [arrivals[hop] for hop in group if hop]
        if group[0] == 0:
            joined = jnp.concatenate(own + [packed[:, width:]], axis=1)
            joined, weights = lax.optimization_barrier((joined, weights))
        else:
            joined = jnp.concatenate(own, axis=0)
            joined, received = lax.optimization_barrier((joined, received))
            tiles[-len(received) :] = received
        first = len(tiles)
        received = [to_lane(joined, step) for step in chip_steps]
        tiles += own + received
        for index, hop in enumerate(group):
            if group[0] == 0:
                place_of = (first, 0, width) if hop else (0, 0, width)
                row, at = 0, width if hop else width + lanes
            else:
                place_of = (first + index, 0, width)
                row, at = index * part_rows, width
            spots[hop] = [place_of] + [
                (first + len(own) + chip, row, at) for chip in range(chips - 1)
            ]
    where_tiles = [spots[hop] for hop in range(dp_count)]

    table_rows = dp_count * part_rows + seqs
    chunks = width // lanes
    sublanes = -(-seq_dev // 8) * 8
    kept, sent, last_all, partners = pl.pallas_call(
        functools.partial(table_kernel, (seq_dev, tok_dev, where_tiles, len(tiles))),
        out_shape=[
            jax.ShapeDtypeStruct((table_rows, lanes), bf16),
            jax.ShapeDtypeStruct((table_rows, lanes), bf16),
            jax.ShapeDtypeStruct((seqs, width), bf16),
            jax.ShapeDtypeStruct((seqs, lanes), f32),
        ],
        in_specs=[in_smem] + [in_vmem] * len(tiles),
        out_specs=[in_vmem] * 4,
        scratch_shapes=[
            pltpu.VMEM((dp_count, chunks, sublanes, lanes), f32),
            pltpu.VMEM((dp_count, sublanes, lanes), f32),
            pltpu.VMEM((dp_count, sublanes, lanes), f32),
        ],
        compiler_params=params(48 if dp_count > 8 else 12),
        cost_estimate=cost(0, 1 << 20),
        name="tables",
    )(place, *tiles)
    found = to_lane(sent, 1)

    each = seqs // expert_count
    extra = each * width // part_rows
    assert extra % lanes == 0 and part_rows % (width // lanes) == 0

    def expert(group, place, with_last):
        near = 0 in group
        wanted = [spot for hop in group if hop for spot in where_tiles[hop]]
        used = sorted({spot[0] for spot in wanted})
        sources = tuple((used.index(spot[0]), spot[1]) for spot in wanted)
        parts = [tiles[index] for index in used]
        n_outs = chips * len(group)
        total = n_outs * part_rows + (seqs if with_last else 0)
        out_shape = [jax.ShapeDtypeStruct((part_rows, width), bf16)] * n_outs
        scratch = [pltpu.VMEM((total, width), bf16)]
        if with_last:
            wider = jax.ShapeDtypeStruct((part_rows, width + extra), bf16)
            out_shape[n_outs - chips :] = [wider] * chips
            out_shape += [
                jax.ShapeDtypeStruct((seqs, 2 * half_width), f32),
                jax.ShapeDtypeStruct((part_rows, extra), f32),
            ]
            scratch = [
                pltpu.VMEM((expert_count, -(-each // 8) * 8, width), f32),
                pltpu.VMEM((part_rows, extra), f32),
            ] + scratch
        operands = [place] + [tokens] * near + [last_all] * with_last + parts + list(weights)
        return pl.pallas_call(
            functools.partial(
                expert_kernel,
                (tuple(group), chips, part_rows, with_last, sources, len(parts)),
            ),
            out_shape=out_shape,
            in_specs=[in_smem] + [in_vmem] * (len(operands) - 1),
            out_specs=[in_vmem] * len(out_shape),
            scratch_shapes=scratch,
            compiler_params=params(32),
            cost_estimate=cost(2 * total * width * 6 * half_width, 12 << 20),
            name="experts",
        )(*operands)

    def combine(hop, parts, last_sum):
        with_last = last_sum is None
        out_shape = [jax.ShapeDtypeStruct((part_rows, width), f32)]
        if hop:
            out_shape = [jax.ShapeDtypeStruct((part_rows, width + extra), bf16)]
        if with_last:
            out_shape.append(jax.ShapeDtypeStruct((part_rows, extra), bf16))
        operands = [place, kept, found] + [packed] * (hop == 0)
        operands += [last_sum] * (hop > 0 and not with_last) + parts
        return pl.pallas_call(
            functools.partial(combine_kernel, (hop, chips, with_last, width, each)),
            out_shape=out_shape,
            in_specs=[in_smem] + [in_vmem] * (len(operands) - 1),
            out_specs=[in_vmem] * len(out_shape),
            compiler_params=params(8),
            cost_estimate=cost(0, 2 << 20),
            name="combine",
        )(*operands)

    outs = {}
    after = place
    for group in groups:
        out = expert(group, after, group is groups[-1])
        after, _ = lax.optimization_barrier((place, out[0]))
        for index, hop in enumerate(group):
            outs[hop] = out[index * chips : (index + 1) * chips]
    last_projected, own_last = out[-2:]

    returned = {}
    for hop in [0] + list(range(dp_count - 1, 0, -1)):
        first, *sent_back = outs[hop]
        if hop == dp_count - 1:
            sent_back, found, returned[0][1:] = lax.optimization_barrier(
                (sent_back, found, returned[0][1:])
            )
        returned[hop] = [first] + [to_lane(value, step) for value, step in zip(sent_back, chip_steps)]
    homeward = []
    last_sum = None
    for hop in range(dp_count - 1, 0, -1):
        result = combine(hop, returned[hop], last_sum)
        last_sum = result[1] if last_sum is None else last_sum
        homeward.append(to_plane(result[0], hop))
    near_sum = combine(0, returned[0], last_sum)[0]

    own_out, share = pl.pallas_call(
        finish_kernel,
        out_shape=[
            jax.ShapeDtypeStruct((part_rows, width), bf16),
            jax.ShapeDtypeStruct((part_rows, extra), bf16),
        ],
        in_specs=[in_vmem] * (2 + dp_count),
        out_specs=[in_vmem] * 2,
        compiler_params=params(16 if dp_count > 8 else 4),
        cost_estimate=cost(0, 1 << 20),
        name="finish",
    )(near_sum, own_last, last_sum, *homeward)
    shares = [jnp.concatenate([share, to_lane(share, 1)], axis=0)]
    shares += [to_lane(shares[0], step) for step in chip_steps]
    pieces = [own_out] + [to_lane(own_out, step) for step in chip_steps]
    pieces += [to_lane(piece, 1) for piece in pieces]
    layer_out = pl.pallas_call(
        functools.partial(gather_kernel, chips),
        out_shape=jax.ShapeDtypeStruct((tok_dev, width), bf16),
        in_specs=[in_smem] + [in_vmem] * len(pieces),
        out_specs=in_vmem,
        compiler_params=params(4),
        cost_estimate=cost(0, 2 << 20),
        name="gather",
    )(place, *pieces)

    block = min(512, width)
    steps = width // block
    grad_gate_up, grad_down = pl.pallas_call(
        functools.partial(gradient_kernel, chips),
        grid=(steps,),
        out_shape=[
            jax.ShapeDtypeStruct(gate_up.shape, bf16),
            jax.ShapeDtypeStruct(down.shape, bf16),
        ],
        in_specs=[
            *[pl.BlockSpec((2 * part_rows, extra), lambda step: (0, 0))] * chips,
            pl.BlockSpec((seqs, block), lambda step: (0, step)),
            pl.BlockSpec((seqs, 2 * half_width), lambda step: (0, 0)),
            in_smem,
            pl.BlockSpec((table_rows, lanes), lambda step: (0, 0)),
            pl.BlockSpec((table_rows, lanes), lambda step: (0, 0)),
            pl.BlockSpec((seqs, lanes), lambda step: (0, 0)),
            pl.BlockSpec((1, half_width, width), lambda step: (0, 0, 0)),
        ],
        out_specs=[
            pl.BlockSpec((1, block, 2 * half_width), lambda step: (0, step, 0)),
            pl.BlockSpec((1, half_width, block), lambda step: (0, 0, step)),
        ],
        scratch_shapes=[
            pltpu.VMEM((steps, seqs, block), bf16),
            pltpu.VMEM((seqs, half_width), bf16),
            pltpu.VMEM((seqs, 2 * half_width), bf16),
            pltpu.VMEM((expert_count, -(-each // 8) * 8, width), f32),
        ],
        compiler_params=params(24),
        cost_estimate=cost(2 * seqs * width * 4 * half_width, 7 << 20),
        name="gradients",
    )(*shares, last_all, last_projected, place, kept, found, partners, down)
    return (layer_out, grad_gate_up, grad_down)


def solution(mesh):
    return jax.shard_map(
        body,
        mesh=mesh,
        in_specs=(
            P("dp", None),
            P("dp", "expert"),
            P("dp", "expert"),
            P("dp"),
            P(("dp", "expert"), None, None),
            P(("dp", "expert"), None, None),
        ),
        out_specs=(P("dp", None), P(("dp", "expert"), None, None), P(("dp", "expert"), None, None)),
        check_vma=False,
    )
```

```python
import functools

import jax
import jax.numpy as jnp
from jax import lax
from jax.experimental import pallas as pl
from jax.experimental.pallas import tpu as pltpu
from jax.sharding import PartitionSpec as P

logit_divisor = 0.05
grad_scale = 256.0
epsilon = 1e-06
lanes = 128
tail = 16
bf16 = jnp.bfloat16
f32 = jnp.float32

anywhere = pl.BlockSpec(memory_space=pl.ANY)
in_vmem = pl.BlockSpec(memory_space=pltpu.VMEM)
in_smem = pl.BlockSpec(memory_space=pltpu.SMEM)


def params(mebibytes):
    return pltpu.CompilerParams(vmem_limit_bytes=mebibytes << 20)


def cost(flops, moved):
    return pl.CostEstimate(flops=flops, transcendentals=0, bytes_accessed=moved)


def dot(left, right, dims=((1,), (0,)), precision=None):
    return lax.dot_general(
        left, right, (dims, ((), ())), precision=precision, preferred_element_type=f32
    )


def doublings(count):
    steps = [1 << bit for bit in range((count - 1).bit_length())]
    assert 1 << len(steps) == count
    return steps


def column(table, wanted):
    index = lax.broadcasted_iota(jnp.int32, table.shape, 1)
    return jnp.sum(jnp.where(index == wanted, table, 0.0), axis=1, keepdims=True)


def pack_kernel(seq_dev, positives, ids, gates, tokens, out, tile, rows, sems):
    part_rows, width = out.shape[0], tokens.shape[1]
    tok_dev = tokens.shape[0]
    seq_length = tok_dev // seq_dev
    share = rows.shape[2]
    lane = lax.axis_index("expert")
    column_at = pl.multiple_of(lane // 2 * share, lanes)
    start = pl.multiple_of(lane * part_rows, part_rows)
    copies = [
        pltpu.make_async_copy(
            tokens.at[pl.ds((seq + 1) * seq_length - tail, tail), pl.ds(column_at, share)],
            rows.at[seq],
            sems.at[seq],
        )
        for seq in range(seq_dev)
    ]
    own = pltpu.make_async_copy(
        tokens.at[pl.ds(start, part_rows)], out.at[:, pl.ds(0, width)], sems.at[seq_dev]
    )
    own.start()
    for copy in copies:
        copy.start()
    note_rows = tok_dev // lanes
    tile[...] = jnp.zeros_like(tile)
    for index in range(note_rows):
        block = slice(index * lanes, (index + 1) * lanes)
        tile[index : index + 1, :] = ids[:, block].astype(f32)
        tile[note_rows + index : note_rows + index + 1, :] = gates[:, block]
    for seq in range(seq_dev):
        row = 2 * note_rows + seq
        tile[row : row + 1, :] = jnp.full((1, lanes), positives[seq], jnp.int32).astype(f32)
    base = part_rows - seq_dev * (share // lanes)
    for seq in range(seq_dev):
        copies[seq].wait()
        values = rows[seq].astype(f32)
        for chunk in range(share // lanes):
            row = base + chunk * seq_dev + seq
            tile[row : row + 1, :] = values[tail - 1 : tail, chunk * lanes : (chunk + 1) * lanes]
    out[:, width:] = tile[...].astype(bf16)
    own.wait()


def table_kernel(layout, place, *refs):
    seq_dev, tok_dev, where_tiles, n_parts = layout
    parts = refs[:n_parts]
    kept, sent, last_rows, partners, tokens, routes, marks = refs[n_parts:]
    part_rows = parts[0].shape[0]
    dp_count, chunks = tokens.shape[:2]
    note_rows = tok_dev // lanes
    seq_length = tok_dev // seq_dev
    chips = len(where_tiles[0])
    share_chunks = chunks // chips
    base = part_rows - seq_dev * share_chunks
    lane_index = lax.broadcasted_iota(jnp.int32, (part_rows, lanes), 1)
    row_index = lax.broadcasted_iota(jnp.int32, (part_rows, lanes), 0)

    def dense_rows(tile, lane):
        start = lane * part_rows
        picked = lane_index == row_index + start % lanes
        found = []
        for offset in (0, note_rows):
            line = tile[offset : offset + 1, :]
            for index in range(1, note_rows):
                other = tile[offset + index : offset + index + 1, :]
                line = jnp.where(start // lanes == index, other, line)
            found.append(jnp.sum(jnp.where(picked, line, 0.0), axis=1, keepdims=True))
        return jnp.where(lane_index.astype(f32) == found[0], found[1], 0.0)

    for hop in range(dp_count):
        plane = place[0] ^ hop
        sums = [None, None]
        for chip in range(chips):
            source, row, at = where_tiles[hop][chip]
            tile = parts[source][row : row + part_rows, at : at + lanes].astype(f32)
            for index, lane in enumerate((place[1], place[1] ^ 1)):
                value = dense_rows(tile, lane)
                sums[index] = value if chip == 0 else sums[index] + value
            for seq in range(seq_dev):
                at_token = (seq + 1) * seq_length - 1
                row = at_token // lanes
                here = lane_index[:1] == at_token % lanes
                expert, gate = [
                    jnp.sum(
                        jnp.where(here, tile[offset + row : offset + row + 1, :], 0.0),
                        axis=1,
                        keepdims=True,
                    )
                    for offset in (0, note_rows)
                ]
                value = jnp.where(lane_index[:1].astype(f32) == expert, gate, 0.0)
                if chip:
                    value = value + routes[plane, seq : seq + 1, :]
                routes[plane, seq : seq + 1, :] = value
            if chip == 0:
                marks[plane, 0:seq_dev, :] = tile[2 * note_rows : 2 * note_rows + seq_dev, :]
            first = ((place[1] // 2) ^ chip) * share_chunks
            for chunk in range(share_chunks):
                row = base + chunk * seq_dev
                tokens[plane, first + chunk, 0:seq_dev, :] = tile[row : row + seq_dev, :]
        at = slice(hop * part_rows, (hop + 1) * part_rows)
        kept[at, :] = sums[0].astype(bf16)
        sent[at, :] = sums[1].astype(bf16)
    last = dp_count * part_rows
    joined, shared = [], []
    for plane in range(dp_count):
        shared.append(routes[plane, 0:seq_dev, :])
        partners[plane * seq_dev : (plane + 1) * seq_dev, :] = marks[plane, 0:seq_dev, :]
        lines = [tokens[plane, chunk, 0:seq_dev, :] for chunk in range(chunks)]
        joined.append(jnp.concatenate(lines, axis=1))
    last_rows[...] = jnp.concatenate(joined, axis=0).astype(bf16)
    seqs = dp_count * seq_dev
    value = jnp.concatenate(shared, axis=0).astype(bf16)
    kept[last : last + seqs, :] = value
    sent[last : last + seqs, :] = value


def hidden_parts(projected):
    half_width = projected.shape[1] // 2
    gate, up = projected[:, :half_width], projected[:, half_width:]
    sigmoid_gate = jax.nn.sigmoid(gate)
    return gate, up, sigmoid_gate, gate * sigmoid_gate


def spread_rows(values, rows, blocks):
    chunks = values.shape[1] // lanes
    for index in range(values.shape[0] * chunks):
        row, chunk = index // chunks, index % chunks
        spot = slice(index % rows, index % rows + 1)
        block = slice(index // rows * lanes, (index // rows + 1) * lanes)
        blocks[spot, block] = values[row : row + 1, chunk * lanes : (chunk + 1) * lanes]


def expert_kernel(layout, *refs):
    group, chips, part_rows, with_last, sources, n_parts = layout
    refs = list(refs)
    place = refs.pop(0)
    near = 0 in group
    tokens = refs.pop(0) if near else None
    last_rows = refs.pop(0) if with_last else None
    parts, refs = refs[:n_parts], refs[n_parts:]
    weights, refs = refs[:4], refs[4:]
    n_outs = chips * len(group)
    outs, refs = refs[:n_outs], refs[n_outs:]
    if with_last:
        last_projected, own_last, by_lane, tile, *refs = refs
    (rows,) = refs
    width = weights[0].shape[1]
    total = n_outs * part_rows
    spots = [slice(index * part_rows, (index + 1) * part_rows) for index in range(n_outs)]
    if near:
        for chip in range(chips):
            start = pl.multiple_of((place[1] ^ (2 * chip)) * part_rows, part_rows)
            rows[spots[chip], :] = tokens[pl.ds(start, part_rows), :]
    for (index, row), spot in zip(sources, spots[n_outs - len(sources) :]):
        rows[spot, :] = parts[index][row : row + part_rows, :width]
    if with_last:
        rows[total:, :] = last_rows[...]
    result = None
    for half in range(2):
        w_in, w_out = weights[2 * half], weights[2 * half + 1]
        projected = dot(rows[...], w_in[0])
        if half == 0 and with_last:
            last_projected[...] = projected[total:]
        _, up, _, activated = hidden_parts(projected)
        part = dot((activated * up).astype(bf16), w_out[0])
        result = part if half == 0 else result + part
    for out, spot in zip(outs, spots):
        out[:, :width] = result[spot].astype(bf16)
    if with_last:
        each = last_rows.shape[0] // by_lane.shape[0]
        floats = last_rows[...].astype(f32)
        for lane in range(by_lane.shape[0]):
            by_lane[lane, 0:each, :] = floats[lane * each : (lane + 1) * each]
        spread_rows(by_lane[place[1], 0:each, :], part_rows, tile)
        own_last[...] = tile[...]
        for lane in range(by_lane.shape[0]):
            first = total + lane * each
            by_lane[lane, 0:each, :] = result[first : first + each]
        for chip in range(chips):
            spread_rows(by_lane[place[1] ^ (2 * chip), 0:each, :], part_rows, tile)
            outs[n_outs - chips + chip][:, width:] = tile[...].astype(bf16)


def combine_kernel(layout, place, kept, found, *refs):
    hop, chips, with_last, width, each = layout
    own, refs = (refs[0], refs[1:]) if hop == 0 else (None, refs)
    last_in, refs = (refs[0], refs[1:]) if hop and not with_last else (None, refs)
    parts, out = refs[:chips], refs[chips]
    part_rows = out.shape[0]
    first_expert = place[2] - place[1] // 2
    experts = [first_expert + ((place[1] // 2) ^ chip) for chip in range(chips)]
    if with_last:
        last_in = refs[-1]
        table = kept[-2 * chips * each :, :].astype(f32) + found[-2 * chips * each :, :].astype(f32)
        row_index = lax.broadcasted_iota(jnp.int32, table.shape, 0)
        chunks = width // lanes
        for row in range(each):
            mine = jnp.where(row_index == place[1] * each + row, table, 0.0)
            mine = jnp.sum(mine, axis=0, keepdims=True)
            first = row * chunks % part_rows
            spot = slice(first, first + chunks)
            at = row * chunks // part_rows * lanes
            total = None
            for chip in range(chips):
                values = parts[chip][spot, width + at : width + at + lanes].astype(f32)
                term = column(mine, experts[chip]) * values
                total = term if total is None else total + term
            last_in[spot, at : at + lanes] = total.astype(bf16)
    at = slice(hop * part_rows, (hop + 1) * part_rows)
    table = kept[at, :].astype(f32) + found[at, :].astype(f32)
    total = None if hop else own[:, :width].astype(f32)
    for chip in range(chips):
        term = column(table, experts[chip]) * parts[chip][:, :width].astype(f32)
        total = term if total is None else total + term
    out[:, :width] = total.astype(out.dtype)
    if hop:
        out[:, width:] = last_in[...]


def finish_kernel(near, own_last, last_sum, *refs):
    parts, out = refs[:-1], refs[-1]
    width = near.shape[1]
    total = near[...]
    last = last_sum[...].astype(f32)
    for part in parts:
        total = total + part[:, :width].astype(f32)
        last = last + part[:, width:].astype(f32)
    out[:, :width] = total.astype(bf16)
    out[:, width:] = (own_last[...] + last).astype(bf16)


def gather_rows(lane, pieces, out, by_lane, each):
    part_rows, width = pieces[0].shape[0], out.shape[1]
    chunks = width // lanes
    count = len(pieces)
    for index in range(count):
        source = lane ^ (2 * (index % (count // 2))) ^ (index // (count // 2))
        start = pl.multiple_of(source * part_rows, part_rows)
        out[pl.ds(start, part_rows), :] = pieces[index][:, :width]
        values = pieces[index][:, width:].astype(f32)
        for spot in range(each * chunks):
            row, chunk = spot // chunks, spot % chunks
            at = spot // part_rows * lanes
            from_row = spot % part_rows
            by_lane[source, row : row + 1, chunk * lanes : (chunk + 1) * lanes] = values[
                from_row : from_row + 1, at : at + lanes
            ]
    return jnp.concatenate([by_lane[index, 0:each, :] for index in range(count)], axis=0)


def both_ways(coefficient, unit, diagonal):
    count = unit.shape[0]
    if count > 32:
        high = lax.Precision.HIGHEST
        there = dot(coefficient, unit, ((1,), (0,)), high)
        return there + dot(coefficient, unit, ((0,), (0,)), high)
    total = None
    for index in range(count):
        line = jnp.where(diagonal, coefficient[index : index + 1, :], 0.0)
        factor = coefficient[:, index : index + 1] + jnp.sum(line, axis=1, keepdims=True)
        term = factor * unit[index : index + 1, :]
        total = term if total is None else total + term
    return total


def final_kernel(n_pieces, *refs):
    pieces, refs = refs[:n_pieces], refs[n_pieces:]
    last_block, projected, place, kept, found, partners, down, *refs = refs
    layer_out, grad_in, grad_out, route, hidden, slope, by_lane = refs
    step = pl.program_id(0)
    half_width = down.shape[1]
    block = grad_out.shape[2]

    @pl.when(step == 0)
    def _():
        each = projected.shape[0] // by_lane.shape[0]
        values = gather_rows(place[1], pieces, layer_out, by_lane, each)
        count = values.shape[0]
        last = kept.shape[0] - count
        table = kept[last:, :].astype(f32) + found[last:, :].astype(f32)
        row = lax.broadcasted_iota(jnp.int32, (count, count), 0)
        col = lax.broadcasted_iota(jnp.int32, (count, count), 1)
        norms = jnp.sqrt(jnp.sum(values * values, axis=1, keepdims=True) + epsilon)
        norms_line = jnp.sum(jnp.where(row == col, norms, 0.0), axis=0, keepdims=True)
        unit = values / norms
        rows = values.astype(bf16)
        scores = dot(rows, rows, ((1,), (1,))) / (norms * norms_line) / logit_divisor
        exp_scores = jnp.where(row != col, jnp.exp(scores), 0.0)
        probabilities = exp_scores / jnp.sum(exp_scores, axis=1, keepdims=True)
        partner = partners[:, :1].astype(jnp.int32)
        coefficient = grad_scale * (probabilities - jnp.where(col == partner, 1.0, 0.0))
        grad_unit = both_ways(coefficient, unit, row == col) / logit_divisor
        projection = jnp.sum(unit * grad_unit, axis=1, keepdims=True)
        grad_last = (grad_unit - unit * projection) / norms
        route_grad = (column(table, place[2]) * grad_last).astype(bf16)
        for index in range(route.shape[0]):
            route[index] = route_grad[:, index * block : (index + 1) * block]
        grad_hidden = dot(route_grad, down[0], ((1,), (1,)))
        gate, up, sigmoid_gate, activated = hidden_parts(projected[...])
        hidden[...] = (activated * up).astype(bf16)
        gate_slope = sigmoid_gate * (1.0 + gate * (1.0 - sigmoid_gate))
        slope[:, :half_width] = (grad_hidden * up * gate_slope).astype(bf16)
        slope[:, half_width:] = (grad_hidden * activated).astype(bf16)

    grad_in[0] = dot(last_block[...], slope[...], ((0,), (0,))).astype(bf16)
    grad_out[0] = dot(hidden[...], route[step], ((0,), (0,))).astype(bf16)


def body(tokens, expert_ids, gates, positives, gate_up, down):
    dp_count = lax.axis_size("dp")
    expert_count = lax.axis_size("expert")
    chips = expert_count // 2
    experts = dp_count * chips
    tok_dev, width = tokens.shape
    half_width = down.shape[1]
    seq_dev = positives.shape[0]
    seqs = dp_count * seq_dev
    seq_length = tok_dev // seq_dev
    part_rows = tok_dev // expert_count
    plane = lax.axis_index("dp")
    lane = lax.axis_index("expert")
    place = jnp.stack([plane, lane, plane * chips + lane // 2]).astype(jnp.int32)
    assert experts <= lanes and seq_length % tail == 0

    def to_lane(value, step):
        return lax.ppermute(value, "expert", [(j, j ^ step) for j in range(expert_count)])

    def to_plane(value, step):
        return lax.ppermute(value, "dp", [(p, p ^ step) for p in range(dp_count)])

    chip_steps = [2 * step for step in range(1, chips)]
    groups = [range(first, min(first + 2, dp_count)) for first in range(0, dp_count, 2)]

    share = width // chips
    packed = pl.pallas_call(
        functools.partial(pack_kernel, seq_dev),
        out_shape=jax.ShapeDtypeStruct((part_rows, width + lanes), bf16),
        in_specs=[in_smem, in_vmem, in_vmem, pl.BlockSpec(memory_space=pltpu.HBM)],
        out_specs=in_vmem,
        scratch_shapes=[
            pltpu.VMEM((part_rows, lanes), f32),
            pltpu.VMEM((seq_dev, tail, share), bf16),
            pltpu.SemaphoreType.DMA((seq_dev + 1,)),
        ],
        cost_estimate=cost(0, 1 << 19),
        name="pack",
    )(positives, expert_ids.T, gates.T, tokens)
    arrivals = {hop: to_plane(packed, hop) for hop in range(1, dp_count)}
    mate_in = to_lane(gate_up, 1)
    mate_out = to_lane(down, 1)
    weights = (gate_up, down, mate_in, mate_out)

    tiles = [packed]
    spots = {}
    received = None
    for group in groups:
        own = [arrivals[hop] for hop in group if hop]
        if group[0] == 0:
            joined = jnp.concatenate(own + [packed[:, width:]], axis=1)
            joined, weights = lax.optimization_barrier((joined, weights))
        else:
            joined = jnp.concatenate(own, axis=0)
            joined, received = lax.optimization_barrier((joined, received))
            tiles[-len(received) :] = received
        first = len(tiles)
        received = [to_lane(joined, step) for step in chip_steps]
        tiles += own + received
        for index, hop in enumerate(group):
            if group[0] == 0:
                place_of = (first, 0, width) if hop else (0, 0, width)
                row, at = 0, width if hop else width + lanes
            else:
                place_of = (first + index, 0, width)
                row, at = index * part_rows, width
            spots[hop] = [place_of] + [
                (first + len(own) + chip, row, at) for chip in range(chips - 1)
            ]
    where_tiles = [spots[hop] for hop in range(dp_count)]

    table_rows = dp_count * part_rows + seqs
    chunks = width // lanes
    sublanes = -(-seq_dev // 8) * 8
    kept, sent, last_all, partners = pl.pallas_call(
        functools.partial(table_kernel, (seq_dev, tok_dev, where_tiles, len(tiles))),
        out_shape=[
            jax.ShapeDtypeStruct((table_rows, lanes), bf16),
            jax.ShapeDtypeStruct((table_rows, lanes), bf16),
            jax.ShapeDtypeStruct((seqs, width), bf16),
            jax.ShapeDtypeStruct((seqs, lanes), f32),
        ],
        in_specs=[in_smem] + [in_vmem] * len(tiles),
        out_specs=[in_vmem] * 4,
        scratch_shapes=[
            pltpu.VMEM((dp_count, chunks, sublanes, lanes), f32),
            pltpu.VMEM((dp_count, sublanes, lanes), f32),
            pltpu.VMEM((dp_count, sublanes, lanes), f32),
        ],
        compiler_params=params(48 if dp_count > 8 else 12),
        cost_estimate=cost(0, 1 << 20),
        name="tables",
    )(place, *tiles)
    found = to_lane(sent, 1)

    each = seqs // expert_count
    extra = each * width // part_rows
    assert extra % lanes == 0 and part_rows % (width // lanes) == 0

    def expert(group, place, with_last):
        near = 0 in group
        wanted = [spot for hop in group if hop for spot in where_tiles[hop]]
        used = sorted({spot[0] for spot in wanted})
        sources = tuple((used.index(spot[0]), spot[1]) for spot in wanted)
        parts = [tiles[index] for index in used]
        n_outs = chips * len(group)
        total = n_outs * part_rows + (seqs if with_last else 0)
        out_shape = [jax.ShapeDtypeStruct((part_rows, width), bf16)] * n_outs
        scratch = [pltpu.VMEM((total, width), bf16)]
        if with_last:
            wider = jax.ShapeDtypeStruct((part_rows, width + extra), bf16)
            out_shape[n_outs - chips :] = [wider] * chips
            out_shape += [
                jax.ShapeDtypeStruct((seqs, 2 * half_width), f32),
                jax.ShapeDtypeStruct((part_rows, extra), f32),
            ]
            scratch = [
                pltpu.VMEM((expert_count, -(-each // 8) * 8, width), f32),
                pltpu.VMEM((part_rows, extra), f32),
            ] + scratch
        operands = [place] + [tokens] * near + [last_all] * with_last + parts + list(weights)
        return pl.pallas_call(
            functools.partial(
                expert_kernel,
                (tuple(group), chips, part_rows, with_last, sources, len(parts)),
            ),
            out_shape=out_shape,
            in_specs=[in_smem] + [in_vmem] * (len(operands) - 1),
            out_specs=[in_vmem] * len(out_shape),
            scratch_shapes=scratch,
            compiler_params=params(32),
            cost_estimate=cost(2 * total * width * 6 * half_width, 12 << 20),
            name="experts",
        )(*operands)

    def combine(hop, parts, last_sum):
        with_last = last_sum is None
        out_shape = [jax.ShapeDtypeStruct((part_rows, width), f32)]
        if hop:
            out_shape = [jax.ShapeDtypeStruct((part_rows, width + extra), bf16)]
        if with_last:
            out_shape.append(jax.ShapeDtypeStruct((part_rows, extra), bf16))
        operands = [place, kept, found] + [packed] * (hop == 0)
        operands += [last_sum] * (hop > 0 and not with_last) + parts
        return pl.pallas_call(
            functools.partial(combine_kernel, (hop, chips, with_last, width, each)),
            out_shape=out_shape,
            in_specs=[in_smem] + [in_vmem] * (len(operands) - 1),
            out_specs=[in_vmem] * len(out_shape),
            compiler_params=params(8),
            cost_estimate=cost(0, 2 << 20),
            name="combine",
        )(*operands)

    outs = {}
    after = place
    for group in groups:
        out = expert(group, after, group is groups[-1])
        after, _ = lax.optimization_barrier((place, out[0]))
        for index, hop in enumerate(group):
            outs[hop] = out[index * chips : (index + 1) * chips]
    last_projected, own_last = out[-2:]

    returned = {}

    def send_back(hop, after):
        first, *parts = outs[hop]
        parts, after = lax.optimization_barrier((parts, after))
        returned[hop] = [first] + [to_lane(value, step) for value, step in zip(parts, chip_steps)]
        return after

    send_back(0, [])
    send_back(1, [])
    before = 1
    for hop in range(dp_count - 1, 1, -1):
        returned[before][1:], found = send_back(hop, (returned[before][1:], found))
        before = hop
    homeward = []
    last_sum = None
    for hop in range(dp_count - 1, 0, -1):
        result = combine(hop, returned[hop], last_sum)
        last_sum = result[1] if last_sum is None else last_sum
        homeward.append(to_plane(result[0], hop))
    near_sum = combine(0, returned[0], last_sum)[0]

    own_out = pl.pallas_call(
        finish_kernel,
        out_shape=jax.ShapeDtypeStruct((part_rows, width + extra), bf16),
        in_specs=[in_vmem] * (2 + dp_count),
        out_specs=in_vmem,
        compiler_params=params(16 if dp_count > 8 else 4),
        cost_estimate=cost(0, 1 << 20),
        name="finish",
    )(near_sum, own_last, last_sum, *homeward)
    pieces = [own_out] + [to_lane(own_out, step) for step in chip_steps]
    pieces += [to_lane(piece, 1) for piece in pieces]

    block = min(512, width)
    steps = width // block
    layer_out, grad_gate_up, grad_down = pl.pallas_call(
        functools.partial(final_kernel, len(pieces)),
        grid=(steps,),
        out_shape=[
            jax.ShapeDtypeStruct((tok_dev, width), bf16),
            jax.ShapeDtypeStruct(gate_up.shape, bf16),
            jax.ShapeDtypeStruct(down.shape, bf16),
        ],
        in_specs=[
            *[pl.BlockSpec((part_rows, width + extra), lambda step: (0, 0))] * len(pieces),
            pl.BlockSpec((seqs, block), lambda step: (0, step)),
            pl.BlockSpec((seqs, 2 * half_width), lambda step: (0, 0)),
            in_smem,
            pl.BlockSpec((table_rows, lanes), lambda step: (0, 0)),
            pl.BlockSpec((table_rows, lanes), lambda step: (0, 0)),
            pl.BlockSpec((seqs, lanes), lambda step: (0, 0)),
            pl.BlockSpec((1, half_width, width), lambda step: (0, 0, 0)),
        ],
        out_specs=[
            pl.BlockSpec((tok_dev, width), lambda step: (0, 0)),
            pl.BlockSpec((1, block, 2 * half_width), lambda step: (0, step, 0)),
            pl.BlockSpec((1, half_width, block), lambda step: (0, 0, step)),
        ],
        scratch_shapes=[
            pltpu.VMEM((steps, seqs, block), bf16),
            pltpu.VMEM((seqs, half_width), bf16),
            pltpu.VMEM((seqs, 2 * half_width), bf16),
            pltpu.VMEM((expert_count, -(-each // 8) * 8, width), f32),
        ],
        compiler_params=params(24),
        cost_estimate=cost(2 * seqs * width * 4 * half_width, 7 << 20),
        name="final",
    )(*pieces, last_all, last_projected, place, kept, found, partners, down)
    return (layer_out, grad_gate_up, grad_down)


def solution(mesh):
    return jax.shard_map(
        body,
        mesh=mesh,
        in_specs=(
            P("dp", None),
            P("dp", "expert"),
            P("dp", "expert"),
            P("dp"),
            P(("dp", "expert"), None, None),
            P(("dp", "expert"), None, None),
        ),
        out_specs=(P("dp", None), P(("dp", "expert"), None, None), P(("dp", "expert"), None, None)),
        check_vma=False,
    )
```

```python
import functools

import jax
import jax.numpy as jnp
from jax import lax
from jax.experimental import pallas as pl
from jax.experimental.pallas import tpu as pltpu
from jax.sharding import PartitionSpec as P

logit_divisor = 0.05
grad_scale = 256.0
epsilon = 1e-06
lanes = 128
tail = 16
bf16 = jnp.bfloat16
f32 = jnp.float32

anywhere = pl.BlockSpec(memory_space=pl.ANY)
in_vmem = pl.BlockSpec(memory_space=pltpu.VMEM)
in_smem = pl.BlockSpec(memory_space=pltpu.SMEM)


def params(mebibytes):
    return pltpu.CompilerParams(vmem_limit_bytes=mebibytes << 20)


def cost(flops, moved):
    return pl.CostEstimate(flops=flops, transcendentals=0, bytes_accessed=moved)


def dot(left, right, dims=((1,), (0,)), precision=None):
    return lax.dot_general(
        left, right, (dims, ((), ())), precision=precision, preferred_element_type=f32
    )


def doublings(count):
    steps = [1 << bit for bit in range((count - 1).bit_length())]
    assert 1 << len(steps) == count
    return steps


def column(table, wanted):
    index = lax.broadcasted_iota(jnp.int32, table.shape, 1)
    return jnp.sum(jnp.where(index == wanted, table, 0.0), axis=1, keepdims=True)


def pack_kernel(seq_dev, positives, ids, gates, tokens, out, tile, rows, sems):
    part_rows, width = out.shape[0], tokens.shape[1]
    tok_dev = tokens.shape[0]
    seq_length = tok_dev // seq_dev
    share = rows.shape[2]
    lane = lax.axis_index("expert")
    column_at = pl.multiple_of(lane // 2 * share, lanes)
    start = pl.multiple_of(lane * part_rows, part_rows)
    copies = [
        pltpu.make_async_copy(
            tokens.at[pl.ds((seq + 1) * seq_length - tail, tail), pl.ds(column_at, share)],
            rows.at[seq],
            sems.at[seq],
        )
        for seq in range(seq_dev)
    ]
    own = pltpu.make_async_copy(
        tokens.at[pl.ds(start, part_rows)], out.at[:, pl.ds(0, width)], sems.at[seq_dev]
    )
    own.start()
    for copy in copies:
        copy.start()
    note_rows = tok_dev // lanes
    tile[...] = jnp.zeros_like(tile)
    for index in range(note_rows):
        block = slice(index * lanes, (index + 1) * lanes)
        tile[index : index + 1, :] = ids[:, block].astype(f32)
        tile[note_rows + index : note_rows + index + 1, :] = gates[:, block]
    for seq in range(seq_dev):
        row = 2 * note_rows + seq
        tile[row : row + 1, :] = jnp.full((1, lanes), positives[seq], jnp.int32).astype(f32)
    base = part_rows - seq_dev * (share // lanes)
    for seq in range(seq_dev):
        copies[seq].wait()
        values = rows[seq].astype(f32)
        for chunk in range(share // lanes):
            row = base + chunk * seq_dev + seq
            tile[row : row + 1, :] = values[tail - 1 : tail, chunk * lanes : (chunk + 1) * lanes]
    out[:, width:] = tile[...].astype(bf16)
    own.wait()


def table_kernel(layout, place, *refs):
    seq_dev, tok_dev, where_tiles, n_parts = layout
    parts = refs[:n_parts]
    kept, sent, partners, routes, marks = refs[n_parts:]
    part_rows = parts[0].shape[0]
    dp_count = len(where_tiles)
    note_rows = tok_dev // lanes
    seq_length = tok_dev // seq_dev
    chips = len(where_tiles[0])
    lane_index = lax.broadcasted_iota(jnp.int32, (part_rows, lanes), 1)
    row_index = lax.broadcasted_iota(jnp.int32, (part_rows, lanes), 0)

    def dense_rows(tile, lane):
        start = lane * part_rows
        picked = lane_index == row_index + start % lanes
        found = []
        for offset in (0, note_rows):
            line = tile[offset : offset + 1, :]
            for index in range(1, note_rows):
                other = tile[offset + index : offset + index + 1, :]
                line = jnp.where(start // lanes == index, other, line)
            found.append(jnp.sum(jnp.where(picked, line, 0.0), axis=1, keepdims=True))
        return jnp.where(lane_index.astype(f32) == found[0], found[1], 0.0)

    for hop in range(dp_count):
        plane = place[0] ^ hop
        sums = [None, None]
        for chip in range(chips):
            source, row, at = where_tiles[hop][chip]
            tile = parts[source][row : row + part_rows, at : at + lanes].astype(f32)
            for index, lane in enumerate((place[1], place[1] ^ 1)):
                value = dense_rows(tile, lane)
                sums[index] = value if chip == 0 else sums[index] + value
            for seq in range(seq_dev):
                at_token = (seq + 1) * seq_length - 1
                row = at_token // lanes
                here = lane_index[:1] == at_token % lanes
                expert, gate = [
                    jnp.sum(
                        jnp.where(here, tile[offset + row : offset + row + 1, :], 0.0),
                        axis=1,
                        keepdims=True,
                    )
                    for offset in (0, note_rows)
                ]
                value = jnp.where(lane_index[:1].astype(f32) == expert, gate, 0.0)
                if chip:
                    value = value + routes[plane, seq : seq + 1, :]
                routes[plane, seq : seq + 1, :] = value
            if chip == 0:
                marks[plane, 0:seq_dev, :] = tile[2 * note_rows : 2 * note_rows + seq_dev, :]
        at = slice(hop * part_rows, (hop + 1) * part_rows)
        kept[at, :] = sums[0].astype(bf16)
        sent[at, :] = sums[1].astype(bf16)
    last = dp_count * part_rows
    shared = []
    for plane in range(dp_count):
        shared.append(routes[plane, 0:seq_dev, :])
        partners[plane * seq_dev : (plane + 1) * seq_dev, :] = marks[plane, 0:seq_dev, :]
    seqs = dp_count * seq_dev
    value = jnp.concatenate(shared, axis=0).astype(bf16)
    kept[last : last + seqs, :] = value
    sent[last : last + seqs, :] = value


def hidden_parts(projected):
    half_width = projected.shape[1] // 2
    gate, up = projected[:, :half_width], projected[:, half_width:]
    sigmoid_gate = jax.nn.sigmoid(gate)
    return gate, up, sigmoid_gate, gate * sigmoid_gate


def spread_rows(values, rows, blocks):
    chunks = values.shape[1] // lanes
    for index in range(values.shape[0] * chunks):
        row, chunk = index // chunks, index % chunks
        spot = slice(index % rows, index % rows + 1)
        block = slice(index // rows * lanes, (index // rows + 1) * lanes)
        blocks[spot, block] = values[row : row + 1, chunk * lanes : (chunk + 1) * lanes]


def last_tokens(place, seq_dev, where_tiles, parts, tokens):
    part_rows = parts[0].shape[0]
    dp_count, chunks = tokens.shape[:2]
    chips = len(where_tiles[0])
    share_chunks = chunks // chips
    base = part_rows - seq_dev * share_chunks
    for hop in range(dp_count):
        for chip in range(chips):
            source, row, at = where_tiles[hop][chip]
            tile = parts[source][row : row + part_rows, at : at + lanes].astype(f32)
            first = ((place[1] // 2) ^ chip) * share_chunks
            for chunk in range(share_chunks):
                row = base + chunk * seq_dev
                tokens[place[0] ^ hop, first + chunk, 0:seq_dev, :] = tile[row : row + seq_dev, :]
    joined = []
    for plane in range(dp_count):
        lines = [tokens[plane, chunk, 0:seq_dev, :] for chunk in range(chunks)]
        joined.append(jnp.concatenate(lines, axis=1))
    return jnp.concatenate(joined, axis=0)


def expert_kernel(layout, *refs):
    group, chips, part_rows, seq_dev, where_tiles, used, with_last = layout
    refs = list(refs)
    place = refs.pop(0)
    near = 0 in group
    tokens = refs.pop(0) if near else None
    parts, refs = dict(zip(used, refs)), refs[len(used) :]
    weights, refs = refs[:4], refs[4:]
    n_outs = chips * len(group)
    outs, refs = refs[:n_outs], refs[n_outs:]
    if with_last:
        last_all, last_projected, own_last, by_lane, tile, seq_tokens, *refs = refs
    (rows,) = refs
    width = weights[0].shape[1]
    total = n_outs * part_rows
    spots = [slice(index * part_rows, (index + 1) * part_rows) for index in range(n_outs)]
    for index, spot in enumerate(spots):
        hop, chip = group[index // chips], index % chips
        if hop:
            source, row, _ = where_tiles[hop][chip]
            rows[spot, :] = parts[source][row : row + part_rows, :width]
        else:
            start = pl.multiple_of((place[1] ^ (2 * chip)) * part_rows, part_rows)
            rows[spot, :] = tokens[pl.ds(start, part_rows), :]
    if with_last:
        floats = last_tokens(place, seq_dev, where_tiles, parts, seq_tokens)
        last_all[...] = floats.astype(bf16)
        rows[total:, :] = floats.astype(bf16)
    hidden = []
    for half in range(2):
        projected = dot(rows[...], weights[2 * half][0])
        if half == 0 and with_last:
            last_projected[...] = projected[total:]
        _, up, _, activated = hidden_parts(projected)
        hidden.append((activated * up).astype(bf16))
    block = min(512, width)
    if with_last:
        each = floats.shape[0] // by_lane.shape[0]
    for first in range(0, width, block):
        columns = slice(first, first + block)
        result = dot(hidden[0], weights[1][0, :, columns]) + dot(
            hidden[1], weights[3][0, :, columns]
        )
        for out, spot in zip(outs, spots):
            out[:, columns] = result[spot].astype(bf16)
        if with_last:
            for lane in range(by_lane.shape[0]):
                at = total + lane * each
                by_lane[lane, 0:each, columns] = result[at : at + each]
    if with_last:
        for chip in range(chips):
            spread_rows(by_lane[place[1] ^ (2 * chip), 0:each, :], part_rows, tile)
            outs[n_outs - chips + chip][:, width:] = tile[...].astype(bf16)
        for lane in range(by_lane.shape[0]):
            by_lane[lane, 0:each, :] = floats[lane * each : (lane + 1) * each]
        spread_rows(by_lane[place[1], 0:each, :], part_rows, tile)
        own_last[...] = tile[...]


def combine_kernel(layout, place, kept, found, *refs):
    hop, chips, with_last, width, each = layout
    own, refs = (refs[0], refs[1:]) if hop == 0 else (None, refs)
    last_in, refs = (refs[0], refs[1:]) if hop and not with_last else (None, refs)
    parts, out = refs[:chips], refs[chips]
    part_rows = out.shape[0]
    first_expert = place[2] - place[1] // 2
    experts = [first_expert + ((place[1] // 2) ^ chip) for chip in range(chips)]
    if with_last:
        last_in = refs[-1]
        table = kept[-2 * chips * each :, :].astype(f32) + found[-2 * chips * each :, :].astype(f32)
        row_index = lax.broadcasted_iota(jnp.int32, table.shape, 0)
        chunks = width // lanes
        for row in range(each):
            mine = jnp.where(row_index == place[1] * each + row, table, 0.0)
            mine = jnp.sum(mine, axis=0, keepdims=True)
            first = row * chunks % part_rows
            spot = slice(first, first + chunks)
            at = row * chunks // part_rows * lanes
            total = None
            for chip in range(chips):
                values = parts[chip][spot, width + at : width + at + lanes].astype(f32)
                term = column(mine, experts[chip]) * values
                total = term if total is None else total + term
            last_in[spot, at : at + lanes] = total.astype(bf16)
    at = slice(hop * part_rows, (hop + 1) * part_rows)
    table = kept[at, :].astype(f32) + found[at, :].astype(f32)
    total = None if hop else own[:, :width].astype(f32)
    for chip in range(chips):
        term = column(table, experts[chip]) * parts[chip][:, :width].astype(f32)
        total = term if total is None else total + term
    out[:, :width] = total.astype(out.dtype)
    if hop:
        out[:, width:] = last_in[...]


def finish_kernel(near, own_last, last_sum, *refs):
    parts, out = refs[:-1], refs[-1]
    width = near.shape[1]
    total = near[...]
    last = last_sum[...].astype(f32)
    for part in parts:
        total = total + part[:, :width].astype(f32)
        last = last + part[:, width:].astype(f32)
    out[:, :width] = total.astype(bf16)
    out[:, width:] = (own_last[...] + last).astype(bf16)


def collect_rows(lane, pieces, by_lane, width):
    part_rows, chunks = pieces[0].shape[0], width // lanes
    count = len(pieces)
    each = (pieces[0].shape[1] - width) * part_rows // width
    for index in range(count):
        source = lane ^ (2 * (index % (count // 2))) ^ (index // (count // 2))
        values = pieces[index][:, width:].astype(f32)
        for spot in range(each * chunks):
            row, chunk = spot // chunks, spot % chunks
            at = spot // part_rows * lanes
            from_row = spot % part_rows
            by_lane[source, row : row + 1, chunk * lanes : (chunk + 1) * lanes] = values[
                from_row : from_row + 1, at : at + lanes
            ]
    return jnp.concatenate([by_lane[index, 0:each, :] for index in range(count)], axis=0)


def both_ways(coefficient, unit, diagonal):
    count = unit.shape[0]
    if count > 32:
        high = lax.Precision.HIGHEST
        there = dot(coefficient, unit, ((1,), (0,)), high)
        return there + dot(coefficient, unit, ((0,), (0,)), high)
    total = None
    for index in range(count):
        line = jnp.where(diagonal, coefficient[index : index + 1, :], 0.0)
        factor = coefficient[:, index : index + 1] + jnp.sum(line, axis=1, keepdims=True)
        term = factor * unit[index : index + 1, :]
        total = term if total is None else total + term
    return total


def final_kernel(n_pieces, n_blocks, *refs):
    pieces, refs = refs[:n_pieces], refs[n_pieces:]
    last_all, projected, place, kept, found, partners, down, *refs = refs
    layer_out, grad_in, grad_out, made_in, made_out, by_lane, sems = refs
    part_rows, width = pieces[0].shape[0], layer_out.shape[1]
    copies = []

    def send(source, target):
        copies.append(pltpu.make_async_copy(source, target, sems.at[len(copies)]))
        copies[-1].start()

    for index in range(n_pieces):
        lane = place[1] ^ (2 * (index % (n_pieces // 2))) ^ (index // (n_pieces // 2))
        start = pl.multiple_of(lane * part_rows, part_rows)
        send(pieces[index].at[:, pl.ds(0, width)], layer_out.at[pl.ds(start, part_rows)])
    values = collect_rows(place[1], pieces, by_lane, width)
    count = values.shape[0]
    last = kept.shape[0] - count
    table = kept[last:, :].astype(f32) + found[last:, :].astype(f32)
    row = lax.broadcasted_iota(jnp.int32, (count, count), 0)
    col = lax.broadcasted_iota(jnp.int32, (count, count), 1)
    norms = jnp.sqrt(jnp.sum(values * values, axis=1, keepdims=True) + epsilon)
    norms_line = jnp.sum(jnp.where(row == col, norms, 0.0), axis=0, keepdims=True)
    unit = values / norms
    rows = values.astype(bf16)
    scores = dot(rows, rows, ((1,), (1,))) / (norms * norms_line) / logit_divisor
    exp_scores = jnp.where(row != col, jnp.exp(scores), 0.0)
    probabilities = exp_scores / jnp.sum(exp_scores, axis=1, keepdims=True)
    partner = partners[:, :1].astype(jnp.int32)
    coefficient = grad_scale * (probabilities - jnp.where(col == partner, 1.0, 0.0))
    grad_unit = both_ways(coefficient, unit, row == col) / logit_divisor
    projection = jnp.sum(unit * grad_unit, axis=1, keepdims=True)
    grad_last = (grad_unit - unit * projection) / norms
    route_grad = (column(table, place[2]) * grad_last).astype(bf16)
    grad_hidden = dot(route_grad, down[0], ((1,), (1,)))
    gate, up, sigmoid_gate, activated = hidden_parts(projected[...])
    hidden = (activated * up).astype(bf16)
    gate_slope = sigmoid_gate * (1.0 + gate * (1.0 - sigmoid_gate))
    slope = jnp.concatenate([grad_hidden * up * gate_slope, grad_hidden * activated], axis=1)
    slope = slope.astype(bf16)
    block = width // n_blocks
    for index in range(n_blocks):
        spot = slice(index * block, (index + 1) * block)
        made_in[spot, :] = dot(last_all[:, spot], slope, ((0,), (0,))).astype(bf16)
        send(made_in.at[spot], grad_in.at[0, spot])
    made_out[...] = dot(hidden, route_grad, ((0,), (0,))).astype(bf16)
    send(made_out, grad_out.at[0])
    for copy in copies:
        copy.wait()


def body(tokens, expert_ids, gates, positives, gate_up, down):
    dp_count = lax.axis_size("dp")
    expert_count = lax.axis_size("expert")
    chips = expert_count // 2
    experts = dp_count * chips
    tok_dev, width = tokens.shape
    half_width = down.shape[1]
    seq_dev = positives.shape[0]
    seqs = dp_count * seq_dev
    seq_length = tok_dev // seq_dev
    part_rows = tok_dev // expert_count
    plane = lax.axis_index("dp")
    lane = lax.axis_index("expert")
    place = jnp.stack([plane, lane, plane * chips + lane // 2]).astype(jnp.int32)
    assert experts <= lanes and seq_length % tail == 0

    def to_lane(value, step):
        return lax.ppermute(value, "expert", [(j, j ^ step) for j in range(expert_count)])

    def to_plane(value, step):
        return lax.ppermute(value, "dp", [(p, p ^ step) for p in range(dp_count)])

    chip_steps = [2 * step for step in range(1, chips)]
    groups = [range(first, min(first + 2, dp_count)) for first in range(0, dp_count, 2)]

    share = width // chips
    packed = pl.pallas_call(
        functools.partial(pack_kernel, seq_dev),
        out_shape=jax.ShapeDtypeStruct((part_rows, width + lanes), bf16),
        in_specs=[in_smem, in_vmem, in_vmem, pl.BlockSpec(memory_space=pltpu.HBM)],
        out_specs=in_vmem,
        scratch_shapes=[
            pltpu.VMEM((part_rows, lanes), f32),
            pltpu.VMEM((seq_dev, tail, share), bf16),
            pltpu.SemaphoreType.DMA((seq_dev + 1,)),
        ],
        cost_estimate=cost(0, 1 << 19),
        name="pack",
    )(positives, expert_ids.T, gates.T, tokens)
    arrivals = {hop: to_plane(packed, hop) for hop in range(1, dp_count)}
    mate_in = to_lane(gate_up, 1)
    mate_out = to_lane(down, 1)
    weights = (gate_up, down, mate_in, mate_out)

    tiles = [packed]
    spots = {}
    received = None
    for group in groups:
        own = [arrivals[hop] for hop in group if hop]
        if group[0] == 0:
            joined = jnp.concatenate(own + [packed[:, width:]], axis=1)
            joined, weights = lax.optimization_barrier((joined, weights))
        else:
            joined = jnp.concatenate(own, axis=0)
            joined, received = lax.optimization_barrier((joined, received))
            tiles[-len(received) :] = received
        first = len(tiles)
        received = [to_lane(joined, step) for step in chip_steps]
        tiles += own + received
        for index, hop in enumerate(group):
            if group[0] == 0:
                place_of = (first, 0, width) if hop else (0, 0, width)
                row, at = 0, width if hop else width + lanes
            else:
                place_of = (first + index, 0, width)
                row, at = index * part_rows, width
            spots[hop] = [place_of] + [
                (first + len(own) + chip, row, at) for chip in range(chips - 1)
            ]
    where_tiles = [spots[hop] for hop in range(dp_count)]

    each = seqs // expert_count
    extra = each * width // part_rows
    assert extra % lanes == 0 and part_rows % (width // lanes) == 0

    def expert(group, place, with_last):
        near = 0 in group
        wanted = range(dp_count) if with_last else [hop for hop in group if hop]
        used = sorted({spot[0] for hop in wanted for spot in where_tiles[hop]})
        parts = [tiles[index] for index in used]
        n_outs = chips * len(group)
        total = n_outs * part_rows + (seqs if with_last else 0)
        out_shape = [jax.ShapeDtypeStruct((part_rows, width), bf16)] * n_outs
        scratch = [pltpu.VMEM((total, width), bf16)]
        if with_last:
            wider = jax.ShapeDtypeStruct((part_rows, width + extra), bf16)
            out_shape[n_outs - chips :] = [wider] * chips
            out_shape += [
                jax.ShapeDtypeStruct((seqs, width), bf16),
                jax.ShapeDtypeStruct((seqs, 2 * half_width), f32),
                jax.ShapeDtypeStruct((part_rows, extra), f32),
            ]
            scratch = [
                pltpu.VMEM((expert_count, -(-each // 8) * 8, width), f32),
                pltpu.VMEM((part_rows, extra), f32),
                pltpu.VMEM((dp_count, width // lanes, -(-seq_dev // 8) * 8, lanes), f32),
            ] + scratch
        operands = [place] + [tokens] * near + parts + list(weights)
        layout = (tuple(group), chips, part_rows, seq_dev, where_tiles, used, with_last)
        return pl.pallas_call(
            functools.partial(expert_kernel, layout),
            out_shape=out_shape,
            in_specs=[in_smem] + [in_vmem] * (len(operands) - 1),
            out_specs=[in_vmem] * len(out_shape),
            scratch_shapes=scratch,
            compiler_params=params(32),
            cost_estimate=cost(2 * total * width * 6 * half_width, 12 << 20),
            name="experts",
        )(*operands)

    outs = {}
    after = place
    for group in groups:
        out = expert(group, after, group is groups[-1])
        after, _ = lax.optimization_barrier((place, out[0]))
        for index, hop in enumerate(group):
            outs[hop] = out[index * chips : (index + 1) * chips]
    last_all, last_projected, own_last = out[-3:]

    table_rows = dp_count * part_rows + seqs
    chunks = width // lanes
    sublanes = -(-seq_dev // 8) * 8
    kept, sent, partners = pl.pallas_call(
        functools.partial(table_kernel, (seq_dev, tok_dev, where_tiles, len(tiles))),
        out_shape=[
            jax.ShapeDtypeStruct((table_rows, lanes), bf16),
            jax.ShapeDtypeStruct((table_rows, lanes), bf16),
            jax.ShapeDtypeStruct((seqs, lanes), f32),
        ],
        in_specs=[in_smem] + [in_vmem] * len(tiles),
        out_specs=[in_vmem] * 3,
        scratch_shapes=[
            pltpu.VMEM((dp_count, sublanes, lanes), f32),
            pltpu.VMEM((dp_count, sublanes, lanes), f32),
        ],
        compiler_params=params(48 if dp_count > 8 else 12),
        cost_estimate=cost(0, 1 << 20),
        name="tables",
    )(after, *tiles)
    found = to_lane(sent, 1)

    def combine(hop, parts, last_sum):
        with_last = last_sum is None
        out_shape = [jax.ShapeDtypeStruct((part_rows, width), f32)]
        if hop:
            out_shape = [jax.ShapeDtypeStruct((part_rows, width + extra), bf16)]
        if with_last:
            out_shape.append(jax.ShapeDtypeStruct((part_rows, extra), bf16))
        operands = [place, kept, found] + [packed] * (hop == 0)
        operands += [last_sum] * (hop > 0 and not with_last) + parts
        return pl.pallas_call(
            functools.partial(combine_kernel, (hop, chips, with_last, width, each)),
            out_shape=out_shape,
            in_specs=[in_smem] + [in_vmem] * (len(operands) - 1),
            out_specs=[in_vmem] * len(out_shape),
            compiler_params=params(8),
            cost_estimate=cost(0, 2 << 20),
            name="combine",
        )(*operands)

    returned = {}

    def send_back(hop, after):
        first, *parts = outs[hop]
        parts, after = lax.optimization_barrier((parts, after))
        returned[hop] = [first] + [to_lane(value, step) for value, step in zip(parts, chip_steps)]
        return after

    send_back(0, [])
    send_back(1, [])
    before = 1
    for hop in range(dp_count - 1, 1, -1):
        returned[before][1:] = send_back(hop, returned[before][1:])
        if hop == dp_count - 1:
            returned[hop][1:], found = lax.optimization_barrier((returned[hop][1:], found))
        before = hop
    homeward = []
    last_sum = None
    for hop in range(dp_count - 1, 0, -1):
        result = combine(hop, returned[hop], last_sum)
        last_sum = result[1] if last_sum is None else last_sum
        homeward.append(to_plane(result[0], hop))
    near_sum = combine(0, returned[0], last_sum)[0]

    own_out = pl.pallas_call(
        finish_kernel,
        out_shape=jax.ShapeDtypeStruct((part_rows, width + extra), bf16),
        in_specs=[in_vmem] * (2 + dp_count),
        out_specs=in_vmem,
        compiler_params=params(16 if dp_count > 8 else 4),
        cost_estimate=cost(0, 1 << 20),
        name="finish",
    )(near_sum, own_last, last_sum, *homeward)
    pieces = [own_out] + [to_lane(own_out, step) for step in chip_steps]
    pieces += [to_lane(piece, 1) for piece in pieces]

    n_blocks = width // min(512, width)
    in_hbm = pl.BlockSpec(memory_space=pltpu.HBM)
    layer_out, grad_gate_up, grad_down = pl.pallas_call(
        functools.partial(final_kernel, len(pieces), n_blocks),
        out_shape=[
            jax.ShapeDtypeStruct((tok_dev, width), bf16),
            jax.ShapeDtypeStruct(gate_up.shape, bf16),
            jax.ShapeDtypeStruct(down.shape, bf16),
        ],
        in_specs=[in_vmem] * (len(pieces) + 2) + [in_smem] + [in_vmem] * 4,
        out_specs=[in_hbm] * 3,
        scratch_shapes=[
            pltpu.VMEM((width, 2 * half_width), bf16),
            pltpu.VMEM((half_width, width), bf16),
            pltpu.VMEM((expert_count, -(-each // 8) * 8, width), f32),
            pltpu.SemaphoreType.DMA((len(pieces) + n_blocks + 1,)),
        ],
        compiler_params=params(24),
        cost_estimate=cost(2 * seqs * width * 4 * half_width, 7 << 20),
        name="final",
    )(*pieces, last_all, last_projected, place, kept, found, partners, down)
    return (layer_out, grad_gate_up, grad_down)


def solution(mesh):
    return jax.shard_map(
        body,
        mesh=mesh,
        in_specs=(
            P("dp", None),
            P("dp", "expert"),
            P("dp", "expert"),
            P("dp"),
            P(("dp", "expert"), None, None),
            P(("dp", "expert"), None, None),
        ),
        out_specs=(P("dp", None), P(("dp", "expert"), None, None), P(("dp", "expert"), None, None)),
        check_vma=False,
    )
```

```python
import functools

import jax
import jax.numpy as jnp
from jax import lax
from jax.experimental import pallas as pl
from jax.experimental.pallas import tpu as pltpu
from jax.sharding import PartitionSpec as P

logit_divisor = 0.05
grad_scale = 256.0
epsilon = 1e-06
lanes = 128
tail = 16
bf16 = jnp.bfloat16
f32 = jnp.float32

in_hbm = pl.BlockSpec(memory_space=pltpu.HBM)
in_vmem = pl.BlockSpec(memory_space=pltpu.VMEM)
in_smem = pl.BlockSpec(memory_space=pltpu.SMEM)


def params(mebibytes):
    return pltpu.CompilerParams(vmem_limit_bytes=mebibytes << 20)


def cost(flops, moved):
    return pl.CostEstimate(flops=flops, transcendentals=0, bytes_accessed=moved)


def dot(left, right, dims=((1,), (0,)), precision=None):
    return lax.dot_general(
        left, right, (dims, ((), ())), precision=precision, preferred_element_type=f32
    )


def doublings(count):
    steps = [1 << bit for bit in range((count - 1).bit_length())]
    assert 1 << len(steps) == count
    return steps


def column(table, wanted):
    index = lax.broadcasted_iota(jnp.int32, table.shape, 1)
    return jnp.sum(jnp.where(index == wanted, table, 0.0), axis=1, keepdims=True)


def pack_kernel(seq_dev, positives, ids_in, gates_in, tokens, out, tile, rows, ids, gates, sems):
    part_rows, width = out.shape[0], tokens.shape[1]
    tok_dev = tokens.shape[0]
    seq_length = tok_dev // seq_dev
    share = rows.shape[2]
    lane = lax.axis_index("expert")
    column_at = pl.multiple_of(lane // 2 * share, lanes)
    start = pl.multiple_of(lane * part_rows, part_rows)
    copies = [
        pltpu.make_async_copy(
            tokens.at[pl.ds((seq + 1) * seq_length - tail, tail), pl.ds(column_at, share)],
            rows.at[seq],
            sems.at[seq],
        )
        for seq in range(seq_dev)
    ]
    own = pltpu.make_async_copy(
        tokens.at[pl.ds(start, part_rows)], out.at[:, pl.ds(0, width)], sems.at[seq_dev]
    )
    lines = [
        pltpu.make_async_copy(ids_in, ids, sems.at[seq_dev + 1]),
        pltpu.make_async_copy(gates_in, gates, sems.at[seq_dev + 2]),
    ]
    for copy in lines + [own] + copies:
        copy.start()
    note_rows = tok_dev // lanes
    tile[...] = jnp.zeros_like(tile)
    for copy in lines:
        copy.wait()
    for index in range(note_rows):
        block = slice(index * lanes, (index + 1) * lanes)
        tile[index : index + 1, :] = ids[:, block].astype(f32)
        tile[note_rows + index : note_rows + index + 1, :] = gates[:, block]
    for seq in range(seq_dev):
        row = 2 * note_rows + seq
        tile[row : row + 1, :] = jnp.full((1, lanes), positives[seq], jnp.int32).astype(f32)
    base = part_rows - seq_dev * (share // lanes)
    for seq in range(seq_dev):
        copies[seq].wait()
        values = rows[seq].astype(f32)
        for chunk in range(share // lanes):
            row = base + chunk * seq_dev + seq
            tile[row : row + 1, :] = values[tail - 1 : tail, chunk * lanes : (chunk + 1) * lanes]
    out[:, width:] = tile[...].astype(bf16)
    own.wait()


def table_kernel(layout, place, *refs):
    seq_dev, tok_dev, where_tiles, n_parts = layout
    parts = refs[:n_parts]
    kept, sent, partners, routes, marks = refs[n_parts:]
    part_rows = parts[0].shape[0]
    dp_count = len(where_tiles)
    note_rows = tok_dev // lanes
    seq_length = tok_dev // seq_dev
    chips = len(where_tiles[0])
    lane_index = lax.broadcasted_iota(jnp.int32, (part_rows, lanes), 1)
    row_index = lax.broadcasted_iota(jnp.int32, (part_rows, lanes), 0)

    def dense_rows(tile, lane):
        start = lane * part_rows
        picked = lane_index == row_index + start % lanes
        found = []
        for offset in (0, note_rows):
            line = tile[offset : offset + 1, :]
            for index in range(1, note_rows):
                other = tile[offset + index : offset + index + 1, :]
                line = jnp.where(start // lanes == index, other, line)
            found.append(jnp.sum(jnp.where(picked, line, 0.0), axis=1, keepdims=True))
        return jnp.where(lane_index.astype(f32) == found[0], found[1], 0.0)

    for hop in range(dp_count):
        plane = place[0] ^ hop
        sums = [None, None]
        for chip in range(chips):
            source, row, at = where_tiles[hop][chip]
            tile = parts[source][row : row + part_rows, at : at + lanes].astype(f32)
            for index, lane in enumerate((place[1], place[1] ^ 1)):
                value = dense_rows(tile, lane)
                sums[index] = value if chip == 0 else sums[index] + value
            for seq in range(seq_dev):
                at_token = (seq + 1) * seq_length - 1
                row = at_token // lanes
                here = lane_index[:1] == at_token % lanes
                expert, gate = [
                    jnp.sum(
                        jnp.where(here, tile[offset + row : offset + row + 1, :], 0.0),
                        axis=1,
                        keepdims=True,
                    )
                    for offset in (0, note_rows)
                ]
                value = jnp.where(lane_index[:1].astype(f32) == expert, gate, 0.0)
                if chip:
                    value = value + routes[plane, seq : seq + 1, :]
                routes[plane, seq : seq + 1, :] = value
            if chip == 0:
                marks[plane, 0:seq_dev, :] = tile[2 * note_rows : 2 * note_rows + seq_dev, :]
        at = slice(hop * part_rows, (hop + 1) * part_rows)
        kept[at, :] = sums[0].astype(bf16)
        sent[at, :] = sums[1].astype(bf16)
    last = dp_count * part_rows
    shared = []
    for plane in range(dp_count):
        shared.append(routes[plane, 0:seq_dev, :])
        partners[plane * seq_dev : (plane + 1) * seq_dev, :] = marks[plane, 0:seq_dev, :]
    seqs = dp_count * seq_dev
    value = jnp.concatenate(shared, axis=0).astype(bf16)
    kept[last : last + seqs, :] = value
    sent[last : last + seqs, :] = value


def hidden_parts(projected):
    half_width = projected.shape[1] // 2
    gate, up = projected[:, :half_width], projected[:, half_width:]
    sigmoid_gate = jax.nn.sigmoid(gate)
    return gate, up, sigmoid_gate, gate * sigmoid_gate


def spread_rows(values, rows, blocks):
    chunks = values.shape[1] // lanes
    for index in range(values.shape[0] * chunks):
        row, chunk = index // chunks, index % chunks
        spot = slice(index % rows, index % rows + 1)
        block = slice(index // rows * lanes, (index // rows + 1) * lanes)
        blocks[spot, block] = values[row : row + 1, chunk * lanes : (chunk + 1) * lanes]


def last_tokens(place, seq_dev, where_tiles, parts, tokens):
    part_rows = parts[0].shape[0]
    dp_count, chunks = tokens.shape[:2]
    chips = len(where_tiles[0])
    share_chunks = chunks // chips
    base = part_rows - seq_dev * share_chunks
    for hop in range(dp_count):
        for chip in range(chips):
            source, row, at = where_tiles[hop][chip]
            tile = parts[source][row : row + part_rows, at : at + lanes].astype(f32)
            first = ((place[1] // 2) ^ chip) * share_chunks
            for chunk in range(share_chunks):
                row = base + chunk * seq_dev
                tokens[place[0] ^ hop, first + chunk, 0:seq_dev, :] = tile[row : row + seq_dev, :]
    joined = []
    for plane in range(dp_count):
        lines = [tokens[plane, chunk, 0:seq_dev, :] for chunk in range(chunks)]
        joined.append(jnp.concatenate(lines, axis=1))
    return jnp.concatenate(joined, axis=0)


def expert_kernel(layout, *refs):
    group, chips, part_rows, seq_dev, where_tiles, used, with_last = layout
    refs = list(refs)
    place = refs.pop(0)
    near = 0 in group
    tokens = refs.pop(0) if near else None
    parts, refs = dict(zip(used, refs)), refs[len(used) :]
    weights, refs = refs[:4], refs[4:]
    n_outs = chips * len(group)
    outs, refs = refs[:n_outs], refs[n_outs:]
    if with_last:
        last_all, last_projected, own_last, by_lane, tile, seq_tokens, *refs = refs
    (rows,) = refs
    width = weights[0].shape[1]
    total = n_outs * part_rows
    spots = [slice(index * part_rows, (index + 1) * part_rows) for index in range(n_outs)]
    for index, spot in enumerate(spots):
        hop, chip = group[index // chips], index % chips
        if hop:
            source, row, _ = where_tiles[hop][chip]
            rows[spot, :] = parts[source][row : row + part_rows, :width]
        else:
            start = pl.multiple_of((place[1] ^ (2 * chip)) * part_rows, part_rows)
            rows[spot, :] = tokens[pl.ds(start, part_rows), :]
    if with_last:
        floats = last_tokens(place, seq_dev, where_tiles, parts, seq_tokens)
        last_all[...] = floats.astype(bf16)
        rows[total:, :] = floats.astype(bf16)
    hidden = []
    for half in range(2):
        projected = dot(rows[...], weights[2 * half][0])
        if half == 0 and with_last:
            last_projected[...] = projected[total:]
        _, up, _, activated = hidden_parts(projected)
        hidden.append((activated * up).astype(bf16))
    block = min(512, width)
    if with_last:
        each = floats.shape[0] // by_lane.shape[0]
    for first in range(0, width, block):
        columns = slice(first, first + block)
        result = dot(hidden[0], weights[1][0, :, columns]) + dot(
            hidden[1], weights[3][0, :, columns]
        )
        for out, spot in zip(outs, spots):
            out[:, columns] = result[spot].astype(bf16)
        if with_last:
            for lane in range(by_lane.shape[0]):
                at = total + lane * each
                by_lane[lane, 0:each, columns] = result[at : at + each]
    if with_last:
        for chip in range(chips):
            spread_rows(by_lane[place[1] ^ (2 * chip), 0:each, :], part_rows, tile)
            outs[n_outs - chips + chip][:, width:] = tile[...].astype(bf16)
        for lane in range(by_lane.shape[0]):
            by_lane[lane, 0:each, :] = floats[lane * each : (lane + 1) * each]
        spread_rows(by_lane[place[1], 0:each, :], part_rows, tile)
        own_last[...] = tile[...]


def combine_kernel(layout, place, kept, found, *refs):
    hop, chips, with_last, width, each = layout
    own, refs = (refs[0], refs[1:]) if hop == 0 else (None, refs)
    last_in, refs = (refs[0], refs[1:]) if hop and not with_last else (None, refs)
    parts, out = refs[:chips], refs[chips]
    part_rows = out.shape[0]
    first_expert = place[2] - place[1] // 2
    experts = [first_expert + ((place[1] // 2) ^ chip) for chip in range(chips)]
    if with_last:
        last_in = refs[-1]
        table = kept[-2 * chips * each :, :].astype(f32) + found[-2 * chips * each :, :].astype(f32)
        row_index = lax.broadcasted_iota(jnp.int32, table.shape, 0)
        chunks = width // lanes
        for row in range(each):
            mine = jnp.where(row_index == place[1] * each + row, table, 0.0)
            mine = jnp.sum(mine, axis=0, keepdims=True)
            first = row * chunks % part_rows
            spot = slice(first, first + chunks)
            at = row * chunks // part_rows * lanes
            total = None
            for chip in range(chips):
                values = parts[chip][spot, width + at : width + at + lanes].astype(f32)
                term = column(mine, experts[chip]) * values
                total = term if total is None else total + term
            last_in[spot, at : at + lanes] = total.astype(bf16)
    at = slice(hop * part_rows, (hop + 1) * part_rows)
    table = kept[at, :].astype(f32) + found[at, :].astype(f32)
    total = None if hop else own[:, :width].astype(f32)
    for chip in range(chips):
        term = column(table, experts[chip]) * parts[chip][:, :width].astype(f32)
        total = term if total is None else total + term
    out[:, :width] = total.astype(out.dtype)
    if hop:
        out[:, width:] = last_in[...]


def finish_kernel(near, own_last, last_sum, *refs):
    parts, out = refs[:-1], refs[-1]
    width = near.shape[1]
    total = near[...]
    last = last_sum[...].astype(f32)
    for part in parts:
        total = total + part[:, :width].astype(f32)
        last = last + part[:, width:].astype(f32)
    out[:, :width] = total.astype(bf16)
    out[:, width:] = (own_last[...] + last).astype(bf16)


def collect_rows(lane, pieces, by_lane, width):
    part_rows, chunks = pieces[0].shape[0], width // lanes
    count = len(pieces)
    each = (pieces[0].shape[1] - width) * part_rows // width
    for index in range(count):
        source = lane ^ (2 * (index % (count // 2))) ^ (index // (count // 2))
        values = pieces[index][:, width:].astype(f32)
        for spot in range(each * chunks):
            row, chunk = spot // chunks, spot % chunks
            at = spot // part_rows * lanes
            from_row = spot % part_rows
            by_lane[source, row : row + 1, chunk * lanes : (chunk + 1) * lanes] = values[
                from_row : from_row + 1, at : at + lanes
            ]
    return jnp.concatenate([by_lane[index, 0:each, :] for index in range(count)], axis=0)


def both_ways(coefficient, unit, diagonal):
    count = unit.shape[0]
    if count > 32:
        high = lax.Precision.HIGHEST
        there = dot(coefficient, unit, ((1,), (0,)), high)
        return there + dot(coefficient, unit, ((0,), (0,)), high)
    total = None
    for index in range(count):
        line = jnp.where(diagonal, coefficient[index : index + 1, :], 0.0)
        factor = coefficient[:, index : index + 1] + jnp.sum(line, axis=1, keepdims=True)
        term = factor * unit[index : index + 1, :]
        total = term if total is None else total + term
    return total


def final_kernel(n_pieces, n_blocks, *refs):
    pieces, refs = refs[:n_pieces], refs[n_pieces:]
    last_all, projected, place, kept, found, partners, down, *refs = refs
    layer_out, grad_in, grad_out, made_in, made_out, by_lane, sems = refs
    part_rows, width = pieces[0].shape[0], layer_out.shape[1]
    copies = []

    def send(source, target):
        copies.append(pltpu.make_async_copy(source, target, sems.at[len(copies)]))
        copies[-1].start()

    for index in range(n_pieces):
        lane = place[1] ^ (2 * (index % (n_pieces // 2))) ^ (index // (n_pieces // 2))
        start = pl.multiple_of(lane * part_rows, part_rows)
        send(pieces[index].at[:, pl.ds(0, width)], layer_out.at[pl.ds(start, part_rows)])
    values = collect_rows(place[1], pieces, by_lane, width)
    count = values.shape[0]
    last = kept.shape[0] - count
    table = kept[last:, :].astype(f32) + found[last:, :].astype(f32)
    row = lax.broadcasted_iota(jnp.int32, (count, count), 0)
    col = lax.broadcasted_iota(jnp.int32, (count, count), 1)
    norms = jnp.sqrt(jnp.sum(values * values, axis=1, keepdims=True) + epsilon)
    norms_line = jnp.sum(jnp.where(row == col, norms, 0.0), axis=0, keepdims=True)
    unit = values / norms
    rows = values.astype(bf16)
    scores = dot(rows, rows, ((1,), (1,))) / (norms * norms_line) / logit_divisor
    exp_scores = jnp.where(row != col, jnp.exp(scores), 0.0)
    probabilities = exp_scores / jnp.sum(exp_scores, axis=1, keepdims=True)
    partner = partners[:, :1].astype(jnp.int32)
    coefficient = grad_scale * (probabilities - jnp.where(col == partner, 1.0, 0.0))
    grad_unit = both_ways(coefficient, unit, row == col) / logit_divisor
    projection = jnp.sum(unit * grad_unit, axis=1, keepdims=True)
    grad_last = (grad_unit - unit * projection) / norms
    route_grad = (column(table, place[2]) * grad_last).astype(bf16)
    gate, up, sigmoid_gate, activated = hidden_parts(projected[...])
    hidden = (activated * up).astype(bf16)
    made_out[...] = dot(hidden, route_grad, ((0,), (0,))).astype(bf16)
    send(made_out, grad_out.at[0])
    grad_hidden = dot(route_grad, down[0], ((1,), (1,)))
    gate_slope = sigmoid_gate * (1.0 + gate * (1.0 - sigmoid_gate))
    slope = jnp.concatenate([grad_hidden * up * gate_slope, grad_hidden * activated], axis=1)
    slope = slope.astype(bf16)
    block = width // n_blocks
    for index in range(n_blocks):
        spot = slice(index * block, (index + 1) * block)
        made_in[spot, :] = dot(last_all[:, spot], slope, ((0,), (0,))).astype(bf16)
        send(made_in.at[spot], grad_in.at[0, spot])
    for copy in copies:
        copy.wait()


def body(tokens, expert_ids, gates, positives, gate_up, down):
    dp_count = lax.axis_size("dp")
    expert_count = lax.axis_size("expert")
    chips = expert_count // 2
    experts = dp_count * chips
    tok_dev, width = tokens.shape
    half_width = down.shape[1]
    seq_dev = positives.shape[0]
    seqs = dp_count * seq_dev
    seq_length = tok_dev // seq_dev
    part_rows = tok_dev // expert_count
    plane = lax.axis_index("dp")
    lane = lax.axis_index("expert")
    place = jnp.stack([plane, lane, plane * chips + lane // 2]).astype(jnp.int32)
    assert experts <= lanes and seq_length % tail == 0

    def to_lane(value, step):
        return lax.ppermute(value, "expert", [(j, j ^ step) for j in range(expert_count)])

    def to_plane(value, step):
        return lax.ppermute(value, "dp", [(p, p ^ step) for p in range(dp_count)])

    chip_steps = [2 * step for step in range(1, chips)]
    groups = [range(first, min(first + 2, dp_count)) for first in range(0, dp_count, 2)]

    share = width // chips
    packed = pl.pallas_call(
        functools.partial(pack_kernel, seq_dev),
        out_shape=jax.ShapeDtypeStruct((part_rows, width + lanes), bf16),
        in_specs=[in_smem] + [in_hbm] * 3,
        out_specs=in_vmem,
        scratch_shapes=[
            pltpu.VMEM((part_rows, lanes), f32),
            pltpu.VMEM((seq_dev, tail, share), bf16),
            pltpu.VMEM((1, tok_dev), jnp.int32),
            pltpu.VMEM((1, tok_dev), f32),
            pltpu.SemaphoreType.DMA((seq_dev + 3,)),
        ],
        cost_estimate=cost(0, 1 << 19),
        name="pack",
    )(positives, expert_ids.T, gates.T, tokens)
    arrivals = {hop: to_plane(packed, hop) for hop in range(1, dp_count)}
    mate_in = to_lane(gate_up, 1)
    mate_out = to_lane(down, 1)
    weights = (gate_up, down, mate_in, mate_out)

    tiles = [packed]
    spots = {}
    received = None
    for group in groups:
        own = [arrivals[hop] for hop in group if hop]
        if group[0] == 0:
            joined = jnp.concatenate(own + [packed[:, width:]], axis=1)
            joined, weights = lax.optimization_barrier((joined, weights))
        else:
            joined = jnp.concatenate(own, axis=0)
            joined, received = lax.optimization_barrier((joined, received))
            tiles[-len(received) :] = received
        first = len(tiles)
        received = [to_lane(joined, step) for step in chip_steps]
        tiles += own + received
        for index, hop in enumerate(group):
            if group[0] == 0:
                place_of = (first, 0, width) if hop else (0, 0, width)
                row, at = 0, width if hop else width + lanes
            else:
                place_of = (first + index, 0, width)
                row, at = index * part_rows, width
            spots[hop] = [place_of] + [
                (first + len(own) + chip, row, at) for chip in range(chips - 1)
            ]
    where_tiles = [spots[hop] for hop in range(dp_count)]

    each = seqs // expert_count
    extra = each * width // part_rows
    assert extra % lanes == 0 and part_rows % (width // lanes) == 0

    def expert(group, place, with_last):
        near = 0 in group
        wanted = range(dp_count) if with_last else [hop for hop in group if hop]
        used = sorted({spot[0] for hop in wanted for spot in where_tiles[hop]})
        parts = [tiles[index] for index in used]
        n_outs = chips * len(group)
        total = n_outs * part_rows + (seqs if with_last else 0)
        out_shape = [jax.ShapeDtypeStruct((part_rows, width), bf16)] * n_outs
        scratch = [pltpu.VMEM((total, width), bf16)]
        if with_last:
            wider = jax.ShapeDtypeStruct((part_rows, width + extra), bf16)
            out_shape[n_outs - chips :] = [wider] * chips
            out_shape += [
                jax.ShapeDtypeStruct((seqs, width), bf16),
                jax.ShapeDtypeStruct((seqs, 2 * half_width), f32),
                jax.ShapeDtypeStruct((part_rows, extra), f32),
            ]
            scratch = [
                pltpu.VMEM((expert_count, -(-each // 8) * 8, width), f32),
                pltpu.VMEM((part_rows, extra), f32),
                pltpu.VMEM((dp_count, width // lanes, -(-seq_dev // 8) * 8, lanes), f32),
            ] + scratch
        operands = [place] + [tokens] * near + parts + list(weights)
        layout = (tuple(group), chips, part_rows, seq_dev, where_tiles, used, with_last)
        return pl.pallas_call(
            functools.partial(expert_kernel, layout),
            out_shape=out_shape,
            in_specs=[in_smem] + [in_vmem] * (len(operands) - 1),
            out_specs=[in_vmem] * len(out_shape),
            scratch_shapes=scratch,
            compiler_params=params(32),
            cost_estimate=cost(2 * total * width * 6 * half_width, 12 << 20),
            name="experts",
        )(*operands)

    outs = {}
    after = place
    rest = list(range(dp_count - 2, 1, -1))
    expert_groups = [[0, 1]] + [[dp_count - 1]] * (dp_count > 2)
    expert_groups += [rest[first : first + 2] for first in range(0, len(rest), 2)]
    for group in expert_groups:
        with_last = dp_count - 1 in group
        out = expert(group, after, with_last)
        after, _ = lax.optimization_barrier((place, out[0]))
        for index, hop in enumerate(group):
            outs[hop] = out[index * chips : (index + 1) * chips]
        if with_last:
            last_all, last_projected, own_last = out[-3:]
            tables_place = after

    table_rows = dp_count * part_rows + seqs
    chunks = width // lanes
    sublanes = -(-seq_dev // 8) * 8
    kept, sent, partners = pl.pallas_call(
        functools.partial(table_kernel, (seq_dev, tok_dev, where_tiles, len(tiles))),
        out_shape=[
            jax.ShapeDtypeStruct((table_rows, lanes), bf16),
            jax.ShapeDtypeStruct((table_rows, lanes), bf16),
            jax.ShapeDtypeStruct((seqs, lanes), f32),
        ],
        in_specs=[in_smem] + [in_vmem] * len(tiles),
        out_specs=[in_vmem] * 3,
        scratch_shapes=[
            pltpu.VMEM((dp_count, sublanes, lanes), f32),
            pltpu.VMEM((dp_count, sublanes, lanes), f32),
        ],
        compiler_params=params(48 if dp_count > 8 else 12),
        cost_estimate=cost(0, 1 << 20),
        name="tables",
    )(tables_place, *tiles)
    found = to_lane(sent, 1)

    def combine(hop, parts, last_sum):
        with_last = last_sum is None
        out_shape = [jax.ShapeDtypeStruct((part_rows, width), f32)]
        if hop:
            out_shape = [jax.ShapeDtypeStruct((part_rows, width + extra), bf16)]
        if with_last:
            out_shape.append(jax.ShapeDtypeStruct((part_rows, extra), bf16))
        operands = [place, kept, found] + [packed] * (hop == 0)
        operands += [last_sum] * (hop > 0 and not with_last) + parts
        return pl.pallas_call(
            functools.partial(combine_kernel, (hop, chips, with_last, width, each)),
            out_shape=out_shape,
            in_specs=[in_smem] + [in_vmem] * (len(operands) - 1),
            out_specs=[in_vmem] * len(out_shape),
            compiler_params=params(8),
            cost_estimate=cost(0, 2 << 20),
            name="combine",
        )(*operands)

    returned = {}

    def send_back(hop, gated, after):
        first, *parts = outs[hop]
        free = len(parts) - gated
        parts[free:], after = lax.optimization_barrier((parts[free:], after))
        returned[hop] = [first] + [to_lane(value, step) for value, step in zip(parts, chip_steps)]
        return after

    send_back(1, 0, [])
    if dp_count > 2:
        returned[1][1:] = send_back(dp_count - 1, chips - 1, returned[1][1:])
    before = dp_count - 1
    for hop in rest:
        returned[before][1:], found = send_back(hop, 1, (returned[before][1:], found))
        before = hop
    homeward = []
    last_sum = None
    for hop in range(dp_count - 1, 0, -1):
        result = combine(hop, returned[hop], last_sum)
        if last_sum is None:
            last_sum = result[1]
            last_sum = send_back(0, chips - 1, last_sum)
        homeward.append(to_plane(result[0], hop))
    near_sum = combine(0, returned[0], last_sum)[0]

    own_out = pl.pallas_call(
        finish_kernel,
        out_shape=jax.ShapeDtypeStruct((part_rows, width + extra), bf16),
        in_specs=[in_vmem] * (2 + dp_count),
        out_specs=in_vmem,
        compiler_params=params(16 if dp_count > 8 else 4),
        cost_estimate=cost(0, 1 << 20),
        name="finish",
    )(near_sum, own_last, last_sum, *homeward)
    pieces = [own_out] + [to_lane(own_out, step) for step in chip_steps]
    pieces += [to_lane(piece, 1) for piece in pieces]

    n_blocks = width // min(512, width)
    layer_out, grad_gate_up, grad_down = pl.pallas_call(
        functools.partial(final_kernel, len(pieces), n_blocks),
        out_shape=[
            jax.ShapeDtypeStruct((tok_dev, width), bf16),
            jax.ShapeDtypeStruct(gate_up.shape, bf16),
            jax.ShapeDtypeStruct(down.shape, bf16),
        ],
        in_specs=[in_vmem] * (len(pieces) + 2) + [in_smem] + [in_vmem] * 4,
        out_specs=[in_hbm] * 3,
        scratch_shapes=[
            pltpu.VMEM((width, 2 * half_width), bf16),
            pltpu.VMEM((half_width, width), bf16),
            pltpu.VMEM((expert_count, -(-each // 8) * 8, width), f32),
            pltpu.SemaphoreType.DMA((len(pieces) + n_blocks + 1,)),
        ],
        compiler_params=params(24),
        cost_estimate=cost(2 * seqs * width * 4 * half_width, 7 << 20),
        name="final",
    )(*pieces, last_all, last_projected, place, kept, found, partners, down)
    return (layer_out, grad_gate_up, grad_down)


def solution(mesh):
    return jax.shard_map(
        body,
        mesh=mesh,
        in_specs=(
            P("dp", None),
            P("dp", "expert"),
            P("dp", "expert"),
            P("dp"),
            P(("dp", "expert"), None, None),
            P(("dp", "expert"), None, None),
        ),
        out_specs=(P("dp", None), P(("dp", "expert"), None, None), P(("dp", "expert"), None, None)),
        check_vma=False,
    )
```

```python
import functools

import jax
import jax.numpy as jnp
from jax import lax
from jax.experimental import pallas as pl
from jax.experimental.pallas import tpu as pltpu
from jax.sharding import PartitionSpec as P

logit_divisor = 0.05
grad_scale = 256.0
epsilon = 1e-06
lanes = 128
tail = 16
bf16 = jnp.bfloat16
f32 = jnp.float32

in_hbm = pl.BlockSpec(memory_space=pltpu.HBM)
in_vmem = pl.BlockSpec(memory_space=pltpu.VMEM)
in_smem = pl.BlockSpec(memory_space=pltpu.SMEM)


def params(mebibytes):
    return pltpu.CompilerParams(vmem_limit_bytes=mebibytes << 20)


def cost(flops, moved):
    return pl.CostEstimate(flops=flops, transcendentals=0, bytes_accessed=moved)


def dot(left, right, dims=((1,), (0,)), precision=None):
    return lax.dot_general(
        left, right, (dims, ((), ())), precision=precision, preferred_element_type=f32
    )


def doublings(count):
    steps = [1 << bit for bit in range((count - 1).bit_length())]
    assert 1 << len(steps) == count
    return steps


def column(table, wanted):
    index = lax.broadcasted_iota(jnp.int32, table.shape, 1)
    return jnp.sum(jnp.where(index == wanted, table, 0.0), axis=1, keepdims=True)


def pack_kernel(seq_dev, positives, ids_in, gates_in, tokens, out, tile, rows, ids, gates, sems):
    part_rows, width = out.shape[0], tokens.shape[1]
    tok_dev = tokens.shape[0]
    seq_length = tok_dev // seq_dev
    share = rows.shape[2]
    lane = lax.axis_index("expert")
    column_at = pl.multiple_of(lane // 2 * share, lanes)
    start = pl.multiple_of(lane * part_rows, part_rows)
    copies = [
        pltpu.make_async_copy(
            tokens.at[pl.ds((seq + 1) * seq_length - tail, tail), pl.ds(column_at, share)],
            rows.at[seq],
            sems.at[seq],
        )
        for seq in range(seq_dev)
    ]
    own = pltpu.make_async_copy(
        tokens.at[pl.ds(start, part_rows)], out.at[:, pl.ds(0, width)], sems.at[seq_dev]
    )
    lines = [
        pltpu.make_async_copy(ids_in, ids, sems.at[seq_dev + 1]),
        pltpu.make_async_copy(gates_in, gates, sems.at[seq_dev + 2]),
    ]
    for copy in lines + [own] + copies:
        copy.start()
    note_rows = tok_dev // lanes
    tile[...] = jnp.zeros_like(tile)
    for copy in lines:
        copy.wait()
    for index in range(note_rows):
        block = slice(index * lanes, (index + 1) * lanes)
        tile[index : index + 1, :] = ids[:, block].astype(f32)
        tile[note_rows + index : note_rows + index + 1, :] = gates[:, block]
    for seq in range(seq_dev):
        row = 2 * note_rows + seq
        tile[row : row + 1, :] = jnp.full((1, lanes), positives[seq], jnp.int32).astype(f32)
    base = part_rows - seq_dev * (share // lanes)
    for seq in range(seq_dev):
        copies[seq].wait()
        values = rows[seq].astype(f32)
        for chunk in range(share // lanes):
            row = base + chunk * seq_dev + seq
            tile[row : row + 1, :] = values[tail - 1 : tail, chunk * lanes : (chunk + 1) * lanes]
    out[:, width:] = tile[...].astype(bf16)
    own.wait()


def table_kernel(layout, place, *refs):
    seq_dev, tok_dev, where_tiles, n_parts = layout
    parts = refs[:n_parts]
    kept, sent, partners, routes, marks = refs[n_parts:]
    part_rows = parts[0].shape[0]
    dp_count = len(where_tiles)
    note_rows = tok_dev // lanes
    seq_length = tok_dev // seq_dev
    chips = len(where_tiles[0])
    lane_index = lax.broadcasted_iota(jnp.int32, (part_rows, lanes), 1)
    row_index = lax.broadcasted_iota(jnp.int32, (part_rows, lanes), 0)

    def dense_rows(tile, lane):
        start = lane * part_rows
        picked = lane_index == row_index + start % lanes
        found = []
        for offset in (0, note_rows):
            line = tile[offset : offset + 1, :]
            for index in range(1, note_rows):
                other = tile[offset + index : offset + index + 1, :]
                line = jnp.where(start // lanes == index, other, line)
            found.append(jnp.sum(jnp.where(picked, line, 0.0), axis=1, keepdims=True))
        return jnp.where(lane_index.astype(f32) == found[0], found[1], 0.0)

    for hop in range(dp_count):
        plane = place[0] ^ hop
        sums = [None, None]
        for chip in range(chips):
            source, row, at = where_tiles[hop][chip]
            tile = parts[source][row : row + part_rows, at : at + lanes].astype(f32)
            for index, lane in enumerate((place[1], place[1] ^ 1)):
                value = dense_rows(tile, lane)
                sums[index] = value if chip == 0 else sums[index] + value
            for seq in range(seq_dev):
                at_token = (seq + 1) * seq_length - 1
                row = at_token // lanes
                here = lane_index[:1] == at_token % lanes
                expert, gate = [
                    jnp.sum(
                        jnp.where(here, tile[offset + row : offset + row + 1, :], 0.0),
                        axis=1,
                        keepdims=True,
                    )
                    for offset in (0, note_rows)
                ]
                value = jnp.where(lane_index[:1].astype(f32) == expert, gate, 0.0)
                if chip:
                    value = value + routes[plane, seq : seq + 1, :]
                routes[plane, seq : seq + 1, :] = value
            if chip == 0:
                marks[plane, 0:seq_dev, :] = tile[2 * note_rows : 2 * note_rows + seq_dev, :]
        at = slice(hop * part_rows, (hop + 1) * part_rows)
        kept[at, :] = sums[0].astype(bf16)
        sent[at, :] = sums[1].astype(bf16)
    last = dp_count * part_rows
    shared = []
    for plane in range(dp_count):
        shared.append(routes[plane, 0:seq_dev, :])
        partners[plane * seq_dev : (plane + 1) * seq_dev, :] = marks[plane, 0:seq_dev, :]
    seqs = dp_count * seq_dev
    value = jnp.concatenate(shared, axis=0).astype(bf16)
    kept[last : last + seqs, :] = value
    sent[last : last + seqs, :] = value


def hidden_parts(projected):
    half_width = projected.shape[1] // 2
    gate, up = projected[:, :half_width], projected[:, half_width:]
    sigmoid_gate = jax.nn.sigmoid(gate)
    return gate, up, sigmoid_gate, gate * sigmoid_gate


def spread_rows(values, rows, blocks):
    chunks = values.shape[1] // lanes
    for index in range(values.shape[0] * chunks):
        row, chunk = index // chunks, index % chunks
        spot = slice(index % rows, index % rows + 1)
        block = slice(index // rows * lanes, (index // rows + 1) * lanes)
        blocks[spot, block] = values[row : row + 1, chunk * lanes : (chunk + 1) * lanes]


def last_tokens(place, seq_dev, where_tiles, parts, tokens):
    part_rows = parts[0].shape[0]
    dp_count, chunks = tokens.shape[:2]
    chips = len(where_tiles[0])
    share_chunks = chunks // chips
    base = part_rows - seq_dev * share_chunks
    for hop in range(dp_count):
        for chip in range(chips):
            source, row, at = where_tiles[hop][chip]
            tile = parts[source][row : row + part_rows, at : at + lanes].astype(f32)
            first = ((place[1] // 2) ^ chip) * share_chunks
            for chunk in range(share_chunks):
                row = base + chunk * seq_dev
                tokens[place[0] ^ hop, first + chunk, 0:seq_dev, :] = tile[row : row + seq_dev, :]
    joined = []
    for plane in range(dp_count):
        lines = [tokens[plane, chunk, 0:seq_dev, :] for chunk in range(chunks)]
        joined.append(jnp.concatenate(lines, axis=1))
    return jnp.concatenate(joined, axis=0)


def expert_kernel(layout, *refs):
    group, chips, part_rows, seq_dev, where_tiles, used, with_last = layout
    refs = list(refs)
    place = refs.pop(0)
    near = 0 in group
    tokens = refs.pop(0) if near else None
    parts, refs = dict(zip(used, refs)), refs[len(used) :]
    weights, refs = refs[:4], refs[4:]
    copied, sem = refs[-2:]
    mate_copy = pltpu.make_async_copy(weights[3], copied, sem)
    mate_copy.start()
    weights[3] = copied
    refs = refs[:-2]
    n_outs = chips * len(group)
    outs, refs = refs[:n_outs], refs[n_outs:]
    if with_last:
        last_all, last_projected, own_last, by_lane, tile, seq_tokens, *refs = refs
    (rows,) = refs
    width = weights[0].shape[1]
    total = n_outs * part_rows
    spots = [slice(index * part_rows, (index + 1) * part_rows) for index in range(n_outs)]
    for index, spot in enumerate(spots):
        hop, chip = group[index // chips], index % chips
        if hop:
            source, row, _ = where_tiles[hop][chip]
            rows[spot, :] = parts[source][row : row + part_rows, :width]
        else:
            start = pl.multiple_of((place[1] ^ (2 * chip)) * part_rows, part_rows)
            rows[spot, :] = tokens[pl.ds(start, part_rows), :]
    if with_last:
        floats = last_tokens(place, seq_dev, where_tiles, parts, seq_tokens)
        last_all[...] = floats.astype(bf16)
        rows[total:, :] = floats.astype(bf16)
    hidden = []
    for half in range(2):
        projected = dot(rows[...], weights[2 * half][0])
        if half == 0 and with_last:
            last_projected[...] = projected[total:]
        _, up, _, activated = hidden_parts(projected)
        hidden.append((activated * up).astype(bf16))
    mate_copy.wait()
    block = min(512, width)
    if with_last:
        each = floats.shape[0] // by_lane.shape[0]
    for first in range(0, width, block):
        columns = slice(first, first + block)
        result = dot(hidden[0], weights[1][0, :, columns]) + dot(
            hidden[1], weights[3][0, :, columns]
        )
        for out, spot in zip(outs, spots):
            out[:, columns] = result[spot].astype(bf16)
        if with_last:
            for lane in range(by_lane.shape[0]):
                at = total + lane * each
                by_lane[lane, 0:each, columns] = result[at : at + each]
    if with_last:
        for chip in range(chips):
            spread_rows(by_lane[place[1] ^ (2 * chip), 0:each, :], part_rows, tile)
            outs[n_outs - chips + chip][:, width:] = tile[...].astype(bf16)
        for lane in range(by_lane.shape[0]):
            by_lane[lane, 0:each, :] = floats[lane * each : (lane + 1) * each]
        spread_rows(by_lane[place[1], 0:each, :], part_rows, tile)
        own_last[...] = tile[...]


def combine_kernel(layout, place, kept, found, *refs):
    hop, chips, with_last, width, each = layout
    own, refs = (refs[0], refs[1:]) if hop == 0 else (None, refs)
    last_in, refs = (refs[0], refs[1:]) if hop and not with_last else (None, refs)
    parts, out = refs[:chips], refs[chips]
    part_rows = out.shape[0]
    first_expert = place[2] - place[1] // 2
    experts = [first_expert + ((place[1] // 2) ^ chip) for chip in range(chips)]
    if with_last:
        last_in = refs[-1]
        table = kept[-2 * chips * each :, :].astype(f32) + found[-2 * chips * each :, :].astype(f32)
        row_index = lax.broadcasted_iota(jnp.int32, table.shape, 0)
        chunks = width // lanes
        for row in range(each):
            mine = jnp.where(row_index == place[1] * each + row, table, 0.0)
            mine = jnp.sum(mine, axis=0, keepdims=True)
            first = row * chunks % part_rows
            spot = slice(first, first + chunks)
            at = row * chunks // part_rows * lanes
            total = None
            for chip in range(chips):
                values = parts[chip][spot, width + at : width + at + lanes].astype(f32)
                term = column(mine, experts[chip]) * values
                total = term if total is None else total + term
            last_in[spot, at : at + lanes] = total.astype(bf16)
    at = slice(hop * part_rows, (hop + 1) * part_rows)
    table = kept[at, :].astype(f32) + found[at, :].astype(f32)
    total = None if hop else own[:, :width].astype(f32)
    for chip in range(chips):
        term = column(table, experts[chip]) * parts[chip][:, :width].astype(f32)
        total = term if total is None else total + term
    out[:, :width] = total.astype(out.dtype)
    if hop:
        out[:, width:] = last_in[...]


def finish_kernel(near, own_last, last_sum, *refs):
    parts, out = refs[:-1], refs[-1]
    width = near.shape[1]
    total = near[...]
    last = last_sum[...].astype(f32)
    for part in parts:
        total = total + part[:, :width].astype(f32)
        last = last + part[:, width:].astype(f32)
    out[:, :width] = total.astype(bf16)
    out[:, width:] = (own_last[...] + last).astype(bf16)


def collect_rows(lane, pieces, by_lane, width):
    part_rows, chunks = pieces[0].shape[0], width // lanes
    count = len(pieces)
    each = (pieces[0].shape[1] - width) * part_rows // width
    for index in range(count):
        source = lane ^ (2 * (index % (count // 2))) ^ (index // (count // 2))
        values = pieces[index][:, width:].astype(f32)
        for spot in range(each * chunks):
            row, chunk = spot // chunks, spot % chunks
            at = spot // part_rows * lanes
            from_row = spot % part_rows
            by_lane[source, row : row + 1, chunk * lanes : (chunk + 1) * lanes] = values[
                from_row : from_row + 1, at : at + lanes
            ]
    return jnp.concatenate([by_lane[index, 0:each, :] for index in range(count)], axis=0)


def both_ways(coefficient, unit, diagonal):
    count = unit.shape[0]
    if count > 32:
        high = lax.Precision.HIGHEST
        there = dot(coefficient, unit, ((1,), (0,)), high)
        return there + dot(coefficient, unit, ((0,), (0,)), high)
    total = None
    for index in range(count):
        line = jnp.where(diagonal, coefficient[index : index + 1, :], 0.0)
        factor = coefficient[:, index : index + 1] + jnp.sum(line, axis=1, keepdims=True)
        term = factor * unit[index : index + 1, :]
        total = term if total is None else total + term
    return total


def final_kernel(n_pieces, n_blocks, *refs):
    pieces, refs = refs[:n_pieces], refs[n_pieces:]
    last_all, projected, place, kept, found, partners, down, *refs = refs
    layer_out, grad_in, grad_out, made_in, made_out, by_lane, sems = refs
    part_rows, width = pieces[0].shape[0], layer_out.shape[1]
    copies = []

    def send(source, target):
        copies.append(pltpu.make_async_copy(source, target, sems.at[len(copies)]))
        copies[-1].start()

    for index in range(n_pieces):
        lane = place[1] ^ (2 * (index % (n_pieces // 2))) ^ (index // (n_pieces // 2))
        start = pl.multiple_of(lane * part_rows, part_rows)
        send(pieces[index].at[:, pl.ds(0, width)], layer_out.at[pl.ds(start, part_rows)])
    values = collect_rows(place[1], pieces, by_lane, width)
    count = values.shape[0]
    last = kept.shape[0] - count
    table = kept[last:, :].astype(f32) + found[last:, :].astype(f32)
    row = lax.broadcasted_iota(jnp.int32, (count, count), 0)
    col = lax.broadcasted_iota(jnp.int32, (count, count), 1)
    norms = jnp.sqrt(jnp.sum(values * values, axis=1, keepdims=True) + epsilon)
    norms_line = jnp.sum(jnp.where(row == col, norms, 0.0), axis=0, keepdims=True)
    unit = values / norms
    rows = values.astype(bf16)
    scores = dot(rows, rows, ((1,), (1,))) / (norms * norms_line) / logit_divisor
    exp_scores = jnp.where(row != col, jnp.exp(scores), 0.0)
    probabilities = exp_scores / jnp.sum(exp_scores, axis=1, keepdims=True)
    partner = partners[:, :1].astype(jnp.int32)
    coefficient = grad_scale * (probabilities - jnp.where(col == partner, 1.0, 0.0))
    grad_unit = both_ways(coefficient, unit, row == col) / logit_divisor
    projection = jnp.sum(unit * grad_unit, axis=1, keepdims=True)
    grad_last = (grad_unit - unit * projection) / norms
    route_grad = (column(table, place[2]) * grad_last).astype(bf16)
    gate, up, sigmoid_gate, activated = hidden_parts(projected[...])
    hidden = (activated * up).astype(bf16)
    grad_hidden = dot(route_grad, down[0], ((1,), (1,)))
    gate_slope = sigmoid_gate * (1.0 + gate * (1.0 - sigmoid_gate))
    slope = jnp.concatenate([grad_hidden * up * gate_slope, grad_hidden * activated], axis=1)
    slope = slope.astype(bf16)
    block = width // n_blocks
    for index in range(n_blocks):
        spot = slice(index * block, (index + 1) * block)
        made_in[spot, :] = dot(last_all[:, spot], slope, ((0,), (0,))).astype(bf16)
        send(made_in.at[spot], grad_in.at[0, spot])
    made_out[...] = dot(hidden, route_grad, ((0,), (0,))).astype(bf16)
    send(made_out, grad_out.at[0])
    for copy in copies:
        copy.wait()


def body(tokens, expert_ids, gates, positives, gate_up, down):
    dp_count = lax.axis_size("dp")
    expert_count = lax.axis_size("expert")
    chips = expert_count // 2
    experts = dp_count * chips
    tok_dev, width = tokens.shape
    half_width = down.shape[1]
    seq_dev = positives.shape[0]
    seqs = dp_count * seq_dev
    seq_length = tok_dev // seq_dev
    part_rows = tok_dev // expert_count
    plane = lax.axis_index("dp")
    lane = lax.axis_index("expert")
    place = jnp.stack([plane, lane, plane * chips + lane // 2]).astype(jnp.int32)
    assert experts <= lanes and seq_length % tail == 0

    def to_lane(value, step):
        return lax.ppermute(value, "expert", [(j, j ^ step) for j in range(expert_count)])

    def to_plane(value, step):
        return lax.ppermute(value, "dp", [(p, p ^ step) for p in range(dp_count)])

    chip_steps = [2 * step for step in range(1, chips)]
    groups = [range(first, min(first + 2, dp_count)) for first in range(0, dp_count, 2)]

    share = width // chips
    packed = pl.pallas_call(
        functools.partial(pack_kernel, seq_dev),
        out_shape=jax.ShapeDtypeStruct((part_rows, width + lanes), bf16),
        in_specs=[in_smem] + [in_hbm] * 3,
        out_specs=in_vmem,
        scratch_shapes=[
            pltpu.VMEM((part_rows, lanes), f32),
            pltpu.VMEM((seq_dev, tail, share), bf16),
            pltpu.VMEM((1, tok_dev), jnp.int32),
            pltpu.VMEM((1, tok_dev), f32),
            pltpu.SemaphoreType.DMA((seq_dev + 3,)),
        ],
        cost_estimate=cost(0, 1 << 19),
        name="pack",
    )(positives, expert_ids.T, gates.T, tokens)
    arrivals = {hop: to_plane(packed, hop) for hop in range(1, dp_count)}
    mate_in = to_lane(gate_up, 1)
    mate_out = to_lane(down, 1)
    weights = (gate_up, down, mate_in, mate_out)

    tiles = [packed]
    spots = {}
    received = None
    for group in groups:
        own = [arrivals[hop] for hop in group if hop]
        if group[0] == 0:
            joined = jnp.concatenate(own + [packed[:, width:]], axis=1)
            joined, weights = lax.optimization_barrier((joined, weights))
        else:
            joined = jnp.concatenate(own, axis=0)
            joined, received = lax.optimization_barrier((joined, received))
            tiles[-len(received) :] = received
        first = len(tiles)
        received = [to_lane(joined, step) for step in chip_steps]
        tiles += own + received
        for index, hop in enumerate(group):
            if group[0] == 0:
                place_of = (first, 0, width) if hop else (0, 0, width)
                row, at = 0, width if hop else width + lanes
            else:
                place_of = (first + index, 0, width)
                row, at = index * part_rows, width
            spots[hop] = [place_of] + [
                (first + len(own) + chip, row, at) for chip in range(chips - 1)
            ]
    where_tiles = [spots[hop] for hop in range(dp_count)]

    each = seqs // expert_count
    extra = each * width // part_rows
    assert extra % lanes == 0 and part_rows % (width // lanes) == 0

    def expert(group, place, with_last):
        near = 0 in group
        wanted = range(dp_count) if with_last else [hop for hop in group if hop]
        used = sorted({spot[0] for hop in wanted for spot in where_tiles[hop]})
        parts = [tiles[index] for index in used]
        n_outs = chips * len(group)
        total = n_outs * part_rows + (seqs if with_last else 0)
        out_shape = [jax.ShapeDtypeStruct((part_rows, width), bf16)] * n_outs
        scratch = [pltpu.VMEM((total, width), bf16)]
        if with_last:
            wider = jax.ShapeDtypeStruct((part_rows, width + extra), bf16)
            out_shape[n_outs - chips :] = [wider] * chips
            out_shape += [
                jax.ShapeDtypeStruct((seqs, width), bf16),
                jax.ShapeDtypeStruct((seqs, 2 * half_width), f32),
                jax.ShapeDtypeStruct((part_rows, extra), f32),
            ]
            scratch = [
                pltpu.VMEM((expert_count, -(-each // 8) * 8, width), f32),
                pltpu.VMEM((part_rows, extra), f32),
                pltpu.VMEM((dp_count, width // lanes, -(-seq_dev // 8) * 8, lanes), f32),
            ] + scratch
        operands = [place] + [tokens] * near + parts + list(weights)
        scratch += [pltpu.VMEM(down.shape, bf16), pltpu.SemaphoreType.DMA(())]
        layout = (tuple(group), chips, part_rows, seq_dev, where_tiles, used, with_last)
        return pl.pallas_call(
            functools.partial(expert_kernel, layout),
            out_shape=out_shape,
            in_specs=[in_smem]
            + [in_vmem] * (len(operands) - 2)
            + [pl.BlockSpec(memory_space=pl.ANY)],
            out_specs=[in_vmem] * len(out_shape),
            scratch_shapes=scratch,
            compiler_params=params(32),
            cost_estimate=cost(2 * total * width * 6 * half_width, 12 << 20),
            name="experts",
        )(*operands)

    outs = {}
    after = place
    rest = list(range(dp_count - 2, 1, -1))
    for group in groups:
        with_last = dp_count - 1 in group
        out = expert(group, after, with_last)
        after, _ = lax.optimization_barrier((place, out[0]))
        for index, hop in enumerate(group):
            outs[hop] = list(out[index * chips : (index + 1) * chips])
        if with_last:
            last_all, last_projected, own_last = out[-3:]
            tables_place = after

    table_rows = dp_count * part_rows + seqs
    chunks = width // lanes
    sublanes = -(-seq_dev // 8) * 8
    kept, sent, partners = pl.pallas_call(
        functools.partial(table_kernel, (seq_dev, tok_dev, where_tiles, len(tiles))),
        out_shape=[
            jax.ShapeDtypeStruct((table_rows, lanes), bf16),
            jax.ShapeDtypeStruct((table_rows, lanes), bf16),
            jax.ShapeDtypeStruct((seqs, lanes), f32),
        ],
        in_specs=[in_smem] + [in_vmem] * len(tiles),
        out_specs=[in_vmem] * 3,
        scratch_shapes=[
            pltpu.VMEM((dp_count, sublanes, lanes), f32),
            pltpu.VMEM((dp_count, sublanes, lanes), f32),
        ],
        compiler_params=params(48 if dp_count > 8 else 12),
        cost_estimate=cost(0, 1 << 20),
        name="tables",
    )(tables_place, *tiles)
    found = to_lane(sent, 1)

    def combine(hop, parts, last_sum):
        with_last = last_sum is None
        out_shape = [jax.ShapeDtypeStruct((part_rows, width), f32)]
        if hop:
            out_shape = [jax.ShapeDtypeStruct((part_rows, width + extra), bf16)]
        if with_last:
            out_shape.append(jax.ShapeDtypeStruct((part_rows, extra), bf16))
        operands = [place, kept, found] + [packed] * (hop == 0)
        operands += [last_sum] * (hop > 0 and not with_last) + parts
        return pl.pallas_call(
            functools.partial(combine_kernel, (hop, chips, with_last, width, each)),
            out_shape=out_shape,
            in_specs=[in_smem] + [in_vmem] * (len(operands) - 1),
            out_specs=[in_vmem] * len(out_shape),
            compiler_params=params(8),
            cost_estimate=cost(0, 2 << 20),
            name="combine",
        )(*operands)

    returned = {}

    def send_back(hop, gated, after):
        first, *parts = outs[hop]
        free = len(parts) - gated
        parts[free:], after = lax.optimization_barrier((parts[free:], after))
        returned[hop] = [first] + [to_lane(value, step) for value, step in zip(parts, chip_steps)]
        return after

    send_back(1, 0, [])
    if dp_count > 2:
        returned[1][1:] = send_back(dp_count - 1, chips - 1, returned[1][1:])
    before = dp_count - 1
    for hop in rest:
        returned[before][1:], found = send_back(hop, 1, (returned[before][1:], found))
        before = hop
    homeward = []
    last_sum = None
    for hop in range(dp_count - 1, 0, -1):
        result = combine(hop, returned[hop], last_sum)
        last_sum = result[1] if last_sum is None else last_sum
        homeward.append(to_plane(result[0], hop))
        if hop == min(3, dp_count - 1):
            gate = result[0]
    outs[0][1:], gate = lax.optimization_barrier((outs[0][1:], gate))
    send_back(0, 0, [])
    near_sum = combine(0, returned[0], last_sum)[0]

    own_out = pl.pallas_call(
        finish_kernel,
        out_shape=jax.ShapeDtypeStruct((part_rows, width + extra), bf16),
        in_specs=[in_vmem] * (2 + dp_count),
        out_specs=in_vmem,
        compiler_params=params(16 if dp_count > 8 else 4),
        cost_estimate=cost(0, 1 << 20),
        name="finish",
    )(near_sum, own_last, last_sum, *homeward)
    pieces = [own_out] + [to_lane(own_out, step) for step in chip_steps]
    pieces += [to_lane(piece, 1) for piece in pieces]

    n_blocks = width // min(512, width)
    layer_out, grad_gate_up, grad_down = pl.pallas_call(
        functools.partial(final_kernel, len(pieces), n_blocks),
        out_shape=[
            jax.ShapeDtypeStruct((tok_dev, width), bf16),
            jax.ShapeDtypeStruct(gate_up.shape, bf16),
            jax.ShapeDtypeStruct(down.shape, bf16),
        ],
        in_specs=[in_vmem] * (len(pieces) + 2) + [in_smem] + [in_vmem] * 4,
        out_specs=[in_hbm] * 3,
        scratch_shapes=[
            pltpu.VMEM((width, 2 * half_width), bf16),
            pltpu.VMEM((half_width, width), bf16),
            pltpu.VMEM((expert_count, -(-each // 8) * 8, width), f32),
            pltpu.SemaphoreType.DMA((len(pieces) + n_blocks + 1,)),
        ],
        compiler_params=params(24),
        cost_estimate=cost(2 * seqs * width * 4 * half_width, 7 << 20),
        name="final",
    )(*pieces, last_all, last_projected, place, kept, found, partners, down)
    return (layer_out, grad_gate_up, grad_down)


def solution(mesh):
    return jax.shard_map(
        body,
        mesh=mesh,
        in_specs=(
            P("dp", None),
            P("dp", "expert"),
            P("dp", "expert"),
            P("dp"),
            P(("dp", "expert"), None, None),
            P(("dp", "expert"), None, None),
        ),
        out_specs=(P("dp", None), P(("dp", "expert"), None, None), P(("dp", "expert"), None, None)),
        check_vma=False,
    )
```

```python
import functools

import jax
import jax.numpy as jnp
from jax import lax
from jax.experimental import pallas as pl
from jax.experimental.pallas import tpu as pltpu
from jax.sharding import PartitionSpec as P

logit_divisor = 0.05
grad_scale = 256.0
epsilon = 1e-06
lanes = 128
tail = 16
bf16 = jnp.bfloat16
f32 = jnp.float32

in_hbm = pl.BlockSpec(memory_space=pltpu.HBM)
in_vmem = pl.BlockSpec(memory_space=pltpu.VMEM)
in_smem = pl.BlockSpec(memory_space=pltpu.SMEM)


def params(mebibytes):
    return pltpu.CompilerParams(vmem_limit_bytes=mebibytes << 20)


def cost(flops, moved):
    return pl.CostEstimate(flops=flops, transcendentals=0, bytes_accessed=moved)


def dot(left, right, dims=((1,), (0,)), precision=None):
    return lax.dot_general(
        left, right, (dims, ((), ())), precision=precision, preferred_element_type=f32
    )


def doublings(count):
    steps = [1 << bit for bit in range((count - 1).bit_length())]
    assert 1 << len(steps) == count
    return steps


def column(table, wanted):
    index = lax.broadcasted_iota(jnp.int32, table.shape, 1)
    return jnp.sum(jnp.where(index == wanted, table, 0.0), axis=1, keepdims=True)


def pack_kernel(
    seq_dev, partners, ids_in, gates_in, tokens, out, tile, rows, ids, gates, positives, sems
):
    part_rows, width = out.shape[0], tokens.shape[1]
    tok_dev = tokens.shape[0]
    seq_length = tok_dev // seq_dev
    share = rows.shape[2]
    lane = lax.axis_index("expert")
    column_at = pl.multiple_of(lane // 2 * share, lanes)
    start = pl.multiple_of(lane * part_rows, part_rows)
    copies = [
        pltpu.make_async_copy(
            tokens.at[pl.ds((seq + 1) * seq_length - tail, tail), pl.ds(column_at, share)],
            rows.at[seq],
            sems.at[seq],
        )
        for seq in range(seq_dev)
    ]
    own = pltpu.make_async_copy(
        tokens.at[pl.ds(start, part_rows)], out.at[:, pl.ds(0, width)], sems.at[seq_dev]
    )
    lines = [
        pltpu.make_async_copy(ids_in, ids, sems.at[seq_dev + 1]),
        pltpu.make_async_copy(gates_in, gates, sems.at[seq_dev + 2]),
        pltpu.make_async_copy(partners, positives, sems.at[seq_dev + 3]),
    ]
    for copy in lines + [own] + copies:
        copy.start()
    note_rows = tok_dev // lanes
    tile[...] = jnp.zeros_like(tile)
    for copy in lines:
        copy.wait()
    for index in range(note_rows):
        block = slice(index * lanes, (index + 1) * lanes)
        tile[index : index + 1, :] = ids[:, block].astype(f32)
        tile[note_rows + index : note_rows + index + 1, :] = gates[:, block]
    for seq in range(seq_dev):
        row = 2 * note_rows + seq
        tile[row : row + 1, :] = jnp.full((1, lanes), positives[seq], jnp.int32).astype(f32)
    base = part_rows - seq_dev * (share // lanes)
    for seq in range(seq_dev):
        copies[seq].wait()
        values = rows[seq].astype(f32)
        for chunk in range(share // lanes):
            row = base + chunk * seq_dev + seq
            tile[row : row + 1, :] = values[tail - 1 : tail, chunk * lanes : (chunk + 1) * lanes]
    out[:, width:] = tile[...].astype(bf16)
    own.wait()


def table_kernel(layout, place, *refs):
    seq_dev, tok_dev, where_tiles, n_parts = layout
    parts = refs[:n_parts]
    kept, sent, partners, routes, marks = refs[n_parts:]
    part_rows = parts[0].shape[0]
    dp_count = len(where_tiles)
    note_rows = tok_dev // lanes
    seq_length = tok_dev // seq_dev
    chips = len(where_tiles[0])
    lane_index = lax.broadcasted_iota(jnp.int32, (part_rows, lanes), 1)
    row_index = lax.broadcasted_iota(jnp.int32, (part_rows, lanes), 0)

    def dense_rows(tile, lane):
        start = lane * part_rows
        picked = lane_index == row_index + start % lanes
        found = []
        for offset in (0, note_rows):
            line = tile[offset : offset + 1, :]
            for index in range(1, note_rows):
                other = tile[offset + index : offset + index + 1, :]
                line = jnp.where(start // lanes == index, other, line)
            found.append(jnp.sum(jnp.where(picked, line, 0.0), axis=1, keepdims=True))
        return jnp.where(lane_index.astype(f32) == found[0], found[1], 0.0)

    for hop in range(dp_count):
        plane = place[0] ^ hop
        sums = [None, None]
        for chip in range(chips):
            source, row, at = where_tiles[hop][chip]
            tile = parts[source][row : row + part_rows, at : at + lanes].astype(f32)
            for index, lane in enumerate((place[1], place[1] ^ 1)):
                value = dense_rows(tile, lane)
                sums[index] = value if chip == 0 else sums[index] + value
            for seq in range(seq_dev):
                at_token = (seq + 1) * seq_length - 1
                row = at_token // lanes
                here = lane_index[:1] == at_token % lanes
                expert, gate = [
                    jnp.sum(
                        jnp.where(here, tile[offset + row : offset + row + 1, :], 0.0),
                        axis=1,
                        keepdims=True,
                    )
                    for offset in (0, note_rows)
                ]
                value = jnp.where(lane_index[:1].astype(f32) == expert, gate, 0.0)
                if chip:
                    value = value + routes[plane, seq : seq + 1, :]
                routes[plane, seq : seq + 1, :] = value
            if chip == 0:
                marks[plane, 0:seq_dev, :] = tile[2 * note_rows : 2 * note_rows + seq_dev, :]
        at = slice(hop * part_rows, (hop + 1) * part_rows)
        kept[at, :] = sums[0].astype(bf16)
        sent[at, :] = sums[1].astype(bf16)
    last = dp_count * part_rows
    shared = []
    for plane in range(dp_count):
        shared.append(routes[plane, 0:seq_dev, :])
        partners[plane * seq_dev : (plane + 1) * seq_dev, :] = marks[plane, 0:seq_dev, :]
    seqs = dp_count * seq_dev
    value = jnp.concatenate(shared, axis=0).astype(bf16)
    kept[last : last + seqs, :] = value
    sent[last : last + seqs, :] = value


def hidden_parts(projected):
    half_width = projected.shape[1] // 2
    gate, up = projected[:, :half_width], projected[:, half_width:]
    sigmoid_gate = jax.nn.sigmoid(gate)
    return gate, up, sigmoid_gate, gate * sigmoid_gate


def spread_rows(values, rows, blocks):
    chunks = values.shape[1] // lanes
    for index in range(values.shape[0] * chunks):
        row, chunk = index // chunks, index % chunks
        spot = slice(index % rows, index % rows + 1)
        block = slice(index // rows * lanes, (index // rows + 1) * lanes)
        blocks[spot, block] = values[row : row + 1, chunk * lanes : (chunk + 1) * lanes]


def last_tokens(place, seq_dev, where_tiles, parts, tokens):
    part_rows = parts[0].shape[0]
    dp_count, chunks = tokens.shape[:2]
    chips = len(where_tiles[0])
    share_chunks = chunks // chips
    base = part_rows - seq_dev * share_chunks
    for hop in range(dp_count):
        for chip in range(chips):
            source, row, at = where_tiles[hop][chip]
            tile = parts[source][row : row + part_rows, at : at + lanes].astype(f32)
            first = ((place[1] // 2) ^ chip) * share_chunks
            for chunk in range(share_chunks):
                row = base + chunk * seq_dev
                tokens[place[0] ^ hop, first + chunk, 0:seq_dev, :] = tile[row : row + seq_dev, :]
    joined = []
    for plane in range(dp_count):
        lines = [tokens[plane, chunk, 0:seq_dev, :] for chunk in range(chunks)]
        joined.append(jnp.concatenate(lines, axis=1))
    return jnp.concatenate(joined, axis=0)


def expert_kernel(layout, *refs):
    group, chips, part_rows, seq_dev, where_tiles, used, with_last = layout
    refs = list(refs)
    place = refs.pop(0)
    near = 0 in group
    tokens = refs.pop(0) if near else None
    parts, refs = dict(zip(used, refs)), refs[len(used) :]
    weights, refs = refs[:4], refs[4:]
    n_outs = chips * len(group)
    outs, refs = refs[:n_outs], refs[n_outs:]
    if with_last:
        last_all, last_projected, own_last, by_lane, tile, seq_tokens, *refs = refs
    (rows,) = refs
    width = weights[0].shape[1]
    total = n_outs * part_rows
    spots = [slice(index * part_rows, (index + 1) * part_rows) for index in range(n_outs)]
    for index, spot in enumerate(spots):
        hop, chip = group[index // chips], index % chips
        if hop:
            source, row, _ = where_tiles[hop][chip]
            rows[spot, :] = parts[source][row : row + part_rows, :width]
        else:
            start = pl.multiple_of((place[1] ^ (2 * chip)) * part_rows, part_rows)
            rows[spot, :] = tokens[pl.ds(start, part_rows), :]
    if with_last:
        floats = last_tokens(place, seq_dev, where_tiles, parts, seq_tokens)
        last_all[...] = floats.astype(bf16)
        rows[total:, :] = floats.astype(bf16)
    hidden = []
    for half in range(2):
        projected = dot(rows[...], weights[2 * half][0])
        if half == 0 and with_last:
            last_projected[...] = projected[total:]
        _, up, _, activated = hidden_parts(projected)
        hidden.append((activated * up).astype(bf16))
    block = min(512, width)
    if with_last:
        each = floats.shape[0] // by_lane.shape[0]
    for first in range(0, width, block):
        columns = slice(first, first + block)
        result = dot(hidden[0], weights[1][0, :, columns]) + dot(
            hidden[1], weights[3][0, :, columns]
        )
        for out, spot in zip(outs, spots):
            out[:, columns] = result[spot].astype(bf16)
        if with_last:
            for lane in range(by_lane.shape[0]):
                at = total + lane * each
                by_lane[lane, 0:each, columns] = result[at : at + each]
    if with_last:
        for chip in range(chips):
            spread_rows(by_lane[place[1] ^ (2 * chip), 0:each, :], part_rows, tile)
            outs[n_outs - chips + chip][:, width:] = tile[...].astype(bf16)
        for lane in range(by_lane.shape[0]):
            by_lane[lane, 0:each, :] = floats[lane * each : (lane + 1) * each]
        spread_rows(by_lane[place[1], 0:each, :], part_rows, tile)
        own_last[...] = tile[...]


def combine_kernel(layout, place, kept, found, *refs):
    hop, chips, with_last, width, each = layout
    own, refs = (refs[0], refs[1:]) if hop == 0 else (None, refs)
    last_in, refs = (refs[0], refs[1:]) if hop and not with_last else (None, refs)
    parts, out = refs[:chips], refs[chips]
    part_rows = out.shape[0]
    first_expert = place[2] - place[1] // 2
    experts = [first_expert + ((place[1] // 2) ^ chip) for chip in range(chips)]
    if with_last:
        last_in = refs[-1]
        table = kept[-2 * chips * each :, :].astype(f32) + found[-2 * chips * each :, :].astype(f32)
        row_index = lax.broadcasted_iota(jnp.int32, table.shape, 0)
        chunks = width // lanes
        for row in range(each):
            mine = jnp.where(row_index == place[1] * each + row, table, 0.0)
            mine = jnp.sum(mine, axis=0, keepdims=True)
            first = row * chunks % part_rows
            spot = slice(first, first + chunks)
            at = row * chunks // part_rows * lanes
            total = None
            for chip in range(chips):
                values = parts[chip][spot, width + at : width + at + lanes].astype(f32)
                term = column(mine, experts[chip]) * values
                total = term if total is None else total + term
            last_in[spot, at : at + lanes] = total.astype(bf16)
    at = slice(hop * part_rows, (hop + 1) * part_rows)
    table = kept[at, :].astype(f32) + found[at, :].astype(f32)
    total = None if hop else own[:, :width].astype(f32)
    for chip in range(chips):
        term = column(table, experts[chip]) * parts[chip][:, :width].astype(f32)
        total = term if total is None else total + term
    out[:, :width] = total.astype(out.dtype)
    if hop:
        out[:, width:] = last_in[...]


def finish_kernel(near, own_last, last_sum, *refs):
    parts, out = refs[:-1], refs[-1]
    width = near.shape[1]
    total = near[...]
    last = last_sum[...].astype(f32)
    for part in parts:
        total = total + part[:, :width].astype(f32)
        last = last + part[:, width:].astype(f32)
    out[:, :width] = total.astype(bf16)
    out[:, width:] = (own_last[...] + last).astype(bf16)


def collect_rows(lane, pieces, by_lane, width):
    part_rows, chunks = pieces[0].shape[0], width // lanes
    count = len(pieces)
    each = (pieces[0].shape[1] - width) * part_rows // width
    for index in range(count):
        source = lane ^ (2 * (index % (count // 2))) ^ (index // (count // 2))
        values = pieces[index][:, width:].astype(f32)
        for spot in range(each * chunks):
            row, chunk = spot // chunks, spot % chunks
            at = spot // part_rows * lanes
            from_row = spot % part_rows
            by_lane[source, row : row + 1, chunk * lanes : (chunk + 1) * lanes] = values[
                from_row : from_row + 1, at : at + lanes
            ]
    return jnp.concatenate([by_lane[index, 0:each, :] for index in range(count)], axis=0)


def both_ways(coefficient, unit, diagonal):
    count = unit.shape[0]
    if count > 32:
        high = lax.Precision.HIGHEST
        there = dot(coefficient, unit, ((1,), (0,)), high)
        return there + dot(coefficient, unit, ((0,), (0,)), high)
    total = None
    for index in range(count):
        line = jnp.where(diagonal, coefficient[index : index + 1, :], 0.0)
        factor = coefficient[:, index : index + 1] + jnp.sum(line, axis=1, keepdims=True)
        term = factor * unit[index : index + 1, :]
        total = term if total is None else total + term
    return total


def final_kernel(n_pieces, n_blocks, *refs):
    pieces, refs = refs[:n_pieces], refs[n_pieces:]
    last_all, projected, place, kept, found, partners, down, *refs = refs
    layer_out, grad_in, grad_out, made_in, made_out, by_lane, sems = refs
    part_rows, width = pieces[0].shape[0], layer_out.shape[1]
    copies = []

    def send(source, target):
        copies.append(pltpu.make_async_copy(source, target, sems.at[len(copies)]))
        copies[-1].start()

    for index in range(n_pieces):
        lane = place[1] ^ (2 * (index % (n_pieces // 2))) ^ (index // (n_pieces // 2))
        start = pl.multiple_of(lane * part_rows, part_rows)
        send(pieces[index].at[:, pl.ds(0, width)], layer_out.at[pl.ds(start, part_rows)])
    values = collect_rows(place[1], pieces, by_lane, width)
    count = values.shape[0]
    last = kept.shape[0] - count
    table = kept[last:, :].astype(f32) + found[last:, :].astype(f32)
    row = lax.broadcasted_iota(jnp.int32, (count, count), 0)
    col = lax.broadcasted_iota(jnp.int32, (count, count), 1)
    norms = jnp.sqrt(jnp.sum(values * values, axis=1, keepdims=True) + epsilon)
    norms_line = jnp.sum(jnp.where(row == col, norms, 0.0), axis=0, keepdims=True)
    unit = values / norms
    rows = values.astype(bf16)
    scores = dot(rows, rows, ((1,), (1,))) / (norms * norms_line) / logit_divisor
    exp_scores = jnp.where(row != col, jnp.exp(scores), 0.0)
    probabilities = exp_scores / jnp.sum(exp_scores, axis=1, keepdims=True)
    partner = partners[:, :1].astype(jnp.int32)
    coefficient = grad_scale * (probabilities - jnp.where(col == partner, 1.0, 0.0))
    grad_unit = both_ways(coefficient, unit, row == col) / logit_divisor
    projection = jnp.sum(unit * grad_unit, axis=1, keepdims=True)
    grad_last = (grad_unit - unit * projection) / norms
    route_grad = (column(table, place[2]) * grad_last).astype(bf16)
    gate, up, sigmoid_gate, activated = hidden_parts(projected[...])
    hidden = (activated * up).astype(bf16)
    grad_hidden = dot(route_grad, down[0], ((1,), (1,)))
    gate_slope = sigmoid_gate * (1.0 + gate * (1.0 - sigmoid_gate))
    slope = jnp.concatenate([grad_hidden * up * gate_slope, grad_hidden * activated], axis=1)
    slope = slope.astype(bf16)
    block = width // n_blocks
    for index in range(n_blocks):
        spot = slice(index * block, (index + 1) * block)
        made_in[spot, :] = dot(last_all[:, spot], slope, ((0,), (0,))).astype(bf16)
        send(made_in.at[spot], grad_in.at[0, spot])
    made_out[...] = dot(hidden, route_grad, ((0,), (0,))).astype(bf16)
    send(made_out, grad_out.at[0])
    for copy in copies:
        copy.wait()


def body(tokens, expert_ids, gates, positives, gate_up, down):
    dp_count = lax.axis_size("dp")
    expert_count = lax.axis_size("expert")
    chips = expert_count // 2
    experts = dp_count * chips
    tok_dev, width = tokens.shape
    half_width = down.shape[1]
    seq_dev = positives.shape[0]
    seqs = dp_count * seq_dev
    seq_length = tok_dev // seq_dev
    part_rows = tok_dev // expert_count
    plane = lax.axis_index("dp")
    lane = lax.axis_index("expert")
    place = jnp.stack([plane, lane, plane * chips + lane // 2]).astype(jnp.int32)
    assert experts <= lanes and seq_length % tail == 0

    def to_lane(value, step):
        return lax.ppermute(value, "expert", [(j, j ^ step) for j in range(expert_count)])

    def to_plane(value, step):
        return lax.ppermute(value, "dp", [(p, p ^ step) for p in range(dp_count)])

    chip_steps = [2 * step for step in range(1, chips)]
    groups = [range(first, min(first + 2, dp_count)) for first in range(0, dp_count, 2)]

    share = width // chips
    packed = pl.pallas_call(
        functools.partial(pack_kernel, seq_dev),
        out_shape=jax.ShapeDtypeStruct((part_rows, width + lanes), bf16),
        in_specs=[in_hbm] * 4,
        out_specs=in_vmem,
        scratch_shapes=[
            pltpu.VMEM((part_rows, lanes), f32),
            pltpu.VMEM((seq_dev, tail, share), bf16),
            pltpu.VMEM((1, tok_dev), jnp.int32),
            pltpu.VMEM((1, tok_dev), f32),
            pltpu.SMEM((seq_dev,), jnp.int32),
            pltpu.SemaphoreType.DMA((seq_dev + 4,)),
        ],
        cost_estimate=cost(0, 1 << 19),
        name="pack",
    )(positives, expert_ids.T, gates.T, tokens)
    arrivals = {hop: to_plane(packed, hop) for hop in range(1, dp_count)}
    mate_in = to_lane(gate_up, 1)
    mate_out = to_lane(down, 1)
    weights = (gate_up, down, mate_in, mate_out)

    tiles = [packed]
    spots = {}
    received = None
    for group in groups:
        own = [arrivals[hop] for hop in group if hop]
        if group[0] == 0:
            joined = jnp.concatenate(own + [packed[:, width:]], axis=1)
            joined, weights = lax.optimization_barrier((joined, weights))
        else:
            joined = jnp.concatenate(own, axis=0)
            joined, received = lax.optimization_barrier((joined, received))
            tiles[-len(received) :] = received
        first = len(tiles)
        received = [to_lane(joined, step) for step in chip_steps]
        tiles += own + received
        for index, hop in enumerate(group):
            if group[0] == 0:
                place_of = (first, 0, width) if hop else (0, 0, width)
                row, at = 0, width if hop else width + lanes
            else:
                place_of = (first + index, 0, width)
                row, at = index * part_rows, width
            spots[hop] = [place_of] + [
                (first + len(own) + chip, row, at) for chip in range(chips - 1)
            ]
    where_tiles = [spots[hop] for hop in range(dp_count)]

    each = seqs // expert_count
    extra = each * width // part_rows
    assert extra % lanes == 0 and part_rows % (width // lanes) == 0

    def expert(group, place, with_last):
        near = 0 in group
        wanted = range(dp_count) if with_last else [hop for hop in group if hop]
        used = sorted({spot[0] for hop in wanted for spot in where_tiles[hop]})
        parts = [tiles[index] for index in used]
        n_outs = chips * len(group)
        total = n_outs * part_rows + (seqs if with_last else 0)
        out_shape = [jax.ShapeDtypeStruct((part_rows, width), bf16)] * n_outs
        scratch = [pltpu.VMEM((total, width), bf16)]
        if with_last:
            wider = jax.ShapeDtypeStruct((part_rows, width + extra), bf16)
            out_shape[n_outs - chips :] = [wider] * chips
            out_shape += [
                jax.ShapeDtypeStruct((seqs, width), bf16),
                jax.ShapeDtypeStruct((seqs, 2 * half_width), f32),
                jax.ShapeDtypeStruct((part_rows, extra), f32),
            ]
            scratch = [
                pltpu.VMEM((expert_count, -(-each // 8) * 8, width), f32),
                pltpu.VMEM((part_rows, extra), f32),
                pltpu.VMEM((dp_count, width // lanes, -(-seq_dev // 8) * 8, lanes), f32),
            ] + scratch
        operands = [place] + [tokens] * near + parts + list(weights)
        layout = (tuple(group), chips, part_rows, seq_dev, where_tiles, used, with_last)
        return pl.pallas_call(
            functools.partial(expert_kernel, layout),
            out_shape=out_shape,
            in_specs=[in_smem] + [in_vmem] * (len(operands) - 1),
            out_specs=[in_vmem] * len(out_shape),
            scratch_shapes=scratch,
            compiler_params=params(32),
            cost_estimate=cost(2 * total * width * 6 * half_width, 12 << 20),
            name="experts",
        )(*operands)

    outs = {}
    after = place
    rest = list(range(dp_count - 2, 1, -1))
    for group in groups:
        with_last = dp_count - 1 in group
        out = expert(group, after, with_last)
        after, _ = lax.optimization_barrier((place, out[0]))
        for index, hop in enumerate(group):
            outs[hop] = list(out[index * chips : (index + 1) * chips])
        if with_last:
            last_all, last_projected, own_last = out[-3:]
            tables_place = after

    table_rows = dp_count * part_rows + seqs
    chunks = width // lanes
    sublanes = -(-seq_dev // 8) * 8
    kept, sent, partners = pl.pallas_call(
        functools.partial(table_kernel, (seq_dev, tok_dev, where_tiles, len(tiles))),
        out_shape=[
            jax.ShapeDtypeStruct((table_rows, lanes), bf16),
            jax.ShapeDtypeStruct((table_rows, lanes), bf16),
            jax.ShapeDtypeStruct((seqs, lanes), f32),
        ],
        in_specs=[in_smem] + [in_vmem] * len(tiles),
        out_specs=[in_vmem] * 3,
        scratch_shapes=[
            pltpu.VMEM((dp_count, sublanes, lanes), f32),
            pltpu.VMEM((dp_count, sublanes, lanes), f32),
        ],
        compiler_params=params(48 if dp_count > 8 else 12),
        cost_estimate=cost(0, 1 << 20),
        name="tables",
    )(tables_place, *tiles)
    found = to_lane(sent, 1)

    def combine(hop, parts, last_sum):
        with_last = last_sum is None
        out_shape = [jax.ShapeDtypeStruct((part_rows, width), f32)]
        if hop:
            out_shape = [jax.ShapeDtypeStruct((part_rows, width + extra), bf16)]
        if with_last:
            out_shape.append(jax.ShapeDtypeStruct((part_rows, extra), bf16))
        operands = [place, kept, found] + [packed] * (hop == 0)
        operands += [last_sum] * (hop > 0 and not with_last) + parts
        return pl.pallas_call(
            functools.partial(combine_kernel, (hop, chips, with_last, width, each)),
            out_shape=out_shape,
            in_specs=[in_smem] + [in_vmem] * (len(operands) - 1),
            out_specs=[in_vmem] * len(out_shape),
            compiler_params=params(8),
            cost_estimate=cost(0, 2 << 20),
            name="combine",
        )(*operands)

    returned = {}

    def send_back(hop, gated, after):
        first, *parts = outs[hop]
        free = len(parts) - gated
        parts[free:], after = lax.optimization_barrier((parts[free:], after))
        returned[hop] = [first] + [to_lane(value, step) for value, step in zip(parts, chip_steps)]
        return after

    send_back(1, 0, [])
    if dp_count > 2:
        returned[1][1:-1] = send_back(dp_count - 1, chips - 1, returned[1][1:-1])
    before = dp_count - 1
    for hop in rest:
        returned[before][1:], found = send_back(hop, 1, (returned[before][1:], found))
        before = hop
    homeward = []
    last_sum = None
    for hop in range(dp_count - 1, 0, -1):
        result = combine(hop, returned[hop], last_sum)
        last_sum = result[1] if last_sum is None else last_sum
        homeward.append(to_plane(result[0], hop))
        if hop == min(3, dp_count - 1):
            gate = result[0]
    outs[0][1:], gate = lax.optimization_barrier((outs[0][1:], gate))
    send_back(0, 0, [])
    near_sum = combine(0, returned[0], last_sum)[0]

    own_out = pl.pallas_call(
        finish_kernel,
        out_shape=jax.ShapeDtypeStruct((part_rows, width + extra), bf16),
        in_specs=[in_vmem] * (2 + dp_count),
        out_specs=in_vmem,
        compiler_params=params(16 if dp_count > 8 else 4),
        cost_estimate=cost(0, 1 << 20),
        name="finish",
    )(near_sum, own_last, last_sum, *homeward)
    pieces = [own_out] + [to_lane(own_out, step) for step in chip_steps]
    pieces += [to_lane(piece, 1) for piece in pieces]

    n_blocks = width // min(512, width)
    layer_out, grad_gate_up, grad_down = pl.pallas_call(
        functools.partial(final_kernel, len(pieces), n_blocks),
        out_shape=[
            jax.ShapeDtypeStruct((tok_dev, width), bf16),
            jax.ShapeDtypeStruct(gate_up.shape, bf16),
            jax.ShapeDtypeStruct(down.shape, bf16),
        ],
        in_specs=[in_vmem] * (len(pieces) + 2) + [in_smem] + [in_vmem] * 4,
        out_specs=[in_hbm] * 3,
        scratch_shapes=[
            pltpu.VMEM((width, 2 * half_width), bf16),
            pltpu.VMEM((half_width, width), bf16),
            pltpu.VMEM((expert_count, -(-each // 8) * 8, width), f32),
            pltpu.SemaphoreType.DMA((len(pieces) + n_blocks + 1,)),
        ],
        compiler_params=params(24),
        cost_estimate=cost(2 * seqs * width * 4 * half_width, 7 << 20),
        name="final",
    )(*pieces, last_all, last_projected, place, kept, found, partners, down)
    return (layer_out, grad_gate_up, grad_down)


def solution(mesh):
    return jax.shard_map(
        body,
        mesh=mesh,
        in_specs=(
            P("dp", None),
            P("dp", "expert"),
            P("dp", "expert"),
            P("dp"),
            P(("dp", "expert"), None, None),
            P(("dp", "expert"), None, None),
        ),
        out_specs=(P("dp", None), P(("dp", "expert"), None, None), P(("dp", "expert"), None, None)),
        check_vma=False,
    )
```

```python
import functools

import jax
import jax.numpy as jnp
from jax import lax
from jax.experimental import pallas as pl
from jax.experimental.pallas import tpu as pltpu
from jax.sharding import PartitionSpec as P

logit_divisor = 0.05
grad_scale = 256.0
epsilon = 1e-06
lanes = 128
tail = 16
bf16 = jnp.bfloat16
f32 = jnp.float32

in_hbm = pl.BlockSpec(memory_space=pltpu.HBM)
in_vmem = pl.BlockSpec(memory_space=pltpu.VMEM)
in_smem = pl.BlockSpec(memory_space=pltpu.SMEM)


def params(mebibytes):
    return pltpu.CompilerParams(vmem_limit_bytes=mebibytes << 20)


def cost(flops, moved):
    return pl.CostEstimate(flops=flops, transcendentals=0, bytes_accessed=moved)


def dot(left, right, dims=((1,), (0,)), precision=None):
    return lax.dot_general(
        left, right, (dims, ((), ())), precision=precision, preferred_element_type=f32
    )


def doublings(count):
    steps = [1 << bit for bit in range((count - 1).bit_length())]
    assert 1 << len(steps) == count
    return steps


def column(table, wanted):
    index = lax.broadcasted_iota(jnp.int32, table.shape, 1)
    return jnp.sum(jnp.where(index == wanted, table, 0.0), axis=1, keepdims=True)


def pack_kernel(
    seq_dev, partners, ids_in, gates_in, tokens, out, tile, rows, ids, gates, positives, sems
):
    part_rows, width = out.shape[0], tokens.shape[1]
    tok_dev = tokens.shape[0]
    seq_length = tok_dev // seq_dev
    share = rows.shape[2]
    lane = lax.axis_index("expert")
    column_at = pl.multiple_of(lane // 2 * share, lanes)
    start = pl.multiple_of(lane * part_rows, part_rows)
    copies = [
        pltpu.make_async_copy(
            tokens.at[pl.ds((seq + 1) * seq_length - tail, tail), pl.ds(column_at, share)],
            rows.at[seq],
            sems.at[seq],
        )
        for seq in range(seq_dev)
    ]
    own = pltpu.make_async_copy(
        tokens.at[pl.ds(start, part_rows)], out.at[:, pl.ds(0, width)], sems.at[seq_dev]
    )
    lines = [
        pltpu.make_async_copy(ids_in, ids, sems.at[seq_dev + 1]),
        pltpu.make_async_copy(gates_in, gates, sems.at[seq_dev + 2]),
        pltpu.make_async_copy(partners, positives, sems.at[seq_dev + 3]),
    ]
    for copy in lines + [own] + copies:
        copy.start()
    note_rows = tok_dev // lanes
    tile[...] = jnp.zeros_like(tile)
    for copy in lines:
        copy.wait()
    for index in range(note_rows):
        block = slice(index * lanes, (index + 1) * lanes)
        tile[index : index + 1, :] = ids[:, block].astype(f32)
        tile[note_rows + index : note_rows + index + 1, :] = gates[:, block]
    for seq in range(seq_dev):
        row = 2 * note_rows + seq
        tile[row : row + 1, :] = jnp.full((1, lanes), positives[seq], jnp.int32).astype(f32)
    base = part_rows - seq_dev * (share // lanes)
    for seq in range(seq_dev):
        copies[seq].wait()
        values = rows[seq].astype(f32)
        for chunk in range(share // lanes):
            row = base + chunk * seq_dev + seq
            tile[row : row + 1, :] = values[tail - 1 : tail, chunk * lanes : (chunk + 1) * lanes]
    out[:, width:] = tile[...].astype(bf16)
    own.wait()


def table_kernel(layout, place, *refs):
    seq_dev, tok_dev, where_tiles, n_parts = layout
    parts = refs[:n_parts]
    kept, sent, partners, routes, marks = refs[n_parts:]
    part_rows = parts[0].shape[0]
    dp_count = len(where_tiles)
    note_rows = tok_dev // lanes
    seq_length = tok_dev // seq_dev
    chips = len(where_tiles[0])
    lane_index = lax.broadcasted_iota(jnp.int32, (part_rows, lanes), 1)
    row_index = lax.broadcasted_iota(jnp.int32, (part_rows, lanes), 0)

    def dense_rows(tile, lane):
        start = lane * part_rows
        picked = lane_index == row_index + start % lanes
        found = []
        for offset in (0, note_rows):
            line = tile[offset : offset + 1, :]
            for index in range(1, note_rows):
                other = tile[offset + index : offset + index + 1, :]
                line = jnp.where(start // lanes == index, other, line)
            found.append(jnp.sum(jnp.where(picked, line, 0.0), axis=1, keepdims=True))
        return jnp.where(lane_index.astype(f32) == found[0], found[1], 0.0)

    for hop in range(dp_count):
        plane = place[0] ^ hop
        sums = [None, None]
        for chip in range(chips):
            source, row, at = where_tiles[hop][chip]
            tile = parts[source][row : row + part_rows, at : at + lanes].astype(f32)
            for index, lane in enumerate((place[1], place[1] ^ 1)):
                value = dense_rows(tile, lane)
                sums[index] = value if chip == 0 else sums[index] + value
            for seq in range(seq_dev):
                at_token = (seq + 1) * seq_length - 1
                row = at_token // lanes
                here = lane_index[:1] == at_token % lanes
                expert, gate = [
                    jnp.sum(
                        jnp.where(here, tile[offset + row : offset + row + 1, :], 0.0),
                        axis=1,
                        keepdims=True,
                    )
                    for offset in (0, note_rows)
                ]
                value = jnp.where(lane_index[:1].astype(f32) == expert, gate, 0.0)
                if chip:
                    value = value + routes[plane, seq : seq + 1, :]
                routes[plane, seq : seq + 1, :] = value
            if chip == 0:
                marks[plane, 0:seq_dev, :] = tile[2 * note_rows : 2 * note_rows + seq_dev, :]
        at = slice(hop * part_rows, (hop + 1) * part_rows)
        kept[at, :] = sums[0].astype(bf16)
        sent[at, :] = sums[1].astype(bf16)
    last = dp_count * part_rows
    shared = []
    for plane in range(dp_count):
        shared.append(routes[plane, 0:seq_dev, :])
        partners[plane * seq_dev : (plane + 1) * seq_dev, :] = marks[plane, 0:seq_dev, :]
    seqs = dp_count * seq_dev
    value = jnp.concatenate(shared, axis=0).astype(bf16)
    kept[last : last + seqs, :] = value
    sent[last : last + seqs, :] = value


def hidden_parts(projected):
    half_width = projected.shape[1] // 2
    gate, up = projected[:, :half_width], projected[:, half_width:]
    sigmoid_gate = jax.nn.sigmoid(gate)
    return gate, up, sigmoid_gate, gate * sigmoid_gate


def spread_rows(values, flat):
    count, chunks = values.shape[0], values.shape[1] // lanes
    for chunk in range(chunks):
        flat[pl.ds(chunk, count, stride=chunks), :] = values[:, chunk * lanes : (chunk + 1) * lanes]


def share_of(flat, lane, each, part_rows, chunks):
    size = each * chunks
    start = lane * size
    blocks = [
        flat[pl.ds(pl.multiple_of(start + first, part_rows), part_rows), :]
        for first in range(0, size, part_rows)
    ]
    return blocks[0] if len(blocks) == 1 else jnp.concatenate(blocks, axis=1)


def last_tokens(place, seq_dev, where_tiles, parts, tokens):
    part_rows = parts[0].shape[0]
    dp_count, chunks = tokens.shape[:2]
    chips = len(where_tiles[0])
    share_chunks = chunks // chips
    base = part_rows - seq_dev * share_chunks
    for hop in range(dp_count):
        for chip in range(chips):
            source, row, at = where_tiles[hop][chip]
            tile = parts[source][row : row + part_rows, at : at + lanes].astype(f32)
            first = ((place[1] // 2) ^ chip) * share_chunks
            for chunk in range(share_chunks):
                row = base + chunk * seq_dev
                tokens[place[0] ^ hop, first + chunk, 0:seq_dev, :] = tile[row : row + seq_dev, :]
    joined = []
    for plane in range(dp_count):
        lines = [tokens[plane, chunk, 0:seq_dev, :] for chunk in range(chunks)]
        joined.append(jnp.concatenate(lines, axis=1))
    return jnp.concatenate(joined, axis=0)


def expert_kernel(layout, *refs):
    group, chips, part_rows, seq_dev, where_tiles, used, with_last = layout
    refs = list(refs)
    place = refs.pop(0)
    near = 0 in group
    tokens = refs.pop(0) if near else None
    parts, refs = dict(zip(used, refs)), refs[len(used) :]
    weights, refs = refs[:4], refs[4:]
    n_outs = chips * len(group)
    outs, refs = refs[:n_outs], refs[n_outs:]
    if with_last:
        last_all, last_projected, own_last, flat, seq_tokens, *refs = refs
    (rows,) = refs
    width = weights[0].shape[1]
    total = n_outs * part_rows
    spots = [slice(index * part_rows, (index + 1) * part_rows) for index in range(n_outs)]
    for index, spot in enumerate(spots):
        hop, chip = group[index // chips], index % chips
        if hop:
            source, row, _ = where_tiles[hop][chip]
            rows[spot, :] = parts[source][row : row + part_rows, :width]
        else:
            start = pl.multiple_of((place[1] ^ (2 * chip)) * part_rows, part_rows)
            rows[spot, :] = tokens[pl.ds(start, part_rows), :]
    if with_last:
        floats = last_tokens(place, seq_dev, where_tiles, parts, seq_tokens)
        last_all[...] = floats.astype(bf16)
        rows[total:, :] = floats.astype(bf16)
    hidden = []
    for half in range(2):
        projected = dot(rows[...], weights[2 * half][0])
        if half == 0 and with_last:
            last_projected[...] = projected[total:]
        _, up, _, activated = hidden_parts(projected)
        hidden.append((activated * up).astype(bf16))
    block = min(512, width)
    chunks = width // lanes
    for first in range(0, width, block):
        columns = slice(first, first + block)
        result = dot(hidden[0], weights[1][0, :, columns]) + dot(
            hidden[1], weights[3][0, :, columns]
        )
        for out, spot in zip(outs, spots):
            out[:, columns] = result[spot].astype(bf16)
        if with_last:
            count = result.shape[0] - total
            for at in range(0, block, lanes):
                flat[pl.ds((first + at) // lanes, count, stride=chunks), :] = result[
                    total:, at : at + lanes
                ]
    if with_last:
        each = floats.shape[0] // (2 * chips)
        for chip in range(chips):
            share = share_of(flat, place[1] ^ (2 * chip), each, part_rows, chunks)
            outs[n_outs - chips + chip][:, width:] = share.astype(bf16)
        spread_rows(floats, flat)
        own_last[...] = share_of(flat, place[1], each, part_rows, chunks)


def combine_kernel(layout, place, kept, found, *refs):
    hop, chips, with_last, width, each = layout
    own, refs = (refs[0], refs[1:]) if hop == 0 else (None, refs)
    last_in, refs = (refs[0], refs[1:]) if hop and not with_last else (None, refs)
    parts, out = refs[:chips], refs[chips]
    part_rows = out.shape[0]
    first_expert = place[2] - place[1] // 2
    experts = [first_expert + ((place[1] // 2) ^ chip) for chip in range(chips)]
    if with_last:
        last_in = refs[-1]
        table = kept[-2 * chips * each :, :].astype(f32) + found[-2 * chips * each :, :].astype(f32)
        row_index = lax.broadcasted_iota(jnp.int32, table.shape, 0)
        chunks = width // lanes
        for row in range(each):
            mine = jnp.where(row_index == place[1] * each + row, table, 0.0)
            mine = jnp.sum(mine, axis=0, keepdims=True)
            first = row * chunks % part_rows
            spot = slice(first, first + chunks)
            at = row * chunks // part_rows * lanes
            total = None
            for chip in range(chips):
                values = parts[chip][spot, width + at : width + at + lanes].astype(f32)
                term = column(mine, experts[chip]) * values
                total = term if total is None else total + term
            last_in[spot, at : at + lanes] = total.astype(bf16)
    at = slice(hop * part_rows, (hop + 1) * part_rows)
    table = kept[at, :].astype(f32) + found[at, :].astype(f32)
    total = None if hop else own[:, :width].astype(f32)
    for chip in range(chips):
        term = column(table, experts[chip]) * parts[chip][:, :width].astype(f32)
        total = term if total is None else total + term
    out[:, :width] = total.astype(out.dtype)
    if hop:
        out[:, width:] = last_in[...]


def finish_kernel(near, own_last, last_sum, *refs):
    parts, out = refs[:-1], refs[-1]
    width = near.shape[1]
    total = near[...]
    last = last_sum[...].astype(f32)
    for part in parts:
        total = total + part[:, :width].astype(f32)
        last = last + part[:, width:].astype(f32)
    out[:, :width] = total.astype(bf16)
    out[:, width:] = (own_last[...] + last).astype(bf16)


def collect_rows(lane, pieces, flat, width):
    part_rows, chunks = pieces[0].shape[0], width // lanes
    count = len(pieces)
    size = flat.shape[0] // count
    for index in range(count):
        source = lane ^ (2 * (index % (count // 2))) ^ (index // (count // 2))
        for first in range(0, size, part_rows):
            at = width + first // part_rows * lanes
            start = pl.multiple_of(source * size + first, part_rows)
            flat[pl.ds(start, part_rows), :] = pieces[index][:, at : at + lanes].astype(f32)
    rows = flat.shape[0] // chunks
    columns = [flat[pl.ds(chunk, rows, stride=chunks), :] for chunk in range(chunks)]
    return jnp.concatenate(columns, axis=1)


def both_ways(coefficient, unit, diagonal):
    count = unit.shape[0]
    if count > 32:
        high = lax.Precision.HIGHEST
        there = dot(coefficient, unit, ((1,), (0,)), high)
        return there + dot(coefficient, unit, ((0,), (0,)), high)
    total = None
    for index in range(count):
        line = jnp.where(diagonal, coefficient[index : index + 1, :], 0.0)
        factor = coefficient[:, index : index + 1] + jnp.sum(line, axis=1, keepdims=True)
        term = factor * unit[index : index + 1, :]
        total = term if total is None else total + term
    return total


def final_kernel(n_pieces, n_blocks, *refs):
    pieces, refs = refs[:n_pieces], refs[n_pieces:]
    last_all, projected, place, kept, found, partners, down, *refs = refs
    layer_out, grad_in, grad_out, made_in, made_out, flat, sems = refs
    part_rows, width = pieces[0].shape[0], layer_out.shape[1]
    copies = []

    def send(source, target):
        copies.append(pltpu.make_async_copy(source, target, sems.at[len(copies)]))
        copies[-1].start()

    for index in range(n_pieces):
        lane = place[1] ^ (2 * (index % (n_pieces // 2))) ^ (index // (n_pieces // 2))
        start = pl.multiple_of(lane * part_rows, part_rows)
        send(pieces[index].at[:, pl.ds(0, width)], layer_out.at[pl.ds(start, part_rows)])
    values = collect_rows(place[1], pieces, flat, width)
    count = values.shape[0]
    last = kept.shape[0] - count
    table = kept[last:, :].astype(f32) + found[last:, :].astype(f32)
    row = lax.broadcasted_iota(jnp.int32, (count, count), 0)
    col = lax.broadcasted_iota(jnp.int32, (count, count), 1)
    norms = jnp.sqrt(jnp.sum(values * values, axis=1, keepdims=True) + epsilon)
    norms_line = jnp.sum(jnp.where(row == col, norms, 0.0), axis=0, keepdims=True)
    unit = values / norms
    rows = values.astype(bf16)
    scores = dot(rows, rows, ((1,), (1,))) / (norms * norms_line) / logit_divisor
    exp_scores = jnp.where(row != col, jnp.exp(scores), 0.0)
    probabilities = exp_scores / jnp.sum(exp_scores, axis=1, keepdims=True)
    partner = partners[:, :1].astype(jnp.int32)
    coefficient = grad_scale * (probabilities - jnp.where(col == partner, 1.0, 0.0))
    grad_unit = both_ways(coefficient, unit, row == col) / logit_divisor
    projection = jnp.sum(unit * grad_unit, axis=1, keepdims=True)
    grad_last = (grad_unit - unit * projection) / norms
    route_grad = (column(table, place[2]) * grad_last).astype(bf16)
    gate, up, sigmoid_gate, activated = hidden_parts(projected[...])
    hidden = (activated * up).astype(bf16)
    grad_hidden = dot(down[0], route_grad, ((1,), (1,))).T
    gate_slope = sigmoid_gate * (1.0 + gate * (1.0 - sigmoid_gate))
    slope = jnp.concatenate([grad_hidden * up * gate_slope, grad_hidden * activated], axis=1)
    slope = slope.astype(bf16)
    block = width // n_blocks
    for index in range(n_blocks):
        spot = slice(index * block, (index + 1) * block)
        made_in[spot, :] = dot(last_all[:, spot], slope, ((0,), (0,))).astype(bf16)
        send(made_in.at[spot], grad_in.at[0, spot])
    made_out[...] = dot(hidden, route_grad, ((0,), (0,))).astype(bf16)
    send(made_out, grad_out.at[0])
    for copy in copies:
        copy.wait()


def body(tokens, expert_ids, gates, positives, gate_up, down):
    dp_count = lax.axis_size("dp")
    expert_count = lax.axis_size("expert")
    chips = expert_count // 2
    experts = dp_count * chips
    tok_dev, width = tokens.shape
    half_width = down.shape[1]
    seq_dev = positives.shape[0]
    seqs = dp_count * seq_dev
    seq_length = tok_dev // seq_dev
    part_rows = tok_dev // expert_count
    plane = lax.axis_index("dp")
    lane = lax.axis_index("expert")
    place = jnp.stack([plane, lane, plane * chips + lane // 2]).astype(jnp.int32)
    assert experts <= lanes and seq_length % tail == 0

    def to_lane(value, step):
        return lax.ppermute(value, "expert", [(j, j ^ step) for j in range(expert_count)])

    def to_plane(value, step):
        return lax.ppermute(value, "dp", [(p, p ^ step) for p in range(dp_count)])

    chip_steps = [2 * step for step in range(1, chips)]
    groups = [range(first, min(first + 2, dp_count)) for first in range(0, dp_count, 2)]

    share = width // chips
    packed = pl.pallas_call(
        functools.partial(pack_kernel, seq_dev),
        out_shape=jax.ShapeDtypeStruct((part_rows, width + lanes), bf16),
        in_specs=[in_hbm] * 4,
        out_specs=in_vmem,
        scratch_shapes=[
            pltpu.VMEM((part_rows, lanes), f32),
            pltpu.VMEM((seq_dev, tail, share), bf16),
            pltpu.VMEM((1, tok_dev), jnp.int32),
            pltpu.VMEM((1, tok_dev), f32),
            pltpu.SMEM((seq_dev,), jnp.int32),
            pltpu.SemaphoreType.DMA((seq_dev + 4,)),
        ],
        cost_estimate=cost(0, 1 << 19),
        name="pack",
    )(positives, expert_ids.T, gates.T, tokens)
    arrivals = {hop: to_plane(packed, hop) for hop in range(1, dp_count)}
    mate_in = to_lane(gate_up, 1)
    mate_out = to_lane(down, 1)
    weights = (gate_up, down, mate_in, mate_out)

    tiles = [packed]
    spots = {}
    received = None
    for group in groups:
        own = [arrivals[hop] for hop in group if hop]
        if group[0] == 0:
            joined = jnp.concatenate(own + [packed[:, width:]], axis=1)
            joined, weights = lax.optimization_barrier((joined, weights))
        else:
            joined = jnp.concatenate(own, axis=0)
            joined, received = lax.optimization_barrier((joined, received))
            tiles[-len(received) :] = received
        first = len(tiles)
        received = [to_lane(joined, step) for step in chip_steps]
        tiles += own + received
        for index, hop in enumerate(group):
            if group[0] == 0:
                place_of = (first, 0, width) if hop else (0, 0, width)
                row, at = 0, width if hop else width + lanes
            else:
                place_of = (first + index, 0, width)
                row, at = index * part_rows, width
            spots[hop] = [place_of] + [
                (first + len(own) + chip, row, at) for chip in range(chips - 1)
            ]
    where_tiles = [spots[hop] for hop in range(dp_count)]

    each = seqs // expert_count
    extra = each * width // part_rows
    assert extra % lanes == 0 and part_rows % (width // lanes) == 0

    def expert(group, place, with_last):
        near = 0 in group
        wanted = range(dp_count) if with_last else [hop for hop in group if hop]
        used = sorted({spot[0] for hop in wanted for spot in where_tiles[hop]})
        parts = [tiles[index] for index in used]
        n_outs = chips * len(group)
        total = n_outs * part_rows + (seqs if with_last else 0)
        out_shape = [jax.ShapeDtypeStruct((part_rows, width), bf16)] * n_outs
        scratch = [pltpu.VMEM((total, width), bf16)]
        if with_last:
            wider = jax.ShapeDtypeStruct((part_rows, width + extra), bf16)
            out_shape[n_outs - chips :] = [wider] * chips
            out_shape += [
                jax.ShapeDtypeStruct((seqs, width), bf16),
                jax.ShapeDtypeStruct((seqs, 2 * half_width), f32),
                jax.ShapeDtypeStruct((part_rows, extra), f32),
            ]
            scratch = [
                pltpu.VMEM((seqs * (width // lanes), lanes), f32),
                pltpu.VMEM((dp_count, width // lanes, -(-seq_dev // 8) * 8, lanes), f32),
            ] + scratch
        operands = [place] + [tokens] * near + parts + list(weights)
        layout = (tuple(group), chips, part_rows, seq_dev, where_tiles, used, with_last)
        return pl.pallas_call(
            functools.partial(expert_kernel, layout),
            out_shape=out_shape,
            in_specs=[in_smem] + [in_vmem] * (len(operands) - 1),
            out_specs=[in_vmem] * len(out_shape),
            scratch_shapes=scratch,
            compiler_params=params(32),
            cost_estimate=cost(2 * total * width * 6 * half_width, 12 << 20),
            name="experts",
        )(*operands)

    outs = {}
    after = place
    rest = list(range(dp_count - 2, 1, -1))
    for group in groups:
        with_last = dp_count - 1 in group
        out = expert(group, after, with_last)
        after, _ = lax.optimization_barrier((place, out[0]))
        for index, hop in enumerate(group):
            outs[hop] = list(out[index * chips : (index + 1) * chips])
        if with_last:
            last_all, last_projected, own_last = out[-3:]
            tables_place = after

    table_rows = dp_count * part_rows + seqs
    chunks = width // lanes
    sublanes = -(-seq_dev // 8) * 8
    kept, sent, partners = pl.pallas_call(
        functools.partial(table_kernel, (seq_dev, tok_dev, where_tiles, len(tiles))),
        out_shape=[
            jax.ShapeDtypeStruct((table_rows, lanes), bf16),
            jax.ShapeDtypeStruct((table_rows, lanes), bf16),
            jax.ShapeDtypeStruct((seqs, lanes), f32),
        ],
        in_specs=[in_smem] + [in_vmem] * len(tiles),
        out_specs=[in_vmem] * 3,
        scratch_shapes=[
            pltpu.VMEM((dp_count, sublanes, lanes), f32),
            pltpu.VMEM((dp_count, sublanes, lanes), f32),
        ],
        compiler_params=params(48 if dp_count > 8 else 12),
        cost_estimate=cost(0, 1 << 20),
        name="tables",
    )(tables_place, *tiles)
    found = to_lane(sent, 1)

    def combine(hop, parts, last_sum):
        with_last = last_sum is None
        out_shape = [jax.ShapeDtypeStruct((part_rows, width), f32)]
        if hop:
            out_shape = [jax.ShapeDtypeStruct((part_rows, width + extra), bf16)]
        if with_last:
            out_shape.append(jax.ShapeDtypeStruct((part_rows, extra), bf16))
        operands = [place, kept, found] + [packed] * (hop == 0)
        operands += [last_sum] * (hop > 0 and not with_last) + parts
        return pl.pallas_call(
            functools.partial(combine_kernel, (hop, chips, with_last, width, each)),
            out_shape=out_shape,
            in_specs=[in_smem] + [in_vmem] * (len(operands) - 1),
            out_specs=[in_vmem] * len(out_shape),
            compiler_params=params(8),
            cost_estimate=cost(0, 2 << 20),
            name="combine",
        )(*operands)

    returned = {}

    def send_back(hop, gated, after):
        first, *parts = outs[hop]
        free = len(parts) - gated
        parts[free:], after = lax.optimization_barrier((parts[free:], after))
        returned[hop] = [first] + [to_lane(value, step) for value, step in zip(parts, chip_steps)]
        return after

    send_back(1, 0, [])
    if dp_count > 2:
        returned[1][1:] = send_back(dp_count - 1, chips - 1, returned[1][1:])
    before = dp_count - 1
    for hop in rest:
        returned[before][1:], found = send_back(hop, 1, (returned[before][1:], found))
        before = hop
    homeward = []
    last_sum = None
    for hop in range(dp_count - 1, 0, -1):
        result = combine(hop, returned[hop], last_sum)
        last_sum = result[1] if last_sum is None else last_sum
        homeward.append(to_plane(result[0], hop))
        if hop == min(3, dp_count - 1):
            gate = result[0]
    outs[0][1:], gate = lax.optimization_barrier((outs[0][1:], gate))
    send_back(0, 0, [])
    near_sum = combine(0, returned[0], last_sum)[0]

    own_out = pl.pallas_call(
        finish_kernel,
        out_shape=jax.ShapeDtypeStruct((part_rows, width + extra), bf16),
        in_specs=[in_vmem] * (2 + dp_count),
        out_specs=in_vmem,
        compiler_params=params(16 if dp_count > 8 else 4),
        cost_estimate=cost(0, 1 << 20),
        name="finish",
    )(near_sum, own_last, last_sum, *homeward)
    pieces = [own_out] + [to_lane(own_out, step) for step in chip_steps]
    pieces += [to_lane(piece, 1) for piece in pieces]

    n_blocks = width // min(512, width)
    layer_out, grad_gate_up, grad_down = pl.pallas_call(
        functools.partial(final_kernel, len(pieces), n_blocks),
        out_shape=[
            jax.ShapeDtypeStruct((tok_dev, width), bf16),
            jax.ShapeDtypeStruct(gate_up.shape, bf16),
            jax.ShapeDtypeStruct(down.shape, bf16),
        ],
        in_specs=[in_vmem] * (len(pieces) + 2) + [in_smem] + [in_vmem] * 4,
        out_specs=[in_hbm] * 3,
        scratch_shapes=[
            pltpu.VMEM((width, 2 * half_width), bf16),
            pltpu.VMEM((half_width, width), bf16),
            pltpu.VMEM((seqs * (width // lanes), lanes), f32),
            pltpu.SemaphoreType.DMA((len(pieces) + n_blocks + 1,)),
        ],
        compiler_params=params(24),
        cost_estimate=cost(2 * seqs * width * 4 * half_width, 7 << 20),
        name="final",
    )(*pieces, last_all, last_projected, place, kept, found, partners, down)
    return (layer_out, grad_gate_up, grad_down)


def solution(mesh):
    return jax.shard_map(
        body,
        mesh=mesh,
        in_specs=(
            P("dp", None),
            P("dp", "expert"),
            P("dp", "expert"),
            P("dp"),
            P(("dp", "expert"), None, None),
            P(("dp", "expert"), None, None),
        ),
        out_specs=(P("dp", None), P(("dp", "expert"), None, None), P(("dp", "expert"), None, None)),
        check_vma=False,
    )
```

```python
import functools

import jax
import jax.numpy as jnp
from jax import lax
from jax.experimental import pallas as pl
from jax.experimental.pallas import tpu as pltpu
from jax.sharding import PartitionSpec as P

logit_divisor = 0.05
grad_scale = 256.0
epsilon = 1e-06
lanes = 128
tail = 16
bf16 = jnp.bfloat16
f32 = jnp.float32

in_hbm = pl.BlockSpec(memory_space=pltpu.HBM)
in_vmem = pl.BlockSpec(memory_space=pltpu.VMEM)


def params(mebibytes):
    return pltpu.CompilerParams(vmem_limit_bytes=mebibytes << 20)


def cost(flops, moved):
    return pl.CostEstimate(flops=flops, transcendentals=0, bytes_accessed=moved)


def dot(left, right, dims=((1,), (0,)), precision=None):
    return lax.dot_general(
        left, right, (dims, ((), ())), precision=precision, preferred_element_type=f32
    )


def doublings(count):
    steps = [1 << bit for bit in range((count - 1).bit_length())]
    assert 1 << len(steps) == count
    return steps


def position():
    plane, lane = lax.axis_index("dp"), lax.axis_index("expert")
    return plane, lane, plane * (lax.axis_size("expert") // 2) + lane // 2


def column(table, wanted):
    index = lax.broadcasted_iota(jnp.int32, table.shape, 1)
    return jnp.sum(jnp.where(index == wanted, table, 0.0), axis=1, keepdims=True)


def pack_kernel(
    seq_dev, partners, ids_in, gates_in, tokens, out, tile, rows, ids, gates, positives, sems
):
    part_rows, width = out.shape[0], tokens.shape[1]
    tok_dev = tokens.shape[0]
    seq_length = tok_dev // seq_dev
    share = rows.shape[2]
    lane = lax.axis_index("expert")
    column_at = pl.multiple_of(lane // 2 * share, lanes)
    start = pl.multiple_of(lane * part_rows, part_rows)
    copies = [
        pltpu.make_async_copy(
            tokens.at[pl.ds((seq + 1) * seq_length - tail, tail), pl.ds(column_at, share)],
            rows.at[seq],
            sems.at[seq],
        )
        for seq in range(seq_dev)
    ]
    own = pltpu.make_async_copy(
        tokens.at[pl.ds(start, part_rows)], out.at[:, pl.ds(0, width)], sems.at[seq_dev]
    )
    lines = [
        pltpu.make_async_copy(ids_in, ids, sems.at[seq_dev + 1]),
        pltpu.make_async_copy(gates_in, gates, sems.at[seq_dev + 2]),
        pltpu.make_async_copy(partners, positives, sems.at[seq_dev + 3]),
    ]
    for copy in lines + [own] + copies:
        copy.start()
    note_rows = tok_dev // lanes
    tile[...] = jnp.zeros_like(tile)
    for copy in lines:
        copy.wait()
    for index in range(note_rows):
        block = slice(index * lanes, (index + 1) * lanes)
        tile[index : index + 1, :] = ids[:, block].astype(f32)
        tile[note_rows + index : note_rows + index + 1, :] = gates[:, block]
    for seq in range(seq_dev):
        row = 2 * note_rows + seq
        tile[row : row + 1, :] = jnp.full((1, lanes), positives[seq], jnp.int32).astype(f32)
    base = part_rows - seq_dev * (share // lanes)
    for seq in range(seq_dev):
        copies[seq].wait()
        values = rows[seq].astype(f32)
        for chunk in range(share // lanes):
            row = base + chunk * seq_dev + seq
            tile[row : row + 1, :] = values[tail - 1 : tail, chunk * lanes : (chunk + 1) * lanes]
    out[:, width:] = tile[...].astype(bf16)
    own.wait()


def table_kernel(layout, *refs):
    seq_dev, tok_dev, where_tiles, n_parts = layout
    place = position()
    parts = refs[:n_parts]
    kept, sent, partners, routes, marks = refs[n_parts:]
    part_rows = parts[0].shape[0]
    dp_count = len(where_tiles)
    note_rows = tok_dev // lanes
    seq_length = tok_dev // seq_dev
    chips = len(where_tiles[0])
    lane_index = lax.broadcasted_iota(jnp.int32, (part_rows, lanes), 1)
    row_index = lax.broadcasted_iota(jnp.int32, (part_rows, lanes), 0)

    def dense_rows(tile, lane):
        start = lane * part_rows
        picked = lane_index == row_index + start % lanes
        found = []
        for offset in (0, note_rows):
            line = tile[offset : offset + 1, :]
            for index in range(1, note_rows):
                other = tile[offset + index : offset + index + 1, :]
                line = jnp.where(start // lanes == index, other, line)
            found.append(jnp.sum(jnp.where(picked, line, 0.0), axis=1, keepdims=True))
        return jnp.where(lane_index.astype(f32) == found[0], found[1], 0.0)

    for hop in range(dp_count):
        plane = place[0] ^ hop
        sums = [None, None]
        for chip in range(chips):
            source, row, at = where_tiles[hop][chip]
            tile = parts[source][row : row + part_rows, at : at + lanes].astype(f32)
            for index, lane in enumerate((place[1], place[1] ^ 1)):
                value = dense_rows(tile, lane)
                sums[index] = value if chip == 0 else sums[index] + value
            for seq in range(seq_dev):
                at_token = (seq + 1) * seq_length - 1
                row = at_token // lanes
                here = lane_index[:1] == at_token % lanes
                expert, gate = [
                    jnp.sum(
                        jnp.where(here, tile[offset + row : offset + row + 1, :], 0.0),
                        axis=1,
                        keepdims=True,
                    )
                    for offset in (0, note_rows)
                ]
                value = jnp.where(lane_index[:1].astype(f32) == expert, gate, 0.0)
                if chip:
                    value = value + routes[plane, seq : seq + 1, :]
                routes[plane, seq : seq + 1, :] = value
            if chip == 0:
                marks[plane, 0:seq_dev, :] = tile[2 * note_rows : 2 * note_rows + seq_dev, :]
        at = slice(hop * part_rows, (hop + 1) * part_rows)
        kept[at, :] = sums[0].astype(bf16)
        sent[at, :] = sums[1].astype(bf16)
    last = dp_count * part_rows
    shared = []
    for plane in range(dp_count):
        shared.append(routes[plane, 0:seq_dev, :])
        partners[plane * seq_dev : (plane + 1) * seq_dev, :] = marks[plane, 0:seq_dev, :]
    seqs = dp_count * seq_dev
    value = jnp.concatenate(shared, axis=0).astype(bf16)
    kept[last : last + seqs, :] = value
    sent[last : last + seqs, :] = value


def hidden_parts(projected):
    half_width = projected.shape[1] // 2
    gate, up = projected[:, :half_width], projected[:, half_width:]
    sigmoid_gate = jax.nn.sigmoid(gate)
    return gate, up, sigmoid_gate, gate * sigmoid_gate


def spread_rows(values, flat):
    count, chunks = values.shape[0], values.shape[1] // lanes
    for chunk in range(chunks):
        flat[pl.ds(chunk, count, stride=chunks), :] = values[:, chunk * lanes : (chunk + 1) * lanes]


def share_of(flat, lane, each, part_rows, chunks):
    size = each * chunks
    start = lane * size
    blocks = [
        flat[pl.ds(pl.multiple_of(start + first, part_rows), part_rows), :]
        for first in range(0, size, part_rows)
    ]
    return blocks[0] if len(blocks) == 1 else jnp.concatenate(blocks, axis=1)


def last_tokens(place, seq_dev, where_tiles, parts, tokens):
    part_rows = parts[0].shape[0]
    dp_count, chunks = tokens.shape[:2]
    chips = len(where_tiles[0])
    share_chunks = chunks // chips
    base = part_rows - seq_dev * share_chunks
    for hop in range(dp_count):
        for chip in range(chips):
            source, row, at = where_tiles[hop][chip]
            tile = parts[source][row : row + part_rows, at : at + lanes].astype(f32)
            first = ((place[1] // 2) ^ chip) * share_chunks
            for chunk in range(share_chunks):
                row = base + chunk * seq_dev
                tokens[place[0] ^ hop, first + chunk, 0:seq_dev, :] = tile[row : row + seq_dev, :]
    joined = []
    for plane in range(dp_count):
        lines = [tokens[plane, chunk, 0:seq_dev, :] for chunk in range(chunks)]
        joined.append(jnp.concatenate(lines, axis=1))
    return jnp.concatenate(joined, axis=0)


def expert_kernel(layout, *refs):
    group, chips, part_rows, seq_dev, where_tiles, used, with_last = layout
    refs = list(refs)
    place = position()
    near = 0 in group
    tokens = refs.pop(0) if near else None
    parts, refs = dict(zip(used, refs)), refs[len(used) :]
    weights, refs = refs[:4], refs[4:]
    n_outs = chips * len(group)
    outs, refs = refs[:n_outs], refs[n_outs:]
    if with_last:
        last_all, last_projected, own_last, flat, seq_tokens, *refs = refs
    (rows,) = refs
    width = weights[0].shape[1]
    total = n_outs * part_rows
    spots = [slice(index * part_rows, (index + 1) * part_rows) for index in range(n_outs)]
    for index, spot in enumerate(spots):
        hop, chip = group[index // chips], index % chips
        if hop:
            source, row, _ = where_tiles[hop][chip]
            rows[spot, :] = parts[source][row : row + part_rows, :width]
        else:
            start = pl.multiple_of((place[1] ^ (2 * chip)) * part_rows, part_rows)
            rows[spot, :] = tokens[pl.ds(start, part_rows), :]
    if with_last:
        floats = last_tokens(place, seq_dev, where_tiles, parts, seq_tokens)
        last_all[...] = floats.astype(bf16)
        rows[total:, :] = floats.astype(bf16)
    hidden = []
    for half in range(2):
        projected = dot(rows[...], weights[2 * half][0])
        if half == 0 and with_last:
            last_projected[...] = projected[total:]
        _, up, _, activated = hidden_parts(projected)
        hidden.append((activated * up).astype(bf16))
    block = min(512, width)
    chunks = width // lanes
    for first in range(0, width, block):
        columns = slice(first, first + block)
        result = dot(hidden[0], weights[1][0, :, columns]) + dot(
            hidden[1], weights[3][0, :, columns]
        )
        for out, spot in zip(outs, spots):
            out[:, columns] = result[spot].astype(bf16)
        if with_last:
            count = result.shape[0] - total
            for at in range(0, block, lanes):
                flat[pl.ds((first + at) // lanes, count, stride=chunks), :] = result[
                    total:, at : at + lanes
                ]
    if with_last:
        each = floats.shape[0] // (2 * chips)
        for chip in range(chips):
            share = share_of(flat, place[1] ^ (2 * chip), each, part_rows, chunks)
            outs[n_outs - chips + chip][:, width:] = share.astype(bf16)
        spread_rows(floats, flat)
        own_last[...] = share_of(flat, place[1], each, part_rows, chunks)


def combine_kernel(layout, kept, found, *refs):
    hop, chips, with_last, width, each = layout
    place = position()
    own, refs = (refs[0], refs[1:]) if hop == 0 else (None, refs)
    last_in, refs = (refs[0], refs[1:]) if hop and not with_last else (None, refs)
    parts, out = refs[:chips], refs[chips]
    part_rows = out.shape[0]
    first_expert = place[2] - place[1] // 2
    experts = [first_expert + ((place[1] // 2) ^ chip) for chip in range(chips)]
    if with_last:
        last_in = refs[-1]
        table = kept[-2 * chips * each :, :].astype(f32) + found[-2 * chips * each :, :].astype(f32)
        row_index = lax.broadcasted_iota(jnp.int32, table.shape, 0)
        chunks = width // lanes
        for row in range(each):
            mine = jnp.where(row_index == place[1] * each + row, table, 0.0)
            mine = jnp.sum(mine, axis=0, keepdims=True)
            first = row * chunks % part_rows
            spot = slice(first, first + chunks)
            at = row * chunks // part_rows * lanes
            total = None
            for chip in range(chips):
                values = parts[chip][spot, width + at : width + at + lanes].astype(f32)
                term = column(mine, experts[chip]) * values
                total = term if total is None else total + term
            last_in[spot, at : at + lanes] = total.astype(bf16)
    at = slice(hop * part_rows, (hop + 1) * part_rows)
    table = kept[at, :].astype(f32) + found[at, :].astype(f32)
    total = None if hop else own[:, :width].astype(f32)
    for chip in range(chips):
        term = column(table, experts[chip]) * parts[chip][:, :width].astype(f32)
        total = term if total is None else total + term
    out[:, :width] = total.astype(out.dtype)
    if hop:
        out[:, width:] = last_in[...]


def finish_kernel(near, own_last, last_sum, *refs):
    parts, out = refs[:-1], refs[-1]
    width = near.shape[1]
    total = near[...]
    last = last_sum[...].astype(f32)
    for part in parts:
        total = total + part[:, :width].astype(f32)
        last = last + part[:, width:].astype(f32)
    out[:, :width] = total.astype(bf16)
    out[:, width:] = (own_last[...] + last).astype(bf16)


def collect_rows(lane, pieces, flat, width):
    part_rows, chunks = pieces[0].shape[0], width // lanes
    count = len(pieces)
    size = flat.shape[0] // count
    for index in range(count):
        source = lane ^ (2 * (index % (count // 2))) ^ (index // (count // 2))
        for first in range(0, size, part_rows):
            at = width + first // part_rows * lanes
            start = pl.multiple_of(source * size + first, part_rows)
            flat[pl.ds(start, part_rows), :] = pieces[index][:, at : at + lanes].astype(f32)
    rows = flat.shape[0] // chunks
    columns = [flat[pl.ds(chunk, rows, stride=chunks), :] for chunk in range(chunks)]
    return jnp.concatenate(columns, axis=1)


def both_ways(coefficient, unit, diagonal):
    count = unit.shape[0]
    if count > 32:
        high = lax.Precision.HIGHEST
        there = dot(coefficient, unit, ((1,), (0,)), high)
        return there + dot(coefficient, unit, ((0,), (0,)), high)
    total = None
    for index in range(count):
        line = jnp.where(diagonal, coefficient[index : index + 1, :], 0.0)
        factor = coefficient[:, index : index + 1] + jnp.sum(line, axis=1, keepdims=True)
        term = factor * unit[index : index + 1, :]
        total = term if total is None else total + term
    return total


def final_kernel(n_pieces, n_blocks, *refs):
    pieces, refs = refs[:n_pieces], refs[n_pieces:]
    last_all, projected, kept, found, partners, down, *refs = refs
    place = position()
    layer_out, grad_in, grad_out, made_in, made_out, flat, sems = refs
    part_rows, width = pieces[0].shape[0], layer_out.shape[1]
    copies = []

    def send(source, target):
        copies.append(pltpu.make_async_copy(source, target, sems.at[len(copies)]))
        copies[-1].start()

    for index in range(n_pieces):
        lane = place[1] ^ (2 * (index % (n_pieces // 2))) ^ (index // (n_pieces // 2))
        start = pl.multiple_of(lane * part_rows, part_rows)
        send(pieces[index].at[:, pl.ds(0, width)], layer_out.at[pl.ds(start, part_rows)])
    values = collect_rows(place[1], pieces, flat, width)
    count = values.shape[0]
    last = kept.shape[0] - count
    table = kept[last:, :].astype(f32) + found[last:, :].astype(f32)
    row = lax.broadcasted_iota(jnp.int32, (count, count), 0)
    col = lax.broadcasted_iota(jnp.int32, (count, count), 1)
    norms = jnp.sqrt(jnp.sum(values * values, axis=1, keepdims=True) + epsilon)
    norms_line = jnp.sum(jnp.where(row == col, norms, 0.0), axis=0, keepdims=True)
    unit = values / norms
    rows = values.astype(bf16)
    scores = dot(rows, rows, ((1,), (1,))) / (norms * norms_line) / logit_divisor
    exp_scores = jnp.where(row != col, jnp.exp(scores), 0.0)
    probabilities = exp_scores / jnp.sum(exp_scores, axis=1, keepdims=True)
    partner = partners[:, :1].astype(jnp.int32)
    coefficient = grad_scale * (probabilities - jnp.where(col == partner, 1.0, 0.0))
    grad_unit = both_ways(coefficient, unit, row == col) / logit_divisor
    projection = jnp.sum(unit * grad_unit, axis=1, keepdims=True)
    grad_last = (grad_unit - unit * projection) / norms
    route_grad = (column(table, place[2]) * grad_last).astype(bf16)
    gate, up, sigmoid_gate, activated = hidden_parts(projected[...])
    hidden = (activated * up).astype(bf16)
    grad_hidden = dot(route_grad, down[0], ((1,), (1,)))
    gate_slope = sigmoid_gate * (1.0 + gate * (1.0 - sigmoid_gate))
    slope = jnp.concatenate([grad_hidden * up * gate_slope, grad_hidden * activated], axis=1)
    slope = slope.astype(bf16)
    block = width // n_blocks
    for index in range(n_blocks):
        spot = slice(index * block, (index + 1) * block)
        made_in[spot, :] = dot(last_all[:, spot], slope, ((0,), (0,))).astype(bf16)
        send(made_in.at[spot], grad_in.at[0, spot])
    made_out[...] = dot(hidden, route_grad, ((0,), (0,))).astype(bf16)
    send(made_out, grad_out.at[0])
    for copy in copies:
        copy.wait()


def body(tokens, expert_ids, gates, positives, gate_up, down):
    dp_count = lax.axis_size("dp")
    expert_count = lax.axis_size("expert")
    chips = expert_count // 2
    experts = dp_count * chips
    tok_dev, width = tokens.shape
    half_width = down.shape[1]
    seq_dev = positives.shape[0]
    seqs = dp_count * seq_dev
    seq_length = tok_dev // seq_dev
    part_rows = tok_dev // expert_count
    assert experts <= lanes and seq_length % tail == 0

    def to_lane(value, step):
        return lax.ppermute(value, "expert", [(j, j ^ step) for j in range(expert_count)])

    def to_plane(value, step):
        return lax.ppermute(value, "dp", [(p, p ^ step) for p in range(dp_count)])

    chip_steps = [2 * step for step in range(1, chips)]
    groups = [range(first, min(first + 2, dp_count)) for first in range(0, dp_count, 2)]

    share = width // chips
    packed = pl.pallas_call(
        functools.partial(pack_kernel, seq_dev),
        out_shape=jax.ShapeDtypeStruct((part_rows, width + lanes), bf16),
        in_specs=[in_hbm] * 4,
        out_specs=in_vmem,
        scratch_shapes=[
            pltpu.VMEM((part_rows, lanes), f32),
            pltpu.VMEM((seq_dev, tail, share), bf16),
            pltpu.VMEM((1, tok_dev), jnp.int32),
            pltpu.VMEM((1, tok_dev), f32),
            pltpu.SMEM((seq_dev,), jnp.int32),
            pltpu.SemaphoreType.DMA((seq_dev + 4,)),
        ],
        cost_estimate=cost(0, 1 << 19),
        name="pack",
    )(positives, expert_ids.T, gates.T, tokens)
    arrivals = {hop: to_plane(packed, hop) for hop in range(1, dp_count)}
    mate_in = to_lane(gate_up, 1)
    mate_out = to_lane(down, 1)
    weights = (gate_up, down, mate_in, mate_out)

    tiles = [packed]
    spots = {}
    received = None
    for group in groups:
        own = [arrivals[hop] for hop in group if hop]
        if group[0] == 0:
            joined = jnp.concatenate(own + [packed[:, width:]], axis=1)
            joined, weights = lax.optimization_barrier((joined, weights))
        else:
            joined = jnp.concatenate(own, axis=0)
            joined, received = lax.optimization_barrier((joined, received))
            tiles[-len(received) :] = received
        first = len(tiles)
        received = [to_lane(joined, step) for step in chip_steps]
        tiles += own + received
        for index, hop in enumerate(group):
            if group[0] == 0:
                place_of = (first, 0, width) if hop else (0, 0, width)
                row, at = 0, width if hop else width + lanes
            else:
                place_of = (first + index, 0, width)
                row, at = index * part_rows, width
            spots[hop] = [place_of] + [
                (first + len(own) + chip, row, at) for chip in range(chips - 1)
            ]
    where_tiles = [spots[hop] for hop in range(dp_count)]

    each = seqs // expert_count
    extra = each * width // part_rows
    assert extra % lanes == 0 and part_rows % (width // lanes) == 0

    def expert(group, after, with_last):
        near = 0 in group
        wanted = range(dp_count) if with_last else [hop for hop in group if hop]
        used = sorted({spot[0] for hop in wanted for spot in where_tiles[hop]})
        parts = [tiles[index] for index in used]
        n_outs = chips * len(group)
        total = n_outs * part_rows + (seqs if with_last else 0)
        out_shape = [jax.ShapeDtypeStruct((part_rows, width), bf16)] * n_outs
        scratch = [pltpu.VMEM((total, width), bf16)]
        if with_last:
            wider = jax.ShapeDtypeStruct((part_rows, width + extra), bf16)
            out_shape[n_outs - chips :] = [wider] * chips
            out_shape += [
                jax.ShapeDtypeStruct((seqs, width), bf16),
                jax.ShapeDtypeStruct((seqs, 2 * half_width), f32),
                jax.ShapeDtypeStruct((part_rows, extra), f32),
            ]
            scratch = [
                pltpu.VMEM((seqs * (width // lanes), lanes), f32),
                pltpu.VMEM((dp_count, width // lanes, -(-seq_dev // 8) * 8, lanes), f32),
            ] + scratch
        if after is not None:
            parts[0], _ = lax.optimization_barrier((parts[0], after))
        operands = [tokens] * near + parts + list(weights)
        layout = (tuple(group), chips, part_rows, seq_dev, where_tiles, used, with_last)
        return pl.pallas_call(
            functools.partial(expert_kernel, layout),
            out_shape=out_shape,
            in_specs=[in_vmem] * len(operands),
            out_specs=[in_vmem] * len(out_shape),
            scratch_shapes=scratch,
            compiler_params=params(32),
            cost_estimate=cost(2 * total * width * 6 * half_width, 12 << 20),
            name="experts",
        )(*operands)

    outs = {}
    after = None
    rest = list(range(dp_count - 2, 1, -1))
    for group in groups:
        with_last = dp_count - 1 in group
        out = expert(group, after, with_last)
        after = out[0]
        for index, hop in enumerate(group):
            outs[hop] = list(out[index * chips : (index + 1) * chips])
        if with_last:
            last_all, last_projected, own_last = out[-3:]
            first_tile, _ = lax.optimization_barrier((tiles[0], out[0]))

    table_rows = dp_count * part_rows + seqs
    chunks = width // lanes
    sublanes = -(-seq_dev // 8) * 8
    tiles[0] = first_tile
    kept, sent, partners = pl.pallas_call(
        functools.partial(table_kernel, (seq_dev, tok_dev, where_tiles, len(tiles))),
        out_shape=[
            jax.ShapeDtypeStruct((table_rows, lanes), bf16),
            jax.ShapeDtypeStruct((table_rows, lanes), bf16),
            jax.ShapeDtypeStruct((seqs, lanes), f32),
        ],
        in_specs=[in_vmem] * len(tiles),
        out_specs=[in_vmem] * 3,
        scratch_shapes=[
            pltpu.VMEM((dp_count, sublanes, lanes), f32),
            pltpu.VMEM((dp_count, sublanes, lanes), f32),
        ],
        compiler_params=params(48 if dp_count > 8 else 12),
        cost_estimate=cost(0, 1 << 20),
        name="tables",
    )(*tiles)
    found = to_lane(sent, 1)

    def combine(hop, parts, last_sum):
        with_last = last_sum is None
        out_shape = [jax.ShapeDtypeStruct((part_rows, width), f32)]
        if hop:
            out_shape = [jax.ShapeDtypeStruct((part_rows, width + extra), bf16)]
        if with_last:
            out_shape.append(jax.ShapeDtypeStruct((part_rows, extra), bf16))
        operands = [kept, found] + [packed] * (hop == 0)
        operands += [last_sum] * (hop > 0 and not with_last) + parts
        return pl.pallas_call(
            functools.partial(combine_kernel, (hop, chips, with_last, width, each)),
            out_shape=out_shape,
            in_specs=[in_vmem] * len(operands),
            out_specs=[in_vmem] * len(out_shape),
            compiler_params=params(8),
            cost_estimate=cost(0, 2 << 20),
            name="combine",
        )(*operands)

    returned = {}

    def send_back(hop, gated, after):
        first, *parts = outs[hop]
        free = len(parts) - gated
        parts[free:], after = lax.optimization_barrier((parts[free:], after))
        returned[hop] = [first] + [to_lane(value, step) for value, step in zip(parts, chip_steps)]
        return after

    send_back(1, 0, [])
    if dp_count > 2:
        returned[1][1:] = send_back(dp_count - 1, chips - 1, returned[1][1:])
    before = dp_count - 1
    for hop in rest:
        returned[before][1:], found = send_back(hop, 1, (returned[before][1:], found))
        before = hop
    homeward = []
    last_sum = None
    for hop in range(dp_count - 1, 0, -1):
        result = combine(hop, returned[hop], last_sum)
        last_sum = result[1] if last_sum is None else last_sum
        homeward.append(to_plane(result[0], hop))
        if hop == min(3, dp_count - 1):
            gate = result[0]
    outs[0][1:], gate = lax.optimization_barrier((outs[0][1:], gate))
    send_back(0, 0, [])
    near_sum = combine(0, returned[0], last_sum)[0]

    own_out = pl.pallas_call(
        finish_kernel,
        out_shape=jax.ShapeDtypeStruct((part_rows, width + extra), bf16),
        in_specs=[in_vmem] * (2 + dp_count),
        out_specs=in_vmem,
        compiler_params=params(16 if dp_count > 8 else 4),
        cost_estimate=cost(0, 1 << 20),
        name="finish",
    )(near_sum, own_last, last_sum, *homeward)
    pieces = [own_out] + [to_lane(own_out, step) for step in chip_steps]
    pieces += [to_lane(piece, 1) for piece in pieces]

    n_blocks = width // min(512, width)
    layer_out, grad_gate_up, grad_down = pl.pallas_call(
        functools.partial(final_kernel, len(pieces), n_blocks),
        out_shape=[
            jax.ShapeDtypeStruct((tok_dev, width), bf16),
            jax.ShapeDtypeStruct(gate_up.shape, bf16),
            jax.ShapeDtypeStruct(down.shape, bf16),
        ],
        in_specs=[in_vmem] * (len(pieces) + 6),
        out_specs=[in_hbm] * 3,
        scratch_shapes=[
            pltpu.VMEM((width, 2 * half_width), bf16),
            pltpu.VMEM((half_width, width), bf16),
            pltpu.VMEM((seqs * (width // lanes), lanes), f32),
            pltpu.SemaphoreType.DMA((len(pieces) + n_blocks + 1,)),
        ],
        compiler_params=params(24),
        cost_estimate=cost(2 * seqs * width * 4 * half_width, 7 << 20),
        name="final",
    )(*pieces, last_all, last_projected, kept, found, partners, down)
    return (layer_out, grad_gate_up, grad_down)


def solution(mesh):
    return jax.shard_map(
        body,
        mesh=mesh,
        in_specs=(
            P("dp", None),
            P("dp", "expert"),
            P("dp", "expert"),
            P("dp"),
            P(("dp", "expert"), None, None),
            P(("dp", "expert"), None, None),
        ),
        out_specs=(P("dp", None), P(("dp", "expert"), None, None), P(("dp", "expert"), None, None)),
        check_vma=False,
    )
```

```python
import functools

import jax
import jax.numpy as jnp
from jax import lax
from jax.experimental import pallas as pl
from jax.experimental.pallas import tpu as pltpu
from jax.sharding import PartitionSpec as P

logit_divisor = 0.05
grad_scale = 256.0
epsilon = 1e-06
lanes = 128
tail = 16
bf16 = jnp.bfloat16
f32 = jnp.float32

in_hbm = pl.BlockSpec(memory_space=pltpu.HBM)
in_vmem = pl.BlockSpec(memory_space=pltpu.VMEM)


def params(mebibytes):
    return pltpu.CompilerParams(vmem_limit_bytes=mebibytes << 20)


def cost(flops, moved):
    return pl.CostEstimate(flops=flops, transcendentals=0, bytes_accessed=moved)


def dot(left, right, dims=((1,), (0,)), precision=None):
    return lax.dot_general(
        left, right, (dims, ((), ())), precision=precision, preferred_element_type=f32
    )


def doublings(count):
    steps = [1 << bit for bit in range((count - 1).bit_length())]
    assert 1 << len(steps) == count
    return steps


def position():
    plane, lane = lax.axis_index("dp"), lax.axis_index("expert")
    return plane, lane, plane * (lax.axis_size("expert") // 2) + lane // 2


def column(table, wanted):
    index = lax.broadcasted_iota(jnp.int32, table.shape, 1)
    return jnp.sum(jnp.where(index == wanted, table, 0.0), axis=1, keepdims=True)


def pack_kernel(
    seq_dev, partners, ids_in, gates_in, tokens, out, tile, rows, ids, gates, positives, sems
):
    part_rows, width = out.shape[0], tokens.shape[1]
    tok_dev = tokens.shape[0]
    seq_length = tok_dev // seq_dev
    share = rows.shape[2]
    lane = lax.axis_index("expert")
    column_at = pl.multiple_of(lane // 2 * share, lanes)
    start = pl.multiple_of(lane * part_rows, part_rows)
    copies = [
        pltpu.make_async_copy(
            tokens.at[pl.ds((seq + 1) * seq_length - tail, tail), pl.ds(column_at, share)],
            rows.at[seq],
            sems.at[seq],
        )
        for seq in range(seq_dev)
    ]
    own = pltpu.make_async_copy(
        tokens.at[pl.ds(start, part_rows)], out.at[:, pl.ds(0, width)], sems.at[seq_dev]
    )
    lines = [
        pltpu.make_async_copy(ids_in, ids, sems.at[seq_dev + 1]),
        pltpu.make_async_copy(gates_in, gates, sems.at[seq_dev + 2]),
        pltpu.make_async_copy(partners, positives, sems.at[seq_dev + 3]),
    ]
    for copy in lines + [own] + copies:
        copy.start()
    note_rows = tok_dev // lanes
    tile[...] = jnp.zeros_like(tile)
    for copy in lines:
        copy.wait()
    for index in range(note_rows):
        block = slice(index * lanes, (index + 1) * lanes)
        tile[index : index + 1, :] = ids[:, block].astype(f32)
        tile[note_rows + index : note_rows + index + 1, :] = gates[:, block]
    for seq in range(seq_dev):
        row = 2 * note_rows + seq
        tile[row : row + 1, :] = jnp.full((1, lanes), positives[seq], jnp.int32).astype(f32)
    base = part_rows - seq_dev * (share // lanes)
    for seq in range(seq_dev):
        copies[seq].wait()
        values = rows[seq].astype(f32)
        for chunk in range(share // lanes):
            row = base + chunk * seq_dev + seq
            tile[row : row + 1, :] = values[tail - 1 : tail, chunk * lanes : (chunk + 1) * lanes]
    out[:, width:] = tile[...].astype(bf16)
    own.wait()


def table_kernel(layout, *refs):
    seq_dev, tok_dev, where_tiles, n_parts = layout
    place = position()
    parts = refs[:n_parts]
    kept, sent, partners, routes, marks = refs[n_parts:]
    part_rows = parts[0].shape[0]
    dp_count = len(where_tiles)
    note_rows = tok_dev // lanes
    seq_length = tok_dev // seq_dev
    chips = len(where_tiles[0])
    lane_index = lax.broadcasted_iota(jnp.int32, (part_rows, lanes), 1)
    row_index = lax.broadcasted_iota(jnp.int32, (part_rows, lanes), 0)

    def dense_rows(tile, lane):
        start = lane * part_rows
        picked = lane_index == row_index + start % lanes
        found = []
        for offset in (0, note_rows):
            line = tile[offset : offset + 1, :]
            for index in range(1, note_rows):
                other = tile[offset + index : offset + index + 1, :]
                line = jnp.where(start // lanes == index, other, line)
            found.append(jnp.sum(jnp.where(picked, line, 0.0), axis=1, keepdims=True))
        return jnp.where(lane_index.astype(f32) == found[0], found[1], 0.0)

    for hop in range(dp_count):
        plane = place[0] ^ hop
        sums = [None, None]
        for chip in range(chips):
            source, row, at = where_tiles[hop][chip]
            tile = parts[source][row : row + part_rows, at : at + lanes].astype(f32)
            for index, lane in enumerate((place[1], place[1] ^ 1)):
                value = dense_rows(tile, lane)
                sums[index] = value if chip == 0 else sums[index] + value
            for seq in range(seq_dev):
                at_token = (seq + 1) * seq_length - 1
                row = at_token // lanes
                here = lane_index[:1] == at_token % lanes
                expert, gate = [
                    jnp.sum(
                        jnp.where(here, tile[offset + row : offset + row + 1, :], 0.0),
                        axis=1,
                        keepdims=True,
                    )
                    for offset in (0, note_rows)
                ]
                value = jnp.where(lane_index[:1].astype(f32) == expert, gate, 0.0)
                if chip:
                    value = value + routes[plane, seq : seq + 1, :]
                routes[plane, seq : seq + 1, :] = value
            if chip == 0:
                marks[plane, 0:seq_dev, :] = tile[2 * note_rows : 2 * note_rows + seq_dev, :]
        at = slice(hop * part_rows, (hop + 1) * part_rows)
        kept[at, :] = sums[0].astype(bf16)
        sent[at, :] = sums[1].astype(bf16)
    last = dp_count * part_rows
    shared = []
    for plane in range(dp_count):
        shared.append(routes[plane, 0:seq_dev, :])
        partners[plane * seq_dev : (plane + 1) * seq_dev, :] = marks[plane, 0:seq_dev, :]
    seqs = dp_count * seq_dev
    value = jnp.concatenate(shared, axis=0).astype(bf16)
    kept[last : last + seqs, :] = value
    sent[last : last + seqs, :] = value


def hidden_parts(projected):
    half_width = projected.shape[1] // 2
    gate, up = projected[:, :half_width], projected[:, half_width:]
    sigmoid_gate = jax.nn.sigmoid(gate)
    return gate, up, sigmoid_gate, gate * sigmoid_gate


def spread_rows(values, flat):
    count, chunks = values.shape[0], values.shape[1] // lanes
    for chunk in range(chunks):
        flat[pl.ds(chunk, count, stride=chunks), :] = values[:, chunk * lanes : (chunk + 1) * lanes]


def share_of(flat, lane, each, part_rows, chunks):
    size = each * chunks
    start = lane * size
    blocks = [
        flat[pl.ds(pl.multiple_of(start + first, part_rows), part_rows), :]
        for first in range(0, size, part_rows)
    ]
    return blocks[0] if len(blocks) == 1 else jnp.concatenate(blocks, axis=1)


def last_tokens(place, seq_dev, where_tiles, parts, tokens):
    part_rows = parts[0].shape[0]
    dp_count, chunks = tokens.shape[:2]
    chips = len(where_tiles[0])
    share_chunks = chunks // chips
    base = part_rows - seq_dev * share_chunks
    for hop in range(dp_count):
        for chip in range(chips):
            source, row, at = where_tiles[hop][chip]
            tile = parts[source][row : row + part_rows, at : at + lanes].astype(f32)
            first = ((place[1] // 2) ^ chip) * share_chunks
            for chunk in range(share_chunks):
                row = base + chunk * seq_dev
                tokens[place[0] ^ hop, first + chunk, 0:seq_dev, :] = tile[row : row + seq_dev, :]
    joined = []
    for plane in range(dp_count):
        lines = [tokens[plane, chunk, 0:seq_dev, :] for chunk in range(chunks)]
        joined.append(jnp.concatenate(lines, axis=1))
    return jnp.concatenate(joined, axis=0)


def expert_kernel(layout, *refs):
    group, chips, part_rows, seq_dev, where_tiles, used, with_last = layout
    refs = list(refs)
    place = position()
    near = 0 in group
    tokens = refs.pop(0) if near else None
    parts, refs = dict(zip(used, refs)), refs[len(used) :]
    weights, refs = refs[:4], refs[4:]
    n_outs = chips * len(group)
    outs, refs = refs[:n_outs], refs[n_outs:]
    if with_last:
        last_all, last_projected, own_last, flat, seq_tokens, *refs = refs
    (rows,) = refs
    width = weights[0].shape[1]
    total = n_outs * part_rows
    spots = [slice(index * part_rows, (index + 1) * part_rows) for index in range(n_outs)]
    for index, spot in enumerate(spots):
        hop, chip = group[index // chips], index % chips
        if hop:
            source, row, _ = where_tiles[hop][chip]
            rows[spot, :] = parts[source][row : row + part_rows, :width]
        else:
            start = pl.multiple_of((place[1] ^ (2 * chip)) * part_rows, part_rows)
            rows[spot, :] = tokens[pl.ds(start, part_rows), :]
    if with_last:
        floats = last_tokens(place, seq_dev, where_tiles, parts, seq_tokens)
        last_all[...] = floats.astype(bf16)
        rows[total:, :] = floats.astype(bf16)
    hidden = []
    for half in range(2):
        projected = dot(rows[...], weights[2 * half][0])
        if half == 0 and with_last:
            last_projected[...] = projected[total:]
        _, up, _, activated = hidden_parts(projected)
        hidden.append((activated * up).astype(bf16))
    block = min(512, width)
    chunks = width // lanes
    for first in range(0, width, block):
        columns = slice(first, first + block)
        result = dot(hidden[0], weights[1][0, :, columns]) + dot(
            hidden[1], weights[3][0, :, columns]
        )
        for out, spot in zip(outs, spots):
            out[:, columns] = result[spot].astype(bf16)
        if with_last:
            count = result.shape[0] - total
            for at in range(0, block, lanes):
                flat[pl.ds((first + at) // lanes, count, stride=chunks), :] = result[
                    total:, at : at + lanes
                ]
    if with_last:
        each = floats.shape[0] // (2 * chips)
        for chip in range(chips):
            share = share_of(flat, place[1] ^ (2 * chip), each, part_rows, chunks)
            outs[n_outs - chips + chip][:, width:] = share.astype(bf16)
        spread_rows(floats, flat)
        own_last[...] = share_of(flat, place[1], each, part_rows, chunks)


def combine_kernel(layout, kept, found, *refs):
    hop, chips, with_last, width, each = layout
    place = position()
    own, refs = (refs[0], refs[1:]) if hop == 0 else (None, refs)
    last_in, refs = (refs[0], refs[1:]) if hop and not with_last else (None, refs)
    parts, out = refs[:chips], refs[chips]
    part_rows = out.shape[0]
    first_expert = place[2] - place[1] // 2
    experts = [first_expert + ((place[1] // 2) ^ chip) for chip in range(chips)]
    if with_last:
        last_in = refs[-1]
        table = kept[-2 * chips * each :, :].astype(f32) + found[-2 * chips * each :, :].astype(f32)
        row_index = lax.broadcasted_iota(jnp.int32, table.shape, 0)
        chunks = width // lanes
        for row in range(each):
            mine = jnp.where(row_index == place[1] * each + row, table, 0.0)
            mine = jnp.sum(mine, axis=0, keepdims=True)
            first = row * chunks % part_rows
            spot = slice(first, first + chunks)
            at = row * chunks // part_rows * lanes
            total = None
            for chip in range(chips):
                values = parts[chip][spot, width + at : width + at + lanes].astype(f32)
                term = column(mine, experts[chip]) * values
                total = term if total is None else total + term
            last_in[spot, at : at + lanes] = total.astype(bf16)
    at = slice(hop * part_rows, (hop + 1) * part_rows)
    table = kept[at, :].astype(f32) + found[at, :].astype(f32)
    total = None if hop else own[:, :width].astype(f32)
    for chip in range(chips):
        term = column(table, experts[chip]) * parts[chip][:, :width].astype(f32)
        total = term if total is None else total + term
    out[:, :width] = total.astype(out.dtype)
    if hop:
        out[:, width:] = last_in[...]


def finish_kernel(near, own_last, last_sum, *refs):
    parts, out = refs[:-1], refs[-1]
    width = near.shape[1]
    total = near[...]
    last = last_sum[...].astype(f32)
    for part in parts:
        total = total + part[:, :width].astype(f32)
        last = last + part[:, width:].astype(f32)
    out[:, :width] = total.astype(bf16)
    out[:, width:] = (own_last[...] + last).astype(bf16)


def collect_rows(lane, pieces, flat, width):
    part_rows, chunks = pieces[0].shape[0], width // lanes
    count = len(pieces)
    size = flat.shape[0] // count
    for index in range(count):
        source = lane ^ (2 * (index % (count // 2))) ^ (index // (count // 2))
        for first in range(0, size, part_rows):
            at = width + first // part_rows * lanes
            start = pl.multiple_of(source * size + first, part_rows)
            flat[pl.ds(start, part_rows), :] = pieces[index][:, at : at + lanes].astype(f32)
    rows = flat.shape[0] // chunks
    columns = [flat[pl.ds(chunk, rows, stride=chunks), :] for chunk in range(chunks)]
    return jnp.concatenate(columns, axis=1)


def both_ways(coefficient, unit, diagonal):
    count = unit.shape[0]
    if count > 32:
        high = lax.Precision.HIGHEST
        there = dot(coefficient, unit, ((1,), (0,)), high)
        return there + dot(coefficient, unit, ((0,), (0,)), high)
    total = None
    for index in range(count):
        line = jnp.where(diagonal, coefficient[index : index + 1, :], 0.0)
        factor = coefficient[:, index : index + 1] + jnp.sum(line, axis=1, keepdims=True)
        term = factor * unit[index : index + 1, :]
        total = term if total is None else total + term
    return total


def final_kernel(n_pieces, n_blocks, *refs):
    pieces, refs = refs[:n_pieces], refs[n_pieces:]
    last_all, projected, kept, found, partners, down, *refs = refs
    place = position()
    layer_out, grad_in, grad_out, made_in, made_out, flat, sems = refs
    part_rows, width = pieces[0].shape[0], layer_out.shape[1]
    copies = []

    def send(source, target):
        copies.append(pltpu.make_async_copy(source, target, sems.at[len(copies)]))
        copies[-1].start()

    for index in range(n_pieces):
        lane = place[1] ^ (2 * (index % (n_pieces // 2))) ^ (index // (n_pieces // 2))
        start = pl.multiple_of(lane * part_rows, part_rows)
        send(pieces[index].at[:, pl.ds(0, width)], layer_out.at[pl.ds(start, part_rows)])
    values = collect_rows(place[1], pieces, flat, width)
    count = values.shape[0]
    last = kept.shape[0] - count
    table = kept[last:, :].astype(f32) + found[last:, :].astype(f32)
    row = lax.broadcasted_iota(jnp.int32, (count, count), 0)
    col = lax.broadcasted_iota(jnp.int32, (count, count), 1)
    norms = jnp.sqrt(jnp.sum(values * values, axis=1, keepdims=True) + epsilon)
    norms_line = jnp.sum(jnp.where(row == col, norms, 0.0), axis=0, keepdims=True)
    unit = values / norms
    rows = values.astype(bf16)
    scores = dot(rows, rows, ((1,), (1,))) / (norms * norms_line) / logit_divisor
    exp_scores = jnp.where(row != col, jnp.exp(scores), 0.0)
    probabilities = exp_scores / jnp.sum(exp_scores, axis=1, keepdims=True)
    partner = partners[:, :1].astype(jnp.int32)
    coefficient = grad_scale * (probabilities - jnp.where(col == partner, 1.0, 0.0))
    grad_unit = both_ways(coefficient, unit, row == col) / logit_divisor
    projection = jnp.sum(unit * grad_unit, axis=1, keepdims=True)
    grad_last = (grad_unit - unit * projection) / norms
    route_grad = (column(table, place[2]) * grad_last).astype(bf16)
    gate, up, sigmoid_gate, activated = hidden_parts(projected[...])
    hidden = (activated * up).astype(bf16)
    grad_hidden = dot(route_grad, down[0], ((1,), (1,)))
    gate_slope = sigmoid_gate * (1.0 + gate * (1.0 - sigmoid_gate))
    slope = jnp.concatenate([grad_hidden * up * gate_slope, grad_hidden * activated], axis=1)
    slope = slope.astype(bf16)
    block = width // n_blocks
    for index in range(n_blocks):
        spot = slice(index * block, (index + 1) * block)
        made_in[spot, :] = dot(last_all[:, spot], slope, ((0,), (0,))).astype(bf16)
        send(made_in.at[spot], grad_in.at[0, spot])
    made_out[...] = dot(hidden, route_grad, ((0,), (0,))).astype(bf16)
    send(made_out, grad_out.at[0])
    for copy in copies:
        copy.wait()


def body(tokens, expert_ids, gates, positives, gate_up, down):
    dp_count = lax.axis_size("dp")
    expert_count = lax.axis_size("expert")
    chips = expert_count // 2
    experts = dp_count * chips
    tok_dev, width = tokens.shape
    half_width = down.shape[1]
    seq_dev = positives.shape[0]
    seqs = dp_count * seq_dev
    seq_length = tok_dev // seq_dev
    part_rows = tok_dev // expert_count
    assert experts <= lanes and seq_length % tail == 0

    def to_lane(value, step):
        return lax.ppermute(value, "expert", [(j, j ^ step) for j in range(expert_count)])

    def to_plane(value, step):
        return lax.ppermute(value, "dp", [(p, p ^ step) for p in range(dp_count)])

    chip_steps = [2 * step for step in range(1, chips)]
    groups = [range(first, min(first + 2, dp_count)) for first in range(0, dp_count, 2)]

    share = width // chips
    packed = pl.pallas_call(
        functools.partial(pack_kernel, seq_dev),
        out_shape=jax.ShapeDtypeStruct((part_rows, width + lanes), bf16),
        in_specs=[in_hbm] * 4,
        out_specs=in_vmem,
        scratch_shapes=[
            pltpu.VMEM((part_rows, lanes), f32),
            pltpu.VMEM((seq_dev, tail, share), bf16),
            pltpu.VMEM((1, tok_dev), jnp.int32),
            pltpu.VMEM((1, tok_dev), f32),
            pltpu.SMEM((seq_dev,), jnp.int32),
            pltpu.SemaphoreType.DMA((seq_dev + 4,)),
        ],
        cost_estimate=cost(0, 1 << 19),
        name="pack",
    )(positives, expert_ids.T, gates.T, tokens)
    arrivals = {hop: to_plane(packed, hop) for hop in range(1, dp_count)}
    mate_in = to_lane(gate_up, 1)
    mate_out = to_lane(down, 1)
    weights = (gate_up, down, mate_in, mate_out)

    tiles = [packed]
    spots = {}
    received = None
    for group in groups:
        own = [arrivals[hop] for hop in group if hop]
        if group[0] == 0:
            joined = jnp.concatenate(own + [packed[:, width:]], axis=1)
            joined, weights = lax.optimization_barrier((joined, weights))
        else:
            joined = jnp.concatenate(own, axis=0)
            joined, received = lax.optimization_barrier((joined, received))
            tiles[-len(received) :] = received
        first = len(tiles)
        received = [to_lane(joined, step) for step in chip_steps]
        tiles += own + received
        for index, hop in enumerate(group):
            if group[0] == 0:
                place_of = (first, 0, width) if hop else (0, 0, width)
                row, at = 0, width if hop else width + lanes
            else:
                place_of = (first + index, 0, width)
                row, at = index * part_rows, width
            spots[hop] = [place_of] + [
                (first + len(own) + chip, row, at) for chip in range(chips - 1)
            ]
    where_tiles = [spots[hop] for hop in range(dp_count)]

    each = seqs // expert_count
    extra = each * width // part_rows
    assert extra % lanes == 0 and part_rows % (width // lanes) == 0

    def expert(group, after, with_last):
        near = 0 in group
        wanted = range(dp_count) if with_last else [hop for hop in group if hop]
        used = sorted({spot[0] for hop in wanted for spot in where_tiles[hop]})
        parts = [tiles[index] for index in used]
        n_outs = chips * len(group)
        total = n_outs * part_rows + (seqs if with_last else 0)
        out_shape = [jax.ShapeDtypeStruct((part_rows, width), bf16)] * n_outs
        scratch = [pltpu.VMEM((total, width), bf16)]
        if with_last:
            wider = jax.ShapeDtypeStruct((part_rows, width + extra), bf16)
            out_shape[n_outs - chips :] = [wider] * chips
            out_shape += [
                jax.ShapeDtypeStruct((seqs, width), bf16),
                jax.ShapeDtypeStruct((seqs, 2 * half_width), f32),
                jax.ShapeDtypeStruct((part_rows, extra), f32),
            ]
            scratch = [
                pltpu.VMEM((seqs * (width // lanes), lanes), f32),
                pltpu.VMEM((dp_count, width // lanes, -(-seq_dev // 8) * 8, lanes), f32),
            ] + scratch
        if after is not None:
            parts[0], _ = lax.optimization_barrier((parts[0], after))
        operands = [tokens] * near + parts + list(weights)
        layout = (tuple(group), chips, part_rows, seq_dev, where_tiles, used, with_last)
        return pl.pallas_call(
            functools.partial(expert_kernel, layout),
            out_shape=out_shape,
            in_specs=[in_vmem] * len(operands),
            out_specs=[in_vmem] * len(out_shape),
            scratch_shapes=scratch,
            compiler_params=params(32),
            cost_estimate=cost(2 * total * width * 6 * half_width, 12 << 20),
            name="experts",
        )(*operands)

    outs = {}
    after = None
    rest = list(range(dp_count - 2, 1, -1))
    for group in groups:
        with_last = dp_count - 1 in group
        out = expert(group, after, with_last)
        after = out[0]
        for index, hop in enumerate(group):
            outs[hop] = list(out[index * chips : (index + 1) * chips])
        if with_last:
            last_all, last_projected, own_last = out[-3:]
            first_tile, _ = lax.optimization_barrier((tiles[0], out[0]))

    table_rows = dp_count * part_rows + seqs
    chunks = width // lanes
    sublanes = -(-seq_dev // 8) * 8
    tiles[0] = first_tile
    kept, sent, partners = pl.pallas_call(
        functools.partial(table_kernel, (seq_dev, tok_dev, where_tiles, len(tiles))),
        out_shape=[
            jax.ShapeDtypeStruct((table_rows, lanes), bf16),
            jax.ShapeDtypeStruct((table_rows, lanes), bf16),
            jax.ShapeDtypeStruct((seqs, lanes), f32),
        ],
        in_specs=[in_vmem] * len(tiles),
        out_specs=[in_vmem] * 3,
        scratch_shapes=[
            pltpu.VMEM((dp_count, sublanes, lanes), f32),
            pltpu.VMEM((dp_count, sublanes, lanes), f32),
        ],
        compiler_params=params(48 if dp_count > 8 else 12),
        cost_estimate=cost(0, 1 << 20),
        name="tables",
    )(*tiles)
    found = to_lane(sent, 1)

    def combine(hop, parts, last_sum):
        with_last = last_sum is None
        out_shape = [jax.ShapeDtypeStruct((part_rows, width), f32)]
        if hop:
            out_shape = [jax.ShapeDtypeStruct((part_rows, width + extra), bf16)]
        if with_last:
            out_shape.append(jax.ShapeDtypeStruct((part_rows, extra), bf16))
        operands = [kept, found] + [packed] * (hop == 0)
        operands += [last_sum] * (hop > 0 and not with_last) + parts
        return pl.pallas_call(
            functools.partial(combine_kernel, (hop, chips, with_last, width, each)),
            out_shape=out_shape,
            in_specs=[in_vmem] * len(operands),
            out_specs=[in_vmem] * len(out_shape),
            compiler_params=params(8),
            cost_estimate=cost(0, 2 << 20),
            name="combine",
        )(*operands)

    returned = {}

    def send_back(hop, gated, after):
        first, *parts = outs[hop]
        free = len(parts) - gated
        parts[free:], after = lax.optimization_barrier((parts[free:], after))
        returned[hop] = [first] + [to_lane(value, step) for value, step in zip(parts, chip_steps)]
        return after

    send_back(1, 0, [])
    if dp_count > 2:
        returned[1][1:] = send_back(dp_count - 1, chips - 1, returned[1][1:])
    before = dp_count - 1
    for hop in rest:
        returned[before][-1], found = send_back(hop, 1, (returned[before][-1], found))
        before = hop
    homeward = []
    last_sum = None
    for hop in range(dp_count - 1, 0, -1):
        result = combine(hop, returned[hop], last_sum)
        last_sum = result[1] if last_sum is None else last_sum
        homeward.append(to_plane(result[0], hop))
        if hop == min(3, dp_count - 1):
            gate = result[0]
    outs[0][1:], gate = lax.optimization_barrier((outs[0][1:], gate))
    send_back(0, 0, [])
    near_sum = combine(0, returned[0], last_sum)[0]

    own_out = pl.pallas_call(
        finish_kernel,
        out_shape=jax.ShapeDtypeStruct((part_rows, width + extra), bf16),
        in_specs=[in_vmem] * (2 + dp_count),
        out_specs=in_vmem,
        compiler_params=params(16 if dp_count > 8 else 4),
        cost_estimate=cost(0, 1 << 20),
        name="finish",
    )(near_sum, own_last, last_sum, *homeward)
    pieces = [own_out] + [to_lane(own_out, step) for step in chip_steps]
    pieces += [to_lane(piece, 1) for piece in pieces]

    n_blocks = width // min(512, width)
    layer_out, grad_gate_up, grad_down = pl.pallas_call(
        functools.partial(final_kernel, len(pieces), n_blocks),
        out_shape=[
            jax.ShapeDtypeStruct((tok_dev, width), bf16),
            jax.ShapeDtypeStruct(gate_up.shape, bf16),
            jax.ShapeDtypeStruct(down.shape, bf16),
        ],
        in_specs=[in_vmem] * (len(pieces) + 6),
        out_specs=[in_hbm] * 3,
        scratch_shapes=[
            pltpu.VMEM((width, 2 * half_width), bf16),
            pltpu.VMEM((half_width, width), bf16),
            pltpu.VMEM((seqs * (width // lanes), lanes), f32),
            pltpu.SemaphoreType.DMA((len(pieces) + n_blocks + 1,)),
        ],
        compiler_params=params(24),
        cost_estimate=cost(2 * seqs * width * 4 * half_width, 7 << 20),
        name="final",
    )(*pieces, last_all, last_projected, kept, found, partners, down)
    return (layer_out, grad_gate_up, grad_down)


def solution(mesh):
    return jax.shard_map(
        body,
        mesh=mesh,
        in_specs=(
            P("dp", None),
            P("dp", "expert"),
            P("dp", "expert"),
            P("dp"),
            P(("dp", "expert"), None, None),
            P(("dp", "expert"), None, None),
        ),
        out_specs=(P("dp", None), P(("dp", "expert"), None, None), P(("dp", "expert"), None, None)),
        check_vma=False,
    )
```

```python
import functools

import jax
import jax.numpy as jnp
from jax import lax
from jax.experimental import pallas as pl
from jax.experimental.pallas import tpu as pltpu
from jax.sharding import PartitionSpec as P

logit_divisor = 0.05
grad_scale = 256.0
epsilon = 1e-06
lanes = 128
tail = 16
bf16 = jnp.bfloat16
f32 = jnp.float32

in_hbm = pl.BlockSpec(memory_space=pltpu.HBM)
in_vmem = pl.BlockSpec(memory_space=pltpu.VMEM)


def params(mebibytes):
    return pltpu.CompilerParams(vmem_limit_bytes=mebibytes << 20)


def cost(flops, moved):
    return pl.CostEstimate(flops=flops, transcendentals=0, bytes_accessed=moved)


def dot(left, right, dims=((1,), (0,)), precision=None):
    return lax.dot_general(
        left, right, (dims, ((), ())), precision=precision, preferred_element_type=f32
    )


def doublings(count):
    steps = [1 << bit for bit in range((count - 1).bit_length())]
    assert 1 << len(steps) == count
    return steps


def position():
    plane, lane = lax.axis_index("dp"), lax.axis_index("expert")
    return plane, lane, plane * (lax.axis_size("expert") // 2) + lane // 2


def column(table, wanted):
    index = lax.broadcasted_iota(jnp.int32, table.shape, 1)
    return jnp.sum(jnp.where(index == wanted, table, 0.0), axis=1, keepdims=True)


def pack_kernel(
    seq_dev, partners, ids_in, gates_in, tokens, out, tile, rows, ids, gates, positives, sems
):
    part_rows, width = out.shape[0], tokens.shape[1]
    tok_dev = tokens.shape[0]
    seq_length = tok_dev // seq_dev
    share = rows.shape[2]
    lane = lax.axis_index("expert")
    column_at = pl.multiple_of(lane // 2 * share, lanes)
    start = pl.multiple_of(lane * part_rows, part_rows)
    copies = [
        pltpu.make_async_copy(
            tokens.at[pl.ds((seq + 1) * seq_length - tail, tail), pl.ds(column_at, share)],
            rows.at[seq],
            sems.at[seq],
        )
        for seq in range(seq_dev)
    ]
    own = pltpu.make_async_copy(
        tokens.at[pl.ds(start, part_rows)], out.at[:, pl.ds(0, width)], sems.at[seq_dev]
    )
    lines = [
        pltpu.make_async_copy(ids_in, ids, sems.at[seq_dev + 1]),
        pltpu.make_async_copy(gates_in, gates, sems.at[seq_dev + 2]),
        pltpu.make_async_copy(partners, positives, sems.at[seq_dev + 3]),
    ]
    for copy in lines + [own] + copies:
        copy.start()
    note_rows = tok_dev // lanes
    tile[...] = jnp.zeros_like(tile)
    for copy in lines:
        copy.wait()
    for index in range(note_rows):
        block = slice(index * lanes, (index + 1) * lanes)
        tile[index : index + 1, :] = ids[:, block].astype(f32)
        tile[note_rows + index : note_rows + index + 1, :] = gates[:, block]
    for seq in range(seq_dev):
        row = 2 * note_rows + seq
        tile[row : row + 1, :] = jnp.full((1, lanes), positives[seq], jnp.int32).astype(f32)
    base = part_rows - seq_dev * (share // lanes)
    for seq in range(seq_dev):
        copies[seq].wait()
        values = rows[seq].astype(f32)
        for chunk in range(share // lanes):
            row = base + chunk * seq_dev + seq
            tile[row : row + 1, :] = values[tail - 1 : tail, chunk * lanes : (chunk + 1) * lanes]
    out[:, width:] = tile[...].astype(bf16)
    own.wait()


def table_kernel(layout, *refs):
    seq_dev, tok_dev, where_tiles, n_parts = layout
    place = position()
    parts = refs[:n_parts]
    kept, sent, partners, routes, marks = refs[n_parts:]
    part_rows = parts[0].shape[0]
    dp_count = len(where_tiles)
    note_rows = tok_dev // lanes
    seq_length = tok_dev // seq_dev
    chips = len(where_tiles[0])
    lane_index = lax.broadcasted_iota(jnp.int32, (part_rows, lanes), 1)
    row_index = lax.broadcasted_iota(jnp.int32, (part_rows, lanes), 0)

    def dense_rows(tile, lane):
        start = lane * part_rows
        picked = lane_index == row_index + start % lanes
        found = []
        for offset in (0, note_rows):
            line = tile[offset : offset + 1, :]
            for index in range(1, note_rows):
                other = tile[offset + index : offset + index + 1, :]
                line = jnp.where(start // lanes == index, other, line)
            found.append(jnp.sum(jnp.where(picked, line, 0.0), axis=1, keepdims=True))
        return jnp.where(lane_index.astype(f32) == found[0], found[1], 0.0)

    for hop in range(dp_count):
        plane = place[0] ^ hop
        sums = [None, None]
        for chip in range(chips):
            source, row, at = where_tiles[hop][chip]
            tile = parts[source][row : row + part_rows, at : at + lanes].astype(f32)
            for index, lane in enumerate((place[1], place[1] ^ 1)):
                value = dense_rows(tile, lane)
                sums[index] = value if chip == 0 else sums[index] + value
            for seq in range(seq_dev):
                at_token = (seq + 1) * seq_length - 1
                row = at_token // lanes
                here = lane_index[:1] == at_token % lanes
                expert, gate = [
                    jnp.sum(
                        jnp.where(here, tile[offset + row : offset + row + 1, :], 0.0),
                        axis=1,
                        keepdims=True,
                    )
                    for offset in (0, note_rows)
                ]
                value = jnp.where(lane_index[:1].astype(f32) == expert, gate, 0.0)
                if chip:
                    value = value + routes[plane, seq : seq + 1, :]
                routes[plane, seq : seq + 1, :] = value
            if chip == 0:
                marks[plane, 0:seq_dev, :] = tile[2 * note_rows : 2 * note_rows + seq_dev, :]
        at = slice(hop * part_rows, (hop + 1) * part_rows)
        kept[at, :] = sums[0].astype(bf16)
        sent[at, :] = sums[1].astype(bf16)
    last = dp_count * part_rows
    shared = []
    for plane in range(dp_count):
        shared.append(routes[plane, 0:seq_dev, :])
        partners[plane * seq_dev : (plane + 1) * seq_dev, :] = marks[plane, 0:seq_dev, :]
    seqs = dp_count * seq_dev
    value = jnp.concatenate(shared, axis=0).astype(bf16)
    kept[last : last + seqs, :] = value
    sent[last : last + seqs, :] = value


def hidden_parts(projected):
    half_width = projected.shape[1] // 2
    gate, up = projected[:, :half_width], projected[:, half_width:]
    sigmoid_gate = jax.nn.sigmoid(gate)
    return gate, up, sigmoid_gate, gate * sigmoid_gate


def spread_rows(values, flat):
    count, chunks = values.shape[0], values.shape[1] // lanes
    for chunk in range(chunks):
        flat[pl.ds(chunk, count, stride=chunks), :] = values[:, chunk * lanes : (chunk + 1) * lanes]


def share_of(flat, lane, each, part_rows, chunks):
    size = each * chunks
    start = lane * size
    blocks = [
        flat[pl.ds(pl.multiple_of(start + first, part_rows), part_rows), :]
        for first in range(0, size, part_rows)
    ]
    return blocks[0] if len(blocks) == 1 else jnp.concatenate(blocks, axis=1)


def last_tokens(place, seq_dev, where_tiles, parts, tokens):
    part_rows = parts[0].shape[0]
    dp_count, chunks = tokens.shape[:2]
    chips = len(where_tiles[0])
    share_chunks = chunks // chips
    base = part_rows - seq_dev * share_chunks
    for hop in range(dp_count):
        for chip in range(chips):
            source, row, at = where_tiles[hop][chip]
            tile = parts[source][row : row + part_rows, at : at + lanes].astype(f32)
            first = ((place[1] // 2) ^ chip) * share_chunks
            for chunk in range(share_chunks):
                row = base + chunk * seq_dev
                tokens[place[0] ^ hop, first + chunk, 0:seq_dev, :] = tile[row : row + seq_dev, :]
    joined = []
    for plane in range(dp_count):
        lines = [tokens[plane, chunk, 0:seq_dev, :] for chunk in range(chunks)]
        joined.append(jnp.concatenate(lines, axis=1))
    return jnp.concatenate(joined, axis=0)


def expert_kernel(layout, *refs):
    group, chips, part_rows, seq_dev, where_tiles, used, with_last = layout
    refs = list(refs)
    place = position()
    near = 0 in group
    tokens = refs.pop(0) if near else None
    parts, refs = dict(zip(used, refs)), refs[len(used) :]
    weights, refs = refs[:4], refs[4:]
    n_outs = chips * len(group)
    outs, refs = refs[:n_outs], refs[n_outs:]
    if with_last:
        last_all, last_projected, own_last, flat, seq_tokens, *refs = refs
    (rows,) = refs
    width = weights[0].shape[1]
    total = n_outs * part_rows
    spots = [slice(index * part_rows, (index + 1) * part_rows) for index in range(n_outs)]
    for index, spot in enumerate(spots):
        hop, chip = group[index // chips], index % chips
        if hop:
            source, row, _ = where_tiles[hop][chip]
            rows[spot, :] = parts[source][row : row + part_rows, :width]
        else:
            start = pl.multiple_of((place[1] ^ (2 * chip)) * part_rows, part_rows)
            rows[spot, :] = tokens[pl.ds(start, part_rows), :]
    if with_last:
        floats = last_tokens(place, seq_dev, where_tiles, parts, seq_tokens)
        last_all[...] = floats.astype(bf16)
        rows[total:, :] = floats.astype(bf16)
    hidden = []
    for half in range(2):
        projected = dot(rows[...], weights[2 * half][0])
        if half == 0 and with_last:
            last_projected[...] = projected[total:]
        _, up, _, activated = hidden_parts(projected)
        hidden.append((activated * up).astype(bf16))
    block = min(512, width)
    chunks = width // lanes
    for first in range(0, width, block):
        columns = slice(first, first + block)
        result = dot(hidden[0], weights[1][0, :, columns]) + dot(
            hidden[1], weights[3][0, :, columns]
        )
        for out, spot in zip(outs, spots):
            out[:, columns] = result[spot].astype(bf16)
        if with_last:
            count = result.shape[0] - total
            for at in range(0, block, lanes):
                flat[pl.ds((first + at) // lanes, count, stride=chunks), :] = result[
                    total:, at : at + lanes
                ]
    if with_last:
        each = floats.shape[0] // (2 * chips)
        for chip in range(chips):
            share = share_of(flat, place[1] ^ (2 * chip), each, part_rows, chunks)
            outs[n_outs - chips + chip][:, width:] = share.astype(bf16)
        spread_rows(floats, flat)
        own_last[...] = share_of(flat, place[1], each, part_rows, chunks)


def combine_kernel(layout, kept, found, *refs):
    hop, chips, with_last, width, each = layout
    place = position()
    own, refs = (refs[0], refs[1:]) if hop == 0 else (None, refs)
    last_in, refs = (refs[0], refs[1:]) if hop and not with_last else (None, refs)
    parts, out = refs[:chips], refs[chips]
    part_rows = out.shape[0]
    first_expert = place[2] - place[1] // 2
    experts = [first_expert + ((place[1] // 2) ^ chip) for chip in range(chips)]
    if with_last:
        last_in = refs[-1]
        table = kept[-2 * chips * each :, :].astype(f32) + found[-2 * chips * each :, :].astype(f32)
        row_index = lax.broadcasted_iota(jnp.int32, table.shape, 0)
        chunks = width // lanes
        for row in range(each):
            mine = jnp.where(row_index == place[1] * each + row, table, 0.0)
            mine = jnp.sum(mine, axis=0, keepdims=True)
            first = row * chunks % part_rows
            spot = slice(first, first + chunks)
            at = row * chunks // part_rows * lanes
            total = None
            for chip in range(chips):
                values = parts[chip][spot, width + at : width + at + lanes].astype(f32)
                term = column(mine, experts[chip]) * values
                total = term if total is None else total + term
            last_in[spot, at : at + lanes] = total.astype(bf16)
    at = slice(hop * part_rows, (hop + 1) * part_rows)
    table = kept[at, :].astype(f32) + found[at, :].astype(f32)
    total = None if hop else own[:, :width].astype(f32)
    for chip in range(chips):
        term = column(table, experts[chip]) * parts[chip][:, :width].astype(f32)
        total = term if total is None else total + term
    out[:, :width] = total.astype(out.dtype)
    if hop:
        out[:, width:] = last_in[...]


def finish_kernel(near, own_last, last_sum, *refs):
    parts, out = refs[:-1], refs[-1]
    width = near.shape[1]
    total = near[...]
    last = last_sum[...].astype(f32)
    for part in parts:
        total = total + part[:, :width].astype(f32)
        last = last + part[:, width:].astype(f32)
    out[:, :width] = total.astype(bf16)
    out[:, width:] = (own_last[...] + last).astype(bf16)


def collect_rows(lane, pieces, flat, width):
    part_rows, chunks = pieces[0].shape[0], width // lanes
    count = len(pieces)
    size = flat.shape[0] // count
    for index in range(count):
        source = lane ^ (2 * (index % (count // 2))) ^ (index // (count // 2))
        for first in range(0, size, part_rows):
            at = width + first // part_rows * lanes
            start = pl.multiple_of(source * size + first, part_rows)
            flat[pl.ds(start, part_rows), :] = pieces[index][:, at : at + lanes].astype(f32)
    rows = flat.shape[0] // chunks
    columns = [flat[pl.ds(chunk, rows, stride=chunks), :] for chunk in range(chunks)]
    return jnp.concatenate(columns, axis=1)


def both_ways(coefficient, unit, diagonal):
    count = unit.shape[0]
    if count > 32:
        high = lax.Precision.HIGHEST
        there = dot(coefficient, unit, ((1,), (0,)), high)
        return there + dot(coefficient, unit, ((0,), (0,)), high)
    total = None
    for index in range(count):
        line = jnp.where(diagonal, coefficient[index : index + 1, :], 0.0)
        factor = coefficient[:, index : index + 1] + jnp.sum(line, axis=1, keepdims=True)
        term = factor * unit[index : index + 1, :]
        total = term if total is None else total + term
    return total


def final_kernel(n_pieces, n_blocks, *refs):
    pieces, refs = refs[:n_pieces], refs[n_pieces:]
    last_all, projected, kept, found, partners, down, *refs = refs
    place = position()
    layer_out, grad_in, grad_out, made_in, made_out, flat, sems = refs
    part_rows, width = pieces[0].shape[0], layer_out.shape[1]
    copies = []

    def send(source, target):
        copies.append(pltpu.make_async_copy(source, target, sems.at[len(copies)]))
        copies[-1].start()

    for index in range(n_pieces):
        lane = place[1] ^ (2 * (index % (n_pieces // 2))) ^ (index // (n_pieces // 2))
        start = pl.multiple_of(lane * part_rows, part_rows)
        send(pieces[index].at[:, pl.ds(0, width)], layer_out.at[pl.ds(start, part_rows)])
    values = collect_rows(place[1], pieces, flat, width)
    count = values.shape[0]
    last = kept.shape[0] - count
    table = kept[last:, :].astype(f32) + found[last:, :].astype(f32)
    row = lax.broadcasted_iota(jnp.int32, (count, count), 0)
    col = lax.broadcasted_iota(jnp.int32, (count, count), 1)
    norms = jnp.sqrt(jnp.sum(values * values, axis=1, keepdims=True) + epsilon)
    norms_line = jnp.sum(jnp.where(row == col, norms, 0.0), axis=0, keepdims=True)
    unit = values / norms
    rows = values.astype(bf16)
    scores = dot(rows, rows, ((1,), (1,))) / (norms * norms_line) / logit_divisor
    exp_scores = jnp.where(row != col, jnp.exp(scores), 0.0)
    probabilities = exp_scores / jnp.sum(exp_scores, axis=1, keepdims=True)
    partner = partners[:, :1].astype(jnp.int32)
    coefficient = grad_scale * (probabilities - jnp.where(col == partner, 1.0, 0.0))
    grad_unit = both_ways(coefficient, unit, row == col) / logit_divisor
    projection = jnp.sum(unit * grad_unit, axis=1, keepdims=True)
    grad_last = (grad_unit - unit * projection) / norms
    route_grad = (column(table, place[2]) * grad_last).astype(bf16)
    gate, up, sigmoid_gate, activated = hidden_parts(projected[...])
    hidden = (activated * up).astype(bf16)
    grad_hidden = dot(route_grad, down[0], ((1,), (1,)))
    gate_slope = sigmoid_gate * (1.0 + gate * (1.0 - sigmoid_gate))
    slope = jnp.concatenate([grad_hidden * up * gate_slope, grad_hidden * activated], axis=1)
    slope = slope.astype(bf16)
    block = width // n_blocks
    for index in range(n_blocks):
        spot = slice(index * block, (index + 1) * block)
        made_in[spot, :] = dot(last_all[:, spot], slope, ((0,), (0,))).astype(bf16)
        send(made_in.at[spot], grad_in.at[0, spot])
    made_out[...] = dot(hidden, route_grad, ((0,), (0,))).astype(bf16)
    send(made_out, grad_out.at[0])
    for copy in copies:
        copy.wait()


def body(tokens, expert_ids, gates, positives, gate_up, down):
    dp_count = lax.axis_size("dp")
    expert_count = lax.axis_size("expert")
    chips = expert_count // 2
    experts = dp_count * chips
    tok_dev, width = tokens.shape
    half_width = down.shape[1]
    seq_dev = positives.shape[0]
    seqs = dp_count * seq_dev
    seq_length = tok_dev // seq_dev
    part_rows = tok_dev // expert_count
    assert experts <= lanes and seq_length % tail == 0

    def to_lane(value, step):
        return lax.ppermute(value, "expert", [(j, j ^ step) for j in range(expert_count)])

    def to_plane(value, step):
        return lax.ppermute(value, "dp", [(p, p ^ step) for p in range(dp_count)])

    chip_steps = [2 * step for step in range(1, chips)]
    groups = [range(first, min(first + 2, dp_count)) for first in range(0, dp_count, 2)]

    share = width // chips
    packed = pl.pallas_call(
        functools.partial(pack_kernel, seq_dev),
        out_shape=jax.ShapeDtypeStruct((part_rows, width + lanes), bf16),
        in_specs=[in_hbm] * 4,
        out_specs=in_vmem,
        scratch_shapes=[
            pltpu.VMEM((part_rows, lanes), f32),
            pltpu.VMEM((seq_dev, tail, share), bf16),
            pltpu.VMEM((1, tok_dev), jnp.int32),
            pltpu.VMEM((1, tok_dev), f32),
            pltpu.SMEM((seq_dev,), jnp.int32),
            pltpu.SemaphoreType.DMA((seq_dev + 4,)),
        ],
        cost_estimate=cost(0, 1 << 19),
        name="pack",
    )(positives, expert_ids.T, gates.T, tokens)
    arrivals = {hop: to_plane(packed, hop) for hop in range(1, dp_count)}
    mate_in = to_lane(gate_up, 1)
    mate_out = to_lane(down, 1)
    weights = (gate_up, down, mate_in, mate_out)

    tiles = [packed]
    spots = {}
    received = None
    for group in groups:
        own = [arrivals[hop] for hop in group if hop]
        if group[0] == 0:
            joined = jnp.concatenate(own + [packed[:, width:]], axis=1)
            joined, weights = lax.optimization_barrier((joined, weights))
        else:
            joined = jnp.concatenate(own, axis=0)
            joined, received = lax.optimization_barrier((joined, received))
            tiles[-len(received) :] = received
        first = len(tiles)
        received = [to_lane(joined, step) for step in chip_steps]
        tiles += own + received
        for index, hop in enumerate(group):
            if group[0] == 0:
                place_of = (first, 0, width) if hop else (0, 0, width)
                row, at = 0, width if hop else width + lanes
            else:
                place_of = (first + index, 0, width)
                row, at = index * part_rows, width
            spots[hop] = [place_of] + [
                (first + len(own) + chip, row, at) for chip in range(chips - 1)
            ]
    where_tiles = [spots[hop] for hop in range(dp_count)]

    each = seqs // expert_count
    extra = each * width // part_rows
    assert extra % lanes == 0 and part_rows % (width // lanes) == 0

    def expert(group, after, with_last):
        near = 0 in group
        wanted = range(dp_count) if with_last else [hop for hop in group if hop]
        used = sorted({spot[0] for hop in wanted for spot in where_tiles[hop]})
        parts = [tiles[index] for index in used]
        n_outs = chips * len(group)
        total = n_outs * part_rows + (seqs if with_last else 0)
        out_shape = [jax.ShapeDtypeStruct((part_rows, width), bf16)] * n_outs
        scratch = [pltpu.VMEM((total, width), bf16)]
        if with_last:
            wider = jax.ShapeDtypeStruct((part_rows, width + extra), bf16)
            out_shape[n_outs - chips :] = [wider] * chips
            out_shape += [
                jax.ShapeDtypeStruct((seqs, width), bf16),
                jax.ShapeDtypeStruct((seqs, 2 * half_width), f32),
                jax.ShapeDtypeStruct((part_rows, extra), f32),
            ]
            scratch = [
                pltpu.VMEM((seqs * (width // lanes), lanes), f32),
                pltpu.VMEM((dp_count, width // lanes, -(-seq_dev // 8) * 8, lanes), f32),
            ] + scratch
        if after is not None:
            parts[0], _ = lax.optimization_barrier((parts[0], after))
        operands = [tokens] * near + parts + list(weights)
        layout = (tuple(group), chips, part_rows, seq_dev, where_tiles, used, with_last)
        return pl.pallas_call(
            functools.partial(expert_kernel, layout),
            out_shape=out_shape,
            in_specs=[in_vmem] * len(operands),
            out_specs=[in_vmem] * len(out_shape),
            scratch_shapes=scratch,
            compiler_params=params(32),
            cost_estimate=cost(2 * total * width * 6 * half_width, 12 << 20),
            name="experts",
        )(*operands)

    outs = {}
    after = None
    rest = list(range(dp_count - 2, 1, -1))
    for group in groups:
        with_last = dp_count - 1 in group
        out = expert(group, after, with_last)
        after = out[0]
        for index, hop in enumerate(group):
            outs[hop] = list(out[index * chips : (index + 1) * chips])
        if with_last:
            last_all, last_projected, own_last = out[-3:]
            first_tile, _ = lax.optimization_barrier((tiles[0], out[0]))

    table_rows = dp_count * part_rows + seqs
    chunks = width // lanes
    sublanes = -(-seq_dev // 8) * 8
    tiles[0] = first_tile
    kept, sent, partners = pl.pallas_call(
        functools.partial(table_kernel, (seq_dev, tok_dev, where_tiles, len(tiles))),
        out_shape=[
            jax.ShapeDtypeStruct((table_rows, lanes), bf16),
            jax.ShapeDtypeStruct((table_rows, lanes), bf16),
            jax.ShapeDtypeStruct((seqs, lanes), f32),
        ],
        in_specs=[in_vmem] * len(tiles),
        out_specs=[in_vmem] * 3,
        scratch_shapes=[
            pltpu.VMEM((dp_count, sublanes, lanes), f32),
            pltpu.VMEM((dp_count, sublanes, lanes), f32),
        ],
        compiler_params=params(48 if dp_count > 8 else 12),
        cost_estimate=cost(0, 1 << 20),
        name="tables",
    )(*tiles)
    found = to_lane(sent, 1)

    def combine(hop, parts, last_sum):
        with_last = last_sum is None
        out_shape = [jax.ShapeDtypeStruct((part_rows, width), f32)]
        if hop:
            out_shape = [jax.ShapeDtypeStruct((part_rows, width + extra), bf16)]
        if with_last:
            out_shape.append(jax.ShapeDtypeStruct((part_rows, extra), bf16))
        operands = [kept, found] + [packed] * (hop == 0)
        operands += [last_sum] * (hop > 0 and not with_last) + parts
        return pl.pallas_call(
            functools.partial(combine_kernel, (hop, chips, with_last, width, each)),
            out_shape=out_shape,
            in_specs=[in_vmem] * len(operands),
            out_specs=[in_vmem] * len(out_shape),
            compiler_params=params(8),
            cost_estimate=cost(0, 2 << 20),
            name="combine",
        )(*operands)

    returned = {}

    def send_back(hop, gated, after):
        first, *parts = outs[hop]
        free = len(parts) - gated
        parts[free:], after = lax.optimization_barrier((parts[free:], after))
        returned[hop] = [first] + [to_lane(value, step) for value, step in zip(parts, chip_steps)]
        return after

    send_back(1, 0, [])
    if dp_count > 2:
        returned[1][1:] = send_back(dp_count - 1, chips - 1, returned[1][1:])
    before = dp_count - 1
    for hop in rest:
        returned[before][-1], found = send_back(hop, 1, (returned[before][-1], found))
        before = hop
    homeward = []
    last_sum = None
    for hop in range(dp_count - 1, 0, -1):
        result = combine(hop, returned[hop], last_sum)
        last_sum = result[1] if last_sum is None else last_sum
        homeward.append(to_plane(result[0], hop))
        if hop == min(3, dp_count - 1):
            gate = result[0]
        if hop == min(2, dp_count - 1):
            near_gate = result[0]
    outs[0][-1], gate = lax.optimization_barrier((outs[0][-1], gate))
    outs[0][1:-1], near_gate = lax.optimization_barrier((outs[0][1:-1], near_gate))
    send_back(0, 0, [])
    near_sum = combine(0, returned[0], last_sum)[0]

    own_out = pl.pallas_call(
        finish_kernel,
        out_shape=jax.ShapeDtypeStruct((part_rows, width + extra), bf16),
        in_specs=[in_vmem] * (2 + dp_count),
        out_specs=in_vmem,
        compiler_params=params(16 if dp_count > 8 else 4),
        cost_estimate=cost(0, 1 << 20),
        name="finish",
    )(near_sum, own_last, last_sum, *homeward)
    pieces = [own_out] + [to_lane(own_out, step) for step in chip_steps]
    pieces += [to_lane(piece, 1) for piece in pieces]

    n_blocks = width // min(512, width)
    layer_out, grad_gate_up, grad_down = pl.pallas_call(
        functools.partial(final_kernel, len(pieces), n_blocks),
        out_shape=[
            jax.ShapeDtypeStruct((tok_dev, width), bf16),
            jax.ShapeDtypeStruct(gate_up.shape, bf16),
            jax.ShapeDtypeStruct(down.shape, bf16),
        ],
        in_specs=[in_vmem] * (len(pieces) + 6),
        out_specs=[in_hbm] * 3,
        scratch_shapes=[
            pltpu.VMEM((width, 2 * half_width), bf16),
            pltpu.VMEM((half_width, width), bf16),
            pltpu.VMEM((seqs * (width // lanes), lanes), f32),
            pltpu.SemaphoreType.DMA((len(pieces) + n_blocks + 1,)),
        ],
        compiler_params=params(24),
        cost_estimate=cost(2 * seqs * width * 4 * half_width, 7 << 20),
        name="final",
    )(*pieces, last_all, last_projected, kept, found, partners, down)
    return (layer_out, grad_gate_up, grad_down)


def solution(mesh):
    return jax.shard_map(
        body,
        mesh=mesh,
        in_specs=(
            P("dp", None),
            P("dp", "expert"),
            P("dp", "expert"),
            P("dp"),
            P(("dp", "expert"), None, None),
            P(("dp", "expert"), None, None),
        ),
        out_specs=(P("dp", None), P(("dp", "expert"), None, None), P(("dp", "expert"), None, None)),
        check_vma=False,
    )
```

```python
import functools

import jax
import jax.numpy as jnp
from jax import lax
from jax.experimental import pallas as pl
from jax.experimental.pallas import tpu as pltpu
from jax.sharding import PartitionSpec as P

logit_divisor = 0.05
grad_scale = 256.0
epsilon = 1e-06
lanes = 128
tail = 16
bf16 = jnp.bfloat16
f32 = jnp.float32

in_hbm = pl.BlockSpec(memory_space=pltpu.HBM)
in_vmem = pl.BlockSpec(memory_space=pltpu.VMEM)


def params(mebibytes):
    return pltpu.CompilerParams(vmem_limit_bytes=mebibytes << 20)


def cost(flops, moved):
    return pl.CostEstimate(flops=flops, transcendentals=0, bytes_accessed=moved)


def dot(left, right, dims=((1,), (0,)), precision=None):
    return lax.dot_general(
        left, right, (dims, ((), ())), precision=precision, preferred_element_type=f32
    )


def doublings(count):
    steps = [1 << bit for bit in range((count - 1).bit_length())]
    assert 1 << len(steps) == count
    return steps


def position():
    plane, lane = lax.axis_index("dp"), lax.axis_index("expert")
    return plane, lane, plane * (lax.axis_size("expert") // 2) + lane // 2


def column(table, wanted):
    index = lax.broadcasted_iota(jnp.int32, table.shape, 1)
    return jnp.sum(jnp.where(index == wanted, table, 0.0), axis=1, keepdims=True)


def pack_kernel(
    seq_dev, partners, ids_in, gates_in, tokens, out, tile, rows, ids, gates, positives, sems
):
    part_rows, width = out.shape[0], tokens.shape[1]
    tok_dev = tokens.shape[0]
    seq_length = tok_dev // seq_dev
    share = rows.shape[2]
    lane = lax.axis_index("expert")
    column_at = pl.multiple_of(lane // 2 * share, lanes)
    start = pl.multiple_of(lane * part_rows, part_rows)
    copies = [
        pltpu.make_async_copy(
            tokens.at[pl.ds((seq + 1) * seq_length - tail, tail), pl.ds(column_at, share)],
            rows.at[seq],
            sems.at[seq],
        )
        for seq in range(seq_dev)
    ]
    own = pltpu.make_async_copy(
        tokens.at[pl.ds(start, part_rows)], out.at[:, pl.ds(0, width)], sems.at[seq_dev]
    )
    lines = [
        pltpu.make_async_copy(ids_in, ids, sems.at[seq_dev + 1]),
        pltpu.make_async_copy(gates_in, gates, sems.at[seq_dev + 2]),
        pltpu.make_async_copy(partners, positives, sems.at[seq_dev + 3]),
    ]
    for copy in lines + [own] + copies:
        copy.start()
    note_rows = tok_dev // lanes
    tile[...] = jnp.zeros_like(tile)
    for copy in lines:
        copy.wait()
    for index in range(note_rows):
        block = slice(index * lanes, (index + 1) * lanes)
        tile[index : index + 1, :] = ids[:, block].astype(f32)
        tile[note_rows + index : note_rows + index + 1, :] = gates[:, block]
    for seq in range(seq_dev):
        row = 2 * note_rows + seq
        tile[row : row + 1, :] = jnp.full((1, lanes), positives[seq], jnp.int32).astype(f32)
    base = part_rows - seq_dev * (share // lanes)
    for seq in range(seq_dev):
        copies[seq].wait()
        values = rows[seq].astype(f32)
        for chunk in range(share // lanes):
            row = base + chunk * seq_dev + seq
            tile[row : row + 1, :] = values[tail - 1 : tail, chunk * lanes : (chunk + 1) * lanes]
    out[:, width:] = tile[...].astype(bf16)
    own.wait()


def table_kernel(layout, *refs):
    seq_dev, tok_dev, where_tiles, n_parts = layout
    place = position()
    parts = refs[:n_parts]
    kept, sent, partners, routes, marks = refs[n_parts:]
    part_rows = parts[0].shape[0]
    dp_count = len(where_tiles)
    note_rows = tok_dev // lanes
    seq_length = tok_dev // seq_dev
    chips = len(where_tiles[0])
    lane_index = lax.broadcasted_iota(jnp.int32, (part_rows, lanes), 1)
    row_index = lax.broadcasted_iota(jnp.int32, (part_rows, lanes), 0)

    def dense_rows(tile, lane):
        start = lane * part_rows
        picked = lane_index == row_index + start % lanes
        found = []
        for offset in (0, note_rows):
            line = tile[offset : offset + 1, :]
            for index in range(1, note_rows):
                other = tile[offset + index : offset + index + 1, :]
                line = jnp.where(start // lanes == index, other, line)
            found.append(jnp.sum(jnp.where(picked, line, 0.0), axis=1, keepdims=True))
        return jnp.where(lane_index.astype(f32) == found[0], found[1], 0.0)

    for hop in range(dp_count):
        plane = place[0] ^ hop
        sums = [None, None]
        for chip in range(chips):
            source, row, at = where_tiles[hop][chip]
            tile = parts[source][row : row + part_rows, at : at + lanes].astype(f32)
            for index, lane in enumerate((place[1], place[1] ^ 1)):
                value = dense_rows(tile, lane)
                sums[index] = value if chip == 0 else sums[index] + value
            for seq in range(seq_dev):
                at_token = (seq + 1) * seq_length - 1
                row = at_token // lanes
                here = lane_index[:1] == at_token % lanes
                expert, gate = [
                    jnp.sum(
                        jnp.where(here, tile[offset + row : offset + row + 1, :], 0.0),
                        axis=1,
                        keepdims=True,
                    )
                    for offset in (0, note_rows)
                ]
                value = jnp.where(lane_index[:1].astype(f32) == expert, gate, 0.0)
                if chip:
                    value = value + routes[plane, seq : seq + 1, :]
                routes[plane, seq : seq + 1, :] = value
            if chip == 0:
                marks[plane, 0:seq_dev, :] = tile[2 * note_rows : 2 * note_rows + seq_dev, :]
        at = slice(hop * part_rows, (hop + 1) * part_rows)
        kept[at, :] = sums[0].astype(bf16)
        sent[at, :] = sums[1].astype(bf16)
    last = dp_count * part_rows
    shared = []
    for plane in range(dp_count):
        shared.append(routes[plane, 0:seq_dev, :])
        partners[plane * seq_dev : (plane + 1) * seq_dev, :] = marks[plane, 0:seq_dev, :]
    seqs = dp_count * seq_dev
    value = jnp.concatenate(shared, axis=0).astype(bf16)
    kept[last : last + seqs, :] = value
    sent[last : last + seqs, :] = value


def hidden_parts(projected):
    half_width = projected.shape[1] // 2
    gate, up = projected[:, :half_width], projected[:, half_width:]
    sigmoid_gate = jax.nn.sigmoid(gate)
    return gate, up, sigmoid_gate, gate * sigmoid_gate


def spread_rows(values, flat):
    count, chunks = values.shape[0], values.shape[1] // lanes
    for chunk in range(chunks):
        flat[pl.ds(chunk, count, stride=chunks), :] = values[:, chunk * lanes : (chunk + 1) * lanes]


def share_of(flat, lane, each, part_rows, chunks):
    size = each * chunks
    start = lane * size
    blocks = [
        flat[pl.ds(pl.multiple_of(start + first, part_rows), part_rows), :]
        for first in range(0, size, part_rows)
    ]
    return blocks[0] if len(blocks) == 1 else jnp.concatenate(blocks, axis=1)


def last_tokens(place, seq_dev, where_tiles, parts, tokens):
    part_rows = parts[0].shape[0]
    dp_count, chunks = tokens.shape[:2]
    chips = len(where_tiles[0])
    share_chunks = chunks // chips
    base = part_rows - seq_dev * share_chunks
    for hop in range(dp_count):
        for chip in range(chips):
            source, row, at = where_tiles[hop][chip]
            tile = parts[source][row : row + part_rows, at : at + lanes].astype(f32)
            first = ((place[1] // 2) ^ chip) * share_chunks
            for chunk in range(share_chunks):
                row = base + chunk * seq_dev
                tokens[place[0] ^ hop, first + chunk, 0:seq_dev, :] = tile[row : row + seq_dev, :]
    joined = []
    for plane in range(dp_count):
        lines = [tokens[plane, chunk, 0:seq_dev, :] for chunk in range(chunks)]
        joined.append(jnp.concatenate(lines, axis=1))
    return jnp.concatenate(joined, axis=0)


def expert_kernel(layout, *refs):
    group, chips, part_rows, seq_dev, where_tiles, used, with_last = layout
    refs = list(refs)
    place = position()
    near = 0 in group
    tokens = refs.pop(0) if near else None
    parts, refs = dict(zip(used, refs)), refs[len(used) :]
    weights, refs = refs[:4], refs[4:]
    n_outs = chips * len(group)
    outs, refs = refs[:n_outs], refs[n_outs:]
    if with_last:
        last_all, last_projected, own_last, flat, seq_tokens, *refs = refs
    rows, sems = refs
    width = weights[0].shape[1]
    total = n_outs * part_rows
    copies = []
    spots = [slice(index * part_rows, (index + 1) * part_rows) for index in range(n_outs)]
    for index, spot in enumerate(spots):
        hop, chip = group[index // chips], index % chips
        if hop:
            source, row, _ = where_tiles[hop][chip]
            rows[spot, :] = parts[source][row : row + part_rows, :width]
        else:
            start = pl.multiple_of((place[1] ^ (2 * chip)) * part_rows, part_rows)
            copies.append(
                pltpu.make_async_copy(
                    tokens.at[pl.ds(start, part_rows)], rows.at[pl.ds(spot.start, part_rows)],
                    sems.at[chip],
                )
            )
            copies[-1].start()
    if with_last:
        floats = last_tokens(place, seq_dev, where_tiles, parts, seq_tokens)
        last_all[...] = floats.astype(bf16)
        rows[total:, :] = floats.astype(bf16)
    for copy in copies:
        copy.wait()
    hidden = []
    for half in range(2):
        projected = dot(rows[...], weights[2 * half][0])
        if half == 0 and with_last:
            last_projected[...] = projected[total:]
        _, up, _, activated = hidden_parts(projected)
        hidden.append((activated * up).astype(bf16))
    block = min(512, width)
    chunks = width // lanes
    for first in range(0, width, block):
        columns = slice(first, first + block)
        result = dot(hidden[0], weights[1][0, :, columns]) + dot(
            hidden[1], weights[3][0, :, columns]
        )
        for out, spot in zip(outs, spots):
            out[:, columns] = result[spot].astype(bf16)
        if with_last:
            count = result.shape[0] - total
            for at in range(0, block, lanes):
                flat[pl.ds((first + at) // lanes, count, stride=chunks), :] = result[
                    total:, at : at + lanes
                ]
    if with_last:
        each = floats.shape[0] // (2 * chips)
        for chip in range(chips):
            share = share_of(flat, place[1] ^ (2 * chip), each, part_rows, chunks)
            outs[n_outs - chips + chip][:, width:] = share.astype(bf16)
        spread_rows(floats, flat)
        own_last[...] = share_of(flat, place[1], each, part_rows, chunks)


def combine_kernel(layout, kept, found, *refs):
    hop, chips, with_last, width, each = layout
    place = position()
    own, refs = (refs[0], refs[1:]) if hop == 0 else (None, refs)
    last_in, refs = (refs[0], refs[1:]) if hop and not with_last else (None, refs)
    parts, out = refs[:chips], refs[chips]
    part_rows = out.shape[0]
    first_expert = place[2] - place[1] // 2
    experts = [first_expert + ((place[1] // 2) ^ chip) for chip in range(chips)]
    if with_last:
        last_in = refs[-1]
        table = kept[-2 * chips * each :, :].astype(f32) + found[-2 * chips * each :, :].astype(f32)
        row_index = lax.broadcasted_iota(jnp.int32, table.shape, 0)
        chunks = width // lanes
        for row in range(each):
            mine = jnp.where(row_index == place[1] * each + row, table, 0.0)
            mine = jnp.sum(mine, axis=0, keepdims=True)
            first = row * chunks % part_rows
            spot = slice(first, first + chunks)
            at = row * chunks // part_rows * lanes
            total = None
            for chip in range(chips):
                values = parts[chip][spot, width + at : width + at + lanes].astype(f32)
                term = column(mine, experts[chip]) * values
                total = term if total is None else total + term
            last_in[spot, at : at + lanes] = total.astype(bf16)
    at = slice(hop * part_rows, (hop + 1) * part_rows)
    table = kept[at, :].astype(f32) + found[at, :].astype(f32)
    total = None if hop else own[:, :width].astype(f32)
    for chip in range(chips):
        term = column(table, experts[chip]) * parts[chip][:, :width].astype(f32)
        total = term if total is None else total + term
    out[:, :width] = total.astype(out.dtype)
    if hop:
        out[:, width:] = last_in[...]


def finish_kernel(near, own_last, last_sum, *refs):
    parts, out = refs[:-1], refs[-1]
    width = near.shape[1]
    total = near[...]
    last = last_sum[...].astype(f32)
    for part in parts:
        total = total + part[:, :width].astype(f32)
        last = last + part[:, width:].astype(f32)
    out[:, :width] = total.astype(bf16)
    out[:, width:] = (own_last[...] + last).astype(bf16)


def collect_rows(lane, pieces, flat, width):
    part_rows, chunks = pieces[0].shape[0], width // lanes
    count = len(pieces)
    size = flat.shape[0] // count
    for index in range(count):
        source = lane ^ (2 * (index % (count // 2))) ^ (index // (count // 2))
        for first in range(0, size, part_rows):
            at = width + first // part_rows * lanes
            start = pl.multiple_of(source * size + first, part_rows)
            flat[pl.ds(start, part_rows), :] = pieces[index][:, at : at + lanes].astype(f32)
    rows = flat.shape[0] // chunks
    columns = [flat[pl.ds(chunk, rows, stride=chunks), :] for chunk in range(chunks)]
    return jnp.concatenate(columns, axis=1)


def both_ways(coefficient, unit, diagonal):
    count = unit.shape[0]
    if count > 32:
        high = lax.Precision.HIGHEST
        there = dot(coefficient, unit, ((1,), (0,)), high)
        return there + dot(coefficient, unit, ((0,), (0,)), high)
    total = None
    for index in range(count):
        line = jnp.where(diagonal, coefficient[index : index + 1, :], 0.0)
        factor = coefficient[:, index : index + 1] + jnp.sum(line, axis=1, keepdims=True)
        term = factor * unit[index : index + 1, :]
        total = term if total is None else total + term
    return total


def final_kernel(n_pieces, n_blocks, *refs):
    pieces, refs = refs[:n_pieces], refs[n_pieces:]
    last_all, projected, kept, found, partners, down, *refs = refs
    place = position()
    layer_out, grad_in, grad_out, made_in, made_out, flat, sems = refs
    part_rows, width = pieces[0].shape[0], layer_out.shape[1]
    copies = []

    def send(source, target):
        copies.append(pltpu.make_async_copy(source, target, sems.at[len(copies)]))
        copies[-1].start()

    for index in range(n_pieces):
        lane = place[1] ^ (2 * (index % (n_pieces // 2))) ^ (index // (n_pieces // 2))
        start = pl.multiple_of(lane * part_rows, part_rows)
        send(pieces[index].at[:, pl.ds(0, width)], layer_out.at[pl.ds(start, part_rows)])
    values = collect_rows(place[1], pieces, flat, width)
    count = values.shape[0]
    last = kept.shape[0] - count
    table = kept[last:, :].astype(f32) + found[last:, :].astype(f32)
    row = lax.broadcasted_iota(jnp.int32, (count, count), 0)
    col = lax.broadcasted_iota(jnp.int32, (count, count), 1)
    norms = jnp.sqrt(jnp.sum(values * values, axis=1, keepdims=True) + epsilon)
    norms_line = jnp.sum(jnp.where(row == col, norms, 0.0), axis=0, keepdims=True)
    unit = values / norms
    rows = values.astype(bf16)
    scores = dot(rows, rows, ((1,), (1,))) / (norms * norms_line) / logit_divisor
    exp_scores = jnp.where(row != col, jnp.exp(scores), 0.0)
    probabilities = exp_scores / jnp.sum(exp_scores, axis=1, keepdims=True)
    partner = partners[:, :1].astype(jnp.int32)
    coefficient = grad_scale * (probabilities - jnp.where(col == partner, 1.0, 0.0))
    grad_unit = both_ways(coefficient, unit, row == col) / logit_divisor
    projection = jnp.sum(unit * grad_unit, axis=1, keepdims=True)
    grad_last = (grad_unit - unit * projection) / norms
    route_grad = (column(table, place[2]) * grad_last).astype(bf16)
    gate, up, sigmoid_gate, activated = hidden_parts(projected[...])
    hidden = (activated * up).astype(bf16)
    grad_hidden = dot(route_grad, down[0], ((1,), (1,)))
    gate_slope = sigmoid_gate * (1.0 + gate * (1.0 - sigmoid_gate))
    slope = jnp.concatenate([grad_hidden * up * gate_slope, grad_hidden * activated], axis=1)
    slope = slope.astype(bf16)
    block = width // n_blocks
    for index in range(n_blocks):
        spot = slice(index * block, (index + 1) * block)
        made_in[spot, :] = dot(last_all[:, spot], slope, ((0,), (0,))).astype(bf16)
        send(made_in.at[spot], grad_in.at[0, spot])
    made_out[...] = dot(hidden, route_grad, ((0,), (0,))).astype(bf16)
    send(made_out, grad_out.at[0])
    for copy in copies:
        copy.wait()


def body(tokens, expert_ids, gates, positives, gate_up, down):
    dp_count = lax.axis_size("dp")
    expert_count = lax.axis_size("expert")
    chips = expert_count // 2
    experts = dp_count * chips
    tok_dev, width = tokens.shape
    half_width = down.shape[1]
    seq_dev = positives.shape[0]
    seqs = dp_count * seq_dev
    seq_length = tok_dev // seq_dev
    part_rows = tok_dev // expert_count
    assert experts <= lanes and seq_length % tail == 0

    def to_lane(value, step):
        return lax.ppermute(value, "expert", [(j, j ^ step) for j in range(expert_count)])

    def to_plane(value, step):
        return lax.ppermute(value, "dp", [(p, p ^ step) for p in range(dp_count)])

    chip_steps = [2 * step for step in range(1, chips)]
    groups = [range(first, min(first + 2, dp_count)) for first in range(0, dp_count, 2)]

    share = width // chips
    packed = pl.pallas_call(
        functools.partial(pack_kernel, seq_dev),
        out_shape=jax.ShapeDtypeStruct((part_rows, width + lanes), bf16),
        in_specs=[in_hbm] * 4,
        out_specs=in_vmem,
        scratch_shapes=[
            pltpu.VMEM((part_rows, lanes), f32),
            pltpu.VMEM((seq_dev, tail, share), bf16),
            pltpu.VMEM((1, tok_dev), jnp.int32),
            pltpu.VMEM((1, tok_dev), f32),
            pltpu.SMEM((seq_dev,), jnp.int32),
            pltpu.SemaphoreType.DMA((seq_dev + 4,)),
        ],
        cost_estimate=cost(0, 1 << 19),
        name="pack",
    )(positives, expert_ids.T, gates.T, tokens)
    arrivals = {hop: to_plane(packed, hop) for hop in range(1, dp_count)}
    mate_in = to_lane(gate_up, 1)
    mate_out = to_lane(down, 1)
    weights = (gate_up, down, mate_in, mate_out)

    tiles = [packed]
    spots = {}
    received = None
    for group in groups:
        own = [arrivals[hop] for hop in group if hop]
        if group[0] == 0:
            joined = jnp.concatenate(own + [packed[:, width:]], axis=1)
            joined, weights = lax.optimization_barrier((joined, weights))
        else:
            joined = jnp.concatenate(own, axis=0)
            joined, received = lax.optimization_barrier((joined, received))
            tiles[-len(received) :] = received
        first = len(tiles)
        received = [to_lane(joined, step) for step in chip_steps]
        tiles += own + received
        for index, hop in enumerate(group):
            if group[0] == 0:
                place_of = (first, 0, width) if hop else (0, 0, width)
                row, at = 0, width if hop else width + lanes
            else:
                place_of = (first + index, 0, width)
                row, at = index * part_rows, width
            spots[hop] = [place_of] + [
                (first + len(own) + chip, row, at) for chip in range(chips - 1)
            ]
    where_tiles = [spots[hop] for hop in range(dp_count)]

    each = seqs // expert_count
    extra = each * width // part_rows
    assert extra % lanes == 0 and part_rows % (width // lanes) == 0

    def expert(group, after, with_last):
        near = 0 in group
        wanted = range(dp_count) if with_last else [hop for hop in group if hop]
        used = sorted({spot[0] for hop in wanted for spot in where_tiles[hop]})
        parts = [tiles[index] for index in used]
        n_outs = chips * len(group)
        total = n_outs * part_rows + (seqs if with_last else 0)
        out_shape = [jax.ShapeDtypeStruct((part_rows, width), bf16)] * n_outs
        scratch = [pltpu.VMEM((total, width), bf16)]
        if with_last:
            wider = jax.ShapeDtypeStruct((part_rows, width + extra), bf16)
            out_shape[n_outs - chips :] = [wider] * chips
            out_shape += [
                jax.ShapeDtypeStruct((seqs, width), bf16),
                jax.ShapeDtypeStruct((seqs, 2 * half_width), f32),
                jax.ShapeDtypeStruct((part_rows, extra), f32),
            ]
            scratch = [
                pltpu.VMEM((seqs * (width // lanes), lanes), f32),
                pltpu.VMEM((dp_count, width // lanes, -(-seq_dev // 8) * 8, lanes), f32),
            ] + scratch
        if after is not None:
            parts[0], _ = lax.optimization_barrier((parts[0], after))
        scratch.append(pltpu.SemaphoreType.DMA((chips,)))
        operands = [tokens] * near + parts + list(weights)
        layout = (tuple(group), chips, part_rows, seq_dev, where_tiles, used, with_last)
        return pl.pallas_call(
            functools.partial(expert_kernel, layout),
            out_shape=out_shape,
            in_specs=[in_hbm] * near + [in_vmem] * (len(operands) - near),
            out_specs=[in_vmem] * len(out_shape),
            scratch_shapes=scratch,
            compiler_params=params(32),
            cost_estimate=cost(2 * total * width * 6 * half_width, 12 << 20),
            name="experts",
        )(*operands)

    outs = {}
    after = None
    rest = list(range(dp_count - 2, 1, -1))
    for group in groups:
        with_last = dp_count - 1 in group
        out = expert(group, after, with_last)
        after = out[0]
        for index, hop in enumerate(group):
            outs[hop] = list(out[index * chips : (index + 1) * chips])
        if with_last:
            last_all, last_projected, own_last = out[-3:]
            first_tile, _ = lax.optimization_barrier((tiles[0], out[0]))

    table_rows = dp_count * part_rows + seqs
    chunks = width // lanes
    sublanes = -(-seq_dev // 8) * 8
    tiles[0] = first_tile
    kept, sent, partners = pl.pallas_call(
        functools.partial(table_kernel, (seq_dev, tok_dev, where_tiles, len(tiles))),
        out_shape=[
            jax.ShapeDtypeStruct((table_rows, lanes), bf16),
            jax.ShapeDtypeStruct((table_rows, lanes), bf16),
            jax.ShapeDtypeStruct((seqs, lanes), f32),
        ],
        in_specs=[in_vmem] * len(tiles),
        out_specs=[in_vmem] * 3,
        scratch_shapes=[
            pltpu.VMEM((dp_count, sublanes, lanes), f32),
            pltpu.VMEM((dp_count, sublanes, lanes), f32),
        ],
        compiler_params=params(48 if dp_count > 8 else 12),
        cost_estimate=cost(0, 1 << 20),
        name="tables",
    )(*tiles)
    found = to_lane(sent, 1)

    def combine(hop, parts, last_sum):
        with_last = last_sum is None
        out_shape = [jax.ShapeDtypeStruct((part_rows, width), f32)]
        if hop:
            out_shape = [jax.ShapeDtypeStruct((part_rows, width + extra), bf16)]
        if with_last:
            out_shape.append(jax.ShapeDtypeStruct((part_rows, extra), bf16))
        operands = [kept, found] + [packed] * (hop == 0)
        operands += [last_sum] * (hop > 0 and not with_last) + parts
        return pl.pallas_call(
            functools.partial(combine_kernel, (hop, chips, with_last, width, each)),
            out_shape=out_shape,
            in_specs=[in_vmem] * len(operands),
            out_specs=[in_vmem] * len(out_shape),
            compiler_params=params(8),
            cost_estimate=cost(0, 2 << 20),
            name="combine",
        )(*operands)

    returned = {}

    def send_back(hop, gated, after):
        first, *parts = outs[hop]
        free = len(parts) - gated
        parts[free:], after = lax.optimization_barrier((parts[free:], after))
        returned[hop] = [first] + [to_lane(value, step) for value, step in zip(parts, chip_steps)]
        return after

    send_back(1, 0, [])
    if dp_count > 2:
        returned[1][1:] = send_back(dp_count - 1, chips - 1, returned[1][1:])
    before = dp_count - 1
    for hop in rest:
        returned[before][-1], found = send_back(hop, 1, (returned[before][-1], found))
        before = hop
    homeward = []
    last_sum = None
    for hop in range(dp_count - 1, 0, -1):
        result = combine(hop, returned[hop], last_sum)
        last_sum = result[1] if last_sum is None else last_sum
        homeward.append(to_plane(result[0], hop))
        if hop == min(3, dp_count - 1):
            gate = result[0]
    outs[0][1:], gate = lax.optimization_barrier((outs[0][1:], gate))
    send_back(0, 0, [])
    near_sum = combine(0, returned[0], last_sum)[0]

    own_out = pl.pallas_call(
        finish_kernel,
        out_shape=jax.ShapeDtypeStruct((part_rows, width + extra), bf16),
        in_specs=[in_vmem] * (2 + dp_count),
        out_specs=in_vmem,
        compiler_params=params(16 if dp_count > 8 else 4),
        cost_estimate=cost(0, 1 << 20),
        name="finish",
    )(near_sum, own_last, last_sum, *homeward)
    pieces = [own_out] + [to_lane(own_out, step) for step in chip_steps]
    pieces += [to_lane(piece, 1) for piece in pieces]

    n_blocks = width // min(512, width)
    layer_out, grad_gate_up, grad_down = pl.pallas_call(
        functools.partial(final_kernel, len(pieces), n_blocks),
        out_shape=[
            jax.ShapeDtypeStruct((tok_dev, width), bf16),
            jax.ShapeDtypeStruct(gate_up.shape, bf16),
            jax.ShapeDtypeStruct(down.shape, bf16),
        ],
        in_specs=[in_vmem] * (len(pieces) + 6),
        out_specs=[in_hbm] * 3,
        scratch_shapes=[
            pltpu.VMEM((width, 2 * half_width), bf16),
            pltpu.VMEM((half_width, width), bf16),
            pltpu.VMEM((seqs * (width // lanes), lanes), f32),
            pltpu.SemaphoreType.DMA((len(pieces) + n_blocks + 1,)),
        ],
        compiler_params=params(24),
        cost_estimate=cost(2 * seqs * width * 4 * half_width, 7 << 20),
        name="final",
    )(*pieces, last_all, last_projected, kept, found, partners, down)
    return (layer_out, grad_gate_up, grad_down)


def solution(mesh):
    return jax.shard_map(
        body,
        mesh=mesh,
        in_specs=(
            P("dp", None),
            P("dp", "expert"),
            P("dp", "expert"),
            P("dp"),
            P(("dp", "expert"), None, None),
            P(("dp", "expert"), None, None),
        ),
        out_specs=(P("dp", None), P(("dp", "expert"), None, None), P(("dp", "expert"), None, None)),
        check_vma=False,
    )
```

```python
import functools

import jax
import jax.numpy as jnp
from jax import lax
from jax.experimental import pallas as pl
from jax.experimental.pallas import tpu as pltpu
from jax.sharding import PartitionSpec as P

logit_divisor = 0.05
grad_scale = 256.0
epsilon = 1e-06
lanes = 128
tail = 16
bf16 = jnp.bfloat16
f32 = jnp.float32

in_hbm = pl.BlockSpec(memory_space=pltpu.HBM)
in_vmem = pl.BlockSpec(memory_space=pltpu.VMEM)


def params(mebibytes):
    return pltpu.CompilerParams(vmem_limit_bytes=mebibytes << 20)


def cost(flops, moved):
    return pl.CostEstimate(flops=flops, transcendentals=0, bytes_accessed=moved)


def dot(left, right, dims=((1,), (0,)), precision=None):
    return lax.dot_general(
        left, right, (dims, ((), ())), precision=precision, preferred_element_type=f32
    )


def doublings(count):
    steps = [1 << bit for bit in range((count - 1).bit_length())]
    assert 1 << len(steps) == count
    return steps


def position():
    plane, lane = lax.axis_index("dp"), lax.axis_index("expert")
    return plane, lane, plane * (lax.axis_size("expert") // 2) + lane // 2


def column(table, wanted):
    index = lax.broadcasted_iota(jnp.int32, table.shape, 1)
    return jnp.sum(jnp.where(index == wanted, table, 0.0), axis=1, keepdims=True)


def pack_kernel(
    seq_dev, partners, ids_in, gates_in, tokens, out, tile, rows, ids, gates, positives, sems
):
    part_rows, width = out.shape[0], tokens.shape[1]
    tok_dev = tokens.shape[0]
    seq_length = tok_dev // seq_dev
    share = rows.shape[2]
    lane = lax.axis_index("expert")
    column_at = pl.multiple_of(lane // 2 * share, lanes)
    start = pl.multiple_of(lane * part_rows, part_rows)
    copies = [
        pltpu.make_async_copy(
            tokens.at[pl.ds((seq + 1) * seq_length - tail, tail), pl.ds(column_at, share)],
            rows.at[seq],
            sems.at[seq],
        )
        for seq in range(seq_dev)
    ]
    own = pltpu.make_async_copy(
        tokens.at[pl.ds(start, part_rows)], out.at[:, pl.ds(0, width)], sems.at[seq_dev]
    )
    lines = [
        pltpu.make_async_copy(ids_in, ids, sems.at[seq_dev + 1]),
        pltpu.make_async_copy(gates_in, gates, sems.at[seq_dev + 2]),
        pltpu.make_async_copy(partners, positives, sems.at[seq_dev + 3]),
    ]
    for copy in lines + [own] + copies:
        copy.start()
    note_rows = tok_dev // lanes
    tile[...] = jnp.zeros_like(tile)
    for copy in lines:
        copy.wait()
    for index in range(note_rows):
        block = slice(index * lanes, (index + 1) * lanes)
        tile[index : index + 1, :] = ids[:, block].astype(f32)
        tile[note_rows + index : note_rows + index + 1, :] = gates[:, block]
    for seq in range(seq_dev):
        row = 2 * note_rows + seq
        tile[row : row + 1, :] = jnp.full((1, lanes), positives[seq], jnp.int32).astype(f32)
    base = part_rows - seq_dev * (share // lanes)
    for seq in range(seq_dev):
        copies[seq].wait()
        values = rows[seq].astype(f32)
        for chunk in range(share // lanes):
            row = base + chunk * seq_dev + seq
            tile[row : row + 1, :] = values[tail - 1 : tail, chunk * lanes : (chunk + 1) * lanes]
    out[:, width:] = tile[...].astype(bf16)
    own.wait()


def table_kernel(layout, *refs):
    seq_dev, tok_dev, where_tiles, n_parts = layout
    place = position()
    parts = refs[:n_parts]
    kept, sent, partners, routes, marks = refs[n_parts:]
    part_rows = parts[0].shape[0]
    dp_count = len(where_tiles)
    note_rows = tok_dev // lanes
    seq_length = tok_dev // seq_dev
    chips = len(where_tiles[0])
    lane_index = lax.broadcasted_iota(jnp.int32, (part_rows, lanes), 1)
    row_index = lax.broadcasted_iota(jnp.int32, (part_rows, lanes), 0)

    def dense_rows(tile, lane):
        start = lane * part_rows
        picked = lane_index == row_index + start % lanes
        found = []
        for offset in (0, note_rows):
            line = tile[offset : offset + 1, :]
            for index in range(1, note_rows):
                other = tile[offset + index : offset + index + 1, :]
                line = jnp.where(start // lanes == index, other, line)
            found.append(jnp.sum(jnp.where(picked, line, 0.0), axis=1, keepdims=True))
        return jnp.where(lane_index.astype(f32) == found[0], found[1], 0.0)

    for hop in range(dp_count):
        plane = place[0] ^ hop
        sums = [None, None]
        for chip in range(chips):
            source, row, at = where_tiles[hop][chip]
            tile = parts[source][row : row + part_rows, at : at + lanes].astype(f32)
            for index, lane in enumerate((place[1], place[1] ^ 1)):
                value = dense_rows(tile, lane)
                sums[index] = value if chip == 0 else sums[index] + value
            for seq in range(seq_dev):
                at_token = (seq + 1) * seq_length - 1
                row = at_token // lanes
                here = lane_index[:1] == at_token % lanes
                expert, gate = [
                    jnp.sum(
                        jnp.where(here, tile[offset + row : offset + row + 1, :], 0.0),
                        axis=1,
                        keepdims=True,
                    )
                    for offset in (0, note_rows)
                ]
                value = jnp.where(lane_index[:1].astype(f32) == expert, gate, 0.0)
                if chip:
                    value = value + routes[plane, seq : seq + 1, :]
                routes[plane, seq : seq + 1, :] = value
            if chip == 0:
                marks[plane, 0:seq_dev, :] = tile[2 * note_rows : 2 * note_rows + seq_dev, :]
        at = slice(hop * part_rows, (hop + 1) * part_rows)
        kept[at, :] = sums[0].astype(bf16)
        sent[at, :] = sums[1].astype(bf16)
    last = dp_count * part_rows
    shared = []
    for plane in range(dp_count):
        shared.append(routes[plane, 0:seq_dev, :])
        partners[plane * seq_dev : (plane + 1) * seq_dev, :] = marks[plane, 0:seq_dev, :]
    seqs = dp_count * seq_dev
    value = jnp.concatenate(shared, axis=0).astype(bf16)
    kept[last : last + seqs, :] = value
    sent[last : last + seqs, :] = value


def hidden_parts(projected):
    half_width = projected.shape[1] // 2
    gate, up = projected[:, :half_width], projected[:, half_width:]
    sigmoid_gate = jax.nn.sigmoid(gate)
    return gate, up, sigmoid_gate, gate * sigmoid_gate


def spread_rows(values, flat):
    count, chunks = values.shape[0], values.shape[1] // lanes
    for chunk in range(chunks):
        flat[pl.ds(chunk, count, stride=chunks), :] = values[:, chunk * lanes : (chunk + 1) * lanes]


def share_of(flat, lane, each, part_rows, chunks):
    size = each * chunks
    start = lane * size
    blocks = [
        flat[pl.ds(pl.multiple_of(start + first, part_rows), part_rows), :]
        for first in range(0, size, part_rows)
    ]
    return blocks[0] if len(blocks) == 1 else jnp.concatenate(blocks, axis=1)


def last_tokens(place, seq_dev, where_tiles, parts, tokens):
    part_rows = parts[0].shape[0]
    dp_count, chunks = tokens.shape[:2]
    chips = len(where_tiles[0])
    share_chunks = chunks // chips
    base = part_rows - seq_dev * share_chunks
    for hop in range(dp_count):
        for chip in range(chips):
            source, row, at = where_tiles[hop][chip]
            tile = parts[source][row : row + part_rows, at : at + lanes].astype(f32)
            first = ((place[1] // 2) ^ chip) * share_chunks
            for chunk in range(share_chunks):
                row = base + chunk * seq_dev
                tokens[place[0] ^ hop, first + chunk, 0:seq_dev, :] = tile[row : row + seq_dev, :]
    joined = []
    for plane in range(dp_count):
        lines = [tokens[plane, chunk, 0:seq_dev, :] for chunk in range(chunks)]
        joined.append(jnp.concatenate(lines, axis=1))
    return jnp.concatenate(joined, axis=0)


def expert_kernel(layout, *refs):
    group, chips, part_rows, seq_dev, where_tiles, used, with_last = layout
    refs = list(refs)
    place = position()
    near = 0 in group
    tokens = refs.pop(0) if near else None
    parts, refs = dict(zip(used, refs)), refs[len(used) :]
    weights, refs = refs[:4], refs[4:]
    n_outs = chips * len(group)
    outs, refs = refs[:n_outs], refs[n_outs:]
    if with_last:
        last_all, last_projected, own_last, flat, seq_tokens, *refs = refs
    (rows,) = refs
    width = weights[0].shape[1]
    total = n_outs * part_rows
    spots = [slice(index * part_rows, (index + 1) * part_rows) for index in range(n_outs)]
    for index, spot in enumerate(spots):
        hop, chip = group[index // chips], index % chips
        if hop:
            source, row, _ = where_tiles[hop][chip]
            rows[spot, :] = parts[source][row : row + part_rows, :width]
        else:
            start = pl.multiple_of((place[1] ^ (2 * chip)) * part_rows, part_rows)
            rows[spot, :] = tokens[pl.ds(start, part_rows), :]
    if with_last:
        floats = last_tokens(place, seq_dev, where_tiles, parts, seq_tokens)
        last_all[...] = floats.astype(bf16)
        rows[total:, :] = floats.astype(bf16)
    hidden = []
    for half in range(2):
        projected = dot(rows[...], weights[2 * half][0])
        if half == 0 and with_last:
            last_projected[...] = projected[total:]
        _, up, _, activated = hidden_parts(projected)
        hidden.append((activated * up).astype(bf16))
    block = min(512, width)
    chunks = width // lanes
    for first in range(0, width, block):
        columns = slice(first, first + block)
        result = dot(hidden[0], weights[1][0, :, columns]) + dot(
            hidden[1], weights[3][0, :, columns]
        )
        for out, spot in zip(outs, spots):
            out[:, columns] = result[spot].astype(bf16)
        if with_last:
            count = result.shape[0] - total
            for at in range(0, block, lanes):
                flat[pl.ds((first + at) // lanes, count, stride=chunks), :] = result[
                    total:, at : at + lanes
                ]
    if with_last:
        each = floats.shape[0] // (2 * chips)
        for chip in range(chips):
            share = share_of(flat, place[1] ^ (2 * chip), each, part_rows, chunks)
            outs[n_outs - chips + chip][:, width:] = share.astype(bf16)
        spread_rows(floats, flat)
        own_last[...] = share_of(flat, place[1], each, part_rows, chunks)


def combine_kernel(layout, kept, found, *refs):
    hop, chips, with_last, width, each = layout
    place = position()
    own, refs = (refs[0], refs[1:]) if hop == 0 else (None, refs)
    last_in, refs = (refs[0], refs[1:]) if hop and not with_last else (None, refs)
    parts, out = refs[:chips], refs[chips]
    part_rows = out.shape[0]
    first_expert = place[2] - place[1] // 2
    experts = [first_expert + ((place[1] // 2) ^ chip) for chip in range(chips)]
    if with_last:
        last_in = refs[-1]
        table = kept[-2 * chips * each :, :].astype(f32) + found[-2 * chips * each :, :].astype(f32)
        row_index = lax.broadcasted_iota(jnp.int32, table.shape, 0)
        chunks = width // lanes
        for row in range(each):
            mine = jnp.where(row_index == place[1] * each + row, table, 0.0)
            mine = jnp.sum(mine, axis=0, keepdims=True)
            first = row * chunks % part_rows
            spot = slice(first, first + chunks)
            at = row * chunks // part_rows * lanes
            total = None
            for chip in range(chips):
                values = parts[chip][spot, width + at : width + at + lanes].astype(f32)
                term = column(mine, experts[chip]) * values
                total = term if total is None else total + term
            last_in[spot, at : at + lanes] = total.astype(bf16)
    at = slice(hop * part_rows, (hop + 1) * part_rows)
    table = kept[at, :].astype(f32) + found[at, :].astype(f32)
    total = None if hop else own[:, :width].astype(f32)
    for chip in range(chips):
        term = column(table, experts[chip]) * parts[chip][:, :width].astype(f32)
        total = term if total is None else total + term
    out[:, :width] = total.astype(out.dtype)
    if hop:
        out[:, width:] = last_in[...]


def finish_kernel(near, own_last, last_sum, *refs):
    parts, out = refs[:-1], refs[-1]
    width = near.shape[1]
    total = near[...]
    last = last_sum[...].astype(f32)
    for part in parts:
        total = total + part[:, :width].astype(f32)
        last = last + part[:, width:].astype(f32)
    out[:, :width] = total.astype(bf16)
    out[:, width:] = (own_last[...] + last).astype(bf16)


def collect_rows(lane, pieces, flat, width):
    part_rows, chunks = pieces[0].shape[0], width // lanes
    count = len(pieces)
    size = flat.shape[0] // count
    for index in range(count):
        source = lane ^ (2 * (index % (count // 2))) ^ (index // (count // 2))
        for first in range(0, size, part_rows):
            at = width + first // part_rows * lanes
            start = pl.multiple_of(source * size + first, part_rows)
            flat[pl.ds(start, part_rows), :] = pieces[index][:, at : at + lanes].astype(f32)
    rows = flat.shape[0] // chunks
    columns = [flat[pl.ds(chunk, rows, stride=chunks), :] for chunk in range(chunks)]
    return jnp.concatenate(columns, axis=1)


def both_ways(coefficient, unit, diagonal):
    count = unit.shape[0]
    if count > 32:
        high = lax.Precision.HIGHEST
        there = dot(coefficient, unit, ((1,), (0,)), high)
        return there + dot(coefficient, unit, ((0,), (0,)), high)
    total = None
    for index in range(count):
        line = jnp.where(diagonal, coefficient[index : index + 1, :], 0.0)
        factor = coefficient[:, index : index + 1] + jnp.sum(line, axis=1, keepdims=True)
        term = factor * unit[index : index + 1, :]
        total = term if total is None else total + term
    return total


def final_kernel(n_pieces, n_blocks, *refs):
    pieces, refs = refs[:n_pieces], refs[n_pieces:]
    last_all, projected, kept, found, partners, down, *refs = refs
    place = position()
    layer_out, grad_in, grad_out, made_in, made_out, flat, sems = refs
    part_rows, width = pieces[0].shape[0], layer_out.shape[1]
    copies = []

    def send(source, target):
        copies.append(pltpu.make_async_copy(source, target, sems.at[len(copies)]))
        copies[-1].start()

    for index in range(n_pieces):
        lane = place[1] ^ (2 * (index % (n_pieces // 2))) ^ (index // (n_pieces // 2))
        start = pl.multiple_of(lane * part_rows, part_rows)
        send(pieces[index].at[:, pl.ds(0, width)], layer_out.at[pl.ds(start, part_rows)])
    values = collect_rows(place[1], pieces, flat, width)
    count = values.shape[0]
    last = kept.shape[0] - count
    table = kept[last:, :].astype(f32) + found[last:, :].astype(f32)
    row = lax.broadcasted_iota(jnp.int32, (count, count), 0)
    col = lax.broadcasted_iota(jnp.int32, (count, count), 1)
    norms = jnp.sqrt(jnp.sum(values * values, axis=1, keepdims=True) + epsilon)
    norms_line = jnp.sum(jnp.where(row == col, norms, 0.0), axis=0, keepdims=True)
    unit = values / norms
    rows = values.astype(bf16)
    scores = dot(rows, rows, ((1,), (1,))) / (norms * norms_line) / logit_divisor
    exp_scores = jnp.where(row != col, jnp.exp(scores), 0.0)
    probabilities = exp_scores / jnp.sum(exp_scores, axis=1, keepdims=True)
    partner = partners[:, :1].astype(jnp.int32)
    coefficient = grad_scale * (probabilities - jnp.where(col == partner, 1.0, 0.0))
    grad_unit = both_ways(coefficient, unit, row == col) / logit_divisor
    projection = jnp.sum(unit * grad_unit, axis=1, keepdims=True)
    grad_last = (grad_unit - unit * projection) / norms
    route_grad = (column(table, place[2]) * grad_last).astype(bf16)
    gate, up, sigmoid_gate, activated = hidden_parts(projected[...])
    hidden = (activated * up).astype(bf16)
    grad_hidden = dot(route_grad, down[0], ((1,), (1,)))
    gate_slope = sigmoid_gate * (1.0 + gate * (1.0 - sigmoid_gate))
    slope = jnp.concatenate([grad_hidden * up * gate_slope, grad_hidden * activated], axis=1)
    slope = slope.astype(bf16)
    block = width // n_blocks
    for index in range(n_blocks):
        spot = slice(index * block, (index + 1) * block)
        made_in[spot, :] = dot(last_all[:, spot], slope, ((0,), (0,))).astype(bf16)
        send(made_in.at[spot], grad_in.at[0, spot])
        if index == 0:
            made_out[...] = dot(hidden, route_grad, ((0,), (0,))).astype(bf16)
            send(made_out, grad_out.at[0])
    for copy in copies:
        copy.wait()


def body(tokens, expert_ids, gates, positives, gate_up, down):
    dp_count = lax.axis_size("dp")
    expert_count = lax.axis_size("expert")
    chips = expert_count // 2
    experts = dp_count * chips
    tok_dev, width = tokens.shape
    half_width = down.shape[1]
    seq_dev = positives.shape[0]
    seqs = dp_count * seq_dev
    seq_length = tok_dev // seq_dev
    part_rows = tok_dev // expert_count
    assert experts <= lanes and seq_length % tail == 0

    def to_lane(value, step):
        return lax.ppermute(value, "expert", [(j, j ^ step) for j in range(expert_count)])

    def to_plane(value, step):
        return lax.ppermute(value, "dp", [(p, p ^ step) for p in range(dp_count)])

    chip_steps = [2 * step for step in range(1, chips)]
    groups = [range(first, min(first + 2, dp_count)) for first in range(0, dp_count, 2)]

    share = width // chips
    packed = pl.pallas_call(
        functools.partial(pack_kernel, seq_dev),
        out_shape=jax.ShapeDtypeStruct((part_rows, width + lanes), bf16),
        in_specs=[in_hbm] * 4,
        out_specs=in_vmem,
        scratch_shapes=[
            pltpu.VMEM((part_rows, lanes), f32),
            pltpu.VMEM((seq_dev, tail, share), bf16),
            pltpu.VMEM((1, tok_dev), jnp.int32),
            pltpu.VMEM((1, tok_dev), f32),
            pltpu.SMEM((seq_dev,), jnp.int32),
            pltpu.SemaphoreType.DMA((seq_dev + 4,)),
        ],
        cost_estimate=cost(0, 1 << 19),
        name="pack",
    )(positives, expert_ids.T, gates.T, tokens)
    arrivals = {hop: to_plane(packed, hop) for hop in range(1, dp_count)}
    mate_in = to_lane(gate_up, 1)
    mate_out = to_lane(down, 1)
    weights = (gate_up, down, mate_in, mate_out)

    tiles = [packed]
    spots = {}
    received = None
    for group in groups:
        own = [arrivals[hop] for hop in group if hop]
        if group[0] == 0:
            joined = jnp.concatenate(own + [packed[:, width:]], axis=1)
            joined, weights = lax.optimization_barrier((joined, weights))
        else:
            joined = jnp.concatenate(own, axis=0)
            joined, received = lax.optimization_barrier((joined, received))
            tiles[-len(received) :] = received
        first = len(tiles)
        received = [to_lane(joined, step) for step in chip_steps]
        tiles += own + received
        for index, hop in enumerate(group):
            if group[0] == 0:
                place_of = (first, 0, width) if hop else (0, 0, width)
                row, at = 0, width if hop else width + lanes
            else:
                place_of = (first + index, 0, width)
                row, at = index * part_rows, width
            spots[hop] = [place_of] + [
                (first + len(own) + chip, row, at) for chip in range(chips - 1)
            ]
    where_tiles = [spots[hop] for hop in range(dp_count)]

    each = seqs // expert_count
    extra = each * width // part_rows
    assert extra % lanes == 0 and part_rows % (width // lanes) == 0

    def expert(group, after, with_last):
        near = 0 in group
        wanted = range(dp_count) if with_last else [hop for hop in group if hop]
        used = sorted({spot[0] for hop in wanted for spot in where_tiles[hop]})
        parts = [tiles[index] for index in used]
        n_outs = chips * len(group)
        total = n_outs * part_rows + (seqs if with_last else 0)
        out_shape = [jax.ShapeDtypeStruct((part_rows, width), bf16)] * n_outs
        scratch = [pltpu.VMEM((total, width), bf16)]
        if with_last:
            wider = jax.ShapeDtypeStruct((part_rows, width + extra), bf16)
            out_shape[n_outs - chips :] = [wider] * chips
            out_shape += [
                jax.ShapeDtypeStruct((seqs, width), bf16),
                jax.ShapeDtypeStruct((seqs, 2 * half_width), f32),
                jax.ShapeDtypeStruct((part_rows, extra), f32),
            ]
            scratch = [
                pltpu.VMEM((seqs * (width // lanes), lanes), f32),
                pltpu.VMEM((dp_count, width // lanes, -(-seq_dev // 8) * 8, lanes), f32),
            ] + scratch
        if after is not None:
            parts[0], _ = lax.optimization_barrier((parts[0], after))
        operands = [tokens] * near + parts + list(weights)
        layout = (tuple(group), chips, part_rows, seq_dev, where_tiles, used, with_last)
        return pl.pallas_call(
            functools.partial(expert_kernel, layout),
            out_shape=out_shape,
            in_specs=[in_vmem] * len(operands),
            out_specs=[in_vmem] * len(out_shape),
            scratch_shapes=scratch,
            compiler_params=params(32),
            cost_estimate=cost(2 * total * width * 6 * half_width, 12 << 20),
            name="experts",
        )(*operands)

    outs = {}
    after = None
    rest = list(range(dp_count - 2, 1, -1))
    for group in groups:
        with_last = dp_count - 1 in group
        out = expert(group, after, with_last)
        after = out[0]
        for index, hop in enumerate(group):
            outs[hop] = list(out[index * chips : (index + 1) * chips])
        if with_last:
            last_all, last_projected, own_last = out[-3:]
            first_tile, _ = lax.optimization_barrier((tiles[0], out[0]))

    table_rows = dp_count * part_rows + seqs
    chunks = width // lanes
    sublanes = -(-seq_dev // 8) * 8
    tiles[0] = first_tile
    kept, sent, partners = pl.pallas_call(
        functools.partial(table_kernel, (seq_dev, tok_dev, where_tiles, len(tiles))),
        out_shape=[
            jax.ShapeDtypeStruct((table_rows, lanes), bf16),
            jax.ShapeDtypeStruct((table_rows, lanes), bf16),
            jax.ShapeDtypeStruct((seqs, lanes), f32),
        ],
        in_specs=[in_vmem] * len(tiles),
        out_specs=[in_vmem] * 3,
        scratch_shapes=[
            pltpu.VMEM((dp_count, sublanes, lanes), f32),
            pltpu.VMEM((dp_count, sublanes, lanes), f32),
        ],
        compiler_params=params(48 if dp_count > 8 else 12),
        cost_estimate=cost(0, 1 << 20),
        name="tables",
    )(*tiles)
    found = to_lane(sent, 1)

    def combine(hop, parts, last_sum):
        with_last = last_sum is None
        out_shape = [jax.ShapeDtypeStruct((part_rows, width), f32)]
        if hop:
            out_shape = [jax.ShapeDtypeStruct((part_rows, width + extra), bf16)]
        if with_last:
            out_shape.append(jax.ShapeDtypeStruct((part_rows, extra), bf16))
        operands = [kept, found] + [packed] * (hop == 0)
        operands += [last_sum] * (hop > 0 and not with_last) + parts
        return pl.pallas_call(
            functools.partial(combine_kernel, (hop, chips, with_last, width, each)),
            out_shape=out_shape,
            in_specs=[in_vmem] * len(operands),
            out_specs=[in_vmem] * len(out_shape),
            compiler_params=params(8),
            cost_estimate=cost(0, 2 << 20),
            name="combine",
        )(*operands)

    returned = {}

    def send_back(hop, gated, after):
        first, *parts = outs[hop]
        free = len(parts) - gated
        parts[free:], after = lax.optimization_barrier((parts[free:], after))
        returned[hop] = [first] + [to_lane(value, step) for value, step in zip(parts, chip_steps)]
        return after

    send_back(1, 0, [])
    if dp_count > 2:
        returned[1][1:] = send_back(dp_count - 1, chips - 1, returned[1][1:])
    before = dp_count - 1
    for hop in rest:
        returned[before][-1], found = send_back(hop, 1, (returned[before][-1], found))
        before = hop
    homeward = []
    last_sum = None
    for hop in range(dp_count - 1, 0, -1):
        result = combine(hop, returned[hop], last_sum)
        last_sum = result[1] if last_sum is None else last_sum
        homeward.append(to_plane(result[0], hop))
        if hop == min(3, dp_count - 1):
            gate = result[0]
    outs[0][1:], gate = lax.optimization_barrier((outs[0][1:], gate))
    send_back(0, 0, [])
    near_sum = combine(0, returned[0], last_sum)[0]

    own_out = pl.pallas_call(
        finish_kernel,
        out_shape=jax.ShapeDtypeStruct((part_rows, width + extra), bf16),
        in_specs=[in_vmem] * (2 + dp_count),
        out_specs=in_vmem,
        compiler_params=params(16 if dp_count > 8 else 4),
        cost_estimate=cost(0, 1 << 20),
        name="finish",
    )(near_sum, own_last, last_sum, *homeward)
    pieces = [own_out] + [to_lane(own_out, step) for step in chip_steps]
    pieces += [to_lane(piece, 1) for piece in pieces]

    n_blocks = width // min(512, width)
    layer_out, grad_gate_up, grad_down = pl.pallas_call(
        functools.partial(final_kernel, len(pieces), n_blocks),
        out_shape=[
            jax.ShapeDtypeStruct((tok_dev, width), bf16),
            jax.ShapeDtypeStruct(gate_up.shape, bf16),
            jax.ShapeDtypeStruct(down.shape, bf16),
        ],
        in_specs=[in_vmem] * (len(pieces) + 6),
        out_specs=[in_hbm] * 3,
        scratch_shapes=[
            pltpu.VMEM((width, 2 * half_width), bf16),
            pltpu.VMEM((half_width, width), bf16),
            pltpu.VMEM((seqs * (width // lanes), lanes), f32),
            pltpu.SemaphoreType.DMA((len(pieces) + n_blocks + 1,)),
        ],
        compiler_params=params(24),
        cost_estimate=cost(2 * seqs * width * 4 * half_width, 7 << 20),
        name="final",
    )(*pieces, last_all, last_projected, kept, found, partners, down)
    return (layer_out, grad_gate_up, grad_down)


def solution(mesh):
    return jax.shard_map(
        body,
        mesh=mesh,
        in_specs=(
            P("dp", None),
            P("dp", "expert"),
            P("dp", "expert"),
            P("dp"),
            P(("dp", "expert"), None, None),
            P(("dp", "expert"), None, None),
        ),
        out_specs=(P("dp", None), P(("dp", "expert"), None, None), P(("dp", "expert"), None, None)),
        check_vma=False,
    )
```
